32 devices in a mesh: scale: 4 (over x, core), space: 8 (over z, y).
Axes of the slice: x: 2, y: 2, z: 4, core: 2. Of those that a mesh axis runs over, the one named last changes fastest.
Arguments:
- features: bfloat16 [4, 32, 128, 512], P('scale', 'space'), may hold values from -6 to 6
- valid_rows: int32 [4], replicated, may hold values from 8 to 32, as said below
- conv_master: float32 [3, 4608, 512], P(None, 'space'), may hold values from -0.125 to 0.125
- head_master: float32 [917504], P(('scale', 'space')), may hold values from -0.25 to 0.25
- vectors: float32 [5120], replicated
- conv_first: float32 [3, 4608, 512], P(None, 'space'), may hold values from -40 to 40
- conv_second: float32 [3, 4608, 512], P(None, 'space'), may hold values from 186.14845 to 744.5938
- head_first: float32 [917504], P(('scale', 'space')), may hold values from -40 to 40
- head_second: float32 [917504], P(('scale', 'space')), may hold values from 186.14845 to 744.5938
- vec_first: float32 [5120], replicated
- vec_second: float32 [5120], replicated
- statistics: float32 [3, 512, 512], replicated, as said below
- bases: float32 [3, 512, 512], replicated, as said below
- cotangent: bfloat16 [32, 128, 1792], P('space'), may hold values from -6 to 6
Outputs:
- merged: bfloat16 [32, 128, 1792], P('space')
- features_grad: bfloat16 [4, 32, 128, 512], P('scale', 'space')
- conv_first_new: float32 [3, 4608, 512], P(None, 'space')
- conv_second_new: float32 [3, 4608, 512], P(None, 'space')
- conv_new: float32 [3, 4608, 512], P(None, 'space')
- head_first_new: float32 [917504], P(('scale', 'space'))
- head_second_new: float32 [917504], P(('scale', 'space'))
- head_new: float32 [917504], P(('scale', 'space'))
- vec_first_new: float32 [5120], replicated
- vec_second_new: float32 [5120], replicated
- vec_new: float32 [5120], replicated
- statistics_new: float32 [3, 512, 512], replicated
- bases_new: float32 [3, 512, 512], replicated
The draws below stay inside these ranges and needn't reach their ends.
Inputs may be any that keep to these rules, and one draw needn't show every extreme that they name: `valid_rows`: one scale, drawn from the seed, fills all 32 rows. `statistics`: each matrix is symmetric positive definite. `bases`: each matrix is orthogonal.
All inputs are finite; a program needn't handle non-finite values.
Results may differ from the reference program's by a relative error of at most 0.014.
Values may be sent and summed in bfloat16 or wider, within the bound.
A program may use at most 256 MiB of HBM per device.

```python
import math
from functools import partial
import jax
import jax.numpy as jnp
from jax import lax

C = 512
NH = 7
HD = 256
LAYERS = 3
STEP = 5
WID = 128
GROUPS = 4
ROWS = 32
F = 1792
VEC = 5120


def pixel_root():
    return (0.6 * GROUPS * ROWS * WID) ** 0.5


def segment_scales():
    return jnp.concatenate([jnp.full((3 * C + F,), 0.7, jnp.float32), jnp.full((F,), 0.04, jnp.float32)]) * pixel_root()


def draw_valid_rows(key, part):
    key = jax.random.fold_in(key, 11)
    first_key, second_key = jax.random.split(key)
    drawn = jax.random.randint(first_key, (GROUPS,), ROWS // 4, ROWS + 1)
    filled = jax.random.randint(second_key, (), 0, GROUPS)
    return jnp.where(jnp.arange(GROUPS) == filled, ROWS, drawn).astype(jnp.int32)


def draw_vectors(key, part):
    key = jax.random.fold_in(key, 12)
    first_key, second_key = jax.random.split(key)
    biases = 0.3 * jax.random.normal(first_key, (3 * C + F,), jnp.float32)
    spread = jax.random.uniform(second_key, (F,), jnp.float32, math.log(0.8), math.log(1.25))
    rising = 8.0 * jnp.exp(math.log(3.0) * jnp.arange(F, dtype=jnp.float32) / F + spread)
    return jnp.concatenate([biases, rising])


def draw_vec_first(key, part):
    key = jax.random.fold_in(key, 13)
    return 0.111 * segment_scales() * jax.random.normal(key, (VEC,), jnp.float32)


def draw_vec_second(key, part):
    key = jax.random.fold_in(key, 14)
    factor = jnp.exp(jax.random.uniform(key, (VEC,), jnp.float32, 0.0, math.log(4.0)))
    scales = segment_scales()
    return 0.0526 * scales * scales * factor


def draw_statistics(key, part):
    key = jax.random.fold_in(key, 15)
    first_key, second_key = jax.random.split(key)
    unit = 0.0526 * 0.36 * 0.6 * GROUPS * ROWS * WID * 9 * C
    diagonal = unit * jnp.exp(jax.random.uniform(first_key, (LAYERS, C), jnp.float32, 0.0, math.log(4.0)))
    noise = jax.random.normal(second_key, (LAYERS, C, C), jnp.float32) * (0.2 * unit / math.sqrt(C))
    symmetric = 0.5 * (noise + jnp.transpose(noise, (0, 2, 1)))
    return symmetric + jnp.eye(C, dtype=jnp.float32)[None] * diagonal[:, :, None]


def draw_bases(key, part):
    key = jax.random.fold_in(key, 16)
    stacked = []
    for which_layer in range(LAYERS):
        layer_key = jax.random.fold_in(key, which_layer)
        sign_key, order_key = jax.random.split(layer_key)
        signs = jnp.where(jax.random.bernoulli(sign_key, 0.5, (C,)), 1.0, -1.0).astype(jnp.float32)
        order = jax.random.permutation(order_key, C)
        column = order.astype(jnp.float32)[None, :]
        position = jnp.arange(C, dtype=jnp.float32)[:, None] + 0.5
        norming = jnp.where(order[None, :] == 0, math.sqrt(1.0 / C), math.sqrt(2.0 / C))
        stacked.append(signs[:, None] * norming * jnp.cos(math.pi * position * column / C))
    return jnp.stack(stacked)


def block_levels(rng, dims, cuts, smallest, largest):
    level = 1.0
    for dim, blocks in cuts:
        steps = jax.random.uniform(jax.random.fold_in(jax.random.fold_in(rng, 6), dim), (blocks,), jnp.float32, smallest / len(cuts), largest / len(cuts))
        level = level * jnp.repeat(jnp.exp(steps), dims[dim] // blocks).reshape((-1,) + (1,) * (len(dims) - 1 - dim))
    return level


def bell_draw(stream_key, extent, scale, limit, pieces=(), kind=jnp.bfloat16):
    values = jax.random.normal(stream_key, extent, jnp.float32) * scale
    if len(pieces) > 0:
        values = block_levels(stream_key, extent, pieces, -0.22, 0.18) * values
    return jnp.clip(values, min=-limit, max=limit).astype(kind)


def setup_inputs(seed: int = 0) -> dict:
    keys = jax.random.split(jax.random.key(seed), 15)
    features = bell_draw(keys[0], (GROUPS, ROWS, WID, C), 1.0, 6.0, ((0, 4), (1, 8)))
    valid_rows = draw_valid_rows(jax.random.fold_in(keys[14], 71), 0)
    conv_master = bell_draw(keys[2], (LAYERS, 9 * C, C), (9 * C // 2) ** -0.5, 0.125, ((1, 8),), jnp.float32)
    head_master = bell_draw(keys[3], (C * F,), C ** -0.5, 0.25, ((0, 32),), jnp.float32)
    vectors = draw_vectors(jax.random.fold_in(keys[14], 71), 0)
    conv_first = bell_draw(keys[5], (LAYERS, 9 * C, C), (0.111 * 0.6 * (0.6 * GROUPS * ROWS * WID) ** 0.5), 40.0, ((1, 8),), jnp.float32)
    conv_second = jnp.clip(jnp.exp(math.log(744.5938) - 1.3862944 * jax.random.uniform(keys[6], (LAYERS, 9 * C, C), jnp.float32) ** block_levels(keys[6], (LAYERS, 9 * C, C), ((1, 8),), -0.2, 0.2)), 186.14845, 744.5938)
    head_first = bell_draw(keys[7], (C * F,), (0.111 * 0.6 * (0.6 * GROUPS * ROWS * WID) ** 0.5), 40.0, ((0, 32),), jnp.float32)
    head_second = jnp.clip(jnp.exp(math.log(744.5938) - 1.3862944 * jax.random.uniform(keys[8], (C * F,), jnp.float32) ** block_levels(keys[8], (C * F,), ((0, 32),), -0.2, 0.2)), 186.14845, 744.5938)
    vec_first = draw_vec_first(jax.random.fold_in(keys[14], 71), 0)
    vec_second = draw_vec_second(jax.random.fold_in(keys[14], 71), 0)
    statistics = draw_statistics(jax.random.fold_in(keys[14], 71), 0)
    bases = draw_bases(jax.random.fold_in(keys[14], 71), 0)
    cotangent = bell_draw(keys[13], (ROWS, WID, F), 1.0, 6.0, ((0, 8),))
    return dict(features=features, valid_rows=valid_rows, conv_master=conv_master, head_master=head_master, vectors=vectors, conv_first=conv_first, conv_second=conv_second, head_first=head_first, head_second=head_second, vec_first=vec_first, vec_second=vec_second, statistics=statistics, bases=bases, cotangent=cotangent)


BETA_ONE = 0.9
BETA_TWO = 0.95
EPSILON = 1e-08
DECAY = 0.01
RATE_CONV = 0.04
RATE_HEAD = 0.08
RATE_BIAS = 0.5
RATE_GAIN = 20.0

@jax.custom_vjp
def low(v):
    return lax.optimization_barrier(v.astype(jnp.bfloat16)).astype(jnp.float32)

@jax.custom_vjp
def low_back(v):
    return v

def low_keep(v):
    return (low(v), None)

def low_pass(kept, grad):
    return (grad,)

def back_keep(v):
    return (v, None)

def back_low(kept, grad):
    return (low(grad),)
low.defvjp(low_keep, low_pass)
low_back.defvjp(back_keep, back_low)

def convolve(active, kernel):
    return lax.conv_general_dilated(active, kernel, (1, 1), ((1, 1), (1, 1)), dimension_numbers=('NHWC', 'HWIO', 'NHWC'), precision=lax.Precision.HIGHEST, preferred_element_type=jnp.float32)

def forward(features, conv_w, head_w, vectors, valid_rows):
    conv_used = low(conv_w)
    head_used = low(head_w).reshape(C, F)
    conv_bias = vectors[:3 * C].reshape(3, C)
    head_bias = vectors[3 * C:3 * C + F]
    head_gain = vectors[3 * C + F:]
    row_masks = (jnp.arange(ROWS, dtype=jnp.int32)[None, :] < valid_rows[:, None]).astype(jnp.float32)
    counts = lax.optimization_barrier(jnp.sum(row_masks, 0))
    summed = jnp.zeros((ROWS, WID, F), jnp.float32)
    for which_group in range(GROUPS):
        active = features[which_group][None]
        row_mask = row_masks[which_group][None, :, None, None]
        for which_layer in range(3):
            inputs = low(active)
            kernel = conv_used[which_layer].reshape(3, 3, C, C)
            hidden = low_back(convolve(inputs, kernel) + conv_bias[which_layer])
            active = jax.nn.gelu(hidden) * row_mask
        flattened = low(active[0]).reshape(ROWS * WID, C)
        projected = low_back(jnp.dot(flattened.astype(jnp.float32), head_used.astype(jnp.float32), precision=lax.Precision.HIGHEST, preferred_element_type=jnp.float32) + head_bias)
        per_head = projected.reshape(-1, NH, HD)
        normed = (per_head * lax.rsqrt(lax.optimization_barrier(jnp.sum(per_head * per_head, -1, keepdims=True)) + 1e-06)).reshape(ROWS, WID, F)
        summed = summed + normed * head_gain * row_masks[which_group][:, None, None]
    return summed / counts[:, None, None]

def moments(grads, first, second):
    first_new = BETA_ONE * first + (1.0 - BETA_ONE) * grads
    second_new = BETA_TWO * second + (1.0 - BETA_TWO) * grads * grads
    direction = first_new / (1.0 - BETA_ONE ** STEP) / (jnp.sqrt(second_new / (1.0 - BETA_TWO ** STEP)) + EPSILON)
    return (first_new, second_new, direction)

def renew(stats_new, bases):
    product = jnp.einsum('lcd,lde->lce', stats_new, bases, precision=lax.Precision.HIGHEST)
    gram = jnp.einsum('lce,lcf->lef', product, product, precision=lax.Precision.HIGHEST)
    lower = jnp.linalg.cholesky(gram)
    solved = jax.vmap(lambda factor, matrix: jax.scipy.linalg.solve_triangular(factor, matrix.T, lower=True))(lower, product)
    return jnp.transpose(solved, (0, 2, 1))

def vector_rates():
    return jnp.concatenate([jnp.full((3 * C + F,), RATE_BIAS, jnp.float32), jnp.full((F,), RATE_GAIN, jnp.float32)])

def reference(features, valid_rows, conv_master, head_master, vectors, conv_first, conv_second, head_first, head_second, vec_first, vec_second, statistics, bases, cotangent):
    result, pullback = jax.vjp(partial(forward, valid_rows=valid_rows), features.astype(jnp.float32), conv_master, head_master, vectors)
    grad_input, grad_conv, grad_head, grad_vec = pullback(cotangent.astype(jnp.float32))
    rotated = jnp.einsum('lrc,lcd->lrd', grad_conv, bases, precision=lax.Precision.HIGHEST)
    conv_first_new, conv_second_new, direction = moments(rotated, conv_first, conv_second)
    turned = jnp.einsum('lrd,lcd->lrc', direction, bases, precision=lax.Precision.HIGHEST)
    conv_new = conv_master - RATE_CONV * (turned + DECAY * conv_master)
    head_first_new, head_second_new, head_dir = moments(grad_head, head_first, head_second)
    head_new = head_master - RATE_HEAD * (head_dir + DECAY * head_master)
    vec_first_new, vec_second_new, vec_dir = moments(grad_vec, vec_first, vec_second)
    vec_new = vectors - vector_rates() * (vec_dir + DECAY * vectors)
    stats_new = BETA_TWO * statistics + (1.0 - BETA_TWO) * jnp.einsum('lrc,lrd->lcd', grad_conv, grad_conv, precision=lax.Precision.HIGHEST)
    bases_new = renew(stats_new, bases)
    return (result.astype(jnp.bfloat16), grad_input.astype(jnp.bfloat16), conv_first_new, conv_second_new, conv_new, head_first_new, head_second_new, head_new, vec_first_new, vec_second_new, vec_new, stats_new, bases_new)
```

```python
from functools import partial

import jax
import jax.experimental.pallas as pl
import jax.experimental.pallas.tpu as pltpu
import jax.numpy as jnp
from jax import lax
from jax.sharding import PartitionSpec as P

NH = 7
HD = 256
STEP = 5


BETA_ONE = 0.9
BETA_TWO = 0.95
EPSILON = 1e-08
DECAY = 0.01
RATE_CONV = 0.04
RATE_HEAD = 0.08
RATE_BIAS = 0.5
RATE_GAIN = 20.0
VMEM_LIMIT = 60 * 2**20


MESH = pl.DeviceIdType.MESH
LANES = 128


def place():
    scale, space = lax.axis_index("scale"), lax.axis_index("space")
    across, core = scale // 2, lax.rem(scale, 2)
    deep, side = space // 2, lax.rem(space, 2)
    return (across, core, deep, side)


def at(across, core, deep, side):
    return (2 * across + core, 2 * deep + side)


def greet(peers):
    barrier = pltpu.get_barrier_semaphore()
    for peer in peers:
        pl.semaphore_signal(barrier, inc=1, device_id=peer, device_id_type=MESH)
    pl.semaphore_wait(barrier, len(peers))


def remote(source, target, send, receive, device):
    return pltpu.make_async_remote_copy(
        src_ref=source,
        dst_ref=target,
        send_sem=send,
        recv_sem=receive,
        device_id=device,
        device_id_type=MESH,
    )


def lanes(index, count=1):
    return pl.ds(pl.multiple_of(index * LANES, LANES), count * LANES)


def partners(deep_count):
    across, core, deep, side = place()
    peers = [
        at(across, 1 - core, deep, side),
        at(1 - across, core, deep, side),
        at(across, core, deep, 1 - side),
    ]
    peers += [
        at(across, core, lax.rem(deep + hop, deep_count), side) for hop in range(1, deep_count)
    ]
    return peers


def gather_kernel(layers, deep_count, master, full, own, local_sem, sends, receives):
    across, core, deep, side = place()
    block = 2 * core + across
    greet(partners(deep_count))

    def chunk_of(hop):
        source = lax.rem(deep - hop + deep_count, deep_count)
        return (source, lax.rem(source, 2))

    def first(layer, hop):
        piece = own.at[layer, :, lanes(block)]
        target = full.at[layer, deep, side, :, lanes(block)]
        to = at(across, core, lax.rem(deep + hop, deep_count), side)
        return remote(piece, target, sends.at[0, layer, hop], receives.at[0, layer, hop], to)

    def first_in(layer, hop):
        source, unused = chunk_of(hop)
        piece = full.at[layer, source, side, :, lanes(block)]
        return remote(
            piece, piece, sends.at[0, layer, hop], receives.at[0, layer, hop], at(across, core, deep, side)
        )

    def second(layer, hop, incoming):
        source, odd = chunk_of(hop)
        there_side = lax.rem(side + 1 - odd, 2)
        there_across = lax.rem(across + odd, 2)
        to = at(there_across, core, deep, there_side)
        if incoming:
            piece = full.at[layer, source, there_side, :, lanes(2 * core + there_across)]
        else:
            piece = full.at[layer, source, side, :, lanes(block)]
        return remote(piece, piece, sends.at[1, layer, hop], receives.at[1, layer, hop], to)

    def third(layer, hop, half, incoming):
        source, odd = chunk_of(hop)
        there_side = lax.rem(side + odd, 2)
        there_across = lax.rem(across + 1 - odd, 2)
        to = at(there_across, core, deep, there_side)
        here = there_side if incoming else side
        lane = there_across if incoming else across
        piece_side = (1 - odd) * half + odd * here
        piece_lane = 2 * core + (1 - odd) * lane + odd * half
        piece = full.at[layer, source, piece_side, :, lanes(piece_lane)]
        return remote(
            piece, piece, sends.at[2 + half, layer, hop], receives.at[2 + half, layer, hop], to
        )

    def fourth(layer, hop, incoming):
        source, unused = chunk_of(hop)
        column = 1 - core if incoming else core
        piece = full.at[layer, source, :, :, lanes(2 * column, 2)]
        to = at(across, 1 - core, deep, side)
        return remote(piece, piece, sends.at[4, layer, hop], receives.at[4, layer, hop], to)

    def local(layer):
        return pltpu.make_async_copy(
            own.at[layer, :, lanes(block)],
            full.at[layer, deep, side, :, lanes(block)],
            local_sem.at[layer],
        )

    def each(low, action):
        def step(hop, carry):
            action(hop)
            return carry

        lax.fori_loop(low, deep_count, step, 0)

    for layer in range(layers):
        own[layer] = master[layer].astype(jnp.bfloat16)
        local(layer).start()
        each(1, lambda hop: first(layer, hop).start())

    def go_second(layer):
        local(layer).wait()
        second(layer, 0, False).start()

        def step(hop):
            first_in(layer, hop).wait_recv()
            second(layer, hop, False).start()

        each(1, step)

    def go_third(layer):
        def step(hop):
            second(layer, hop, True).wait_recv()
            third(layer, hop, 0, False).start()
            third(layer, hop, 1, False).start()

        each(0, step)

    def go_fourth(layer):
        def step(hop):
            third(layer, hop, 0, True).wait_recv()
            third(layer, hop, 1, True).wait_recv()
            fourth(layer, hop, False).start()

        each(0, step)

    stages = [go_second, go_third, go_fourth]
    for turn in range(layers + 2):
        for lag in (0, 1, 2):
            if 0 <= turn - lag < layers:
                stages[lag](turn - lag)

    for layer in range(layers):

        def finish(hop):
            fourth(layer, hop, True).wait_recv()
            second(layer, hop, False).wait_send()
            third(layer, hop, 0, False).wait_send()
            third(layer, hop, 1, False).wait_send()
            fourth(layer, hop, False).wait_send()

        each(0, finish)
        each(1, lambda hop: first(layer, hop).wait_send())


def gather_weights(master, space_count):
    layers, rows, columns = master.shape
    deep_count = space_count // 2
    full = pl.pallas_call(
        partial(gather_kernel, layers, deep_count),
        out_shape=jax.ShapeDtypeStruct((layers, deep_count, 2, rows, columns), jnp.bfloat16),
        in_specs=[pl.BlockSpec(memory_space=pltpu.VMEM)],
        out_specs=pl.BlockSpec(memory_space=pl.ANY),
        scratch_shapes=[
            pltpu.VMEM((layers, rows, columns), jnp.bfloat16),
            pltpu.SemaphoreType.DMA((layers,)),
            pltpu.SemaphoreType.DMA((5, layers, deep_count)),
            pltpu.SemaphoreType.DMA((5, layers, deep_count)),
        ],
        compiler_params=pltpu.CompilerParams(
            collective_id=0, has_side_effects=True, vmem_limit_bytes=VMEM_LIMIT
        ),
    )(master)
    return full.reshape(layers, space_count * rows, columns)


def reduce_kernel(
    layers, deep_count, grads, total, mine, core_in, second_in, kept, third_in, last, last_in, acc, local_sem, sends, receives
):
    across, core, deep, side = place()
    block = 2 * core + across
    steps = layers * deep_count

    def split(step):
        layer, hop = step // deep_count, lax.rem(step, deep_count)
        target = lax.rem(deep + hop, deep_count)
        return (layer, hop, target, lax.rem(target, 2))

    def first(step):
        layer, hop, target, odd = split(step)
        return remote(
            grads.at[layer, target, :, :, lanes(2 * (1 - core), 2)],
            core_in.at[step],
            sends.at[0, step],
            receives.at[0, step],
            at(across, 1 - core, deep, side),
        )

    def load(step):
        layer, hop, target, odd = split(step)
        return pltpu.make_async_copy(
            grads.at[layer, target, :, :, lanes(2 * core, 2)], mine.at[step], local_sem.at[step]
        )

    def second(step, half):
        layer, hop, target, odd = split(step)
        piece_side = (1 - odd) * half + odd * (1 - side)
        piece_lane = (1 - odd) * (1 - across) + odd * half
        to = at(lax.rem(across + 1 - odd, 2), core, deep, lax.rem(side + odd, 2))
        return remote(
            mine.at[step, piece_side, :, lanes(piece_lane)],
            second_in.at[step, half],
            sends.at[1 + half, step],
            receives.at[1 + half, step],
            to,
        )

    def third(step):
        layer, hop, target, odd = split(step)
        keep = (1 - odd) * side + odd * across
        to = at(lax.rem(across + odd, 2), core, deep, lax.rem(side + 1 - odd, 2))
        return remote(
            kept.at[step, 1 - keep],
            third_in.at[step],
            sends.at[3, step],
            receives.at[3, step],
            to,
        )

    def fourth(step):
        layer, hop, target, odd = split(step)
        return remote(
            last.at[step],
            last_in.at[step],
            sends.at[4, step],
            receives.at[4, step],
            at(across, core, target, side),
        )

    def fifth(layer, incoming):
        lane = 2 * core + (1 - across if incoming else across)
        piece = total.at[layer, :, lanes(lane)]
        to = at(1 - across, core, deep, side)
        return remote(piece, piece, sends.at[5, layer], receives.at[5, layer], to)

    def sixth(layer, incoming):
        column = 1 - core if incoming else core
        piece = total.at[layer, :, lanes(2 * column, 2)]
        to = at(across, 1 - core, deep, side)
        return remote(piece, piece, sends.at[6, layer], receives.at[6, layer], to)

    def run(low, high, action):
        def body(step, carry):
            action(step)
            return carry

        lax.fori_loop(low, high, body, 0)

    run(0, steps, lambda step: load(step).start())
    greet(partners(deep_count))
    run(0, steps, lambda step: first(step).start())

    def wide(left, right):
        return left.astype(jnp.float32) + right.astype(jnp.float32)

    def go_second(step):
        load(step).wait()
        first(step).wait_recv()
        mine[step] = wide(mine[step], core_in[step]).astype(jnp.bfloat16)
        second(step, 0).start()
        second(step, 1).start()

    def go_third(step):
        layer, hop, target, odd = split(step)
        for half in range(2):
            second(step, half).wait_recv()
            keep_side = (1 - odd) * half + odd * side
            keep_lane = (1 - odd) * across + odd * half
            kept[step, half] = wide(
                mine[step, keep_side, :, lanes(keep_lane)], second_in[step, half]
            ).astype(jnp.bfloat16)
        third(step).start()

    def go_fourth(step):
        layer, hop, target, odd = split(step)
        third(step).wait_recv()
        keep = (1 - odd) * side + odd * across
        last[step] = wide(kept[step, keep], third_in[step]).astype(jnp.bfloat16)

        @pl.when(hop > 0)
        def unused():
            fourth(step).start()

    lag_third, lag_fourth = 2, 4

    def turn(step):
        @pl.when(step < steps)
        def go():
            go_second(step)

        @pl.when(jnp.logical_and(step >= lag_third, step < steps + lag_third))
        def go_next():
            go_third(step - lag_third)

        @pl.when(step >= lag_fourth)
        def go_last():
            go_fourth(step - lag_fourth)

    run(0, steps + lag_fourth, turn)

    def close(layer):
        acc[...] = last[layer * deep_count].astype(jnp.float32)

        def add(hop):
            step = layer * deep_count + hop
            fourth(step).wait_recv()
            acc[...] += last_in[step].astype(jnp.float32)

        run(1, deep_count, add)
        total[layer, :, lanes(block)] = acc[...].astype(jnp.bfloat16)
        fifth(layer, False).start()

    def spread(layer):
        fifth(layer, True).wait_recv()
        sixth(layer, False).start()

    run(0, layers, close)
    run(0, layers, spread)

    def finish(layer):
        sixth(layer, True).wait_recv()
        fifth(layer, False).wait_send()
        sixth(layer, False).wait_send()

    run(0, layers, finish)

    def drain(step):
        layer, hop, target, odd = split(step)
        first(step).wait_send()
        second(step, 0).wait_send()
        second(step, 1).wait_send()
        third(step).wait_send()

        @pl.when(hop > 0)
        def unused():
            fourth(step).wait_send()

    run(0, steps, drain)


def reduce_grads(grads, space_count):
    layers, all_rows, columns = grads.shape
    deep_count, rows = space_count // 2, all_rows // space_count
    steps = layers * deep_count
    low = jnp.bfloat16
    return pl.pallas_call(
        partial(reduce_kernel, layers, deep_count),
        out_shape=jax.ShapeDtypeStruct((layers, rows, columns), low),
        in_specs=[pl.BlockSpec(memory_space=pl.ANY)],
        out_specs=pl.BlockSpec(memory_space=pltpu.VMEM),
        scratch_shapes=[
            pltpu.VMEM((steps, 2, rows, 2 * LANES), low),
            pltpu.VMEM((steps, 2, rows, 2 * LANES), low),
            pltpu.VMEM((steps, 2, rows, LANES), low),
            pltpu.VMEM((steps, 2, rows, LANES), low),
            pltpu.VMEM((steps, rows, LANES), low),
            pltpu.VMEM((steps, rows, LANES), low),
            pltpu.VMEM((steps, rows, LANES), low),
            pltpu.VMEM((rows, LANES), jnp.float32),
            pltpu.SemaphoreType.DMA((steps,)),
            pltpu.SemaphoreType.DMA((7, steps)),
            pltpu.SemaphoreType.DMA((7, steps)),
        ],
        compiler_params=pltpu.CompilerParams(
            collective_id=1, has_side_effects=True, vmem_limit_bytes=VMEM_LIMIT
        ),
    )(grads.reshape(layers, deep_count, 2, rows, columns))


HI=lax.Precision.HIGHEST
def dot(a,b,ca,cb,precision=HI):
    return lax.dot_general(a,b,(((ca,),(cb,)),((),())),precision=precision,preferred_element_type=jnp.float32)

def eliminate(blocks, off, size):
    nl=len(blocks); nb=size//8
    sub=lax.broadcasted_iota(jnp.int32,(8,1),0)
    for k in range(size):
        b0=k//8; kr=k%8
        for l in range(nl):
            bl=blocks[l]
            row=bl[b0][kr:kr+1,:]
            inv=1.0/bl[b0][kr:kr+1,off+k:off+k+1]
            srow=row*inv
            for b in range(b0,nb):
                if b==b0:
                    if kr==7: continue
                    col=jnp.where(sub>kr,bl[b][:,off+k:off+k+1],0.0)
                else:
                    col=bl[b][:,off+k:off+k+1]
                bl[b]=bl[b]-col*srow
    out=[]
    lane=lax.broadcasted_iota(jnp.int32,(8,blocks[0][0].shape[1]),1)
    row8=lax.broadcasted_iota(jnp.int32,(8,blocks[0][0].shape[1]),0)
    for l in range(nl):
        res=[]
        for b in range(nb):
            v=blocks[l][b]
            d=jnp.sum(jnp.where(lane==row8+(off+8*b),v,0.0),1,keepdims=True)
            res.append(v*lax.rsqrt(d))
        out.append(jnp.concatenate(res,0))
    return out

def renew_kernel(layers, B, sum_ref, stat_ref, base_ref, sn_ref, bn_ref, m_ref, row_ref):
    C=stat_ref.shape[-1]
    D=128
    for l in range(layers):
        sn=BETA_TWO*stat_ref[l]+(1.0-BETA_TWO)*sum_ref[l]
        sn_ref[l]=sn
        pt=dot(base_ref[l],sn,0,0)
        m_ref[l,:,C:2*C]=pt
        m_ref[l,:,0:C]=dot(pt,pt,1,1)
    eye=(lax.broadcasted_iota(jnp.int32,(D,D),0)==lax.broadcasted_iota(jnp.int32,(D,D),1)).astype(jnp.float32)
    def outer(k,c):
        ks=pl.ds(pl.multiple_of(k*D,D),D)
        panels=[jnp.concatenate([m_ref[l,ks,ks],eye],1) for l in range(layers)]
        invs=[]
        done=[[] for _ in range(layers)]
        for j in range(D//B):
            blocks=[[p[8*i:8*i+8] for i in range(B//8)] for p in panels]
            tops=eliminate(blocks,B*j,B)
            for l in range(layers):
                done[l].append(tops[l][:,D:])
                if j<D//B-1:
                    panels[l]=panels[l][B:]-dot(tops[l][:,B*(j+1):D],tops[l],0,0)
        for l in range(layers):
            linv=jnp.concatenate(done[l],0)
            row_ref[l]=dot(linv,m_ref[l,ks,:],1,0)
            m_ref[l,ks,C:2*C]=row_ref[l,:,C:2*C]
        def inner(i,c2):
            is_=pl.ds(pl.multiple_of(i*D,D),D)
            for l in range(layers):
                m_ref[l,is_,:]=m_ref[l,is_,:]-dot(row_ref[l,:,is_],row_ref[l],0,0)
            return c2
        lax.fori_loop(k+1,C//D,inner,0)
        return c
    lax.fori_loop(0,C//D,outer,0)
    for l in range(layers):
        bn_ref[l]=m_ref[l,:,C:2*C].T

def renew(summed, statistics, bases, B=64):
    L,C,_=statistics.shape
    v=pl.BlockSpec(memory_space=pltpu.VMEM)
    sh=jax.ShapeDtypeStruct((L,C,C),jnp.float32)
    return pl.pallas_call(partial(renew_kernel,L,B),out_shape=(sh,sh),in_specs=[v]*3,out_specs=[v]*2,
      scratch_shapes=[pltpu.VMEM((L,C,2*C),jnp.float32),pltpu.VMEM((L,128,2*C),jnp.float32)],
      compiler_params=pltpu.CompilerParams(vmem_limit_bytes=VMEM_LIMIT))(summed,statistics,bases)


def padded_2(block, sides, width):
    for axis, dim in sides:
        count = lax.axis_size(axis)
        forward = [(i, i + 1) for i in range(count - 1)]
        backward = [(target, source) for source, target in forward]
        low = lax.ppermute(
            lax.slice_in_dim(block, block.shape[dim] - width, None, axis=dim), axis, forward
        )
        high = lax.ppermute(lax.slice_in_dim(block, 0, width, axis=dim), axis, backward)
        block = jnp.concatenate([low, block, high], axis=dim)
    return block


def widen(rows_in):
    return jnp.pad(rows_in, ((0, 0), (1, 1), (0, 0)))


def convolve_valid(padded, kernel):
    return lax.conv_general_dilated(
        padded[None],
        kernel,
        (1, 1),
        "VALID",
        dimension_numbers=("NHWC", "HWIO", "NHWC"),
        preferred_element_type=jnp.float32,
    )[0]


def moments(grads, first, second):
    first_new = BETA_ONE * first + (1.0 - BETA_ONE) * grads
    second_new = BETA_TWO * second + (1.0 - BETA_TWO) * grads * grads
    direction = (
        first_new
        / (1.0 - BETA_ONE**STEP)
        / (jnp.sqrt(second_new / (1.0 - BETA_TWO**STEP)) + EPSILON)
    )
    return (first_new, second_new, direction)


def local(
    features,
    valid_rows,
    conv_master,
    head_master,
    vectors,
    conv_first,
    conv_second,
    head_first,
    head_second,
    vec_first,
    vec_second,
    statistics,
    bases,
    cotangent,
):
    channels = features.shape[3]
    rows_dev = features.shape[1]
    width = features.shape[2]
    head_width = cotangent.shape[2]
    conv_used = gather_weights(conv_master, lax.axis_size("space"))
    head_flat = lax.all_gather(
        head_master.astype(jnp.bfloat16), ("scale", "space"), axis=0, tiled=True
    )
    head_used = head_flat.reshape(channels, head_width)
    conv_bias = vectors[: 3 * channels].reshape(3, channels)
    head_bias = vectors[3 * channels : 3 * channels + head_width]
    head_gain = vectors[3 * channels + head_width :]
    row_index = lax.axis_index("space") * rows_dev + jnp.arange(rows_dev, dtype=jnp.int32)
    row_mask = (row_index < valid_rows[lax.axis_index("scale")]).astype(jnp.float32)
    counts = jnp.sum((row_index[None, :] < valid_rows[:, None]).astype(jnp.float32), 0)
    mask_cube = row_mask[:, None, None]
    inputs = features[0]
    kept_hidden = []
    kept_inputs = []
    kernels = []
    for which_layer in range(3):
        padded = widen(padded_2(inputs, (("space", 0),), 1))
        kernel = conv_used[which_layer].reshape(3, 3, channels, channels)
        hidden = convolve_valid(padded, kernel) + conv_bias[which_layer]
        kept_hidden.append(hidden)
        kernels.append(kernel)
        kept_inputs.append(padded)
        inputs = (jax.nn.gelu(hidden) * mask_cube).astype(jnp.bfloat16)
    flattened = inputs.reshape(rows_dev * width, channels)
    projected = jnp.dot(flattened, head_used, preferred_element_type=jnp.float32) + head_bias
    per_head = projected.reshape(-1, NH, HD)
    inverse = lax.rsqrt(jnp.sum(per_head * per_head, -1, keepdims=True) + 1e-06)
    normed_head = per_head * inverse
    normed = normed_head.reshape(-1, head_width)
    weights_row = (row_mask / counts)[:, None, None]
    term = (normed * head_gain).reshape(rows_dev, width, head_width) * weights_row
    merged = lax.psum(term.astype(jnp.bfloat16), "scale")
    d_out = (cotangent.astype(jnp.float32) * weights_row).reshape(-1, head_width)
    grad_gain = jnp.sum(normed * d_out, 0)
    d_normed = (d_out * head_gain).reshape(-1, NH, HD)
    d_proj = inverse * (d_normed - normed_head * jnp.sum(normed_head * d_normed, -1, keepdims=True))
    d_low = d_proj.reshape(-1, head_width).astype(jnp.bfloat16)
    grad_head_bias = jnp.sum(d_low.astype(jnp.float32), 0)
    grad_head = jnp.einsum("pc,pf->cf", flattened, d_low, preferred_element_type=jnp.float32)
    d_active = jnp.einsum(
        "pf,cf->pc", d_low, head_used, preferred_element_type=jnp.float32
    ).reshape(rows_dev, width, channels)
    conv_grads = [None, None, None]
    bias_grads = [None, None, None]
    for which_layer in (2, 1, 0):
        unused, gelu_pull = jax.vjp(jax.nn.gelu, kept_hidden[which_layer])
        d_hidden = gelu_pull(d_active * mask_cube)[0].astype(jnp.bfloat16)
        bias_grads[which_layer] = jnp.sum(d_hidden.astype(jnp.float32), (0, 1))
        padded_in = kept_inputs[which_layer]
        tap_grads = []
        for tap_row in range(3):
            for tap_col in range(3):
                window = padded_in[tap_row : tap_row + rows_dev, tap_col : tap_col + width, :]
                tap_grads.append(
                    jnp.einsum("rwi,rwo->io", window, d_hidden, preferred_element_type=jnp.float32)
                )
        conv_grads[which_layer] = jnp.stack(tap_grads).reshape(9 * channels, channels)
        d_padded = widen(padded_2(d_hidden, (("space", 0),), 1))
        flipped = jnp.transpose(jnp.flip(kernels[which_layer], (0, 1)), (0, 1, 3, 2))
        d_active = convolve_valid(d_padded, flipped)
    features_grad = d_active.astype(jnp.bfloat16)[None]
    stacked_grads = jnp.stack(conv_grads).astype(jnp.bfloat16)
    owned_conv = reduce_grads(stacked_grads, lax.axis_size("space")).astype(jnp.float32)
    owned_head = lax.psum_scatter(
        grad_head.reshape(-1), ("scale", "space"), scatter_dimension=0, tiled=True
    )
    partial_stats = jnp.einsum(
        "lrc,lrd->lcd", owned_conv, owned_conv, precision=lax.Precision.HIGHEST
    ) / lax.axis_size("scale")
    vec_partial = jnp.concatenate([jnp.concatenate(bias_grads), grad_head_bias, grad_gain])
    summed_stats, grad_vec = lax.psum((partial_stats, vec_partial), ("scale", "space"))
    rotated = jnp.einsum("lrc,lcd->lrd", owned_conv, bases, precision=lax.Precision.HIGHEST)
    conv_first_new, conv_second_new, direction = moments(rotated, conv_first, conv_second)
    turned = jnp.einsum("lrd,lcd->lrc", direction, bases, precision=lax.Precision.HIGHEST)
    conv_new = conv_master - RATE_CONV * (turned + DECAY * conv_master)
    head_first_new, head_second_new, head_dir = moments(owned_head, head_first, head_second)
    head_new = head_master - RATE_HEAD * (head_dir + DECAY * head_master)
    vec_first_new, vec_second_new, vec_dir = moments(grad_vec, vec_first, vec_second)
    rates = jnp.concatenate(
        [
            jnp.full((3 * channels + head_width,), RATE_BIAS, jnp.float32),
            jnp.full((head_width,), RATE_GAIN, jnp.float32),
        ]
    )
    vec_new = vectors - rates * (vec_dir + DECAY * vectors)
    stats_new, bases_new = renew(summed_stats, statistics, bases)
    return (
        merged,
        features_grad,
        conv_first_new,
        conv_second_new,
        conv_new,
        head_first_new,
        head_second_new,
        head_new,
        vec_first_new,
        vec_second_new,
        vec_new,
        stats_new,
        bases_new,
    )


def solution(mesh):
    in_specs = (
        P("scale", "space", None, None),
        P(),
        P(None, "space", None),
        P(("scale", "space")),
        P(),
        P(None, "space", None),
        P(None, "space", None),
        P(("scale", "space")),
        P(("scale", "space")),
        P(),
        P(),
        P(),
        P(),
        P("space", None, None),
    )
    out_specs = (
        P("space", None, None),
        P("scale", "space", None, None),
        P(None, "space", None),
        P(None, "space", None),
        P(None, "space", None),
        P(("scale", "space")),
        P(("scale", "space")),
        P(("scale", "space")),
        P(),
        P(),
        P(),
        P(),
        P(),
    )
    return jax.shard_map(local, mesh=mesh, in_specs=in_specs, out_specs=out_specs, check_vma=False)
```

```python
from functools import partial

import jax
import jax.experimental.pallas as pl
import jax.experimental.pallas.tpu as pltpu
import jax.numpy as jnp
from jax import lax
from jax.sharding import PartitionSpec as P

NH = 7
HD = 256
STEP = 5


BETA_ONE = 0.9
BETA_TWO = 0.95
EPSILON = 1e-08
DECAY = 0.01
RATE_CONV = 0.04
RATE_HEAD = 0.08
RATE_BIAS = 0.5
RATE_GAIN = 20.0
VMEM_LIMIT = 60 * 2**20
GELU_SCALE = 0.7978845608028654
GELU_CUBE = 0.044715


MESH = pl.DeviceIdType.MESH
LANES = 128


def place():
    scale, space = lax.axis_index("scale"), lax.axis_index("space")
    across, core = scale // 2, lax.rem(scale, 2)
    deep, side = space // 2, lax.rem(space, 2)
    return (across, core, deep, side)


def at(across, core, deep, side):
    return (2 * across + core, 2 * deep + side)


def greet(peers):
    barrier = pltpu.get_barrier_semaphore()
    for peer in peers:
        pl.semaphore_signal(barrier, inc=1, device_id=peer, device_id_type=MESH)
    pl.semaphore_wait(barrier, len(peers))


def remote(source, target, send, receive, device):
    return pltpu.make_async_remote_copy(
        src_ref=source,
        dst_ref=target,
        send_sem=send,
        recv_sem=receive,
        device_id=device,
        device_id_type=MESH,
    )


def lanes(index, count=1):
    return pl.ds(pl.multiple_of(index * LANES, LANES), count * LANES)


def partners(deep_count):
    across, core, deep, side = place()
    peers = [
        at(across, 1 - core, deep, side),
        at(1 - across, core, deep, side),
        at(across, core, deep, 1 - side),
    ]
    peers += [
        at(across, core, lax.rem(deep + hop, deep_count), side) for hop in range(1, deep_count)
    ]
    return peers


def gather_kernel(
    layers,
    deep_count,
    master,
    head_master,
    full,
    head_full,
    own,
    head_own,
    local_sem,
    sends,
    receives,
    head_sends,
    head_receives,
):
    across, core, deep, side = place()
    block = 2 * core + across
    greet(partners(deep_count))

    def chunk_of(hop):
        source = lax.rem(deep - hop + deep_count, deep_count)
        return (source, lax.rem(source, 2))

    def first(layer, hop):
        piece = own.at[layer, :, lanes(block)]
        target = full.at[layer, deep, side, :, lanes(block)]
        to = at(across, core, lax.rem(deep + hop, deep_count), side)
        return remote(piece, target, sends.at[0, layer, hop], receives.at[0, layer, hop], to)

    def first_in(layer, hop):
        source, unused = chunk_of(hop)
        piece = full.at[layer, source, side, :, lanes(block)]
        return remote(
            piece, piece, sends.at[0, layer, hop], receives.at[0, layer, hop], at(across, core, deep, side)
        )

    def second(layer, hop, incoming):
        source, odd = chunk_of(hop)
        there_side = lax.rem(side + 1 - odd, 2)
        there_across = lax.rem(across + odd, 2)
        to = at(there_across, core, deep, there_side)
        if incoming:
            piece = full.at[layer, source, there_side, :, lanes(2 * core + there_across)]
        else:
            piece = full.at[layer, source, side, :, lanes(block)]
        return remote(piece, piece, sends.at[1, layer, hop], receives.at[1, layer, hop], to)

    def third(layer, hop, half, incoming):
        source, odd = chunk_of(hop)
        there_side = lax.rem(side + odd, 2)
        there_across = lax.rem(across + 1 - odd, 2)
        to = at(there_across, core, deep, there_side)
        here = there_side if incoming else side
        lane = there_across if incoming else across
        piece_side = (1 - odd) * half + odd * here
        piece_lane = 2 * core + (1 - odd) * lane + odd * half
        piece = full.at[layer, source, piece_side, :, lanes(piece_lane)]
        return remote(
            piece, piece, sends.at[2 + half, layer, hop], receives.at[2 + half, layer, hop], to
        )

    def fourth(layer, hop, incoming):
        source, unused = chunk_of(hop)
        column = 1 - core if incoming else core
        piece = full.at[layer, source, :, :, lanes(2 * column, 2)]
        to = at(across, 1 - core, deep, side)
        return remote(piece, piece, sends.at[4, layer, hop], receives.at[4, layer, hop], to)

    def local(layer):
        return pltpu.make_async_copy(
            own.at[layer, :, lanes(block)],
            full.at[layer, deep, side, :, lanes(block)],
            local_sem.at[layer],
        )

    def each(low, action):
        def step(hop, carry):
            action(hop)
            return carry

        lax.fori_loop(low, deep_count, step, 0)

    def head_local():
        return pltpu.make_async_copy(
            head_own, head_full.at[across, core, deep, side], local_sem.at[layers]
        )

    def head_first(hop):
        to = at(across, core, lax.rem(deep + hop, deep_count), side)
        target = head_full.at[across, core, deep, side]
        return remote(head_own, target, head_sends.at[hop], head_receives.at[hop], to)

    def head_first_in(hop):
        piece = head_full.at[across, core, lax.rem(deep - hop + deep_count, deep_count), side]
        to = at(across, core, deep, side)
        return remote(piece, piece, head_sends.at[hop], head_receives.at[hop], to)

    def head_next(which, incoming):
        if which == 0:
            to = at(across, core, deep, 1 - side)
            piece = head_full.at[across, core, :, 1 - side if incoming else side]
        elif which == 1:
            to = at(1 - across, core, deep, side)
            piece = head_full.at[1 - across if incoming else across, core]
        else:
            to = at(across, 1 - core, deep, side)
            piece = head_full.at[:, 1 - core if incoming else core]
        slot = deep_count + which
        return remote(piece, piece, head_sends.at[slot], head_receives.at[slot], to)

    def go_head(which):
        if which == 0:
            head_local().wait()
            each(1, lambda hop: head_first_in(hop).wait_recv())
        else:
            head_next(which - 1, True).wait_recv()
        if which < 3:
            head_next(which, False).start()

    for layer in range(layers):
        own[layer] = master[layer].astype(jnp.bfloat16)
        local(layer).start()
        each(1, lambda hop: first(layer, hop).start())
        if layer == 0:
            head_own[...] = head_master[...].astype(jnp.bfloat16)
            head_local().start()
            each(1, lambda hop: head_first(hop).start())

    def go_second(layer):
        local(layer).wait()
        second(layer, 0, False).start()

        def step(hop):
            first_in(layer, hop).wait_recv()
            second(layer, hop, False).start()

        each(1, step)

    def go_third(layer):
        def step(hop):
            second(layer, hop, True).wait_recv()
            third(layer, hop, 0, False).start()
            third(layer, hop, 1, False).start()

        each(0, step)

    def go_fourth(layer):
        def step(hop):
            third(layer, hop, 0, True).wait_recv()
            third(layer, hop, 1, True).wait_recv()
            fourth(layer, hop, False).start()

        each(0, step)

    stages = [go_second, go_third, go_fourth]
    for turn in range(layers + 2):
        for lag in (0, 1, 2):
            if 0 <= turn - lag < layers:
                stages[lag](turn - lag)
        if turn >= 1:
            go_head(turn - 1)
    each(1, lambda hop: head_first(hop).wait_send())
    for which in range(3):
        head_next(which, False).wait_send()

    for layer in range(layers):

        def finish(hop):
            fourth(layer, hop, True).wait_recv()
            second(layer, hop, False).wait_send()
            third(layer, hop, 0, False).wait_send()
            third(layer, hop, 1, False).wait_send()
            fourth(layer, hop, False).wait_send()

        each(0, finish)
        each(1, lambda hop: first(layer, hop).wait_send())


def gather_weights(master, head_master, space_count):
    layers, rows, columns = master.shape
    deep_count = space_count // 2
    anywhere = pl.BlockSpec(memory_space=pl.ANY)
    head_shape = (2, 2, deep_count, 2) + head_master.shape
    full, head_full = pl.pallas_call(
        partial(gather_kernel, layers, deep_count),
        out_shape=(
            jax.ShapeDtypeStruct((layers, deep_count, 2, rows, columns), jnp.bfloat16),
            jax.ShapeDtypeStruct(head_shape, jnp.bfloat16),
        ),
        in_specs=[pl.BlockSpec(memory_space=pltpu.VMEM)] * 2,
        out_specs=[anywhere, anywhere],
        scratch_shapes=[
            pltpu.VMEM((layers, rows, columns), jnp.bfloat16),
            pltpu.VMEM(head_master.shape, jnp.bfloat16),
            pltpu.SemaphoreType.DMA((layers + 1,)),
            pltpu.SemaphoreType.DMA((5, layers, deep_count)),
            pltpu.SemaphoreType.DMA((5, layers, deep_count)),
            pltpu.SemaphoreType.DMA((deep_count + 3,)),
            pltpu.SemaphoreType.DMA((deep_count + 3,)),
        ],
        compiler_params=pltpu.CompilerParams(
            collective_id=0, has_side_effects=True, vmem_limit_bytes=VMEM_LIMIT
        ),
    )(master, head_master)
    return (
        full.reshape(layers, space_count * rows, columns),
        head_full.reshape(-1, head_master.shape[1]),
    )


def reduce_kernel(
    layers,
    deep_count,
    grads,
    vector,
    total,
    stats,
    vector_total,
    mine,
    core_in,
    second_in,
    kept,
    third_in,
    last,
    last_in,
    acc,
    stat_own,
    stat_in,
    stat_deep,
    vector_out,
    vector_in,
    vector_deep,
    local_sem,
    sends,
    receives,
    stat_sends,
    stat_receives,
    deep_sends,
    deep_receives,
    vector_sends,
    vector_receives,
):
    across, core, deep, side = place()
    block = 2 * core + across
    steps = layers * deep_count

    def split(step):
        layer, hop = step // deep_count, lax.rem(step, deep_count)
        target = lax.rem(deep + hop, deep_count)
        return (layer, hop, target, lax.rem(target, 2))

    def first(step):
        layer, hop, target, odd = split(step)
        return remote(
            grads.at[layer, target, :, :, lanes(2 * (1 - core), 2)],
            core_in.at[step],
            sends.at[0, step],
            receives.at[0, step],
            at(across, 1 - core, deep, side),
        )

    def load(step):
        layer, hop, target, odd = split(step)
        return pltpu.make_async_copy(
            grads.at[layer, target, :, :, lanes(2 * core, 2)], mine.at[step], local_sem.at[step]
        )

    def second(step, half):
        layer, hop, target, odd = split(step)
        piece_side = (1 - odd) * half + odd * (1 - side)
        piece_lane = (1 - odd) * (1 - across) + odd * half
        to = at(lax.rem(across + 1 - odd, 2), core, deep, lax.rem(side + odd, 2))
        return remote(
            mine.at[step, piece_side, :, lanes(piece_lane)],
            second_in.at[step, half],
            sends.at[1 + half, step],
            receives.at[1 + half, step],
            to,
        )

    def third(step):
        layer, hop, target, odd = split(step)
        keep = (1 - odd) * side + odd * across
        to = at(lax.rem(across + odd, 2), core, deep, lax.rem(side + 1 - odd, 2))
        return remote(
            kept.at[step, 1 - keep],
            third_in.at[step],
            sends.at[3, step],
            receives.at[3, step],
            to,
        )

    def fourth(step):
        layer, hop, target, odd = split(step)
        return remote(
            last.at[step],
            last_in.at[step],
            sends.at[4, step],
            receives.at[4, step],
            at(across, core, target, side),
        )

    def fifth(layer, incoming):
        lane = 2 * core + (1 - across if incoming else across)
        piece = total.at[layer, :, lanes(lane)]
        to = at(1 - across, core, deep, side)
        return remote(piece, piece, sends.at[5, layer], receives.at[5, layer], to)

    def sixth(layer, incoming):
        column = 1 - core if incoming else core
        piece = total.at[layer, :, lanes(2 * column, 2)]
        to = at(across, 1 - core, deep, side)
        return remote(piece, piece, sends.at[6, layer], receives.at[6, layer], to)

    def run(low, high, action):
        def body(step, carry):
            action(step)
            return carry

        lax.fori_loop(low, high, body, 0)

    half_block = LANES // 2

    def stat_side(layer, incoming):
        rows = pl.ds(pl.multiple_of((1 - side) * half_block, half_block), half_block)
        return remote(
            stat_own.at[layer, rows],
            stat_in.at[layer],
            stat_sends.at[0, layer],
            stat_receives.at[0, layer],
            at(across, core, deep, 1 - side),
        )

    def stat_along(layer, hop):
        return remote(
            stat_deep.at[layer, deep],
            stat_deep.at[layer, deep],
            deep_sends.at[layer, hop],
            deep_receives.at[layer, hop],
            at(across, core, lax.rem(deep + hop, deep_count), side),
        )

    def stat_along_in(layer, hop):
        source = lax.rem(deep - hop + deep_count, deep_count)
        return remote(
            stat_deep.at[layer, source],
            stat_deep.at[layer, source],
            deep_sends.at[layer, hop],
            deep_receives.at[layer, hop],
            at(across, core, deep, side),
        )

    def half_rows(which):
        return pl.ds(pl.multiple_of(which * half_block, half_block), half_block)

    def stat_spread(which, layer, incoming):
        if which == 0:
            to = at(across, core, deep, 1 - side)
            piece = stats.at[layer, block, half_rows(1 - side if incoming else side)]
        elif which == 1:
            to = at(1 - across, core, deep, side)
            piece = stats.at[layer, 2 * core + (1 - across if incoming else across)]
        else:
            to = at(across, 1 - core, deep, side)
            piece = stats.at[layer, pl.ds(2 * (1 - core if incoming else core), 2)]
        slot = 1 + which
        return remote(piece, piece, stat_sends.at[slot, layer], stat_receives.at[slot, layer], to)

    def vector_step(which):
        to = (
            at(across, 1 - core, deep, side),
            at(1 - across, core, deep, side),
            at(across, core, deep, 1 - side),
        )[which]
        return remote(
            vector_out.at[which],
            vector_in.at[which],
            vector_sends.at[which],
            vector_receives.at[which],
            to,
        )

    def vector_along(hop):
        return remote(
            vector_deep.at[deep],
            vector_deep.at[deep],
            vector_sends.at[2 + hop],
            vector_receives.at[2 + hop],
            at(across, core, lax.rem(deep + hop, deep_count), side),
        )

    def vector_along_in(hop):
        source = lax.rem(deep - hop + deep_count, deep_count)
        return remote(
            vector_deep.at[source],
            vector_deep.at[source],
            vector_sends.at[2 + hop],
            vector_receives.at[2 + hop],
            at(across, core, deep, side),
        )

    run(0, steps, lambda step: load(step).start())
    greet(partners(deep_count))
    run(0, steps, lambda step: first(step).start())

    def wide(left, right):
        return left.astype(jnp.float32) + right.astype(jnp.float32)

    def go_second(step):
        load(step).wait()
        first(step).wait_recv()
        mine[step] = wide(mine[step], core_in[step]).astype(jnp.bfloat16)
        second(step, 0).start()
        second(step, 1).start()

    def go_third(step):
        layer, hop, target, odd = split(step)
        for half in range(2):
            second(step, half).wait_recv()
            keep_side = (1 - odd) * half + odd * side
            keep_lane = (1 - odd) * across + odd * half
            kept[step, half] = wide(
                mine[step, keep_side, :, lanes(keep_lane)], second_in[step, half]
            ).astype(jnp.bfloat16)
        third(step).start()

    def go_fourth(step):
        layer, hop, target, odd = split(step)
        third(step).wait_recv()
        keep = (1 - odd) * side + odd * across
        last[step] = wide(kept[step, keep], third_in[step]).astype(jnp.bfloat16)

        @pl.when(hop > 0)
        def unused():
            fourth(step).start()

    def close(layer):
        acc[...] = last[layer * deep_count].astype(jnp.float32)

        def add(hop):
            step = layer * deep_count + hop
            fourth(step).wait_recv()
            acc[...] += last_in[step].astype(jnp.float32)

        run(1, deep_count, add)
        total[layer, :, lanes(block)] = acc[...].astype(jnp.bfloat16)
        fifth(layer, False).start()

    def spread(layer):
        fifth(layer, True).wait_recv()
        sixth(layer, False).start()

    def measure(layer):
        sixth(layer, True).wait_recv()
        own_lanes = total[layer, :, lanes(block)]
        stat_own[layer] = lax.dot_general(
            own_lanes,
            total[layer],
            (((0,), (0,)), ((), ())),
            preferred_element_type=jnp.float32,
        ).astype(jnp.bfloat16)
        stat_side(layer, False).start()

    def pair(layer):
        stat_side(layer, True).wait_recv()
        stat_deep[layer, deep] = wide(
            stat_own[layer, half_rows(side)], stat_in[layer]
        ).astype(jnp.bfloat16)
        run(1, deep_count, lambda hop: stat_along(layer, hop).start())

    def settle(layer):
        run(1, deep_count, lambda hop: stat_along_in(layer, hop).wait_recv())
        whole = stat_deep[layer, 0].astype(jnp.float32)
        for source in range(1, deep_count):
            whole += stat_deep[layer, source].astype(jnp.float32)
        stats[layer, block, half_rows(side)] = whole.astype(jnp.bfloat16)
        stat_spread(0, layer, False).start()

    def share_across(layer):
        stat_spread(0, layer, True).wait_recv()
        stat_spread(1, layer, False).start()

    def share_core(layer):
        stat_spread(1, layer, True).wait_recv()
        stat_spread(2, layer, False).start()

    def finish(layer):
        stat_spread(2, layer, True).wait_recv()
        fifth(layer, False).wait_send()
        sixth(layer, False).wait_send()
        stat_side(layer, False).wait_send()
        run(1, deep_count, lambda hop: stat_along(layer, hop).wait_send())
        for which in range(3):
            stat_spread(which, layer, False).wait_send()

    def vector_next(which):
        vector_step(which).wait_recv()
        summed = vector_out[which] + vector_in[which]
        if which < 2:
            vector_out[which + 1] = summed
            vector_step(which + 1).start()
        else:
            vector_deep[deep] = summed
            run(1, deep_count, lambda hop: vector_along(hop).start())

    chunk_work = ((0, go_second), (2, go_third), (4, go_fourth))
    layer_work = (
        (6, close),
        (7, spread),
        (8, measure),
        (9, pair),
        (10, settle),
        (11, share_across),
        (12, share_core),
        (13, finish),
    )
    vector_out[0] = vector[...]
    vector_step(0).start()

    def turn(now):
        for lag, action in chunk_work:

            @pl.when(jnp.logical_and(now >= lag, now < steps + lag))
            def chunk():
                action(now - lag)

        for which in range(3):

            @pl.when(now == 2 * which + 1)
            def exchange():
                vector_next(which)

        for lag, action in layer_work:
            past = now - lag - (deep_count - 1)

            @pl.when(
                jnp.logical_and(
                    jnp.logical_and(past >= 0, past < steps), lax.rem(past, deep_count) == 0
                )
            )
            def whole_layer():
                action(past // deep_count)

    run(0, steps + layer_work[-1][0], turn)

    run(1, deep_count, lambda hop: vector_along_in(hop).wait_recv())
    summed = vector_deep[0]
    for source in range(1, deep_count):
        summed += vector_deep[source]
    vector_total[...] = summed
    for which in range(3):
        vector_step(which).wait_send()
    run(1, deep_count, lambda hop: vector_along(hop).wait_send())

    def drain(step):
        layer, hop, target, odd = split(step)
        first(step).wait_send()
        second(step, 0).wait_send()
        second(step, 1).wait_send()
        third(step).wait_send()

        @pl.when(hop > 0)
        def unused():
            fourth(step).wait_send()

    run(0, steps, drain)


def reduce_grads(grads, vector, space_count):
    layers, all_rows, columns = grads.shape
    deep_count, rows = space_count // 2, all_rows // space_count
    steps = layers * deep_count
    low = jnp.bfloat16
    blocks = columns // LANES
    vmem = pl.BlockSpec(memory_space=pltpu.VMEM)
    vector = vector.reshape(-1, LANES)
    total, stats, vector_total = pl.pallas_call(
        partial(reduce_kernel, layers, deep_count),
        out_shape=(
            jax.ShapeDtypeStruct((layers, rows, columns), low),
            jax.ShapeDtypeStruct((layers, blocks, LANES, columns), low),
            jax.ShapeDtypeStruct(vector.shape, jnp.float32),
        ),
        in_specs=[pl.BlockSpec(memory_space=pl.ANY), vmem],
        out_specs=[vmem, vmem, vmem],
        scratch_shapes=[
            pltpu.VMEM((steps, 2, rows, 2 * LANES), low),
            pltpu.VMEM((steps, 2, rows, 2 * LANES), low),
            pltpu.VMEM((steps, 2, rows, LANES), low),
            pltpu.VMEM((steps, 2, rows, LANES), low),
            pltpu.VMEM((steps, rows, LANES), low),
            pltpu.VMEM((steps, rows, LANES), low),
            pltpu.VMEM((steps, rows, LANES), low),
            pltpu.VMEM((rows, LANES), jnp.float32),
            pltpu.VMEM((layers, LANES, columns), low),
            pltpu.VMEM((layers, LANES // 2, columns), low),
            pltpu.VMEM((layers, deep_count, LANES // 2, columns), low),
            pltpu.VMEM((3,) + vector.shape, jnp.float32),
            pltpu.VMEM((3,) + vector.shape, jnp.float32),
            pltpu.VMEM((deep_count,) + vector.shape, jnp.float32),
            pltpu.SemaphoreType.DMA((steps,)),
            pltpu.SemaphoreType.DMA((7, steps)),
            pltpu.SemaphoreType.DMA((7, steps)),
            pltpu.SemaphoreType.DMA((4, layers)),
            pltpu.SemaphoreType.DMA((4, layers)),
            pltpu.SemaphoreType.DMA((layers, deep_count)),
            pltpu.SemaphoreType.DMA((layers, deep_count)),
            pltpu.SemaphoreType.DMA((2 + deep_count,)),
            pltpu.SemaphoreType.DMA((2 + deep_count,)),
        ],
        compiler_params=pltpu.CompilerParams(
            collective_id=1, has_side_effects=True, vmem_limit_bytes=VMEM_LIMIT
        ),
    )(grads.reshape(layers, deep_count, 2, rows, columns), vector)
    return (total, stats.reshape(layers, columns, columns), vector_total.reshape(-1))


TAPS = 3


def gelu_parts(value):
    inner = GELU_SCALE * (value + GELU_CUBE * value * value * value)
    return jnp.tanh(inner)


def gelu_value(value):
    return 0.5 * value * (1.0 + gelu_parts(value))


def gelu_slope(value):
    bend = gelu_parts(value)
    rise = GELU_SCALE * (1.0 + 3.0 * GELU_CUBE * value * value)
    return 0.5 * (1.0 + bend) + 0.5 * value * (1.0 - bend * bend) * rise


def mix(left, right, left_dim, right_dim):
    return lax.dot_general(
        left,
        right,
        (((left_dim,), (right_dim,)), ((), ())),
        preferred_element_type=jnp.float32,
    )


def work_kernel(
    dims,
    features,
    weights_in,
    head_in,
    conv_bias,
    head_bias,
    head_gain,
    cotangent_in,
    row_values,
    merged,
    features_grad,
    grads_out,
    head_grad,
    conv_bias_grad,
    head_bias_grad,
    gain_grad,
    weights,
    head,
    cotangent,
    wide,
    hidden,
    last,
    last_turned,
    d_wide,
    d_active,
    grads,
    halo,
    term,
    term_in,
    load_sem,
    store_sem,
    send_sem,
    receive_sem,
    term_sends,
    term_receives,
    *head_refs,
):
    layers, rows, width, channels, heads, depth, space_count = dims
    deep_count = space_count // 2
    across, core, deep, side = place()
    spread_head = len(head_refs) > 0
    if spread_head:
        head_parts, core_in, across_in, side_in, deep_in, head_sends, head_receives = head_refs
        head_rows = head_parts.shape[4]
    tile = 2 * LANES
    tiles = channels // tile
    scale, space = lax.axis_index("scale"), lax.axis_index("space")
    low = jnp.bfloat16

    def load(which):
        if which < layers:
            return pltpu.make_async_copy(
                weights_in.at[which], weights.at[which], load_sem.at[which]
            )
        source, target = ((head_in, head), (cotangent_in, cotangent))[which - layers]
        return pltpu.make_async_copy(source, target, load_sem.at[which])

    for which in range(layers + 2):
        load(which).start()

    above, below = space > 0, space < space_count - 1
    barrier = pltpu.get_barrier_semaphore()
    others = [
        at(across, 1 - core, deep, side),
        at(1 - across, core, deep, side),
        at(across, core, deep, 1 - side),
    ]
    if spread_head:
        others += [
            at(across, core, lax.rem(deep + hop, deep_count), side) for hop in range(1, deep_count)
        ]
    for peer in others:
        pl.semaphore_signal(barrier, inc=1, device_id=peer, device_id_type=MESH)
    next_space = space - 1 + 2 * side
    has_next = jnp.logical_and(next_space >= 0, next_space < space_count)

    @pl.when(has_next)
    def greet_next():
        pl.semaphore_signal(
            barrier, inc=1, device_id=(scale, next_space), device_id_type=MESH
        )

    pl.semaphore_wait(barrier, len(others) + has_next.astype(jnp.int32))

    def term_lanes(index, which):
        return pl.ds(pl.multiple_of(index * depth + which * LANES, LANES), LANES)

    def term_step(which, index, incoming=False):
        if which == 0:
            source, target, to = term.at[:, term_lanes(index, 1 - core)], term_in.at[0, index], others[0]
        elif which == 1:
            source, target, to = term.at[:, term_lanes(index, core)], term_in.at[1, index], others[1]
        else:
            source = merged.at[:, term_lanes(index, 1 - core if incoming else core)]
            target, to = source, others[0]
        return remote(
            source, target, term_sends.at[which, index], term_receives.at[which, index], to
        )

    def term_pair(index):
        term_step(0, index).wait_recv()
        lane = term_lanes(index, core)
        both = term[:, lane].astype(jnp.float32) + term_in[0, index].astype(jnp.float32)
        term[:, lane] = both.astype(low)
        term_step(1, index).start()

    def term_total(index):
        term_step(1, index).wait_recv()
        lane = term_lanes(index, core)
        both = term[:, lane].astype(jnp.float32) + term_in[1, index].astype(jnp.float32)
        merged[:, lane] = both.astype(low)
        term_step(2, index).start()

    def term_end(index):
        term_step(2, index, True).wait_recv()
        for which in range(3):
            term_step(which, index).wait_send()

    def head_step(which):
        if which == 0:
            source, target, to = head_parts.at[:, 1 - core], core_in, others[0]
        elif which == 1:
            source, target, to = head_parts.at[1 - across, core], across_in, others[1]
        else:
            source = head_parts.at[across, core, pl.ds(0, deep_count), 1 - side]
            target, to = side_in, others[2]
        return remote(source, target, head_sends.at[which], head_receives.at[which], to)

    def head_along(hop):
        target = lax.rem(deep + hop, deep_count)
        return remote(
            head_parts.at[across, core, target, side],
            deep_in.at[hop],
            head_sends.at[2 + hop],
            head_receives.at[2 + hop],
            at(across, core, target, side),
        )

    def head_next(which):
        if not spread_head:
            return
        head_step(which).wait_recv()
        if which == 0:
            for part in range(2):
                both = head_parts[part, core].astype(jnp.float32) + core_in[part].astype(jnp.float32)
                head_parts[part, core] = both.astype(low)
            head_step(1).start()
        elif which == 1:
            both = head_parts[across, core].astype(jnp.float32) + across_in[...].astype(jnp.float32)
            head_parts[across, core] = both.astype(low)
            head_step(2).start()
        else:
            both = head_parts[across, core, pl.ds(0, deep_count), side].astype(jnp.float32)
            both += side_in[...].astype(jnp.float32)
            head_parts[across, core, pl.ds(0, deep_count), side] = both.astype(low)
            for hop in range(1, deep_count):
                head_along(hop).start()

    def head_end():
        if not spread_head:
            return
        whole = head_parts[across, core, deep, side].astype(jnp.float32)
        for hop in range(1, deep_count):
            head_along(hop).wait_recv()
            whole += deep_in[hop].astype(jnp.float32)
        head_grad[...] = whole
        for which in range(3):
            head_step(which).wait_send()
        for hop in range(1, deep_count):
            head_along(hop).wait_send()

    def up(which, source):
        return remote(
            source,
            halo.at[which, 1],
            send_sem.at[which, 0],
            receive_sem.at[which, 1],
            (scale, space - 1),
        )

    def down(which, source):
        return remote(
            source,
            halo.at[which, 0],
            send_sem.at[which, 1],
            receive_sem.at[which, 0],
            (scale, space + 1),
        )

    def edge(array, row):
        return array.at[pl.ds((row + 1) * width, width), pl.ds(channels, channels)]

    def send_edges(which, array):
        @pl.when(above)
        def go_up():
            up(which, edge(array, 0)).start()

        @pl.when(below)
        def go_down():
            down(which, edge(array, rows - 1)).start()

    column = lax.broadcasted_iota(jnp.int32, (width, 1), 0)

    def put(array, slot, lane, count, value):
        here = pl.ds(slot * width, width)
        left = jnp.where(column == 0, 0.0, pltpu.roll(value, 1, 0))
        right = jnp.where(column == width - 1, 0.0, pltpu.roll(value, width - 1, 0))
        for which, moved in enumerate((left, value, right)):
            start = pl.multiple_of(which * channels + lane, LANES)
            array[here, pl.ds(start, count)] = moved.astype(low)

    def take_edges(which, array):
        for side, present, slot in ((0, above, 0), (1, below, rows + 1)):

            @pl.when(present)
            def arrived():
                if side == 0:
                    up(which, edge(array, 0)).wait_send()
                    down(which, edge(array, 0)).wait_recv()
                else:
                    down(which, edge(array, 0)).wait_send()
                    up(which, edge(array, 0)).wait_recv()
                for part in range(tiles):
                    value = halo[which, side, :, part * tile : (part + 1) * tile]
                    put(array, slot, part * tile, tile, value.astype(jnp.float32))

            @pl.when(jnp.logical_not(present))
            def missing():
                array[pl.ds(slot * width, width), :] = jnp.zeros(
                    (width, TAPS * channels), low
                )

    def loop(count, action):
        def body(index, carry):
            action(index)
            return carry

        lax.fori_loop(0, count, body, 0)

    def spot(index):
        return pl.multiple_of(index * tile, tile)

    pixels = rows * width
    band = TAPS * channels

    for row in range(rows):
        for part in range(tiles):
            value = features[row * width : (row + 1) * width, part * tile : (part + 1) * tile]
            put(wide.at[0], row + 1, part * tile, tile, value.astype(jnp.float32))
    send_edges(0, wide.at[0])

    for layer in range(layers):
        here = wide.at[layer]
        load(layer).wait()

        def middle(part):
            hidden[layer, :, pl.ds(spot(part), tile)] = mix(
                here[width : width + pixels, :],
                weights[layer, band : 2 * band, pl.ds(spot(part), tile)],
                1,
                0,
            )

        loop(tiles, middle)
        take_edges(layer, here)

        def outer(part):
            lane = pl.ds(spot(part), tile)
            total = mix(here[0:pixels, :], weights[layer, 0:band, lane], 1, 0)
            total += mix(
                here[2 * width : 2 * width + pixels, :],
                weights[layer, 2 * band : 3 * band, lane],
                1,
                0,
            )
            hidden[layer, :, lane] += total + conv_bias[layer : layer + 1, lane]
            for row in range(rows):
                span = slice(row * width, (row + 1) * width)
                value = gelu_value(hidden[layer, span, lane]) * row_values[row]
                if layer < layers - 1:
                    put(wide.at[layer + 1], row + 1, spot(part), tile, value)
                else:
                    last[span, lane] = value.astype(low)

        loop(tiles, outer)
        if layer < layers - 1:
            send_edges(layer + 1, wide.at[layer + 1])

    load(layers).wait()
    load(layers + 1).wait()
    last_turned[...] = last[...].astype(jnp.float32).T.astype(low)
    d_active[...] = jnp.zeros_like(d_active)

    def one_head(index):
        lane = pl.ds(pl.multiple_of(index * depth, depth), depth)
        projected = mix(last[...], head[:, lane], 1, 0) + head_bias[:, lane]
        gain = head_gain[:, lane]
        gain_total = jnp.zeros((1, depth), jnp.float32)
        bias_total = jnp.zeros((1, depth), jnp.float32)
        rounded = []
        for row in range(rows):
            span = slice(row * width, (row + 1) * width)
            weight = row_values[rows + row]
            value = projected[span]
            inverse = lax.rsqrt(jnp.sum(value * value, -1, keepdims=True) + 1e-06)
            normed = value * inverse
            scaled = gain * weight
            term[span, lane] = (normed * scaled).astype(low)
            given = cotangent[span, lane].astype(jnp.float32)
            gain_total += jnp.sum(normed * given, 0, keepdims=True) * weight
            d_normed = given * scaled
            along = jnp.sum(normed * d_normed, -1, keepdims=True)
            d_low = (inverse * (d_normed - normed * along)).astype(low)
            bias_total += jnp.sum(d_low.astype(jnp.float32), 0, keepdims=True)
            rounded.append(d_low)
        term_step(0, index).start()
        gain_grad[:, lane] = gain_total
        head_bias_grad[:, lane] = bias_total
        d_low = jnp.concatenate(rounded, 0)
        grad = mix(last_turned[...], d_low, 1, 0)
        if spread_head:
            split = grad.reshape(2, 2, deep_count, 2, head_rows, depth)
            head_parts[:, :, :, :, :, lane] = split.astype(low)
        else:
            head_grad[:, lane] = grad.astype(low)
        d_active[...] += mix(d_low, head[:, lane], 1, 1)

        @pl.when(index > 0)
        def earlier():
            term_pair(index - 1)

    loop(heads, one_head)
    if spread_head:
        head_step(0).start()
    term_pair(heads - 1)

    def store(layer):
        slot = layer % 2
        return pltpu.make_async_copy(grads.at[slot], grads_out.at[layer], store_sem.at[slot])

    for layer in reversed(range(layers)):
        which = 2 * layers - 1 - layer

        def enter(part):
            lane = pl.ds(spot(part), tile)
            total = jnp.zeros((1, tile), jnp.float32)
            for row in range(rows):
                span = slice(row * width, (row + 1) * width)
                slope = gelu_slope(hidden[layer, span, lane])
                value = slope * (row_values[row] * d_active[span, lane])
                value = value.astype(low).astype(jnp.float32)
                total += jnp.sum(value, 0, keepdims=True)
                put(d_wide, row + 1, spot(part), tile, value)
            conv_bias_grad[layer : layer + 1, lane] = total

        loop(tiles, enter)
        send_edges(which, d_wide)
        if layer + 2 < layers:
            store(layer + 2).wait()

        def one_tap(tap):
            tap_row, tap_column = tap // TAPS, lax.rem(tap, TAPS)
            window = wide[
                layer,
                pl.ds(pl.multiple_of(tap_row * width, width), pixels),
                pl.ds(pl.multiple_of(tap_column * channels, channels), channels),
            ]
            d_hidden = d_wide[width : width + pixels, channels : 2 * channels]
            grads[layer % 2, pl.ds(pl.multiple_of(tap * channels, channels), channels), :] = mix(
                window, d_hidden, 0, 0
            ).astype(low)

        loop(TAPS * TAPS, one_tap)
        store(layer).start()
        head_next(layers - 1 - layer)
        take_edges(which, d_wide)

        def back(part):
            total = jnp.zeros((pixels, tile), jnp.float32)
            for tap_row in range(TAPS):
                for tap_column in range(TAPS):
                    window = d_wide[
                        (2 - tap_row) * width : (2 - tap_row) * width + pixels,
                        (2 - tap_column) * channels : (3 - tap_column) * channels,
                    ]
                    first = (TAPS * tap_row + tap_column) * channels
                    total += mix(
                        window, weights[layer, pl.ds(first + spot(part), tile), :], 1, 1
                    )
            d_active[:, pl.ds(spot(part), tile)] = total

        loop(tiles, back)

    loop(heads, term_total)
    features_grad[...] = d_active[...].astype(low)
    head_end()
    loop(heads, term_end)
    for layer in range(min(layers, 2)):
        store(layer).wait()


def run_block(
    features, weights, head, conv_bias, head_bias, head_gain, cotangent, row_values, space_count
):
    rows, width, channels = features.shape
    layers = conv_bias.shape[0]
    head_width = head.shape[1]
    pixels = rows * width
    deep_count = space_count // 2
    head_rows = channels // (4 * space_count)
    spread_head = head_rows % 16 == 0
    low, full = jnp.bfloat16, jnp.float32
    dims = (layers, rows, width, channels, NH, HD, space_count)
    vmem = pl.BlockSpec(memory_space=pltpu.VMEM)
    anywhere = pl.BlockSpec(memory_space=pl.ANY)
    head_scratch = []
    head_out = jax.ShapeDtypeStruct((channels, head_width), low)
    if spread_head:
        head_out = jax.ShapeDtypeStruct((head_rows, head_width), full)
        head_scratch = [
            pltpu.VMEM((2, 2, deep_count, 2, head_rows, head_width), low),
            pltpu.VMEM((2, deep_count, 2, head_rows, head_width), low),
            pltpu.VMEM((deep_count, 2, head_rows, head_width), low),
            pltpu.VMEM((deep_count, head_rows, head_width), low),
            pltpu.VMEM((deep_count, head_rows, head_width), low),
            pltpu.SemaphoreType.DMA((2 + deep_count,)),
            pltpu.SemaphoreType.DMA((2 + deep_count,)),
        ]
    outs = pl.pallas_call(
        partial(work_kernel, dims),
        out_shape=(
            jax.ShapeDtypeStruct((pixels, head_width), low),
            jax.ShapeDtypeStruct((pixels, channels), low),
            jax.ShapeDtypeStruct(weights.shape, low),
            head_out,
            jax.ShapeDtypeStruct((layers, channels), full),
            jax.ShapeDtypeStruct((1, head_width), full),
            jax.ShapeDtypeStruct((1, head_width), full),
        ),
        in_specs=[
            vmem,
            anywhere,
            anywhere,
            vmem,
            vmem,
            vmem,
            anywhere,
            pl.BlockSpec(memory_space=pltpu.SMEM),
        ],
        out_specs=[vmem, vmem, anywhere, vmem, vmem, vmem, vmem],
        scratch_shapes=[
            pltpu.VMEM(weights.shape, low),
            pltpu.VMEM(head.shape, low),
            pltpu.VMEM((pixels, head_width), low),
            pltpu.VMEM((layers, (rows + 2) * width, TAPS * channels), low),
            pltpu.VMEM((layers, pixels, channels), full),
            pltpu.VMEM((pixels, channels), low),
            pltpu.VMEM((channels, pixels), low),
            pltpu.VMEM(((rows + 2) * width, TAPS * channels), low),
            pltpu.VMEM((pixels, channels), full),
            pltpu.VMEM((2,) + weights.shape[1:], low),
            pltpu.VMEM((2 * layers, 2, width, channels), low),
            pltpu.VMEM((pixels, head_width), low),
            pltpu.VMEM((2, NH, pixels, LANES), low),
            pltpu.SemaphoreType.DMA((layers + 2,)),
            pltpu.SemaphoreType.DMA((2,)),
            pltpu.SemaphoreType.DMA((2 * layers, 2)),
            pltpu.SemaphoreType.DMA((2 * layers, 2)),
            pltpu.SemaphoreType.DMA((3, NH)),
            pltpu.SemaphoreType.DMA((3, NH)),
        ]
        + head_scratch,
        compiler_params=pltpu.CompilerParams(
            collective_id=2, has_side_effects=True, vmem_limit_bytes=VMEM_LIMIT
        ),
    )(
        features.reshape(pixels, channels),
        weights,
        head,
        conv_bias,
        head_bias,
        head_gain,
        cotangent.reshape(pixels, head_width),
        row_values,
    )
    merged, features_grad, grads, head_grad, conv_bias_grad, head_bias_grad, gain_grad = outs
    if spread_head:
        head_grad = head_grad.reshape(-1)
    else:
        head_grad = lax.psum_scatter(
            head_grad.astype(full).reshape(-1), ("scale", "space"), scatter_dimension=0, tiled=True
        )
    vector = jnp.concatenate([conv_bias_grad.reshape(-1), head_bias_grad[0], gain_grad[0]])
    return (merged, features_grad, grads, head_grad, vector)


def halves(value):
    high = value.astype(jnp.bfloat16)
    return (high, (value - high.astype(jnp.float32)).astype(jnp.bfloat16))


def dot(left, right, left_dim, right_dim):
    left_high, left_low = halves(left)
    right_high, right_low = halves(right)
    rest = mix(left_high, right_low, left_dim, right_dim) + mix(left_low, right_high, left_dim, right_dim)
    return mix(left_high, right_high, left_dim, right_dim) + rest


def quick(x):
    r=pl.reciprocal(x,approx=True)
    return r*(2.0-x*r)
def eliminate(blocks, off, size, m=8):
    nl=len(blocks); nb=size//8; W=blocks[0][0].shape[1]
    sub=lax.broadcasted_iota(jnp.int32,(8,128),0)
    for k0 in range(0,size,m):
        b0=k0//8; s0=k0%8
        for l in range(nl):
            bl=blocks[l]
            top=bl[b0]
            def colb(b,j):
                return jnp.broadcast_to(bl[b][:,off+k0+j:off+k0+j+1],(8,128))
            c0=[colb(b0,j) for j in range(m)]
            a=[[None]*m for _ in range(m)]
            for j in range(m):
                for i in range(j,m):
                    a[i][j]=jnp.broadcast_to(c0[j][s0+i:s0+i+1,:],(8,128))
            inv=[]; low=[[None]*m for _ in range(m)]
            for k in range(m):
                r=quick(a[k][k]); inv.append(r)
                for i in range(k+1,m):
                    low[i][k]=a[i][k]*r
                for j in range(k+1,m):
                    for i in range(j,m):
                        a[i][j]=a[i][j]-low[i][k]*a[j][k]
            wid=lambda v: jnp.concatenate([v]*(W//128),1)
            rows=[jnp.broadcast_to(top[s0+i:s0+i+1,:],(8,W)) for i in range(m)]
            for i in range(m):
                for k in range(i):
                    rows[i]=rows[i]-wid(low[i][k])*rows[k]
            for b in range(b0,nb):
                if b==b0 and s0+m==8 and m==1: continue
                cs=list(c0) if b==b0 else [colb(b,j) for j in range(m)]
                for j in range(m):
                    for k in range(j):
                        cs[j]=cs[j]-low[j][k]*cs[k]
                acc=bl[b]
                for k in range(m):
                    w=cs[k]*inv[k]
                    if b==b0: w=jnp.where(sub>s0+k,w,0.0)
                    acc=acc-wid(w)*rows[k]
                bl[b]=acc
    out=[]
    lane=lax.broadcasted_iota(jnp.int32,(8,W),1)
    row8=lax.broadcasted_iota(jnp.int32,(8,W),0)
    for l in range(nl):
        res=[]
        for b in range(nb):
            v=blocks[l][b]
            d=jnp.sum(jnp.where(lane==row8+(off+8*b),v,0.0),1,keepdims=True)
            res.append(v*lax.rsqrt(d))
        out.append(jnp.concatenate(res,0))
    return out


def renew_kernel(layers, B, sum_ref, stat_ref, base_ref, sn_ref, bn_ref, m_ref, row_ref):
    C=stat_ref.shape[-1]
    D=128
    for l in range(layers):
        sn=BETA_TWO*stat_ref[l]+(1.0-BETA_TWO)*sum_ref[l]
        sn_ref[l]=sn
        pt=dot(base_ref[l],sn,0,0)
        m_ref[l,:,C:2*C]=pt
        m_ref[l,:,0:C]=dot(pt,pt,1,1)
    eye=(lax.broadcasted_iota(jnp.int32,(D,D),0)==lax.broadcasted_iota(jnp.int32,(D,D),1)).astype(jnp.float32)
    def outer(k,c):
        ks=pl.ds(pl.multiple_of(k*D,D),D)
        panels=[jnp.concatenate([m_ref[l,ks,ks],eye],1) for l in range(layers)]
        invs=[]
        done=[[] for _ in range(layers)]
        for j in range(D//B):
            blocks=[[p[8*i:8*i+8] for i in range(B//8)] for p in panels]
            tops=eliminate(blocks,B*j,B)
            for l in range(layers):
                done[l].append(tops[l][:,D:])
                if j<D//B-1:
                    panels[l]=panels[l][B:]-dot(tops[l][:,B*(j+1):D],tops[l],0,0)
        for l in range(layers):
            linv=jnp.concatenate(done[l],0)
            row_ref[l]=dot(linv,m_ref[l,ks,:],1,0)
            m_ref[l,ks,C:2*C]=row_ref[l,:,C:2*C]
        def inner(i,c2):
            is_=pl.ds(pl.multiple_of(i*D,D),D)
            for l in range(layers):
                m_ref[l,is_,:]=m_ref[l,is_,:]-dot(row_ref[l,:,is_],row_ref[l],0,0)
            return c2
        lax.fori_loop(k+1,C//D,inner,0)
        return c
    lax.fori_loop(0,C//D,outer,0)
    for l in range(layers):
        bn_ref[l]=m_ref[l,:,C:2*C].T

def renew(summed, statistics, bases, B=64):
    L,C,_=statistics.shape
    v=pl.BlockSpec(memory_space=pltpu.VMEM)
    sh=jax.ShapeDtypeStruct((L,C,C),jnp.float32)
    return pl.pallas_call(partial(renew_kernel,L,B),out_shape=(sh,sh),in_specs=[v]*3,out_specs=[v]*2,
      scratch_shapes=[pltpu.VMEM((L,C,2*C),jnp.float32),pltpu.VMEM((L,128,2*C),jnp.float32)],
      compiler_params=pltpu.CompilerParams(vmem_limit_bytes=VMEM_LIMIT))(summed,statistics,bases)


def moments(grads, first, second):
    first_new = BETA_ONE * first + (1.0 - BETA_ONE) * grads
    second_new = BETA_TWO * second + (1.0 - BETA_TWO) * grads * grads
    direction = (
        first_new
        / (1.0 - BETA_ONE**STEP)
        / (jnp.sqrt(second_new / (1.0 - BETA_TWO**STEP)) + EPSILON)
    )
    return (first_new, second_new, direction)


def local(
    features,
    valid_rows,
    conv_master,
    head_master,
    vectors,
    conv_first,
    conv_second,
    head_first,
    head_second,
    vec_first,
    vec_second,
    statistics,
    bases,
    cotangent,
):
    channels = features.shape[3]
    rows_dev = features.shape[1]
    width = features.shape[2]
    head_width = cotangent.shape[2]
    space_count = lax.axis_size("space")
    conv_used, head_used = gather_weights(
        conv_master, head_master.reshape(-1, head_width), space_count
    )
    conv_bias = vectors[: 3 * channels].reshape(3, channels)
    head_bias = vectors[3 * channels : 3 * channels + head_width]
    head_gain = vectors[3 * channels + head_width :]
    row_index = lax.axis_index("space") * rows_dev + jnp.arange(rows_dev, dtype=jnp.int32)
    row_mask = (row_index < valid_rows[lax.axis_index("scale")]).astype(jnp.float32)
    counts = jnp.sum((row_index[None, :] < valid_rows[:, None]).astype(jnp.float32), 0)
    row_values = jnp.concatenate([row_mask, row_mask / counts])
    merged, features_grad, stacked_grads, owned_head, vec_partial = run_block(
        features[0],
        conv_used,
        head_used,
        conv_bias,
        head_bias[None],
        head_gain[None],
        cotangent,
        row_values,
        space_count,
    )
    merged = merged.reshape(cotangent.shape)
    features_grad = features_grad.reshape(features.shape)
    owned_low, summed_stats, grad_vec = reduce_grads(stacked_grads, vec_partial, space_count)
    owned_conv = owned_low.astype(jnp.float32)
    rotated = jnp.einsum("lrc,lcd->lrd", owned_conv, bases, precision=lax.Precision.HIGHEST)
    conv_first_new, conv_second_new, direction = moments(rotated, conv_first, conv_second)
    turned = jnp.einsum("lrd,lcd->lrc", direction, bases, precision=lax.Precision.HIGHEST)
    conv_new = conv_master - RATE_CONV * (turned + DECAY * conv_master)
    head_first_new, head_second_new, head_dir = moments(owned_head, head_first, head_second)
    head_new = head_master - RATE_HEAD * (head_dir + DECAY * head_master)
    vec_first_new, vec_second_new, vec_dir = moments(grad_vec, vec_first, vec_second)
    rates = jnp.concatenate(
        [
            jnp.full((3 * channels + head_width,), RATE_BIAS, jnp.float32),
            jnp.full((head_width,), RATE_GAIN, jnp.float32),
        ]
    )
    vec_new = vectors - rates * (vec_dir + DECAY * vectors)
    stats_new, bases_new = renew(summed_stats.astype(jnp.float32), statistics, bases)
    return (
        merged,
        features_grad,
        conv_first_new,
        conv_second_new,
        conv_new,
        head_first_new,
        head_second_new,
        head_new,
        vec_first_new,
        vec_second_new,
        vec_new,
        stats_new,
        bases_new,
    )


def solution(mesh):
    in_specs = (
        P("scale", "space", None, None),
        P(),
        P(None, "space", None),
        P(("scale", "space")),
        P(),
        P(None, "space", None),
        P(None, "space", None),
        P(("scale", "space")),
        P(("scale", "space")),
        P(),
        P(),
        P(),
        P(),
        P("space", None, None),
    )
    out_specs = (
        P("space", None, None),
        P("scale", "space", None, None),
        P(None, "space", None),
        P(None, "space", None),
        P(None, "space", None),
        P(("scale", "space")),
        P(("scale", "space")),
        P(("scale", "space")),
        P(),
        P(),
        P(),
        P(),
        P(),
    )
    return jax.shard_map(local, mesh=mesh, in_specs=in_specs, out_specs=out_specs, check_vma=False)
```

```python
from functools import partial

import jax
import jax.experimental.pallas as pl
import jax.experimental.pallas.tpu as pltpu
import jax.numpy as jnp
from jax import lax
from jax.sharding import PartitionSpec as P

NH = 7
HD = 256
STEP = 5


BETA_ONE = 0.9
BETA_TWO = 0.95
EPSILON = 1e-08
DECAY = 0.01
RATE_CONV = 0.04
RATE_HEAD = 0.08
RATE_BIAS = 0.5
RATE_GAIN = 20.0
VMEM_LIMIT = 60 * 2**20
GELU_SCALE = 0.7978845608028654
GELU_CUBE = 0.044715


MESH = pl.DeviceIdType.MESH
LANES = 128


def place():
    scale, space = lax.axis_index("scale"), lax.axis_index("space")
    across, core = scale // 2, lax.rem(scale, 2)
    deep, side = space // 2, lax.rem(space, 2)
    return (across, core, deep, side)


def at(across, core, deep, side):
    return (2 * across + core, 2 * deep + side)


def greet(peers):
    barrier = pltpu.get_barrier_semaphore()
    for peer in peers:
        pl.semaphore_signal(barrier, inc=1, device_id=peer, device_id_type=MESH)
    pl.semaphore_wait(barrier, len(peers))


def remote(source, target, send, receive, device):
    return pltpu.make_async_remote_copy(
        src_ref=source,
        dst_ref=target,
        send_sem=send,
        recv_sem=receive,
        device_id=device,
        device_id_type=MESH,
    )


def lanes(index, count=1):
    return pl.ds(pl.multiple_of(index * LANES, LANES), count * LANES)


def partners(deep_count):
    across, core, deep, side = place()
    peers = [
        at(across, 1 - core, deep, side),
        at(1 - across, core, deep, side),
        at(across, core, deep, 1 - side),
    ]
    peers += [
        at(across, core, lax.rem(deep + hop, deep_count), side) for hop in range(1, deep_count)
    ]
    return peers


TAPS = 3


def gelu_parts(value):
    inner = GELU_SCALE * (value + GELU_CUBE * value * value * value)
    return jnp.tanh(inner)


def gelu_value(value):
    return 0.5 * value * (1.0 + gelu_parts(value))


def gelu_slope(value):
    bend = gelu_parts(value)
    rise = GELU_SCALE * (1.0 + 3.0 * GELU_CUBE * value * value)
    return 0.5 * (1.0 + bend) + 0.5 * value * (1.0 - bend * bend) * rise


def mix(left, right, left_dim, right_dim):
    return lax.dot_general(
        left,
        right,
        (((left_dim,), (right_dim,)), ((), ())),
        preferred_element_type=jnp.float32,
    )


def row_weights(valid, rows):
    scale, space = lax.axis_index("scale"), lax.axis_index("space")
    scales = lax.axis_size("scale")
    masks, weights = [], []
    for row in range(rows):
        place_in = space * rows + row
        mask = jnp.where(place_in < valid[scale], 1.0, 0.0)
        count = jnp.float32(0.0)
        for other in range(scales):
            count += jnp.where(place_in < valid[other], 1.0, 0.0)
        masks.append(mask)
        weights.append(jnp.full((1, LANES), mask) / jnp.full((1, LANES), count))
    return (masks, [weight[:, :1] for weight in weights])


def vector_lanes(vectors, start, part):
    row = start // LANES + 2 * part
    return jnp.concatenate([vectors[pl.ds(row, 1), :], vectors[pl.ds(row + 1, 1), :]], 1)


def greet_edges(peers, space_count):
    barrier = pltpu.get_barrier_semaphore()
    scale, space = lax.axis_index("scale"), lax.axis_index("space")
    for peer in peers:
        pl.semaphore_signal(barrier, inc=1, device_id=peer, device_id_type=MESH)
    next_space = space - 1 + 2 * lax.rem(space, 2)
    has_next = jnp.logical_and(next_space >= 0, next_space < space_count)

    @pl.when(has_next)
    def greet_next():
        pl.semaphore_signal(barrier, inc=1, device_id=(scale, next_space), device_id_type=MESH)

    pl.semaphore_wait(barrier, len(peers) + has_next.astype(jnp.int32))


def edge_tools(dims, halo, send_sem, receive_sem):
    rows, width, channels, space_count = dims[1], dims[2], dims[3], dims[6]
    tile = 2 * LANES
    tiles = channels // tile
    scale, space = lax.axis_index("scale"), lax.axis_index("space")
    above, below = space > 0, space < space_count - 1
    low = jnp.bfloat16

    def up(which, source):
        return remote(
            source,
            halo.at[which, 1],
            send_sem.at[which, 0],
            receive_sem.at[which, 1],
            (scale, space - 1),
        )

    def down(which, source):
        return remote(
            source,
            halo.at[which, 0],
            send_sem.at[which, 1],
            receive_sem.at[which, 0],
            (scale, space + 1),
        )

    def edge(array, row):
        return array.at[pl.ds((row + 1) * width, width), pl.ds(channels, channels)]

    def send_edges(which, array):
        @pl.when(above)
        def go_up():
            up(which, edge(array, 0)).start()

        @pl.when(below)
        def go_down():
            down(which, edge(array, rows - 1)).start()

    column = lax.broadcasted_iota(jnp.int32, (width, 1), 0)

    def put(array, slot, lane, count, value):
        here = pl.ds(slot * width, width)
        left = jnp.where(column == 0, 0.0, pltpu.roll(value, 1, 0))
        right = jnp.where(column == width - 1, 0.0, pltpu.roll(value, width - 1, 0))
        for which, moved in enumerate((left, value, right)):
            start = pl.multiple_of(which * channels + lane, LANES)
            array[here, pl.ds(start, count)] = moved.astype(low)

    def take_edges(which, array):
        for side, present, slot in ((0, above, 0), (1, below, rows + 1)):

            @pl.when(present)
            def arrived():
                if side == 0:
                    up(which, edge(array, 0)).wait_send()
                    down(which, edge(array, 0)).wait_recv()
                else:
                    down(which, edge(array, 0)).wait_send()
                    up(which, edge(array, 0)).wait_recv()
                for part in range(tiles):
                    value = halo[which, side, :, part * tile : (part + 1) * tile]
                    put(array, slot, part * tile, tile, value.astype(jnp.float32))

            @pl.when(jnp.logical_not(present))
            def missing():
                array[pl.ds(slot * width, width), :] = jnp.zeros(
                    (width, TAPS * channels), low
                )

    return (send_edges, take_edges, put)


def gather_kernel(
    dims,
    master,
    head_master,
    features,
    vectors,
    valid,
    full,
    head_full,
    wide_out,
    hidden_out,
    last_out,
    own,
    head_own,
    weights,
    wide,
    hidden,
    last,
    halo,
    local_sem,
    sends,
    receives,
    head_sends,
    head_receives,
    load_sem,
    store_sem,
    edge_sends,
    edge_receives,
):
    layers, rows, width, channels, heads, depth, space_count = dims
    deep_count = space_count // 2
    across, core, deep, side = place()
    block = 2 * core + across
    low = jnp.bfloat16
    own[0] = master[0].astype(low)
    greet_edges(partners(deep_count), space_count)

    chunks = layers * deep_count

    def split(chunk):
        rest = chunk - layers
        is_own = chunk < layers
        layer = jnp.where(is_own, chunk, rest // (deep_count - 1))
        hop = jnp.where(is_own, 0, 1 + lax.rem(rest + chunks, deep_count - 1))
        layer, hop = jnp.clip(layer, 0, layers - 1), jnp.clip(hop, 0, deep_count - 1)
        source = lax.rem(deep - hop + deep_count, deep_count)
        return (layer, hop, source, lax.rem(chunk, 2))

    def first(layer, hop):
        piece = own.at[layer, :, lanes(block)]
        target = full.at[layer, deep, side, :, lanes(block)]
        to = at(across, core, lax.rem(deep + hop, deep_count), side)
        return remote(piece, target, sends.at[0, layer, hop], receives.at[0, layer, hop], to)

    def first_in(layer, hop):
        source = lax.rem(deep - hop + deep_count, deep_count)
        piece = full.at[layer, source, side, :, lanes(block)]
        return remote(
            piece, piece, sends.at[0, layer, hop], receives.at[0, layer, hop], at(across, core, deep, side)
        )

    def second(chunk, incoming):
        layer, hop, source, odd = split(chunk)
        there_side = lax.rem(side + 1 - odd, 2)
        there_across = lax.rem(across + odd, 2)
        to = at(there_across, core, deep, there_side)
        if incoming:
            piece = full.at[layer, source, there_side, :, lanes(2 * core + there_across)]
        else:
            piece = full.at[layer, source, side, :, lanes(block)]
        return remote(piece, piece, sends.at[1, layer, hop], receives.at[1, layer, hop], to)

    def third(chunk, half, incoming):
        layer, hop, source, odd = split(chunk)
        there_side = lax.rem(side + odd, 2)
        there_across = lax.rem(across + 1 - odd, 2)
        to = at(there_across, core, deep, there_side)
        here = there_side if incoming else side
        lane = there_across if incoming else across
        piece_side = (1 - odd) * half + odd * here
        piece_lane = 2 * core + (1 - odd) * lane + odd * half
        piece = full.at[layer, source, piece_side, :, lanes(piece_lane)]
        return remote(
            piece, piece, sends.at[2 + half, layer, hop], receives.at[2 + half, layer, hop], to
        )

    def fourth(chunk, incoming):
        layer, hop, source, odd = split(chunk)
        column = 1 - core if incoming else core
        piece = full.at[layer, source, :, :, lanes(2 * column, 2)]
        to = at(across, 1 - core, deep, side)
        return remote(piece, piece, sends.at[4, layer, hop], receives.at[4, layer, hop], to)

    def local(layer):
        return pltpu.make_async_copy(
            own.at[layer, :, lanes(block)],
            full.at[layer, deep, side, :, lanes(block)],
            local_sem.at[layer],
        )

    def each(low, action):
        def step(hop, carry):
            action(hop)
            return carry

        lax.fori_loop(low, deep_count, step, 0)

    def head_local():
        return pltpu.make_async_copy(
            head_own, head_full.at[across, core, deep, side], local_sem.at[layers]
        )

    def head_first(hop):
        to = at(across, core, lax.rem(deep + hop, deep_count), side)
        target = head_full.at[across, core, deep, side]
        return remote(head_own, target, head_sends.at[hop], head_receives.at[hop], to)

    def head_first_in(hop):
        piece = head_full.at[across, core, lax.rem(deep - hop + deep_count, deep_count), side]
        to = at(across, core, deep, side)
        return remote(piece, piece, head_sends.at[hop], head_receives.at[hop], to)

    def head_next(which, incoming):
        if which == 0:
            to = at(across, core, deep, 1 - side)
            piece = head_full.at[across, core, :, 1 - side if incoming else side]
        elif which == 1:
            to = at(1 - across, core, deep, side)
            piece = head_full.at[1 - across if incoming else across, core]
        else:
            to = at(across, 1 - core, deep, side)
            piece = head_full.at[:, 1 - core if incoming else core]
        slot = deep_count + which
        return remote(piece, piece, head_sends.at[slot], head_receives.at[slot], to)

    def go_head(which):
        if which == 0:
            head_local().wait()
            each(1, lambda hop: head_first_in(hop).wait_recv())
        else:
            head_next(which - 1, True).wait_recv()
        if which < 3:
            head_next(which, False).start()

    send_edges, take_edges, put = edge_tools(dims, halo, edge_sends, edge_receives)
    tile = 2 * LANES
    tiles = channels // tile
    pixels = rows * width
    band = TAPS * channels
    masks, unused = row_weights(valid, rows)
    share = band * TAPS // space_count

    def loop(count, action):
        def body(index, carry):
            action(index)
            return carry

        lax.fori_loop(0, count, body, 0)

    def spot(index):
        return pl.multiple_of(index * tile, tile)

    def load(layer, owner):
        start = pl.multiple_of(owner * share, 8)
        return pltpu.make_async_copy(
            full.at[layer, owner // 2, lax.rem(owner, 2)],
            weights.at[layer % 2, pl.ds(start, share)],
            load_sem.at[layer % 2, owner],
        )

    def arrive(layer):
        fourth(layer, True).wait_recv()
        begin = layers + layer * (deep_count - 1)
        loop(deep_count - 1, lambda index: fourth(begin + index, True).wait_recv())
        loop(space_count, lambda owner: load(layer, owner).start())

    def store(which, layer):
        source, target = (
            (wide.at[layer], wide_out.at[layer]),
            (hidden.at[layer], hidden_out.at[layer]),
            (last, last_out),
        )[which]
        return pltpu.make_async_copy(source, target, store_sem.at[which, layer])

    def forward(layer):
        here = wide.at[layer]
        take_edges(layer, here)
        store(0, layer).start()
        loop(space_count, lambda owner: load(layer, owner).wait())

        def outer(part):
            lane = pl.ds(spot(part), tile)
            total = vector_lanes(vectors, layer * channels, part)
            for tap_row in range(TAPS):
                total += mix(
                    here[tap_row * width : tap_row * width + pixels, :],
                    weights[layer % 2, tap_row * band : (tap_row + 1) * band, lane],
                    1,
                    0,
                )
            hidden[layer, :, lane] = total
            for row in range(rows):
                span = slice(row * width, (row + 1) * width)
                value = gelu_value(hidden[layer, span, lane]) * masks[row]
                if layer < layers - 1:
                    put(wide.at[layer + 1], row + 1, spot(part), tile, value)
                else:
                    last[span, lane] = value.astype(low)

        loop(tiles, outer)
        store(1, layer).start()
        if layer < layers - 1:
            send_edges(layer + 1, wide.at[layer + 1])

    def go_second(chunk):
        layer, hop, source, odd = split(chunk)

        @pl.when(hop == 0)
        def own_rows():
            local(layer).wait()

        @pl.when(hop > 0)
        def other_rows():
            first_in(layer, hop).wait_recv()

        second(chunk, False).start()

    def go_third(chunk):
        second(chunk, True).wait_recv()
        third(chunk, 0, False).start()
        third(chunk, 1, False).start()

    def go_fourth(chunk):
        third(chunk, 0, True).wait_recv()
        third(chunk, 1, True).wait_recv()
        fourth(chunk, False).start()

    def go_head_first():
        each(1, lambda hop: head_first(hop).start())

    def go_first(layer):
        each(1, lambda hop: first(layer, hop).start())

    go_first(0)
    local(0).start()
    go_second(0)
    for layer in range(1, layers):
        own[layer] = master[layer].astype(low)
        local(layer).start()
    head_rows, head_blocks = head_own.shape[0], heads * depth // LANES
    for lane in range(head_blocks):
        head_own[:, lane * LANES : (lane + 1) * LANES] = head_master[
            pl.ds(lane, head_rows, stride=head_blocks), :
        ].astype(low)
    head_local().start()
    for row in range(rows):
        for part in range(tiles):
            value = features[row * width : (row + 1) * width, part * tile : (part + 1) * tile]
            put(wide.at[0], row + 1, part * tile, tile, value.astype(jnp.float32))
    send_edges(0, wide.at[0])

    lag_third, lag_fourth = 2, 5
    others = deep_count - 1

    def last_of(layer):
        return layers + others * (layer + 1) - 1 + lag_fourth

    early = min(2, others)
    timed = [(layers + others * (layer - 1) + early, go_first, layer) for layer in range(1, layers)]
    timed += [(layers + early, go_head_first)]
    timed += [(layers + others + 2 * which, go_head, which) for which in range(3)]
    for layer in range(layers - 1):
        timed += [(last_of(layer) + 1, arrive, layer), (last_of(layer) + 2, forward, layer)]

    def turn(now):
        for lag, action in ((0, go_second), (lag_third, go_third), (lag_fourth, go_fourth)):
            begin = max(lag, 1)

            @pl.when(jnp.logical_and(now >= begin, now < chunks + lag))
            def stage():
                action(now - lag)

        for moment, action, *which in timed:

            @pl.when(now == moment)
            def once():
                action(*which)

    loop(chunks + lag_fourth, turn)
    go_head(3)
    arrive(layers - 1)
    forward(layers - 1)
    store(2, 0).start()

    def finish(chunk):
        second(chunk, False).wait_send()
        third(chunk, 0, False).wait_send()
        third(chunk, 1, False).wait_send()
        fourth(chunk, False).wait_send()

    loop(chunks, finish)
    each(1, lambda hop: head_first(hop).wait_send())
    for which in range(3):
        head_next(which, False).wait_send()

    for layer in range(layers):

        each(1, lambda hop: first(layer, hop).wait_send())
        store(0, layer).wait()
        store(1, layer).wait()
    store(2, 0).wait()


def gather_weights(master, head_master, head_width, features, vectors, valid, space_count):
    layers, share, channels = master.shape
    rows, width, unused = features.shape
    deep_count = space_count // 2
    pixels = rows * width
    dims = (layers, rows, width, channels, NH, HD, space_count)
    low, wide_float = jnp.bfloat16, jnp.float32
    anywhere = pl.BlockSpec(memory_space=pl.ANY)
    vmem = pl.BlockSpec(memory_space=pltpu.VMEM)
    head_own = (head_master.shape[0] * LANES // head_width, head_width)
    head_shape = (2, 2, deep_count, 2) + head_own
    wide_shape = (layers, (rows + 2) * width, TAPS * channels)
    full, head_full, wide, hidden, last = pl.pallas_call(
        partial(gather_kernel, dims),
        out_shape=(
            jax.ShapeDtypeStruct((layers, deep_count, 2, share, channels), low),
            jax.ShapeDtypeStruct(head_shape, low),
            jax.ShapeDtypeStruct(wide_shape, low),
            jax.ShapeDtypeStruct((layers, pixels, channels), wide_float),
            jax.ShapeDtypeStruct((pixels, channels), low),
        ),
        in_specs=[vmem] * 4 + [pl.BlockSpec(memory_space=pltpu.SMEM)],
        out_specs=[anywhere] * 5,
        scratch_shapes=[
            pltpu.VMEM(master.shape, low),
            pltpu.VMEM(head_own, low),
            pltpu.VMEM((2, space_count * share, channels), low),
            pltpu.VMEM(wide_shape, low),
            pltpu.VMEM((layers, pixels, channels), wide_float),
            pltpu.VMEM((pixels, channels), low),
            pltpu.VMEM((layers, 2, width, channels), low),
            pltpu.SemaphoreType.DMA((layers + 1,)),
            pltpu.SemaphoreType.DMA((5, layers, deep_count)),
            pltpu.SemaphoreType.DMA((5, layers, deep_count)),
            pltpu.SemaphoreType.DMA((deep_count + 3,)),
            pltpu.SemaphoreType.DMA((deep_count + 3,)),
            pltpu.SemaphoreType.DMA((2, space_count)),
            pltpu.SemaphoreType.DMA((3, layers)),
            pltpu.SemaphoreType.DMA((layers, 2)),
            pltpu.SemaphoreType.DMA((layers, 2)),
        ],
        compiler_params=pltpu.CompilerParams(
            collective_id=0, has_side_effects=True, vmem_limit_bytes=VMEM_LIMIT
        ),
    )(master, head_master, features.reshape(pixels, channels), vectors, valid)
    return (
        full.reshape(layers, space_count * share, channels),
        head_full.reshape(-1, head_width),
        wide,
        hidden,
        last,
    )


def reduce_kernel(
    layers,
    deep_count,
    grads,
    vector,
    total,
    stats,
    vector_total,
    mine,
    core_in,
    second_in,
    kept,
    third_in,
    last,
    last_in,
    acc,
    stat_own,
    stat_in,
    stat_deep,
    vector_out,
    vector_in,
    vector_deep,
    local_sem,
    sends,
    receives,
    stat_sends,
    stat_receives,
    deep_sends,
    deep_receives,
    vector_sends,
    vector_receives,
):
    across, core, deep, side = place()
    block = 2 * core + across
    steps = layers * deep_count

    def split(step):
        layer, hop = step // deep_count, lax.rem(step, deep_count)
        target = lax.rem(deep + hop, deep_count)
        return (layer, hop, target, lax.rem(target, 2))

    def first(step):
        layer, hop, target, odd = split(step)
        return remote(
            grads.at[layer, target, :, :, lanes(2 * (1 - core), 2)],
            core_in.at[step],
            sends.at[0, step],
            receives.at[0, step],
            at(across, 1 - core, deep, side),
        )

    def load(step):
        layer, hop, target, odd = split(step)
        return pltpu.make_async_copy(
            grads.at[layer, target, :, :, lanes(2 * core, 2)], mine.at[step], local_sem.at[step]
        )

    def second(step, half):
        layer, hop, target, odd = split(step)
        piece_side = (1 - odd) * half + odd * (1 - side)
        piece_lane = (1 - odd) * (1 - across) + odd * half
        to = at(lax.rem(across + 1 - odd, 2), core, deep, lax.rem(side + odd, 2))
        return remote(
            mine.at[step, piece_side, :, lanes(piece_lane)],
            second_in.at[step, half],
            sends.at[1 + half, step],
            receives.at[1 + half, step],
            to,
        )

    def third(step):
        layer, hop, target, odd = split(step)
        keep = (1 - odd) * side + odd * across
        to = at(lax.rem(across + odd, 2), core, deep, lax.rem(side + 1 - odd, 2))
        return remote(
            kept.at[step, 1 - keep],
            third_in.at[step],
            sends.at[3, step],
            receives.at[3, step],
            to,
        )

    def fourth(step):
        layer, hop, target, odd = split(step)
        return remote(
            last.at[step],
            last_in.at[step],
            sends.at[4, step],
            receives.at[4, step],
            at(across, core, target, side),
        )

    def fifth(layer, incoming):
        lane = 2 * core + (1 - across if incoming else across)
        piece = total.at[layer, :, lanes(lane)]
        to = at(1 - across, core, deep, side)
        return remote(piece, piece, sends.at[5, layer], receives.at[5, layer], to)

    def sixth(layer, incoming):
        column = 1 - core if incoming else core
        piece = total.at[layer, :, lanes(2 * column, 2)]
        to = at(across, 1 - core, deep, side)
        return remote(piece, piece, sends.at[6, layer], receives.at[6, layer], to)

    def run(low, high, action):
        def body(step, carry):
            action(step)
            return carry

        lax.fori_loop(low, high, body, 0)

    half_block = LANES // 2

    def stat_side(layer, incoming):
        rows = pl.ds(pl.multiple_of((1 - side) * half_block, half_block), half_block)
        return remote(
            stat_own.at[layer, rows],
            stat_in.at[layer],
            stat_sends.at[0, layer],
            stat_receives.at[0, layer],
            at(across, core, deep, 1 - side),
        )

    def stat_along(layer, hop):
        return remote(
            stat_deep.at[layer, deep],
            stat_deep.at[layer, deep],
            deep_sends.at[layer, hop],
            deep_receives.at[layer, hop],
            at(across, core, lax.rem(deep + hop, deep_count), side),
        )

    def stat_along_in(layer, hop):
        source = lax.rem(deep - hop + deep_count, deep_count)
        return remote(
            stat_deep.at[layer, source],
            stat_deep.at[layer, source],
            deep_sends.at[layer, hop],
            deep_receives.at[layer, hop],
            at(across, core, deep, side),
        )

    def half_rows(which):
        return pl.ds(pl.multiple_of(which * half_block, half_block), half_block)

    def stat_spread(which, layer, incoming):
        if which == 0:
            to = at(across, core, deep, 1 - side)
            piece = stats.at[layer, block, half_rows(1 - side if incoming else side)]
        elif which == 1:
            to = at(1 - across, core, deep, side)
            piece = stats.at[layer, 2 * core + (1 - across if incoming else across)]
        else:
            to = at(across, 1 - core, deep, side)
            piece = stats.at[layer, pl.ds(2 * (1 - core if incoming else core), 2)]
        slot = 1 + which
        return remote(piece, piece, stat_sends.at[slot, layer], stat_receives.at[slot, layer], to)

    def vector_step(which):
        to = (
            at(across, 1 - core, deep, side),
            at(1 - across, core, deep, side),
            at(across, core, deep, 1 - side),
        )[which]
        return remote(
            vector_out.at[which],
            vector_in.at[which],
            vector_sends.at[which],
            vector_receives.at[which],
            to,
        )

    def vector_along(hop):
        return remote(
            vector_deep.at[deep],
            vector_deep.at[deep],
            vector_sends.at[2 + hop],
            vector_receives.at[2 + hop],
            at(across, core, lax.rem(deep + hop, deep_count), side),
        )

    def vector_along_in(hop):
        source = lax.rem(deep - hop + deep_count, deep_count)
        return remote(
            vector_deep.at[source],
            vector_deep.at[source],
            vector_sends.at[2 + hop],
            vector_receives.at[2 + hop],
            at(across, core, deep, side),
        )

    def go_first(step):
        load(step).start()
        first(step).start()

    ahead = min(3, steps)
    greet(partners(deep_count))
    run(0, ahead, go_first)

    def wide(left, right):
        return left.astype(jnp.float32) + right.astype(jnp.float32)

    def go_second(step):
        @pl.when(step + ahead < steps)
        def start_next():
            go_first(step + ahead)

        load(step).wait()
        first(step).wait_recv()
        mine[step] = wide(mine[step], core_in[step]).astype(jnp.bfloat16)
        second(step, 0).start()
        second(step, 1).start()

    def go_third(step):
        layer, hop, target, odd = split(step)
        for half in range(2):
            second(step, half).wait_recv()
            keep_side = (1 - odd) * half + odd * side
            keep_lane = (1 - odd) * across + odd * half
            kept[step, half] = wide(
                mine[step, keep_side, :, lanes(keep_lane)], second_in[step, half]
            ).astype(jnp.bfloat16)
        third(step).start()

    def go_fourth(step):
        layer, hop, target, odd = split(step)
        third(step).wait_recv()
        keep = (1 - odd) * side + odd * across
        last[step] = wide(kept[step, keep], third_in[step]).astype(jnp.bfloat16)

        @pl.when(hop > 0)
        def unused():
            fourth(step).start()

    def close(layer):
        acc[...] = last[layer * deep_count].astype(jnp.float32)

        def add(hop):
            step = layer * deep_count + hop
            fourth(step).wait_recv()
            acc[...] += last_in[step].astype(jnp.float32)

        run(1, deep_count, add)
        total[layer, :, lanes(block)] = acc[...].astype(jnp.bfloat16)
        fifth(layer, False).start()

    def spread(layer):
        fifth(layer, True).wait_recv()
        sixth(layer, False).start()

    def measure(layer):
        sixth(layer, True).wait_recv()
        own_lanes = total[layer, :, lanes(block)]
        stat_own[layer] = lax.dot_general(
            own_lanes,
            total[layer],
            (((0,), (0,)), ((), ())),
            preferred_element_type=jnp.float32,
        ).astype(jnp.bfloat16)
        stat_side(layer, False).start()

    def pair(layer):
        stat_side(layer, True).wait_recv()
        stat_deep[layer, deep] = wide(
            stat_own[layer, half_rows(side)], stat_in[layer]
        ).astype(jnp.bfloat16)
        run(1, deep_count, lambda hop: stat_along(layer, hop).start())

    def settle(layer):
        run(1, deep_count, lambda hop: stat_along_in(layer, hop).wait_recv())
        whole = stat_deep[layer, 0].astype(jnp.float32)
        for source in range(1, deep_count):
            whole += stat_deep[layer, source].astype(jnp.float32)
        stats[layer, block, half_rows(side)] = whole.astype(jnp.bfloat16)
        stat_spread(0, layer, False).start()

    def share_across(layer):
        stat_spread(0, layer, True).wait_recv()
        stat_spread(1, layer, False).start()

    def share_core(layer):
        stat_spread(1, layer, True).wait_recv()
        stat_spread(2, layer, False).start()

    def finish(layer):
        stat_spread(2, layer, True).wait_recv()
        fifth(layer, False).wait_send()
        sixth(layer, False).wait_send()
        stat_side(layer, False).wait_send()
        run(1, deep_count, lambda hop: stat_along(layer, hop).wait_send())
        for which in range(3):
            stat_spread(which, layer, False).wait_send()

    def vector_next(which):
        vector_step(which).wait_recv()
        summed = vector_out[which] + vector_in[which]
        if which < 2:
            vector_out[which + 1] = summed
            vector_step(which + 1).start()
        else:
            vector_deep[deep] = summed
            run(1, deep_count, lambda hop: vector_along(hop).start())

    chunk_work = ((0, go_second), (2, go_third), (4, go_fourth))
    layer_work = (
        (6, close),
        (7, spread),
        (8, measure),
        (9, pair),
        (10, settle),
        (11, share_across),
        (12, share_core),
        (13, finish),
    )
    vector_out[0] = vector[...]
    vector_step(0).start()

    def turn(now):
        for lag, action in chunk_work:

            @pl.when(jnp.logical_and(now >= lag, now < steps + lag))
            def chunk():
                action(now - lag)

        for which in range(3):

            @pl.when(now == 2 * which + 1)
            def exchange():
                vector_next(which)

        for lag, action in layer_work:
            past = now - lag - (deep_count - 1)

            @pl.when(
                jnp.logical_and(
                    jnp.logical_and(past >= 0, past < steps), lax.rem(past, deep_count) == 0
                )
            )
            def whole_layer():
                action(past // deep_count)

    run(0, steps + layer_work[-1][0], turn)

    run(1, deep_count, lambda hop: vector_along_in(hop).wait_recv())
    summed = vector_deep[0]
    for source in range(1, deep_count):
        summed += vector_deep[source]
    vector_total[...] = summed
    for which in range(3):
        vector_step(which).wait_send()
    run(1, deep_count, lambda hop: vector_along(hop).wait_send())

    def drain(step):
        layer, hop, target, odd = split(step)
        first(step).wait_send()
        second(step, 0).wait_send()
        second(step, 1).wait_send()
        third(step).wait_send()

        @pl.when(hop > 0)
        def unused():
            fourth(step).wait_send()

    run(0, steps, drain)


def reduce_grads(grads, vector, space_count):
    layers, all_rows, columns = grads.shape
    deep_count, rows = space_count // 2, all_rows // space_count
    steps = layers * deep_count
    low = jnp.bfloat16
    blocks = columns // LANES
    vmem = pl.BlockSpec(memory_space=pltpu.VMEM)
    total, stats, vector_total = pl.pallas_call(
        partial(reduce_kernel, layers, deep_count),
        out_shape=(
            jax.ShapeDtypeStruct((layers, rows, columns), low),
            jax.ShapeDtypeStruct((layers, blocks, LANES, columns), low),
            jax.ShapeDtypeStruct(vector.shape, jnp.float32),
        ),
        in_specs=[pl.BlockSpec(memory_space=pl.ANY), vmem],
        out_specs=[vmem, vmem, vmem],
        scratch_shapes=[
            pltpu.VMEM((steps, 2, rows, 2 * LANES), low),
            pltpu.VMEM((steps, 2, rows, 2 * LANES), low),
            pltpu.VMEM((steps, 2, rows, LANES), low),
            pltpu.VMEM((steps, 2, rows, LANES), low),
            pltpu.VMEM((steps, rows, LANES), low),
            pltpu.VMEM((steps, rows, LANES), low),
            pltpu.VMEM((steps, rows, LANES), low),
            pltpu.VMEM((rows, LANES), jnp.float32),
            pltpu.VMEM((layers, LANES, columns), low),
            pltpu.VMEM((layers, LANES // 2, columns), low),
            pltpu.VMEM((layers, deep_count, LANES // 2, columns), low),
            pltpu.VMEM((3,) + vector.shape, jnp.float32),
            pltpu.VMEM((3,) + vector.shape, jnp.float32),
            pltpu.VMEM((deep_count,) + vector.shape, jnp.float32),
            pltpu.SemaphoreType.DMA((steps,)),
            pltpu.SemaphoreType.DMA((7, steps)),
            pltpu.SemaphoreType.DMA((7, steps)),
            pltpu.SemaphoreType.DMA((4, layers)),
            pltpu.SemaphoreType.DMA((4, layers)),
            pltpu.SemaphoreType.DMA((layers, deep_count)),
            pltpu.SemaphoreType.DMA((layers, deep_count)),
            pltpu.SemaphoreType.DMA((2 + deep_count,)),
            pltpu.SemaphoreType.DMA((2 + deep_count,)),
        ],
        compiler_params=pltpu.CompilerParams(
            collective_id=1, has_side_effects=True, vmem_limit_bytes=VMEM_LIMIT
        ),
    )(grads.reshape(layers, deep_count, 2, rows, columns), vector)
    return (total, stats.reshape(layers, columns, columns), vector_total)


def work_kernel(
    dims,
    weights_in,
    head_in,
    wide_in,
    hidden_in,
    last_in,
    vectors,
    cotangent_in,
    valid,
    merged,
    features_grad,
    grads_out,
    head_grad,
    vector,
    weights,
    head,
    cotangent,
    wide,
    hidden,
    last,
    last_turned,
    d_wide,
    d_active,
    grads,
    halo,
    term,
    term_in,
    load_sem,
    store_sem,
    send_sem,
    receive_sem,
    term_sends,
    term_receives,
    *head_refs,
):
    layers, rows, width, channels, heads, depth, space_count = dims
    deep_count = space_count // 2
    across, core, deep, side = place()
    spread_head = len(head_refs) > 0
    if spread_head:
        head_parts, core_in, across_in, side_in, deep_in, head_sends, head_receives = head_refs
        head_rows = head_parts.shape[4]
    tile = 2 * LANES
    tiles = channels // tile
    low = jnp.bfloat16

    loads = ((last_in, last), (head_in, head), (cotangent_in, cotangent))
    for layer in reversed(range(layers)):
        loads += (
            (hidden_in.at[layer], hidden.at[layer]),
            (wide_in.at[layer], wide.at[layer]),
            (weights_in.at[layer], weights.at[layer]),
        )

    def load(which):
        source, target = loads[which]
        return pltpu.make_async_copy(source, target, load_sem.at[which])

    for which in range(len(loads)):
        load(which).start()

    others = [
        at(across, 1 - core, deep, side),
        at(1 - across, core, deep, side),
        at(across, core, deep, 1 - side),
    ]
    if spread_head:
        others += [
            at(across, core, lax.rem(deep + hop, deep_count), side) for hop in range(1, deep_count)
        ]
    greet_edges(others, space_count)

    def term_lanes(index, which):
        return pl.ds(pl.multiple_of(index * depth + which * LANES, LANES), LANES)

    def term_step(which, index, incoming=False):
        if which == 0:
            source, target, to = term.at[:, term_lanes(index, 1 - core)], term_in.at[0, index], others[0]
        elif which == 1:
            source, target, to = term.at[:, term_lanes(index, core)], term_in.at[1, index], others[1]
        else:
            source = merged.at[:, term_lanes(index, 1 - core if incoming else core)]
            target, to = source, others[0]
        return remote(
            source, target, term_sends.at[which, index], term_receives.at[which, index], to
        )

    def term_pair(index):
        term_step(0, index).wait_recv()
        lane = term_lanes(index, core)
        both = term[:, lane].astype(jnp.float32) + term_in[0, index].astype(jnp.float32)
        term[:, lane] = both.astype(low)
        term_step(1, index).start()

    def term_total(index):
        term_step(1, index).wait_recv()
        lane = term_lanes(index, core)
        both = term[:, lane].astype(jnp.float32) + term_in[1, index].astype(jnp.float32)
        merged[:, lane] = both.astype(low)
        term_step(2, index).start()

    def term_end(index):
        term_step(2, index, True).wait_recv()
        for which in range(3):
            term_step(which, index).wait_send()

    def head_step(which):
        if which == 0:
            source, target, to = head_parts.at[:, 1 - core], core_in, others[0]
        elif which == 1:
            source = head_parts.at[pl.ds(0, 2), core, pl.ds(0, deep_count), 1 - side]
            target, to = side_in, others[2]
        else:
            source = head_parts.at[1 - across, core, pl.ds(0, deep_count), side]
            target, to = across_in, others[1]
        return remote(source, target, head_sends.at[which], head_receives.at[which], to)

    def head_along(hop):
        target = lax.rem(deep + hop, deep_count)
        return remote(
            head_parts.at[across, core, target, side],
            deep_in.at[hop],
            head_sends.at[2 + hop],
            head_receives.at[2 + hop],
            at(across, core, target, side),
        )

    def head_next(which):
        if not spread_head:
            return
        head_step(which).wait_recv()
        if which == 0:
            for part in range(2):
                both = head_parts[part, core].astype(jnp.float32) + core_in[part].astype(jnp.float32)
                head_parts[part, core] = both.astype(low)
            head_step(1).start()
        elif which == 1:
            for part in range(2):
                both = head_parts[part, core, pl.ds(0, deep_count), side].astype(jnp.float32)
                both += side_in[part].astype(jnp.float32)
                head_parts[part, core, pl.ds(0, deep_count), side] = both.astype(low)
            head_step(2).start()
        else:
            both = head_parts[across, core, pl.ds(0, deep_count), side].astype(jnp.float32)
            both += across_in[...].astype(jnp.float32)
            head_parts[across, core, pl.ds(0, deep_count), side] = both.astype(low)
            for hop in range(1, deep_count):
                head_along(hop).start()

    def head_end():
        if not spread_head:
            return
        whole = head_parts[across, core, deep, side].astype(jnp.float32)
        for hop in range(1, deep_count):
            head_along(hop).wait_recv()
            whole += deep_in[hop].astype(jnp.float32)
        blocks = heads * depth // LANES
        for lane in range(blocks):
            head_grad[pl.ds(lane, head_rows, stride=blocks), :] = whole[
                :, lane * LANES : (lane + 1) * LANES
            ]
        for which in range(3):
            head_step(which).wait_send()
        for hop in range(1, deep_count):
            head_along(hop).wait_send()

    send_edges, take_edges, put = edge_tools(dims, halo, send_sem, receive_sem)

    def loop(count, action):
        def body(index, carry):
            action(index)
            return carry

        lax.fori_loop(0, count, body, 0)

    def spot(index):
        return pl.multiple_of(index * tile, tile)

    masks, weights_row = row_weights(valid, rows)

    def put_vector(start, part, value):
        row = start // LANES + 2 * part
        vector[pl.ds(row, 1), :] = value[:, :LANES]
        vector[pl.ds(row + 1, 1), :] = value[:, LANES:]

    pixels = rows * width
    for which in range(3):
        load(which).wait()
    last_turned[...] = last[...].astype(jnp.float32).T.astype(low)
    d_active[...] = jnp.zeros_like(d_active)

    def one_head(index):
        lane = pl.ds(pl.multiple_of(index * depth, depth), depth)
        projected = mix(last[...], head[:, lane], 1, 0)
        projected += vector_lanes(vectors, layers * channels, index)
        gain = vector_lanes(vectors, layers * channels + heads * depth, index)
        gain_total = jnp.zeros((1, depth), jnp.float32)
        bias_total = jnp.zeros((1, depth), jnp.float32)
        rounded = []
        for row in range(rows):
            span = slice(row * width, (row + 1) * width)
            weight = weights_row[row]
            value = projected[span]
            inverse = lax.rsqrt(jnp.sum(value * value, -1, keepdims=True) + 1e-06)
            normed = value * inverse
            scaled = gain * weight
            term[span, lane] = (normed * scaled).astype(low)
            given = cotangent[span, lane].astype(jnp.float32)
            gain_total += jnp.sum(normed * given, 0, keepdims=True) * weight
            d_normed = given * scaled
            along = jnp.sum(normed * d_normed, -1, keepdims=True)
            d_low = (inverse * (d_normed - normed * along)).astype(low)
            bias_total += jnp.sum(d_low.astype(jnp.float32), 0, keepdims=True)
            rounded.append(d_low)
        term_step(0, index).start()
        put_vector(layers * channels + heads * depth, index, gain_total)
        put_vector(layers * channels, index, bias_total)
        d_low = jnp.concatenate(rounded, 0)
        grad = mix(last_turned[...], d_low, 1, 0)
        if spread_head:
            split = grad.reshape(2, 2, deep_count, 2, head_rows, depth)
            head_parts[:, :, :, :, :, lane] = split.astype(low)
        else:
            head_grad[:, lane] = grad.astype(low)
        d_active[...] += mix(d_low, head[:, lane], 1, 1)

        @pl.when(index > 0)
        def earlier():
            term_pair(index - 1)

    loop(heads, one_head)
    if spread_head:
        head_step(0).start()
    term_pair(heads - 1)

    def store(layer):
        slot = layer % 2
        return pltpu.make_async_copy(grads.at[slot], grads_out.at[layer], store_sem.at[slot])

    for layer in reversed(range(layers)):
        which = layers - 1 - layer
        for part in range(3):
            load(3 + 3 * which + part).wait()

        def enter(part):
            lane = pl.ds(spot(part), tile)
            total = jnp.zeros((1, tile), jnp.float32)
            for row in range(rows):
                span = slice(row * width, (row + 1) * width)
                slope = gelu_slope(hidden[layer, span, lane])
                value = slope * (masks[row] * d_active[span, lane])
                value = value.astype(low).astype(jnp.float32)
                total += jnp.sum(value, 0, keepdims=True)
                put(d_wide, row + 1, spot(part), tile, value)
            put_vector(layer * channels, part, total)

        loop(tiles, enter)
        send_edges(which, d_wide)
        if layer + 2 < layers:
            store(layer + 2).wait()

        def one_tap(tap):
            tap_row, tap_column = tap // TAPS, lax.rem(tap, TAPS)
            window = wide[
                layer,
                pl.ds(pl.multiple_of(tap_row * width, width), pixels),
                pl.ds(pl.multiple_of(tap_column * channels, channels), channels),
            ]
            d_hidden = d_wide[width : width + pixels, channels : 2 * channels]
            grads[layer % 2, pl.ds(pl.multiple_of(tap * channels, channels), channels), :] = mix(
                window, d_hidden, 0, 0
            ).astype(low)

        loop(TAPS * TAPS, one_tap)
        store(layer).start()
        head_next(layers - 1 - layer)
        take_edges(which, d_wide)

        def back(part):
            total = jnp.zeros((pixels, tile), jnp.float32)
            for tap_row in range(TAPS):
                for tap_column in range(TAPS):
                    window = d_wide[
                        (2 - tap_row) * width : (2 - tap_row) * width + pixels,
                        (2 - tap_column) * channels : (3 - tap_column) * channels,
                    ]
                    first = (TAPS * tap_row + tap_column) * channels
                    total += mix(
                        window, weights[layer, pl.ds(first + spot(part), tile), :], 1, 1
                    )
            d_active[:, pl.ds(spot(part), tile)] = total

        loop(tiles, back)

    loop(heads, term_total)
    features_grad[...] = d_active[...].astype(low)
    head_end()
    loop(heads, term_end)
    for layer in range(min(layers, 2)):
        store(layer).wait()


def run_block(
    weights, head, wide, hidden, last, vectors, cotangent, valid, space_count
):
    rows, width, unused = cotangent.shape
    layers, unused, channels = weights.shape
    head_width = head.shape[1]
    pixels = rows * width
    deep_count = space_count // 2
    head_rows = channels // (4 * space_count)
    spread_head = head_rows % 16 == 0
    low, full = jnp.bfloat16, jnp.float32
    dims = (layers, rows, width, channels, NH, HD, space_count)
    vmem = pl.BlockSpec(memory_space=pltpu.VMEM)
    anywhere = pl.BlockSpec(memory_space=pl.ANY)
    head_scratch = []
    head_out = jax.ShapeDtypeStruct((channels, head_width), low)
    if spread_head:
        head_out = jax.ShapeDtypeStruct((head_rows * head_width // LANES, LANES), full)
        head_scratch = [
            pltpu.VMEM((2, 2, deep_count, 2, head_rows, head_width), low),
            pltpu.VMEM((2, deep_count, 2, head_rows, head_width), low),
            pltpu.VMEM((deep_count, head_rows, head_width), low),
            pltpu.VMEM((2, deep_count, head_rows, head_width), low),
            pltpu.VMEM((deep_count, head_rows, head_width), low),
            pltpu.SemaphoreType.DMA((2 + deep_count,)),
            pltpu.SemaphoreType.DMA((2 + deep_count,)),
        ]
    outs = pl.pallas_call(
        partial(work_kernel, dims),
        out_shape=(
            jax.ShapeDtypeStruct((pixels, head_width), low),
            jax.ShapeDtypeStruct((pixels, channels), low),
            jax.ShapeDtypeStruct(weights.shape, low),
            head_out,
            jax.ShapeDtypeStruct(vectors.shape, full),
        ),
        in_specs=[
            anywhere,
            anywhere,
            anywhere,
            anywhere,
            anywhere,
            vmem,
            anywhere,
            pl.BlockSpec(memory_space=pltpu.SMEM),
        ],
        out_specs=[vmem, vmem, anywhere, vmem, vmem],
        scratch_shapes=[
            pltpu.VMEM(weights.shape, low),
            pltpu.VMEM(head.shape, low),
            pltpu.VMEM((pixels, head_width), low),
            pltpu.VMEM((layers, (rows + 2) * width, TAPS * channels), low),
            pltpu.VMEM((layers, pixels, channels), full),
            pltpu.VMEM((pixels, channels), low),
            pltpu.VMEM((channels, pixels), low),
            pltpu.VMEM(((rows + 2) * width, TAPS * channels), low),
            pltpu.VMEM((pixels, channels), full),
            pltpu.VMEM((2,) + weights.shape[1:], low),
            pltpu.VMEM((layers, 2, width, channels), low),
            pltpu.VMEM((pixels, head_width), low),
            pltpu.VMEM((2, NH, pixels, LANES), low),
            pltpu.SemaphoreType.DMA((3 * layers + 3,)),
            pltpu.SemaphoreType.DMA((2,)),
            pltpu.SemaphoreType.DMA((layers, 2)),
            pltpu.SemaphoreType.DMA((layers, 2)),
            pltpu.SemaphoreType.DMA((3, NH)),
            pltpu.SemaphoreType.DMA((3, NH)),
        ]
        + head_scratch,
        compiler_params=pltpu.CompilerParams(
            collective_id=2, has_side_effects=True, vmem_limit_bytes=VMEM_LIMIT
        ),
    )(
        weights,
        head,
        wide,
        hidden,
        last,
        vectors,
        cotangent.reshape(pixels, head_width),
        valid,
    )
    merged, features_grad, grads, head_grad, vector = outs
    if not spread_head:
        head_grad = lax.psum_scatter(
            head_grad.astype(full).reshape(-1), ("scale", "space"), scatter_dimension=0, tiled=True
        ).reshape(-1, LANES)
    return (merged, features_grad, grads, head_grad, vector)


def halves(value):
    high = value.astype(jnp.bfloat16)
    return (high, (value - high.astype(jnp.float32)).astype(jnp.bfloat16))


def dot(left, right, left_dim, right_dim):
    left_high, left_low = halves(left)
    right_high, right_low = halves(right)
    rest = mix(left_high, right_low, left_dim, right_dim) + mix(left_low, right_high, left_dim, right_dim)
    return mix(left_high, right_high, left_dim, right_dim) + rest


def quick(x):
    return pl.reciprocal(x,approx=True)
def eliminate(blocks, off, size, m=8):
    nl=len(blocks); nb=size//8; W=blocks[0][0].shape[1]
    sub=lax.broadcasted_iota(jnp.int32,(8,128),0)
    for k0 in range(0,size,m):
        b0=k0//8; s0=k0%8
        for l in range(nl):
            bl=blocks[l]
            top=bl[b0]
            def colb(b,j):
                return jnp.broadcast_to(bl[b][:,off+k0+j:off+k0+j+1],(8,128))
            c0=[colb(b0,j) for j in range(m)]
            a=[[None]*m for _ in range(m)]
            for j in range(m):
                for i in range(j,m):
                    a[i][j]=jnp.broadcast_to(c0[j][s0+i:s0+i+1,:],(8,128))
            inv=[]; low=[[None]*m for _ in range(m)]
            for k in range(m):
                r=quick(a[k][k]); inv.append(r)
                for i in range(k+1,m):
                    low[i][k]=a[i][k]*r
                for j in range(k+1,m):
                    for i in range(j,m):
                        a[i][j]=a[i][j]-low[i][k]*a[j][k]
            wid=lambda v: jnp.concatenate([v]*(W//128),1)
            rows=[jnp.broadcast_to(top[s0+i:s0+i+1,:],(8,W)) for i in range(m)]
            for i in range(m):
                for k in range(i):
                    rows[i]=rows[i]-wid(low[i][k])*rows[k]
            for b in range(b0,nb):
                if b==b0 and s0+m==8 and m==1: continue
                cs=list(c0) if b==b0 else [colb(b,j) for j in range(m)]
                for j in range(m):
                    for k in range(j):
                        cs[j]=cs[j]-low[j][k]*cs[k]
                acc=bl[b]
                for k in range(m):
                    w=cs[k]*inv[k]
                    if b==b0: w=jnp.where(sub>s0+k,w,0.0)
                    acc=acc-wid(w)*rows[k]
                bl[b]=acc
    out=[]
    lane=lax.broadcasted_iota(jnp.int32,(8,W),1)
    row8=lax.broadcasted_iota(jnp.int32,(8,W),0)
    for l in range(nl):
        res=[]
        for b in range(nb):
            v=blocks[l][b]
            d=jnp.sum(jnp.where(lane==row8+(off+8*b),v,0.0),1,keepdims=True)
            res.append(v*lax.rsqrt(d))
        out.append(jnp.concatenate(res,0))
    return out


def moments(grads, first, second):
    first_new = BETA_ONE * first + (1.0 - BETA_ONE) * grads
    second_new = BETA_TWO * second + (1.0 - BETA_TWO) * grads * grads
    direction = (
        first_new
        * (1.0 / (1.0 - BETA_ONE**STEP))
        / (jnp.sqrt(second_new * (1.0 / (1.0 - BETA_TWO**STEP))) + EPSILON)
    )
    return (first_new, second_new, direction)


def update_kernel(
    dims,
    summed,
    statistics,
    bases,
    grads,
    first_in,
    second_in,
    master_in,
    head_grad,
    head_first,
    head_second,
    head_master,
    vector_grad,
    vector_first,
    vector_second,
    vectors,
    stats_new,
    bases_new,
    first_out,
    second_out,
    master_out,
    head_first_new,
    head_second_new,
    head_new,
    vector_first_new,
    vector_second_new,
    vectors_new,
    system,
    pivot,
    first,
    second,
    master,
    load_sem,
    store_sem,
):
    layers, rows, channels, piece, bias_rows, panel = dims
    block = LANES

    def load(which, layer):
        source, target = ((first_in, first), (second_in, second), (master_in, master))[which]
        return pltpu.make_async_copy(
            source.at[layer], target.at[layer], load_sem.at[which, layer]
        )

    def store(which, layer):
        source, target = ((first, first_out), (second, second_out), (master, master_out))[which]
        return pltpu.make_async_copy(
            source.at[layer], target.at[layer], store_sem.at[which, layer]
        )

    for layer in range(layers):
        for which in range(3):
            load(which, layer).start()

    for layer in range(layers):
        fresh = BETA_TWO * statistics[layer] + (1.0 - BETA_TWO) * summed[layer].astype(jnp.float32)
        stats_new[layer] = fresh
        turned = dot(bases[layer], fresh, 0, 0)
        system[layer, :, channels : 2 * channels] = turned
        system[layer, :, 0:channels] = dot(turned, turned, 1, 1)

    head = moments(head_grad[...], head_first[...], head_second[...])
    head_first_new[...] = head[0]
    head_second_new[...] = head[1]
    head_new[...] = head_master[...] - RATE_HEAD * (head[2] + DECAY * head_master[...])
    vec = moments(vector_grad[...], vector_first[...], vector_second[...])
    vector_first_new[...] = vec[0]
    vector_second_new[...] = vec[1]
    row = lax.broadcasted_iota(jnp.int32, vectors.shape, 0)
    rates = jnp.where(row < bias_rows, RATE_BIAS, RATE_GAIN)
    vectors_new[...] = vectors[...] - rates * (vec[2] + DECAY * vectors[...])

    for layer in range(layers):
        for which in range(3):
            load(which, layer).wait()
        high, rest = halves(bases[layer])

        def one_piece(index, carry):
            here = pl.ds(pl.multiple_of(index * piece, piece), piece)
            given = grads[layer, here, :]
            rotated = mix(given, high, 1, 0) + mix(given, rest, 1, 0)
            first_new, second_new, direction = moments(
                rotated, first[layer, here, :], second[layer, here, :]
            )
            first[layer, here, :] = first_new
            second[layer, here, :] = second_new
            up, down = halves(direction)
            back = mix(up, high, 1, 1) + (mix(up, rest, 1, 1) + mix(down, high, 1, 1))
            old = master[layer, here, :]
            master[layer, here, :] = old - RATE_CONV * (back + DECAY * old)
            return carry

        lax.fori_loop(0, rows // piece, one_piece, 0)
        for which in range(3):
            store(which, layer).start()

    eye = (
        lax.broadcasted_iota(jnp.int32, (block, block), 0)
        == lax.broadcasted_iota(jnp.int32, (block, block), 1)
    ).astype(jnp.float32)

    def outer(k, carry):
        here = pl.ds(pl.multiple_of(k * block, block), block)
        panels = [jnp.concatenate([system[layer, here, here], eye], 1) for layer in range(layers)]
        done = [[] for _ in range(layers)]
        for j in range(block // panel):
            blocks = [[p[8 * i : 8 * i + 8] for i in range(panel // 8)] for p in panels]
            tops = eliminate(blocks, panel * j, panel)
            for layer in range(layers):
                done[layer].append(tops[layer][:, block:])
                if j < block // panel - 1:
                    panels[layer] = panels[layer][panel:] - dot(
                        tops[layer][:, panel * (j + 1) : block], tops[layer], 0, 0
                    )
        for layer in range(layers):
            inverse = jnp.concatenate(done[layer], 0)
            pivot[layer] = dot(inverse, system[layer, here, :], 1, 0)
            system[layer, here, channels : 2 * channels] = pivot[layer, :, channels : 2 * channels]

        def inner(i, carry_in):
            below = pl.ds(pl.multiple_of(i * block, block), block)
            for layer in range(layers):
                system[layer, below, :] -= dot(pivot[layer, :, below], pivot[layer], 0, 0)
            return carry_in

        lax.fori_loop(k + 1, channels // block, inner, 0)
        return carry

    lax.fori_loop(0, channels // block, outer, 0)
    for layer in range(layers):
        bases_new[layer] = system[layer, :, channels : 2 * channels].T
        for which in range(3):
            store(which, layer).wait()


def update(summed, statistics, bases, grads, conv, head, vector, bias_rows):
    layers, rows, channels = grads.shape
    piece = 144 if rows % 144 == 0 else rows
    dims = (layers, rows, channels, piece, bias_rows, 32)
    vmem = pl.BlockSpec(memory_space=pltpu.VMEM)
    anywhere = pl.BlockSpec(memory_space=pl.ANY)
    square = jax.ShapeDtypeStruct(statistics.shape, jnp.float32)
    tall = jax.ShapeDtypeStruct(grads.shape, jnp.float32)
    head_shape = jax.ShapeDtypeStruct(head[0].shape, jnp.float32)
    vector_shape = jax.ShapeDtypeStruct(vector[0].shape, jnp.float32)
    return pl.pallas_call(
        partial(update_kernel, dims),
        out_shape=(square,) * 2 + (tall,) * 3 + (head_shape,) * 3 + (vector_shape,) * 3,
        in_specs=[vmem] * 4 + [anywhere] * 3 + [vmem] * 8,
        out_specs=[vmem] * 2 + [anywhere] * 3 + [vmem] * 6,
        scratch_shapes=[
            pltpu.VMEM((layers, channels, 2 * channels), jnp.float32),
            pltpu.VMEM((layers, LANES, 2 * channels), jnp.float32),
            pltpu.VMEM(grads.shape, jnp.float32),
            pltpu.VMEM(grads.shape, jnp.float32),
            pltpu.VMEM(grads.shape, jnp.float32),
            pltpu.SemaphoreType.DMA((3, layers)),
            pltpu.SemaphoreType.DMA((3, layers)),
        ],
        compiler_params=pltpu.CompilerParams(vmem_limit_bytes=VMEM_LIMIT),
    )(summed, statistics, bases, grads, *conv, *head, *vector)


def local(
    features,
    valid_rows,
    conv_master,
    head_master,
    vectors,
    conv_first,
    conv_second,
    head_first,
    head_second,
    vec_first,
    vec_second,
    statistics,
    bases,
    cotangent,
):
    channels = features.shape[3]
    head_width = cotangent.shape[2]
    space_count = lax.axis_size("space")
    vectors, vec_first, vec_second, head_master, head_first, head_second = (
        array.reshape(-1, LANES)
        for array in (vectors, vec_first, vec_second, head_master, head_first, head_second)
    )
    conv_used, head_used, wide, hidden, last = gather_weights(
        conv_master, head_master, head_width, features[0], vectors, valid_rows, space_count
    )
    merged, features_grad, grads, owned_head, vector = run_block(
        conv_used,
        head_used,
        wide,
        hidden,
        last,
        vectors,
        cotangent,
        valid_rows,
        space_count,
    )
    owned_conv, summed_stats, grad_vec = reduce_grads(grads, vector, space_count)
    outs = update(
        summed_stats,
        statistics,
        bases,
        owned_conv,
        (conv_first, conv_second, conv_master),
        (owned_head, head_first, head_second, head_master),
        (grad_vec, vec_first, vec_second, vectors),
        (3 * channels + head_width) // LANES,
    )
    stats_new, bases_new = outs[:2]
    return (
        merged.reshape(cotangent.shape),
        features_grad.reshape(features.shape),
        *outs[2:5],
        *(out.reshape(-1) for out in outs[5:]),
        stats_new,
        bases_new,
    )


def solution(mesh):
    in_specs = (
        P("scale", "space", None, None),
        P(),
        P(None, "space", None),
        P(("scale", "space")),
        P(),
        P(None, "space", None),
        P(None, "space", None),
        P(("scale", "space")),
        P(("scale", "space")),
        P(),
        P(),
        P(),
        P(),
        P("space", None, None),
    )
    out_specs = (
        P("space", None, None),
        P("scale", "space", None, None),
        P(None, "space", None),
        P(None, "space", None),
        P(None, "space", None),
        P(("scale", "space")),
        P(("scale", "space")),
        P(("scale", "space")),
        P(),
        P(),
        P(),
        P(),
        P(),
    )
    return jax.shard_map(local, mesh=mesh, in_specs=in_specs, out_specs=out_specs, check_vma=False)
```

```python
from functools import partial

import jax
import jax.experimental.pallas as pl
import jax.experimental.pallas.tpu as pltpu
import jax.numpy as jnp
from jax import lax
from jax.sharding import PartitionSpec as P

NH = 7
HD = 256
STEP = 5


BETA_ONE = 0.9
BETA_TWO = 0.95
EPSILON = 1e-08
DECAY = 0.01
RATE_CONV = 0.04
RATE_HEAD = 0.08
RATE_BIAS = 0.5
RATE_GAIN = 20.0
VMEM_LIMIT = 60 * 2**20
GELU_SCALE = 0.7978845608028654
GELU_CUBE = 0.044715


MESH = pl.DeviceIdType.MESH
LANES = 128


def place():
    scale, space = lax.axis_index("scale"), lax.axis_index("space")
    across, core = scale // 2, lax.rem(scale, 2)
    deep, side = space // 2, lax.rem(space, 2)
    return (across, core, deep, side)


def at(across, core, deep, side):
    return (2 * across + core, 2 * deep + side)


def greet(peers):
    barrier = pltpu.get_barrier_semaphore()
    for peer in peers:
        pl.semaphore_signal(barrier, inc=1, device_id=peer, device_id_type=MESH)
    pl.semaphore_wait(barrier, len(peers))


def remote(source, target, send, receive, device):
    return pltpu.make_async_remote_copy(
        src_ref=source,
        dst_ref=target,
        send_sem=send,
        recv_sem=receive,
        device_id=device,
        device_id_type=MESH,
    )


def lanes(index, count=1):
    return pl.ds(pl.multiple_of(index * LANES, LANES), count * LANES)


def partners(deep_count):
    across, core, deep, side = place()
    peers = [
        at(across, 1 - core, deep, side),
        at(1 - across, core, deep, side),
        at(across, core, deep, 1 - side),
    ]
    peers += [
        at(across, core, lax.rem(deep + hop, deep_count), side) for hop in range(1, deep_count)
    ]
    return peers


TAPS = 3


def gelu_parts(value):
    inner = GELU_SCALE * (value + GELU_CUBE * value * value * value)
    return jnp.tanh(inner)


def gelu_value(value):
    return 0.5 * value * (1.0 + gelu_parts(value))


def gelu_slope(value):
    bend = gelu_parts(value)
    rise = GELU_SCALE * (1.0 + 3.0 * GELU_CUBE * value * value)
    return 0.5 * (1.0 + bend) + 0.5 * value * (1.0 - bend * bend) * rise


def mix(left, right, left_dim, right_dim):
    return lax.dot_general(
        left,
        right,
        (((left_dim,), (right_dim,)), ((), ())),
        preferred_element_type=jnp.float32,
    )


def row_weights(valid, rows):
    scale, space = lax.axis_index("scale"), lax.axis_index("space")
    scales = lax.axis_size("scale")
    masks, weights = [], []
    for row in range(rows):
        place_in = space * rows + row
        mask = jnp.where(place_in < valid[scale], 1.0, 0.0)
        count = jnp.float32(0.0)
        for other in range(scales):
            count += jnp.where(place_in < valid[other], 1.0, 0.0)
        masks.append(mask)
        weights.append(jnp.full((1, LANES), mask) / jnp.full((1, LANES), count))
    return (masks, [weight[:, :1] for weight in weights])


def vector_lanes(vectors, start, part):
    row = start // LANES + 2 * part
    return jnp.concatenate([vectors[pl.ds(row, 1), :], vectors[pl.ds(row + 1, 1), :]], 1)


def greet_edges(peers, space_count):
    barrier = pltpu.get_barrier_semaphore()
    scale, space = lax.axis_index("scale"), lax.axis_index("space")
    for peer in peers:
        pl.semaphore_signal(barrier, inc=1, device_id=peer, device_id_type=MESH)
    next_space = space - 1 + 2 * lax.rem(space, 2)
    has_next = jnp.logical_and(next_space >= 0, next_space < space_count)

    @pl.when(has_next)
    def greet_next():
        pl.semaphore_signal(barrier, inc=1, device_id=(scale, next_space), device_id_type=MESH)

    pl.semaphore_wait(barrier, len(peers) + has_next.astype(jnp.int32))


def edge_tools(dims, halo, send_sem, receive_sem):
    rows, width, channels, space_count = dims[1], dims[2], dims[3], dims[6]
    tile = 2 * LANES
    tiles = channels // tile
    scale, space = lax.axis_index("scale"), lax.axis_index("space")
    above, below = space > 0, space < space_count - 1
    low = jnp.bfloat16

    def up(which, source):
        return remote(
            source,
            halo.at[which, 1],
            send_sem.at[which, 0],
            receive_sem.at[which, 1],
            (scale, space - 1),
        )

    def down(which, source):
        return remote(
            source,
            halo.at[which, 0],
            send_sem.at[which, 1],
            receive_sem.at[which, 0],
            (scale, space + 1),
        )

    def edge(array, row):
        return array.at[pl.ds((row + 1) * width, width), pl.ds(channels, channels)]

    def send_edges(which, array):
        @pl.when(above)
        def go_up():
            up(which, edge(array, 0)).start()

        @pl.when(below)
        def go_down():
            down(which, edge(array, rows - 1)).start()

    column = lax.broadcasted_iota(jnp.int32, (width, 1), 0)

    def put(array, slot, lane, count, value):
        here = pl.ds(slot * width, width)
        left = jnp.where(column == 0, 0.0, pltpu.roll(value, 1, 0))
        right = jnp.where(column == width - 1, 0.0, pltpu.roll(value, width - 1, 0))
        for which, moved in enumerate((left, value, right)):
            start = pl.multiple_of(which * channels + lane, LANES)
            array[here, pl.ds(start, count)] = moved.astype(low)

    def take_edges(which, array):
        for side, present, slot in ((0, above, 0), (1, below, rows + 1)):

            @pl.when(present)
            def arrived():
                if side == 0:
                    up(which, edge(array, 0)).wait_send()
                    down(which, edge(array, 0)).wait_recv()
                else:
                    down(which, edge(array, 0)).wait_send()
                    up(which, edge(array, 0)).wait_recv()
                for part in range(tiles):
                    value = halo[which, side, :, part * tile : (part + 1) * tile]
                    put(array, slot, part * tile, tile, value.astype(jnp.float32))

            @pl.when(jnp.logical_not(present))
            def missing():
                array[pl.ds(slot * width, width), :] = jnp.zeros(
                    (width, TAPS * channels), low
                )

    return (send_edges, take_edges, put)


def gather_kernel(
    dims,
    master,
    head_master,
    features,
    vectors,
    valid,
    full,
    head_full,
    wide_out,
    hidden_out,
    last_out,
    own,
    head_own,
    weights,
    wide,
    hidden,
    last,
    halo,
    local_sem,
    sends,
    receives,
    head_sends,
    head_receives,
    load_sem,
    store_sem,
    edge_sends,
    edge_receives,
):
    layers, rows, width, channels, heads, depth, space_count = dims
    deep_count = space_count // 2
    across, core, deep, side = place()
    block = 2 * core + across
    low = jnp.bfloat16
    own[0] = master[0].astype(low)
    greet_edges(partners(deep_count), space_count)

    chunks = layers * deep_count

    def split(chunk):
        rest = chunk - layers
        is_own = chunk < layers
        layer = jnp.where(is_own, chunk, rest // (deep_count - 1))
        hop = jnp.where(is_own, 0, 1 + lax.rem(rest + chunks, deep_count - 1))
        layer, hop = jnp.clip(layer, 0, layers - 1), jnp.clip(hop, 0, deep_count - 1)
        source = lax.rem(deep - hop + deep_count, deep_count)
        return (layer, hop, source, lax.rem(chunk, 2))

    def first(layer, hop):
        piece = own.at[layer, :, lanes(block)]
        target = full.at[layer, deep, side, :, lanes(block)]
        to = at(across, core, lax.rem(deep + hop, deep_count), side)
        return remote(piece, target, sends.at[0, layer, hop], receives.at[0, layer, hop], to)

    def first_in(layer, hop):
        source = lax.rem(deep - hop + deep_count, deep_count)
        piece = full.at[layer, source, side, :, lanes(block)]
        return remote(
            piece, piece, sends.at[0, layer, hop], receives.at[0, layer, hop], at(across, core, deep, side)
        )

    def second(chunk, incoming):
        layer, hop, source, odd = split(chunk)
        there_side = lax.rem(side + 1 - odd, 2)
        there_across = lax.rem(across + odd, 2)
        to = at(there_across, core, deep, there_side)
        if incoming:
            piece = full.at[layer, source, there_side, :, lanes(2 * core + there_across)]
        else:
            piece = full.at[layer, source, side, :, lanes(block)]
        return remote(piece, piece, sends.at[1, layer, hop], receives.at[1, layer, hop], to)

    def third(chunk, half, incoming):
        layer, hop, source, odd = split(chunk)
        there_side = lax.rem(side + odd, 2)
        there_across = lax.rem(across + 1 - odd, 2)
        to = at(there_across, core, deep, there_side)
        here = there_side if incoming else side
        lane = there_across if incoming else across
        piece_side = (1 - odd) * half + odd * here
        piece_lane = 2 * core + (1 - odd) * lane + odd * half
        piece = full.at[layer, source, piece_side, :, lanes(piece_lane)]
        return remote(
            piece, piece, sends.at[2 + half, layer, hop], receives.at[2 + half, layer, hop], to
        )

    def fourth(chunk, incoming):
        layer, hop, source, odd = split(chunk)
        column = 1 - core if incoming else core
        piece = full.at[layer, source, :, :, lanes(2 * column, 2)]
        to = at(across, 1 - core, deep, side)
        return remote(piece, piece, sends.at[4, layer, hop], receives.at[4, layer, hop], to)

    def local(layer):
        return pltpu.make_async_copy(
            own.at[layer, :, lanes(block)],
            full.at[layer, deep, side, :, lanes(block)],
            local_sem.at[layer],
        )

    def each(low, action):
        def step(hop, carry):
            action(hop)
            return carry

        lax.fori_loop(low, deep_count, step, 0)

    def head_local():
        return pltpu.make_async_copy(
            head_own, head_full.at[across, core, deep, side], local_sem.at[layers]
        )

    def head_first(hop):
        to = at(across, core, lax.rem(deep + hop, deep_count), side)
        target = head_full.at[across, core, deep, side]
        return remote(head_own, target, head_sends.at[hop], head_receives.at[hop], to)

    def head_first_in(hop):
        piece = head_full.at[across, core, lax.rem(deep - hop + deep_count, deep_count), side]
        to = at(across, core, deep, side)
        return remote(piece, piece, head_sends.at[hop], head_receives.at[hop], to)

    def head_next(which, incoming):
        if which == 0:
            to = at(across, core, deep, 1 - side)
            piece = head_full.at[across, core, :, 1 - side if incoming else side]
        elif which == 1:
            to = at(1 - across, core, deep, side)
            piece = head_full.at[1 - across if incoming else across, core]
        else:
            to = at(across, 1 - core, deep, side)
            piece = head_full.at[:, 1 - core if incoming else core]
        slot = deep_count + which
        return remote(piece, piece, head_sends.at[slot], head_receives.at[slot], to)

    def go_head(which):
        if which == 0:
            head_local().wait()
            each(1, lambda hop: head_first_in(hop).wait_recv())
        else:
            head_next(which - 1, True).wait_recv()
        if which < 3:
            head_next(which, False).start()

    send_edges, take_edges, put = edge_tools(dims, halo, edge_sends, edge_receives)
    tile = 2 * LANES
    tiles = channels // tile
    pixels = rows * width
    band = TAPS * channels
    masks, unused = row_weights(valid, rows)
    share = band * TAPS // space_count

    def loop(count, action):
        def body(index, carry):
            action(index)
            return carry

        lax.fori_loop(0, count, body, 0)

    def spot(index):
        return pl.multiple_of(index * tile, tile)

    def load(layer, owner):
        start = pl.multiple_of(owner * share, 8)
        return pltpu.make_async_copy(
            full.at[layer, owner // 2, lax.rem(owner, 2)],
            weights.at[layer % 2, pl.ds(start, share)],
            load_sem.at[layer % 2, owner],
        )

    def arrive(layer):
        fourth(layer, True).wait_recv()
        begin = layers + layer * (deep_count - 1)
        loop(deep_count - 1, lambda index: fourth(begin + index, True).wait_recv())
        loop(space_count, lambda owner: load(layer, owner).start())

    def store(which, layer):
        source, target = (
            (wide.at[layer], wide_out.at[layer]),
            (hidden.at[layer], hidden_out.at[layer]),
            (last, last_out),
        )[which]
        return pltpu.make_async_copy(source, target, store_sem.at[which, layer])

    def forward(layer):
        here = wide.at[layer]
        take_edges(layer, here)
        store(0, layer).start()
        loop(space_count, lambda owner: load(layer, owner).wait())

        def outer(part):
            lane = pl.ds(spot(part), tile)
            total = vector_lanes(vectors, layer * channels, part)
            for tap_row in range(TAPS):
                total += mix(
                    here[tap_row * width : tap_row * width + pixels, :],
                    weights[layer % 2, tap_row * band : (tap_row + 1) * band, lane],
                    1,
                    0,
                )
            hidden[layer, :, lane] = total
            for row in range(rows):
                span = slice(row * width, (row + 1) * width)
                value = gelu_value(hidden[layer, span, lane]) * masks[row]
                if layer < layers - 1:
                    put(wide.at[layer + 1], row + 1, spot(part), tile, value)
                else:
                    last[span, lane] = value.astype(low)

        loop(tiles, outer)
        store(1, layer).start()
        if layer < layers - 1:
            send_edges(layer + 1, wide.at[layer + 1])

    def go_second(chunk):
        layer, hop, source, odd = split(chunk)

        @pl.when(hop == 0)
        def own_rows():
            local(layer).wait()

        @pl.when(hop > 0)
        def other_rows():
            first_in(layer, hop).wait_recv()

        second(chunk, False).start()

    def go_third(chunk):
        second(chunk, True).wait_recv()
        third(chunk, 0, False).start()
        third(chunk, 1, False).start()

    def go_fourth(chunk):
        third(chunk, 0, True).wait_recv()
        third(chunk, 1, True).wait_recv()
        fourth(chunk, False).start()

    def go_head_first():
        each(1, lambda hop: head_first(hop).start())

    def go_first(layer):
        each(1, lambda hop: first(layer, hop).start())

    go_first(0)
    local(0).start()
    go_second(0)
    for layer in range(1, layers):
        own[layer] = master[layer].astype(low)
        local(layer).start()
    head_rows, head_blocks = head_own.shape[0], heads * depth // LANES
    for lane in range(head_blocks):
        head_own[:, lane * LANES : (lane + 1) * LANES] = head_master[
            pl.ds(lane, head_rows, stride=head_blocks), :
        ].astype(low)
    head_local().start()
    for row in range(rows):
        for part in range(tiles):
            value = features[row * width : (row + 1) * width, part * tile : (part + 1) * tile]
            put(wide.at[0], row + 1, part * tile, tile, value.astype(jnp.float32))
    send_edges(0, wide.at[0])

    lag_third, lag_fourth = 2, 5
    others = deep_count - 1

    def last_of(layer):
        return layers + others * (layer + 1) - 1 + lag_fourth

    early = min(2, others)
    timed = [(layers + others * (layer - 1) + early, go_first, layer) for layer in range(1, layers)]
    timed += [(layers + early, go_head_first)]
    timed += [(layers + others + 2 * which, go_head, which) for which in range(3)]
    for layer in range(layers - 1):
        timed += [(last_of(layer) + 1, arrive, layer), (last_of(layer) + 2, forward, layer)]

    def turn(now):
        for lag, action in ((0, go_second), (lag_third, go_third), (lag_fourth, go_fourth)):
            begin = max(lag, 1)

            @pl.when(jnp.logical_and(now >= begin, now < chunks + lag))
            def stage():
                action(now - lag)

        for moment, action, *which in timed:

            @pl.when(now == moment)
            def once():
                action(*which)

    loop(chunks + lag_fourth, turn)
    go_head(3)
    arrive(layers - 1)
    forward(layers - 1)
    store(2, 0).start()

    def finish(chunk):
        second(chunk, False).wait_send()
        third(chunk, 0, False).wait_send()
        third(chunk, 1, False).wait_send()
        fourth(chunk, False).wait_send()

    loop(chunks, finish)
    each(1, lambda hop: head_first(hop).wait_send())
    for which in range(3):
        head_next(which, False).wait_send()

    for layer in range(layers):

        each(1, lambda hop: first(layer, hop).wait_send())
        store(0, layer).wait()
        store(1, layer).wait()
    store(2, 0).wait()


def gather_weights(master, head_master, head_width, features, vectors, valid, space_count):
    layers, share, channels = master.shape
    rows, width, unused = features.shape
    deep_count = space_count // 2
    pixels = rows * width
    dims = (layers, rows, width, channels, NH, HD, space_count)
    low, wide_float = jnp.bfloat16, jnp.float32
    anywhere = pl.BlockSpec(memory_space=pl.ANY)
    vmem = pl.BlockSpec(memory_space=pltpu.VMEM)
    head_own = (head_master.shape[0] * LANES // head_width, head_width)
    head_shape = (2, 2, deep_count, 2) + head_own
    wide_shape = (layers, (rows + 2) * width, TAPS * channels)
    full, head_full, wide, hidden, last = pl.pallas_call(
        partial(gather_kernel, dims),
        out_shape=(
            jax.ShapeDtypeStruct((layers, deep_count, 2, share, channels), low),
            jax.ShapeDtypeStruct(head_shape, low),
            jax.ShapeDtypeStruct(wide_shape, low),
            jax.ShapeDtypeStruct((layers, pixels, channels), wide_float),
            jax.ShapeDtypeStruct((pixels, channels), low),
        ),
        in_specs=[vmem] * 4 + [pl.BlockSpec(memory_space=pltpu.SMEM)],
        out_specs=[anywhere] * 5,
        scratch_shapes=[
            pltpu.VMEM(master.shape, low),
            pltpu.VMEM(head_own, low),
            pltpu.VMEM((2, space_count * share, channels), low),
            pltpu.VMEM(wide_shape, low),
            pltpu.VMEM((layers, pixels, channels), wide_float),
            pltpu.VMEM((pixels, channels), low),
            pltpu.VMEM((layers, 2, width, channels), low),
            pltpu.SemaphoreType.DMA((layers + 1,)),
            pltpu.SemaphoreType.DMA((5, layers, deep_count)),
            pltpu.SemaphoreType.DMA((5, layers, deep_count)),
            pltpu.SemaphoreType.DMA((deep_count + 3,)),
            pltpu.SemaphoreType.DMA((deep_count + 3,)),
            pltpu.SemaphoreType.DMA((2, space_count)),
            pltpu.SemaphoreType.DMA((3, layers)),
            pltpu.SemaphoreType.DMA((layers, 2)),
            pltpu.SemaphoreType.DMA((layers, 2)),
        ],
        compiler_params=pltpu.CompilerParams(
            collective_id=0, has_side_effects=True, vmem_limit_bytes=VMEM_LIMIT
        ),
    )(master, head_master, features.reshape(pixels, channels), vectors, valid)
    return (
        full.reshape(layers, space_count * share, channels),
        head_full.reshape(-1, head_width),
        wide,
        hidden,
        last,
    )


def reduce_kernel(
    layers,
    deep_count,
    grads,
    vector,
    bases,
    first_in,
    second_moment_in,
    master_in,
    total,
    stats,
    vector_total,
    first_out,
    second_out,
    master_out,
    mine,
    core_in,
    second_in,
    kept,
    third_in,
    last,
    last_in,
    acc,
    stat_own,
    stat_in,
    stat_deep,
    vector_out,
    vector_in,
    vector_deep,
    moment_one,
    moment_two,
    master,
    local_sem,
    sends,
    receives,
    stat_sends,
    stat_receives,
    deep_sends,
    deep_receives,
    vector_sends,
    vector_receives,
    state_loads,
    state_stores,
):
    across, core, deep, side = place()
    block = 2 * core + across
    steps = layers * deep_count

    def split(step):
        layer, hop = step // deep_count, lax.rem(step + 1, deep_count)
        target = lax.rem(deep + hop, deep_count)
        return (layer, hop, target, lax.rem(target, 2))

    def first(step):
        layer, hop, target, odd = split(step)
        return remote(
            grads.at[layer, target, :, :, lanes(2 * (1 - core), 2)],
            core_in.at[step],
            sends.at[0, step],
            receives.at[0, step],
            at(across, 1 - core, deep, side),
        )

    def load(step):
        layer, hop, target, odd = split(step)
        return pltpu.make_async_copy(
            grads.at[layer, target, :, :, lanes(2 * core, 2)], mine.at[step], local_sem.at[step]
        )

    def second(step, half):
        layer, hop, target, odd = split(step)
        piece_side = (1 - odd) * half + odd * (1 - side)
        piece_lane = (1 - odd) * (1 - across) + odd * half
        to = at(lax.rem(across + 1 - odd, 2), core, deep, lax.rem(side + odd, 2))
        return remote(
            mine.at[step, piece_side, :, lanes(piece_lane)],
            second_in.at[step, half],
            sends.at[1 + half, step],
            receives.at[1 + half, step],
            to,
        )

    def third(step):
        layer, hop, target, odd = split(step)
        keep = (1 - odd) * side + odd * across
        to = at(lax.rem(across + odd, 2), core, deep, lax.rem(side + 1 - odd, 2))
        return remote(
            kept.at[step, 1 - keep],
            third_in.at[step],
            sends.at[3, step],
            receives.at[3, step],
            to,
        )

    def fourth(step):
        layer, hop, target, odd = split(step)
        return remote(
            last.at[step],
            last_in.at[step],
            sends.at[4, step],
            receives.at[4, step],
            at(across, core, target, side),
        )

    def fifth(layer, incoming):
        lane = 2 * core + (1 - across if incoming else across)
        piece = total.at[layer, :, lanes(lane)]
        to = at(1 - across, core, deep, side)
        return remote(piece, piece, sends.at[5, layer], receives.at[5, layer], to)

    def sixth(layer, incoming):
        column = 1 - core if incoming else core
        piece = total.at[layer, :, lanes(2 * column, 2)]
        to = at(across, 1 - core, deep, side)
        return remote(piece, piece, sends.at[6, layer], receives.at[6, layer], to)

    def run(low, high, action):
        def body(step, carry):
            action(step)
            return carry

        lax.fori_loop(low, high, body, 0)

    half_block = LANES // 2

    def stat_side(layer, incoming):
        rows = pl.ds(pl.multiple_of((1 - side) * half_block, half_block), half_block)
        return remote(
            stat_own.at[layer, rows],
            stat_in.at[layer],
            stat_sends.at[0, layer],
            stat_receives.at[0, layer],
            at(across, core, deep, 1 - side),
        )

    def stat_along(layer, hop):
        return remote(
            stat_deep.at[layer, deep],
            stat_deep.at[layer, deep],
            deep_sends.at[layer, hop],
            deep_receives.at[layer, hop],
            at(across, core, lax.rem(deep + hop, deep_count), side),
        )

    def stat_along_in(layer, hop):
        source = lax.rem(deep - hop + deep_count, deep_count)
        return remote(
            stat_deep.at[layer, source],
            stat_deep.at[layer, source],
            deep_sends.at[layer, hop],
            deep_receives.at[layer, hop],
            at(across, core, deep, side),
        )

    def half_rows(which):
        return pl.ds(pl.multiple_of(which * half_block, half_block), half_block)

    def stat_spread(which, layer, incoming):
        if which < 3:
            other_side = side if which == 1 else 1 - side
            other_across = across if which == 0 else 1 - across
            to = at(other_across, core, deep, other_side)
            if incoming:
                piece = stats.at[layer, 2 * core + other_across, half_rows(other_side)]
            else:
                piece = stats.at[layer, block, half_rows(side)]
        else:
            to = at(across, 1 - core, deep, side)
            piece = stats.at[layer, pl.ds(2 * (1 - core if incoming else core), 2)]
        slot = 1 + which
        return remote(piece, piece, stat_sends.at[slot, layer], stat_receives.at[slot, layer], to)

    def vector_step(which):
        to = (
            at(across, 1 - core, deep, side),
            at(1 - across, core, deep, side),
            at(across, core, deep, 1 - side),
        )[which]
        return remote(
            vector_out.at[which],
            vector_in.at[which],
            vector_sends.at[which],
            vector_receives.at[which],
            to,
        )

    def vector_along(hop):
        return remote(
            vector_deep.at[deep],
            vector_deep.at[deep],
            vector_sends.at[2 + hop],
            vector_receives.at[2 + hop],
            at(across, core, lax.rem(deep + hop, deep_count), side),
        )

    def vector_along_in(hop):
        source = lax.rem(deep - hop + deep_count, deep_count)
        return remote(
            vector_deep.at[source],
            vector_deep.at[source],
            vector_sends.at[2 + hop],
            vector_receives.at[2 + hop],
            at(across, core, deep, side),
        )

    def go_first(step):
        load(step).start()
        first(step).start()

    ahead = min(3, steps)
    piece_rows = 144 if total.shape[1] % 144 == 0 else total.shape[1]
    states = (
        (first_in, moment_one, first_out),
        (second_moment_in, moment_two, second_out),
        (master_in, master, master_out),
    )

    def load_state(which, layer):
        source, target, unused = states[which]
        return pltpu.make_async_copy(
            source.at[layer], target.at[layer], state_loads.at[which, layer]
        )

    def store_state(which, layer):
        unused, source, target = states[which]
        return pltpu.make_async_copy(
            source.at[layer], target.at[layer], state_stores.at[which, layer]
        )

    greet(partners(deep_count) + [at(1 - across, core, deep, 1 - side)])
    run(0, ahead, go_first)
    for layer in range(layers):
        for which in range(3):
            load_state(which, layer).start()

    def wide(left, right):
        return left.astype(jnp.float32) + right.astype(jnp.float32)

    def go_second(step):
        @pl.when(step + ahead < steps)
        def start_next():
            go_first(step + ahead)

        load(step).wait()
        first(step).wait_recv()
        mine[step] = wide(mine[step], core_in[step]).astype(jnp.bfloat16)
        second(step, 0).start()
        second(step, 1).start()

    def go_third(step):
        layer, hop, target, odd = split(step)
        for half in range(2):
            second(step, half).wait_recv()
            keep_side = (1 - odd) * half + odd * side
            keep_lane = (1 - odd) * across + odd * half
            kept[step, half] = wide(
                mine[step, keep_side, :, lanes(keep_lane)], second_in[step, half]
            ).astype(jnp.bfloat16)
        third(step).start()

    def go_fourth(step):
        layer, hop, target, odd = split(step)
        third(step).wait_recv()
        keep = (1 - odd) * side + odd * across
        last[step] = wide(kept[step, keep], third_in[step]).astype(jnp.bfloat16)

        @pl.when(hop > 0)
        def unused():
            fourth(step).start()

    def close(layer):
        acc[...] = last[layer * deep_count + deep_count - 1].astype(jnp.float32)

        def add(hop):
            step = layer * deep_count + hop - 1
            fourth(step).wait_recv()
            acc[...] += last_in[step].astype(jnp.float32)

        run(1, deep_count, add)
        total[layer, :, lanes(block)] = acc[...].astype(jnp.bfloat16)
        fifth(layer, False).start()

    def spread(layer):
        fifth(layer, True).wait_recv()
        sixth(layer, False).start()

    def measure(layer):
        sixth(layer, True).wait_recv()
        own_lanes = total[layer, :, lanes(block)]
        stat_own[layer] = lax.dot_general(
            own_lanes,
            total[layer],
            (((0,), (0,)), ((), ())),
            preferred_element_type=jnp.float32,
        ).astype(jnp.bfloat16)
        stat_side(layer, False).start()

    def pair(layer):
        stat_side(layer, True).wait_recv()
        stat_deep[layer, deep] = wide(
            stat_own[layer, half_rows(side)], stat_in[layer]
        ).astype(jnp.bfloat16)
        run(1, deep_count, lambda hop: stat_along(layer, hop).start())

    def settle(layer):
        run(1, deep_count, lambda hop: stat_along_in(layer, hop).wait_recv())
        whole = stat_deep[layer, 0].astype(jnp.float32)
        for source in range(1, deep_count):
            whole += stat_deep[layer, source].astype(jnp.float32)
        stats[layer, block, half_rows(side)] = whole.astype(jnp.bfloat16)
        for which in range(3):
            stat_spread(which, layer, False).start()

    def share_core(layer):
        for which in range(3):
            stat_spread(which, layer, True).wait_recv()
        stat_spread(3, layer, False).start()

    def refresh(layer):
        for which in range(3):
            load_state(which, layer).wait()
        high, rest = halves(bases[layer])

        def one_piece(index):
            here = pl.ds(pl.multiple_of(index * piece_rows, piece_rows), piece_rows)
            given = total[layer, here, :]
            rotated = mix(given, high, 1, 0) + mix(given, rest, 1, 0)
            first_new, second_new, direction = moments(
                rotated, moment_one[layer, here, :], moment_two[layer, here, :]
            )
            moment_one[layer, here, :] = first_new
            moment_two[layer, here, :] = second_new
            up, down = halves(direction)
            back = mix(up, high, 1, 1) + (mix(up, rest, 1, 1) + mix(down, high, 1, 1))
            old = master[layer, here, :]
            master[layer, here, :] = old - RATE_CONV * (back + DECAY * old)

        run(0, total.shape[1] // piece_rows, one_piece)
        for which in range(3):
            store_state(which, layer).start()

    def finish(layer):
        stat_spread(3, layer, True).wait_recv()
        fifth(layer, False).wait_send()
        sixth(layer, False).wait_send()
        stat_side(layer, False).wait_send()
        run(1, deep_count, lambda hop: stat_along(layer, hop).wait_send())
        for which in range(4):
            stat_spread(which, layer, False).wait_send()
        for which in range(3):
            store_state(which, layer).wait()

    def vector_next(which):
        vector_step(which).wait_recv()
        summed = vector_out[which] + vector_in[which]
        if which < 2:
            vector_out[which + 1] = summed
            vector_step(which + 1).start()
        else:
            vector_deep[deep] = summed
            run(1, deep_count, lambda hop: vector_along(hop).start())

    chunk_work = ((0, go_second), (2, go_third), (4, go_fourth))
    layer_work = (
        (6, close),
        (7, spread),
        (8, measure),
        (9, pair),
        (10, refresh),
        (11, settle),
        (12, share_core),
        (13, finish),
    )
    vector_out[0] = vector[...]
    vector_step(0).start()

    def turn(now):
        for lag, action in chunk_work:

            @pl.when(jnp.logical_and(now >= lag, now < steps + lag))
            def chunk():
                action(now - lag)

        for which in range(3):

            @pl.when(now == 2 * which + 1)
            def exchange():
                vector_next(which)

        for lag, action in layer_work:
            past = now - lag - (deep_count - 1)

            @pl.when(
                jnp.logical_and(
                    jnp.logical_and(past >= 0, past < steps), lax.rem(past, deep_count) == 0
                )
            )
            def whole_layer():
                action(past // deep_count)

    run(0, steps + layer_work[-1][0], turn)

    run(1, deep_count, lambda hop: vector_along_in(hop).wait_recv())
    summed = vector_deep[0]
    for source in range(1, deep_count):
        summed += vector_deep[source]
    vector_total[...] = summed
    for which in range(3):
        vector_step(which).wait_send()
    run(1, deep_count, lambda hop: vector_along(hop).wait_send())

    def drain(step):
        layer, hop, target, odd = split(step)
        first(step).wait_send()
        second(step, 0).wait_send()
        second(step, 1).wait_send()
        third(step).wait_send()

        @pl.when(hop > 0)
        def unused():
            fourth(step).wait_send()

    run(0, steps, drain)


def reduce_grads(grads, vector, bases, conv, space_count):
    layers, all_rows, columns = grads.shape
    deep_count, rows = space_count // 2, all_rows // space_count
    steps = layers * deep_count
    low = jnp.bfloat16
    blocks = columns // LANES
    vmem = pl.BlockSpec(memory_space=pltpu.VMEM)
    tall = jax.ShapeDtypeStruct((layers, rows, columns), jnp.float32)
    anywhere = pl.BlockSpec(memory_space=pl.ANY)
    total, stats, vector_total, *conv_new = pl.pallas_call(
        partial(reduce_kernel, layers, deep_count),
        out_shape=(
            jax.ShapeDtypeStruct((layers, rows, columns), low),
            jax.ShapeDtypeStruct((layers, blocks, LANES, columns), low),
            jax.ShapeDtypeStruct(vector.shape, jnp.float32),
            tall,
            tall,
            tall,
        ),
        in_specs=[anywhere, vmem, vmem] + [anywhere] * 3,
        out_specs=[vmem] * 3 + [anywhere] * 3,
        scratch_shapes=[
            pltpu.VMEM((steps, 2, rows, 2 * LANES), low),
            pltpu.VMEM((steps, 2, rows, 2 * LANES), low),
            pltpu.VMEM((steps, 2, rows, LANES), low),
            pltpu.VMEM((steps, 2, rows, LANES), low),
            pltpu.VMEM((steps, rows, LANES), low),
            pltpu.VMEM((steps, rows, LANES), low),
            pltpu.VMEM((steps, rows, LANES), low),
            pltpu.VMEM((rows, LANES), jnp.float32),
            pltpu.VMEM((layers, LANES, columns), low),
            pltpu.VMEM((layers, LANES // 2, columns), low),
            pltpu.VMEM((layers, deep_count, LANES // 2, columns), low),
            pltpu.VMEM((3,) + vector.shape, jnp.float32),
            pltpu.VMEM((3,) + vector.shape, jnp.float32),
            pltpu.VMEM((deep_count,) + vector.shape, jnp.float32),
            pltpu.VMEM(tall.shape, jnp.float32),
            pltpu.VMEM(tall.shape, jnp.float32),
            pltpu.VMEM(tall.shape, jnp.float32),
            pltpu.SemaphoreType.DMA((steps,)),
            pltpu.SemaphoreType.DMA((7, steps)),
            pltpu.SemaphoreType.DMA((7, steps)),
            pltpu.SemaphoreType.DMA((5, layers)),
            pltpu.SemaphoreType.DMA((5, layers)),
            pltpu.SemaphoreType.DMA((layers, deep_count)),
            pltpu.SemaphoreType.DMA((layers, deep_count)),
            pltpu.SemaphoreType.DMA((2 + deep_count,)),
            pltpu.SemaphoreType.DMA((2 + deep_count,)),
            pltpu.SemaphoreType.DMA((3, layers)),
            pltpu.SemaphoreType.DMA((3, layers)),
        ],
        compiler_params=pltpu.CompilerParams(
            collective_id=1, has_side_effects=True, vmem_limit_bytes=VMEM_LIMIT
        ),
    )(grads.reshape(layers, deep_count, 2, rows, columns), vector, bases, *conv)
    return (stats.reshape(layers, columns, columns), vector_total, conv_new)


def work_kernel(
    dims,
    weights_in,
    head_in,
    wide_in,
    hidden_in,
    last_in,
    vectors,
    cotangent_in,
    valid,
    merged,
    features_grad,
    grads_out,
    head_grad,
    vector,
    weights,
    head,
    cotangent,
    wide,
    hidden,
    last,
    last_turned,
    d_wide,
    d_active,
    grads,
    halo,
    term,
    term_in,
    load_sem,
    store_sem,
    send_sem,
    receive_sem,
    term_sends,
    term_receives,
    *head_refs,
):
    layers, rows, width, channels, heads, depth, space_count = dims
    deep_count = space_count // 2
    across, core, deep, side = place()
    spread_head = len(head_refs) > 0
    if spread_head:
        head_parts, core_in, across_in, side_in, deep_in, head_sends, head_receives = head_refs
        head_rows = head_parts.shape[4]
    tile = 2 * LANES
    tiles = channels // tile
    low = jnp.bfloat16

    loads = ((last_in, last), (head_in, head), (cotangent_in, cotangent))
    for layer in reversed(range(layers)):
        loads += (
            (hidden_in.at[layer], hidden.at[layer]),
            (wide_in.at[layer], wide.at[layer]),
            (weights_in.at[layer], weights.at[layer]),
        )

    def load(which):
        source, target = loads[which]
        return pltpu.make_async_copy(source, target, load_sem.at[which])

    for which in range(len(loads)):
        load(which).start()

    others = [
        at(across, 1 - core, deep, side),
        at(1 - across, core, deep, side),
        at(across, core, deep, 1 - side),
    ]
    if spread_head:
        others += [
            at(across, core, lax.rem(deep + hop, deep_count), side) for hop in range(1, deep_count)
        ]
    greet_edges(others, space_count)

    def term_lanes(index, which):
        return pl.ds(pl.multiple_of(index * depth + which * LANES, LANES), LANES)

    def term_step(which, index, incoming=False):
        if which == 0:
            source, target, to = term.at[:, term_lanes(index, 1 - core)], term_in.at[0, index], others[0]
        elif which == 1:
            source, target, to = term.at[:, term_lanes(index, core)], term_in.at[1, index], others[1]
        else:
            source = merged.at[:, term_lanes(index, 1 - core if incoming else core)]
            target, to = source, others[0]
        return remote(
            source, target, term_sends.at[which, index], term_receives.at[which, index], to
        )

    def term_pair(index):
        term_step(0, index).wait_recv()
        lane = term_lanes(index, core)
        both = term[:, lane].astype(jnp.float32) + term_in[0, index].astype(jnp.float32)
        term[:, lane] = both.astype(low)
        term_step(1, index).start()

    def term_total(index):
        term_step(1, index).wait_recv()
        lane = term_lanes(index, core)
        both = term[:, lane].astype(jnp.float32) + term_in[1, index].astype(jnp.float32)
        merged[:, lane] = both.astype(low)
        term_step(2, index).start()

    def term_end(index):
        term_step(2, index, True).wait_recv()
        for which in range(3):
            term_step(which, index).wait_send()

    def head_step(which):
        if which == 0:
            source, target, to = head_parts.at[:, 1 - core], core_in, others[0]
        elif which == 1:
            source = head_parts.at[pl.ds(0, 2), core, pl.ds(0, deep_count), 1 - side]
            target, to = side_in, others[2]
        else:
            source = head_parts.at[1 - across, core, pl.ds(0, deep_count), side]
            target, to = across_in, others[1]
        return remote(source, target, head_sends.at[which], head_receives.at[which], to)

    def head_along(hop):
        target = lax.rem(deep + hop, deep_count)
        return remote(
            head_parts.at[across, core, target, side],
            deep_in.at[hop],
            head_sends.at[2 + hop],
            head_receives.at[2 + hop],
            at(across, core, target, side),
        )

    def head_next(which):
        if not spread_head:
            return
        head_step(which).wait_recv()
        if which == 0:
            for part in range(2):
                both = head_parts[part, core].astype(jnp.float32) + core_in[part].astype(jnp.float32)
                head_parts[part, core] = both.astype(low)
            head_step(1).start()
        elif which == 1:
            for part in range(2):
                both = head_parts[part, core, pl.ds(0, deep_count), side].astype(jnp.float32)
                both += side_in[part].astype(jnp.float32)
                head_parts[part, core, pl.ds(0, deep_count), side] = both.astype(low)
            head_step(2).start()
        else:
            both = head_parts[across, core, pl.ds(0, deep_count), side].astype(jnp.float32)
            both += across_in[...].astype(jnp.float32)
            head_parts[across, core, pl.ds(0, deep_count), side] = both.astype(low)
            for hop in range(1, deep_count):
                head_along(hop).start()

    def head_end():
        if not spread_head:
            return
        whole = head_parts[across, core, deep, side].astype(jnp.float32)
        for hop in range(1, deep_count):
            head_along(hop).wait_recv()
            whole += deep_in[hop].astype(jnp.float32)
        blocks = heads * depth // LANES
        for lane in range(blocks):
            head_grad[pl.ds(lane, head_rows, stride=blocks), :] = whole[
                :, lane * LANES : (lane + 1) * LANES
            ]
        for which in range(3):
            head_step(which).wait_send()
        for hop in range(1, deep_count):
            head_along(hop).wait_send()

    send_edges, take_edges, put = edge_tools(dims, halo, send_sem, receive_sem)

    def loop(count, action):
        def body(index, carry):
            action(index)
            return carry

        lax.fori_loop(0, count, body, 0)

    def spot(index):
        return pl.multiple_of(index * tile, tile)

    masks, weights_row = row_weights(valid, rows)

    def put_vector(start, part, value):
        row = start // LANES + 2 * part
        vector[pl.ds(row, 1), :] = value[:, :LANES]
        vector[pl.ds(row + 1, 1), :] = value[:, LANES:]

    pixels = rows * width
    for which in range(3):
        load(which).wait()
    last_turned[...] = last[...].astype(jnp.float32).T.astype(low)
    d_active[...] = jnp.zeros_like(d_active)

    def one_head(index):
        lane = pl.ds(pl.multiple_of(index * depth, depth), depth)
        projected = mix(last[...], head[:, lane], 1, 0)
        projected += vector_lanes(vectors, layers * channels, index)
        gain = vector_lanes(vectors, layers * channels + heads * depth, index)
        gain_total = jnp.zeros((1, depth), jnp.float32)
        bias_total = jnp.zeros((1, depth), jnp.float32)
        rounded = []
        for row in range(rows):
            span = slice(row * width, (row + 1) * width)
            weight = weights_row[row]
            value = projected[span]
            inverse = lax.rsqrt(jnp.sum(value * value, -1, keepdims=True) + 1e-06)
            normed = value * inverse
            scaled = gain * weight
            term[span, lane] = (normed * scaled).astype(low)
            given = cotangent[span, lane].astype(jnp.float32)
            gain_total += jnp.sum(normed * given, 0, keepdims=True) * weight
            d_normed = given * scaled
            along = jnp.sum(normed * d_normed, -1, keepdims=True)
            d_low = (inverse * (d_normed - normed * along)).astype(low)
            bias_total += jnp.sum(d_low.astype(jnp.float32), 0, keepdims=True)
            rounded.append(d_low)
        term_step(0, index).start()
        put_vector(layers * channels + heads * depth, index, gain_total)
        put_vector(layers * channels, index, bias_total)
        d_low = jnp.concatenate(rounded, 0)
        grad = mix(last_turned[...], d_low, 1, 0)
        if spread_head:
            split = grad.reshape(2, 2, deep_count, 2, head_rows, depth)
            head_parts[:, :, :, :, :, lane] = split.astype(low)
        else:
            head_grad[:, lane] = grad.astype(low)
        d_active[...] += mix(d_low, head[:, lane], 1, 1)

        @pl.when(index > 0)
        def earlier():
            term_pair(index - 1)

    loop(heads, one_head)
    if spread_head:
        head_step(0).start()
    term_pair(heads - 1)

    def store(layer):
        slot = layer % 2
        return pltpu.make_async_copy(grads.at[slot], grads_out.at[layer], store_sem.at[slot])

    for layer in reversed(range(layers)):
        which = layers - 1 - layer
        for part in range(3):
            load(3 + 3 * which + part).wait()

        def enter(part):
            lane = pl.ds(spot(part), tile)
            total = jnp.zeros((1, tile), jnp.float32)
            for row in range(rows):
                span = slice(row * width, (row + 1) * width)
                slope = gelu_slope(hidden[layer, span, lane])
                value = slope * (masks[row] * d_active[span, lane])
                value = value.astype(low).astype(jnp.float32)
                total += jnp.sum(value, 0, keepdims=True)
                put(d_wide, row + 1, spot(part), tile, value)
            put_vector(layer * channels, part, total)

        loop(tiles, enter)
        send_edges(which, d_wide)
        if layer + 2 < layers:
            store(layer + 2).wait()

        def one_tap(tap):
            tap_row, tap_column = tap // TAPS, lax.rem(tap, TAPS)
            window = wide[
                layer,
                pl.ds(pl.multiple_of(tap_row * width, width), pixels),
                pl.ds(pl.multiple_of(tap_column * channels, channels), channels),
            ]
            d_hidden = d_wide[width : width + pixels, channels : 2 * channels]
            grads[layer % 2, pl.ds(pl.multiple_of(tap * channels, channels), channels), :] = mix(
                window, d_hidden, 0, 0
            ).astype(low)

        loop(TAPS * TAPS, one_tap)
        store(layer).start()
        head_next(layers - 1 - layer)
        take_edges(which, d_wide)

        def back(part):
            total = jnp.zeros((pixels, tile), jnp.float32)
            for tap_row in range(TAPS):
                for tap_column in range(TAPS):
                    window = d_wide[
                        (2 - tap_row) * width : (2 - tap_row) * width + pixels,
                        (2 - tap_column) * channels : (3 - tap_column) * channels,
                    ]
                    first = (TAPS * tap_row + tap_column) * channels
                    total += mix(
                        window, weights[layer, pl.ds(first + spot(part), tile), :], 1, 1
                    )
            d_active[:, pl.ds(spot(part), tile)] = total

        loop(tiles, back)

    loop(heads, term_total)
    features_grad[...] = d_active[...].astype(low)
    head_end()
    loop(heads, term_end)
    for layer in range(min(layers, 2)):
        store(layer).wait()


def run_block(
    weights, head, wide, hidden, last, vectors, cotangent, valid, space_count
):
    rows, width, unused = cotangent.shape
    layers, unused, channels = weights.shape
    head_width = head.shape[1]
    pixels = rows * width
    deep_count = space_count // 2
    head_rows = channels // (4 * space_count)
    spread_head = head_rows % 16 == 0
    low, full = jnp.bfloat16, jnp.float32
    dims = (layers, rows, width, channels, NH, HD, space_count)
    vmem = pl.BlockSpec(memory_space=pltpu.VMEM)
    anywhere = pl.BlockSpec(memory_space=pl.ANY)
    head_scratch = []
    head_out = jax.ShapeDtypeStruct((channels, head_width), low)
    if spread_head:
        head_out = jax.ShapeDtypeStruct((head_rows * head_width // LANES, LANES), full)
        head_scratch = [
            pltpu.VMEM((2, 2, deep_count, 2, head_rows, head_width), low),
            pltpu.VMEM((2, deep_count, 2, head_rows, head_width), low),
            pltpu.VMEM((deep_count, head_rows, head_width), low),
            pltpu.VMEM((2, deep_count, head_rows, head_width), low),
            pltpu.VMEM((deep_count, head_rows, head_width), low),
            pltpu.SemaphoreType.DMA((2 + deep_count,)),
            pltpu.SemaphoreType.DMA((2 + deep_count,)),
        ]
    outs = pl.pallas_call(
        partial(work_kernel, dims),
        out_shape=(
            jax.ShapeDtypeStruct((pixels, head_width), low),
            jax.ShapeDtypeStruct((pixels, channels), low),
            jax.ShapeDtypeStruct(weights.shape, low),
            head_out,
            jax.ShapeDtypeStruct(vectors.shape, full),
        ),
        in_specs=[
            anywhere,
            anywhere,
            anywhere,
            anywhere,
            anywhere,
            vmem,
            anywhere,
            pl.BlockSpec(memory_space=pltpu.SMEM),
        ],
        out_specs=[vmem, vmem, anywhere, vmem, vmem],
        scratch_shapes=[
            pltpu.VMEM(weights.shape, low),
            pltpu.VMEM(head.shape, low),
            pltpu.VMEM((pixels, head_width), low),
            pltpu.VMEM((layers, (rows + 2) * width, TAPS * channels), low),
            pltpu.VMEM((layers, pixels, channels), full),
            pltpu.VMEM((pixels, channels), low),
            pltpu.VMEM((channels, pixels), low),
            pltpu.VMEM(((rows + 2) * width, TAPS * channels), low),
            pltpu.VMEM((pixels, channels), full),
            pltpu.VMEM((2,) + weights.shape[1:], low),
            pltpu.VMEM((layers, 2, width, channels), low),
            pltpu.VMEM((pixels, head_width), low),
            pltpu.VMEM((2, NH, pixels, LANES), low),
            pltpu.SemaphoreType.DMA((3 * layers + 3,)),
            pltpu.SemaphoreType.DMA((2,)),
            pltpu.SemaphoreType.DMA((layers, 2)),
            pltpu.SemaphoreType.DMA((layers, 2)),
            pltpu.SemaphoreType.DMA((3, NH)),
            pltpu.SemaphoreType.DMA((3, NH)),
        ]
        + head_scratch,
        compiler_params=pltpu.CompilerParams(
            collective_id=2, has_side_effects=True, vmem_limit_bytes=VMEM_LIMIT
        ),
    )(
        weights,
        head,
        wide,
        hidden,
        last,
        vectors,
        cotangent.reshape(pixels, head_width),
        valid,
    )
    merged, features_grad, grads, head_grad, vector = outs
    if not spread_head:
        head_grad = lax.psum_scatter(
            head_grad.astype(full).reshape(-1), ("scale", "space"), scatter_dimension=0, tiled=True
        ).reshape(-1, LANES)
    return (merged, features_grad, grads, head_grad, vector)


def halves(value):
    high = value.astype(jnp.bfloat16)
    return (high, (value - high.astype(jnp.float32)).astype(jnp.bfloat16))


def dot(left, right, left_dim, right_dim):
    left_high, left_low = halves(left)
    right_high, right_low = halves(right)
    rest = mix(left_high, right_low, left_dim, right_dim) + mix(left_low, right_high, left_dim, right_dim)
    return mix(left_high, right_high, left_dim, right_dim) + rest


def quick(x):
    return pl.reciprocal(x,approx=True)
def eliminate(blocks, off, size, m=8):
    nl=len(blocks); nb=size//8; W=blocks[0][0].shape[1]
    sub=lax.broadcasted_iota(jnp.int32,(8,128),0)
    for k0 in range(0,size,m):
        b0=k0//8; s0=k0%8
        for l in range(nl):
            bl=blocks[l]
            top=bl[b0]
            def colb(b,j):
                return jnp.broadcast_to(bl[b][:,off+k0+j:off+k0+j+1],(8,128))
            c0=[colb(b0,j) for j in range(m)]
            a=[[None]*m for _ in range(m)]
            for j in range(m):
                for i in range(j,m):
                    a[i][j]=jnp.broadcast_to(c0[j][s0+i:s0+i+1,:],(8,128))
            inv=[]; low=[[None]*m for _ in range(m)]
            for k in range(m):
                r=quick(a[k][k]); inv.append(r)
                for i in range(k+1,m):
                    low[i][k]=a[i][k]*r
                for j in range(k+1,m):
                    for i in range(j,m):
                        a[i][j]=a[i][j]-low[i][k]*a[j][k]
            wid=lambda v: jnp.concatenate([v]*(W//128),1)
            rows=[jnp.broadcast_to(top[s0+i:s0+i+1,:],(8,W)) for i in range(m)]
            for i in range(m):
                for k in range(i):
                    rows[i]=rows[i]-wid(low[i][k])*rows[k]
            for b in range(b0,nb):
                if b==b0 and s0+m==8 and m==1: continue
                cs=list(c0) if b==b0 else [colb(b,j) for j in range(m)]
                for j in range(m):
                    for k in range(j):
                        cs[j]=cs[j]-low[j][k]*cs[k]
                acc=bl[b]
                for k in range(m):
                    w=cs[k]*inv[k]
                    if b==b0: w=jnp.where(sub>s0+k,w,0.0)
                    acc=acc-wid(w)*rows[k]
                bl[b]=acc
    out=[]
    lane=lax.broadcasted_iota(jnp.int32,(8,W),1)
    row8=lax.broadcasted_iota(jnp.int32,(8,W),0)
    for l in range(nl):
        res=[]
        for b in range(nb):
            v=blocks[l][b]
            d=jnp.sum(jnp.where(lane==row8+(off+8*b),v,0.0),1,keepdims=True)
            res.append(v*lax.rsqrt(d))
        out.append(jnp.concatenate(res,0))
    return out


def moments(grads, first, second):
    first_new = BETA_ONE * first + (1.0 - BETA_ONE) * grads
    second_new = BETA_TWO * second + (1.0 - BETA_TWO) * grads * grads
    direction = (
        first_new
        * (1.0 / (1.0 - BETA_ONE**STEP))
        / (jnp.sqrt(second_new * (1.0 / (1.0 - BETA_TWO**STEP))) + EPSILON)
    )
    return (first_new, second_new, direction)


def update_kernel(
    dims,
    *refs,
):
    moved = dims[4]
    inputs, outputs = refs[: moved + 11], refs[moved + 11 : -1 - moved]
    held = refs[-1 - moved : -1]
    update_body(
        dims, inputs[:moved], outputs[:moved], held, refs[-1], *inputs[moved:], *outputs[moved:]
    )


def update_body(
    dims,
    moved_in,
    moved_out,
    held,
    moved_sem,
    summed,
    statistics,
    bases,
    head_grad,
    head_first,
    head_second,
    head_master,
    vector_grad,
    vector_first,
    vector_second,
    vectors,
    stats_new,
    bases_new,
    head_first_new,
    head_second_new,
    head_new,
    vector_first_new,
    vector_second_new,
    vectors_new,
    system,
    pivot,
):
    layers, channels, bias_rows, panel, moved = dims
    block = LANES

    def take(which):
        return pltpu.make_async_copy(moved_in[which], held[which], moved_sem.at[0, which])

    def give(which):
        return pltpu.make_async_copy(held[which], moved_out[which], moved_sem.at[1, which])

    for which in range(moved):
        take(which).start()

    for layer in range(layers):
        fresh = BETA_TWO * statistics[layer] + (1.0 - BETA_TWO) * summed[layer].astype(jnp.float32)
        stats_new[layer] = fresh
        turned = dot(bases[layer], fresh, 0, 0)
        system[layer, :, channels : 2 * channels] = turned
        system[layer, :, 0:channels] = dot(turned, turned, 1, 1)

    head = moments(head_grad[...], head_first[...], head_second[...])
    head_first_new[...] = head[0]
    head_second_new[...] = head[1]
    head_new[...] = head_master[...] - RATE_HEAD * (head[2] + DECAY * head_master[...])
    vec = moments(vector_grad[...], vector_first[...], vector_second[...])
    vector_first_new[...] = vec[0]
    vector_second_new[...] = vec[1]
    row = lax.broadcasted_iota(jnp.int32, vectors.shape, 0)
    rates = jnp.where(row < bias_rows, RATE_BIAS, RATE_GAIN)
    vectors_new[...] = vectors[...] - rates * (vec[2] + DECAY * vectors[...])

    for which in range(moved):
        take(which).wait()
        give(which).start()
    eye = (
        lax.broadcasted_iota(jnp.int32, (block, block), 0)
        == lax.broadcasted_iota(jnp.int32, (block, block), 1)
    ).astype(jnp.float32)

    def outer(k, carry):
        here = pl.ds(pl.multiple_of(k * block, block), block)
        panels = [jnp.concatenate([system[layer, here, here], eye], 1) for layer in range(layers)]
        done = [[] for _ in range(layers)]
        for j in range(block // panel):
            blocks = [[p[8 * i : 8 * i + 8] for i in range(panel // 8)] for p in panels]
            tops = eliminate(blocks, panel * j, panel)
            for layer in range(layers):
                done[layer].append(tops[layer][:, block:])
                if j < block // panel - 1:
                    panels[layer] = panels[layer][panel:] - dot(
                        tops[layer][:, panel * (j + 1) : block], tops[layer], 0, 0
                    )
        for layer in range(layers):
            inverse = jnp.concatenate(done[layer], 0)
            pivot[layer] = dot(inverse, system[layer, here, :], 1, 0)
            system[layer, here, channels : 2 * channels] = pivot[layer, :, channels : 2 * channels]

        def inner(i, carry_in):
            below = pl.ds(pl.multiple_of(i * block, block), block)
            for layer in range(layers):
                system[layer, below, :] -= dot(pivot[layer, :, below], pivot[layer], 0, 0)
            return carry_in

        lax.fori_loop(k + 1, channels // block, inner, 0)
        return carry

    lax.fori_loop(0, channels // block, outer, 0)
    for layer in range(layers):
        bases_new[layer] = system[layer, :, channels : 2 * channels].T
    for which in range(moved):
        give(which).wait()


def update(arrays, summed, statistics, bases, head, vector, bias_rows):
    layers, channels, unused = statistics.shape
    dims = (layers, channels, bias_rows, 32, len(arrays))
    anywhere = pl.BlockSpec(memory_space=pl.ANY)
    vmem = pl.BlockSpec(memory_space=pltpu.VMEM)
    square = jax.ShapeDtypeStruct(statistics.shape, jnp.float32)
    head_shape = jax.ShapeDtypeStruct(head[0].shape, jnp.float32)
    vector_shape = jax.ShapeDtypeStruct(vector[0].shape, jnp.float32)
    return pl.pallas_call(
        partial(update_kernel, dims),
        out_shape=tuple(jax.ShapeDtypeStruct(array.shape, array.dtype) for array in arrays)
        + (square,) * 2 + (head_shape,) * 3 + (vector_shape,) * 3,
        in_specs=[anywhere] * len(arrays) + [vmem] * 11,
        out_specs=[anywhere] * len(arrays) + [vmem] * 8,
        scratch_shapes=[
            pltpu.VMEM((layers, channels, 2 * channels), jnp.float32),
            pltpu.VMEM((layers, LANES, 2 * channels), jnp.float32),
        ]
        + [pltpu.VMEM(array.shape, array.dtype) for array in arrays]
        + [pltpu.SemaphoreType.DMA((2, len(arrays)))],
        compiler_params=pltpu.CompilerParams(vmem_limit_bytes=VMEM_LIMIT),
        cost_estimate=pl.CostEstimate(
            flops=10**10, bytes_accessed=2 * 10**7, transcendentals=10**4
        ),
    )(*arrays, summed, statistics, bases, *head, *vector)


def local(
    features,
    valid_rows,
    conv_master,
    head_master,
    vectors,
    conv_first,
    conv_second,
    head_first,
    head_second,
    vec_first,
    vec_second,
    statistics,
    bases,
    cotangent,
):
    channels = features.shape[3]
    head_width = cotangent.shape[2]
    space_count = lax.axis_size("space")
    vectors, vec_first, vec_second, head_master, head_first, head_second = (
        array.reshape(-1, LANES)
        for array in (vectors, vec_first, vec_second, head_master, head_first, head_second)
    )
    conv_used, head_used, wide, hidden, last = gather_weights(
        conv_master, head_master, head_width, features[0], vectors, valid_rows, space_count
    )
    merged, features_grad, grads, owned_head, vector = run_block(
        conv_used,
        head_used,
        wide,
        hidden,
        last,
        vectors,
        cotangent,
        valid_rows,
        space_count,
    )
    summed_stats, grad_vec, conv_new = reduce_grads(
        grads, vector, bases, (conv_first, conv_second, conv_master), space_count
    )
    moved = (merged, features_grad, *conv_new)
    outs = update(
        moved,
        summed_stats,
        statistics,
        bases,
        (owned_head, head_first, head_second, head_master),
        (grad_vec, vec_first, vec_second, vectors),
        (3 * channels + head_width) // LANES,
    )
    merged, features_grad, *conv_new = outs[:5]
    stats_new, bases_new = outs[5:7]
    return (
        merged.reshape(cotangent.shape),
        features_grad.reshape(features.shape),
        *conv_new,
        *(out.reshape(-1) for out in outs[7:]),
        stats_new,
        bases_new,
    )


def solution(mesh):
    in_specs = (
        P("scale", "space", None, None),
        P(),
        P(None, "space", None),
        P(("scale", "space")),
        P(),
        P(None, "space", None),
        P(None, "space", None),
        P(("scale", "space")),
        P(("scale", "space")),
        P(),
        P(),
        P(),
        P(),
        P("space", None, None),
    )
    out_specs = (
        P("space", None, None),
        P("scale", "space", None, None),
        P(None, "space", None),
        P(None, "space", None),
        P(None, "space", None),
        P(("scale", "space")),
        P(("scale", "space")),
        P(("scale", "space")),
        P(),
        P(),
        P(),
        P(),
        P(),
    )
    return jax.shard_map(local, mesh=mesh, in_specs=in_specs, out_specs=out_specs, check_vma=False)
```

```python
from functools import partial

import jax
import jax.experimental.pallas as pl
import jax.experimental.pallas.tpu as pltpu
import jax.numpy as jnp
from jax import lax
from jax.sharding import PartitionSpec as P

NH = 7
HD = 256
STEP = 5


BETA_ONE = 0.9
BETA_TWO = 0.95
EPSILON = 1e-08
DECAY = 0.01
RATE_CONV = 0.04
RATE_HEAD = 0.08
RATE_BIAS = 0.5
RATE_GAIN = 20.0
VMEM_LIMIT = 60 * 2**20
GELU_SCALE = 0.7978845608028654
GELU_CUBE = 0.044715


MESH = pl.DeviceIdType.MESH
LANES = 128


def place():
    scale, space = lax.axis_index("scale"), lax.axis_index("space")
    across, core = scale // 2, lax.rem(scale, 2)
    deep, side = space // 2, lax.rem(space, 2)
    return (across, core, deep, side)


def at(across, core, deep, side):
    return (2 * across + core, 2 * deep + side)


def greet(peers):
    barrier = pltpu.get_barrier_semaphore()
    for peer in peers:
        pl.semaphore_signal(barrier, inc=1, device_id=peer, device_id_type=MESH)
    pl.semaphore_wait(barrier, len(peers))


def remote(source, target, send, receive, device):
    return pltpu.make_async_remote_copy(
        src_ref=source,
        dst_ref=target,
        send_sem=send,
        recv_sem=receive,
        device_id=device,
        device_id_type=MESH,
    )


def lanes(index, count=1):
    return pl.ds(pl.multiple_of(index * LANES, LANES), count * LANES)


def partners(deep_count):
    across, core, deep, side = place()
    peers = [
        at(across, 1 - core, deep, side),
        at(1 - across, core, deep, side),
        at(across, core, deep, 1 - side),
    ]
    peers += [
        at(across, core, lax.rem(deep + hop, deep_count), side) for hop in range(1, deep_count)
    ]
    return peers


TAPS = 3


def gelu_parts(value):
    inner = GELU_SCALE * (value + GELU_CUBE * value * value * value)
    return jnp.tanh(inner)


def gelu_value(value):
    return 0.5 * value * (1.0 + gelu_parts(value))


def gelu_slope(value):
    bend = gelu_parts(value)
    rise = GELU_SCALE * (1.0 + 3.0 * GELU_CUBE * value * value)
    return 0.5 * (1.0 + bend) + 0.5 * value * (1.0 - bend * bend) * rise


def mix(left, right, left_dim, right_dim):
    return lax.dot_general(
        left,
        right,
        (((left_dim,), (right_dim,)), ((), ())),
        preferred_element_type=jnp.float32,
    )


def row_weights(valid, rows):
    scale, space = lax.axis_index("scale"), lax.axis_index("space")
    scales = lax.axis_size("scale")
    masks, weights = [], []
    for row in range(rows):
        place_in = space * rows + row
        mask = jnp.where(place_in < valid[scale], 1.0, 0.0)
        count = jnp.float32(0.0)
        for other in range(scales):
            count += jnp.where(place_in < valid[other], 1.0, 0.0)
        masks.append(mask)
        weights.append(jnp.full((1, LANES), mask) / jnp.full((1, LANES), count))
    return (masks, [weight[:, :1] for weight in weights])


def vector_lanes(vectors, start, part):
    row = start // LANES + 2 * part
    return jnp.concatenate([vectors[pl.ds(row, 1), :], vectors[pl.ds(row + 1, 1), :]], 1)


def greet_edges(peers, space_count):
    barrier = pltpu.get_barrier_semaphore()
    scale, space = lax.axis_index("scale"), lax.axis_index("space")
    for peer in peers:
        pl.semaphore_signal(barrier, inc=1, device_id=peer, device_id_type=MESH)
    next_space = space - 1 + 2 * lax.rem(space, 2)
    has_next = jnp.logical_and(next_space >= 0, next_space < space_count)

    @pl.when(has_next)
    def greet_next():
        pl.semaphore_signal(barrier, inc=1, device_id=(scale, next_space), device_id_type=MESH)

    pl.semaphore_wait(barrier, len(peers) + has_next.astype(jnp.int32))


def edge_tools(dims, halo, send_sem, receive_sem):
    rows, width, channels, space_count = dims[1], dims[2], dims[3], dims[6]
    tile = 2 * LANES
    tiles = channels // tile
    scale, space = lax.axis_index("scale"), lax.axis_index("space")
    above, below = space > 0, space < space_count - 1
    low = jnp.bfloat16

    def up(which, source):
        return remote(
            source,
            halo.at[which, 1],
            send_sem.at[which, 0],
            receive_sem.at[which, 1],
            (scale, space - 1),
        )

    def down(which, source):
        return remote(
            source,
            halo.at[which, 0],
            send_sem.at[which, 1],
            receive_sem.at[which, 0],
            (scale, space + 1),
        )

    def edge(array, row):
        return array.at[pl.ds((row + 1) * width, width), pl.ds(channels, channels)]

    def send_edges(which, array):
        @pl.when(above)
        def go_up():
            up(which, edge(array, 0)).start()

        @pl.when(below)
        def go_down():
            down(which, edge(array, rows - 1)).start()

    column = lax.broadcasted_iota(jnp.int32, (width, 1), 0)

    def put(array, slot, lane, count, value):
        here = pl.ds(slot * width, width)
        left = jnp.where(column == 0, 0.0, pltpu.roll(value, 1, 0))
        right = jnp.where(column == width - 1, 0.0, pltpu.roll(value, width - 1, 0))
        for which, moved in enumerate((left, value, right)):
            start = pl.multiple_of(which * channels + lane, LANES)
            array[here, pl.ds(start, count)] = moved.astype(low)

    def take_edges(which, array):
        for side, present, slot in ((0, above, 0), (1, below, rows + 1)):

            @pl.when(present)
            def arrived():
                if side == 0:
                    up(which, edge(array, 0)).wait_send()
                    down(which, edge(array, 0)).wait_recv()
                else:
                    down(which, edge(array, 0)).wait_send()
                    up(which, edge(array, 0)).wait_recv()
                for part in range(tiles):
                    value = halo[which, side, :, part * tile : (part + 1) * tile]
                    put(array, slot, part * tile, tile, value.astype(jnp.float32))

            @pl.when(jnp.logical_not(present))
            def missing():
                array[pl.ds(slot * width, width), :] = jnp.zeros(
                    (width, TAPS * channels), low
                )

    return (send_edges, take_edges, put)


def gather_kernel(
    dims,
    master,
    head_master,
    features,
    vectors,
    valid,
    full,
    head_full,
    wide_out,
    hidden_out,
    last_out,
    own,
    head_own,
    weights,
    wide,
    hidden,
    last,
    halo,
    local_sem,
    sends,
    receives,
    head_sends,
    head_receives,
    load_sem,
    store_sem,
    edge_sends,
    edge_receives,
):
    layers, rows, width, channels, heads, depth, space_count = dims
    deep_count = space_count // 2
    across, core, deep, side = place()
    block = 2 * core + across
    low = jnp.bfloat16
    own[0] = master[0].astype(low)
    greet_edges(partners(deep_count), space_count)

    chunks = layers * deep_count

    def by_distance(index):
        left, right = deep, deep_count - 1 - deep
        short = jnp.minimum(left, right)
        both = (index + 1) // 2 * (2 * lax.rem(index, 2) - 1)
        one = (index - short) * jnp.where(left < right, 1, -1)
        return deep + jnp.where(index <= 2 * short, both, one)

    def split(chunk):
        rest = chunk - layers
        is_own = chunk < layers
        layer = jnp.where(is_own, chunk, rest // (deep_count - 1))
        hop = jnp.where(is_own, 0, 1 + lax.rem(rest + chunks, deep_count - 1))
        layer, hop = jnp.clip(layer, 0, layers - 1), jnp.clip(hop, 0, deep_count - 1)
        source = by_distance(hop)
        odd = jnp.where(is_own, 0, lax.rem(chunk, 2))
        return (layer, hop, source, odd)

    def first(layer, index):
        piece = own.at[layer, :, lanes(block)]
        target = full.at[layer, deep, side, :, lanes(block)]
        there = by_distance(index)
        to = at(across, core, there, side)
        return remote(piece, target, sends.at[0, layer, there], receives.at[0, layer, deep], to)

    def first_in(layer, index):
        source = by_distance(index)
        piece = full.at[layer, source, side, :, lanes(block)]
        return remote(
            piece,
            piece,
            sends.at[0, layer, source],
            receives.at[0, layer, source],
            at(across, core, source, side),
        )

    def second(chunk, incoming):
        layer, hop, source, odd = split(chunk)
        there_side = lax.rem(side + 1 - odd, 2)
        there_across = lax.rem(across + odd, 2)
        to = at(there_across, core, deep, there_side)
        if incoming:
            piece = full.at[layer, source, there_side, :, lanes(2 * core + there_across)]
        else:
            piece = full.at[layer, source, side, :, lanes(block)]
        return remote(piece, piece, sends.at[1, layer, hop], receives.at[1, layer, hop], to)

    def third(chunk, half, incoming):
        layer, hop, source, odd = split(chunk)
        there_side = lax.rem(side + odd, 2)
        there_across = lax.rem(across + 1 - odd, 2)
        to = at(there_across, core, deep, there_side)
        here = there_side if incoming else side
        lane = there_across if incoming else across
        piece_side = (1 - odd) * half + odd * here
        piece_lane = 2 * core + (1 - odd) * lane + odd * half
        piece = full.at[layer, source, piece_side, :, lanes(piece_lane)]
        return remote(
            piece, piece, sends.at[2 + half, layer, hop], receives.at[2 + half, layer, hop], to
        )

    def fourth(chunk, incoming):
        layer, hop, source, odd = split(chunk)
        column = 1 - core if incoming else core
        piece = full.at[layer, source, :, :, lanes(2 * column, 2)]
        to = at(across, 1 - core, deep, side)
        return remote(piece, piece, sends.at[4, layer, hop], receives.at[4, layer, hop], to)

    def own_fourth(layer, incoming):
        column = 1 - core if incoming else core
        piece = full.at[layer, deep, 1 - side, :, lanes(2 * column, 2)]
        to = at(across, 1 - core, deep, side)
        return remote(piece, piece, sends.at[4, layer, 0], receives.at[4, layer, 0], to)

    def local(layer):
        return pltpu.make_async_copy(
            own.at[layer], full.at[layer, deep, side], local_sem.at[layer]
        )

    def each(low, action):
        def step(hop, carry):
            action(hop)
            return carry

        lax.fori_loop(low, deep_count, step, 0)

    def head_local():
        return pltpu.make_async_copy(
            head_own, head_full.at[across, core, deep, side], local_sem.at[layers]
        )

    def head_first(hop):
        to = at(across, core, lax.rem(deep + hop, deep_count), side)
        target = head_full.at[across, core, deep, side]
        return remote(head_own, target, head_sends.at[hop], head_receives.at[hop], to)

    def head_first_in(hop):
        piece = head_full.at[across, core, lax.rem(deep - hop + deep_count, deep_count), side]
        to = at(across, core, deep, side)
        return remote(piece, piece, head_sends.at[hop], head_receives.at[hop], to)

    def head_next(which, incoming):
        if which == 0:
            to = at(across, core, deep, 1 - side)
            piece = head_full.at[across, core, :, 1 - side if incoming else side]
        elif which == 1:
            to = at(1 - across, core, deep, side)
            piece = head_full.at[1 - across if incoming else across, core]
        else:
            to = at(across, 1 - core, deep, side)
            piece = head_full.at[:, 1 - core if incoming else core]
        slot = deep_count + which
        return remote(piece, piece, head_sends.at[slot], head_receives.at[slot], to)

    def go_head(which):
        if which == 0:
            head_local().wait()
            each(1, lambda hop: head_first_in(hop).wait_recv())
        else:
            head_next(which - 1, True).wait_recv()
        if which < 3:
            head_next(which, False).start()

    send_edges, take_edges, put = edge_tools(dims, halo, edge_sends, edge_receives)
    tile = 2 * LANES
    tiles = channels // tile
    pixels = rows * width
    band = TAPS * channels
    masks, unused = row_weights(valid, rows)
    share = band * TAPS // space_count

    def loop(count, action):
        def body(index, carry):
            action(index)
            return carry

        lax.fori_loop(0, count, body, 0)

    def spot(index):
        return pl.multiple_of(index * tile, tile)

    def load(layer, owner):
        start = pl.multiple_of(owner * share, 8)
        return pltpu.make_async_copy(
            full.at[layer, owner // 2, lax.rem(owner, 2)],
            weights.at[layer % 2, pl.ds(start, share)],
            load_sem.at[layer % 2, owner],
        )

    def arrive(layer):
        own_fourth(layer, True).wait_recv()
        begin = layers + layer * (deep_count - 1)
        loop(deep_count - 1, lambda index: fourth(begin + index, True).wait_recv())
        loop(space_count, lambda owner: load(layer, owner).start())

    def store(which, layer):
        source, target = (
            (wide.at[layer], wide_out.at[layer]),
            (hidden.at[layer], hidden_out.at[layer]),
            (last, last_out),
        )[which]
        return pltpu.make_async_copy(source, target, store_sem.at[which, layer])

    def forward(layer):
        here = wide.at[layer]
        take_edges(layer, here)
        store(0, layer).start()
        loop(space_count, lambda owner: load(layer, owner).wait())

        def outer(part):
            lane = pl.ds(spot(part), tile)
            total = vector_lanes(vectors, layer * channels, part)
            for tap_row in range(TAPS):
                total += mix(
                    here[tap_row * width : tap_row * width + pixels, :],
                    weights[layer % 2, tap_row * band : (tap_row + 1) * band, lane],
                    1,
                    0,
                )
            hidden[layer, :, lane] = total
            for row in range(rows):
                span = slice(row * width, (row + 1) * width)
                value = gelu_value(hidden[layer, span, lane]) * masks[row]
                if layer < layers - 1:
                    put(wide.at[layer + 1], row + 1, spot(part), tile, value)
                else:
                    last[span, lane] = value.astype(low)

        loop(tiles, outer)
        store(1, layer).start()
        if layer < layers - 1:
            send_edges(layer + 1, wide.at[layer + 1])

    def go_second(chunk):
        layer, hop, source, odd = split(chunk)

        @pl.when(hop == 0)
        def own_rows():
            local(layer).wait()

        @pl.when(hop > 0)
        def other_rows():
            first_in(layer, hop).wait_recv()
            go_first(chunk - layers + z_ahead)

        second(chunk, False).start()

    def go_third(chunk):
        second(chunk, True).wait_recv()

        @pl.when(chunk < layers)
        def own_rows():
            third(chunk, 1 - side, False).start()

        @pl.when(chunk >= layers)
        def other_rows():
            third(chunk, 0, False).start()
            third(chunk, 1, False).start()

    def go_fourth(chunk):
        @pl.when(chunk < layers)
        def own_rows():
            third(chunk, 1 - side, True).wait_recv()
            own_fourth(chunk, False).start()

        @pl.when(chunk >= layers)
        def other_rows():
            third(chunk, 0, True).wait_recv()
            third(chunk, 1, True).wait_recv()
            fourth(chunk, False).start()

    def go_head_first():
        each(1, lambda hop: head_first(hop).start())

    def go_first(index):
        @pl.when(index < layers * (deep_count - 1))
        def more():
            first(index // (deep_count - 1), 1 + lax.rem(index, deep_count - 1)).start()

    z_ahead = 2
    for index in range(min(z_ahead, deep_count - 1)):
        go_first(index)
    local(0).start()
    go_second(0)
    for layer in range(1, layers):
        own[layer] = master[layer].astype(low)
        local(layer).start()
    head_rows, head_blocks = head_own.shape[0], heads * depth // LANES
    for lane in range(head_blocks):
        head_own[:, lane * LANES : (lane + 1) * LANES] = head_master[
            pl.ds(lane, head_rows, stride=head_blocks), :
        ].astype(low)
    head_local().start()
    for row in range(rows):
        for part in range(tiles):
            value = features[row * width : (row + 1) * width, part * tile : (part + 1) * tile]
            put(wide.at[0], row + 1, part * tile, tile, value.astype(jnp.float32))
    send_edges(0, wide.at[0])

    lag_third, lag_fourth = 2, 4
    others = deep_count - 1

    def last_of(layer):
        return layers + others * (layer + 1) - 1 + lag_fourth

    early = min(2, others)
    timed = [(layers + early, go_head_first)]
    timed += [(layers + others + 2 * which, go_head, which) for which in range(3)]
    for layer in range(layers - 1):
        timed += [(last_of(layer) + 1, arrive, layer), (last_of(layer) + 2, forward, layer)]

    def turn(now):
        for lag, action in ((0, go_second), (lag_third, go_third), (lag_fourth, go_fourth)):
            begin = max(lag, 1)

            @pl.when(jnp.logical_and(now >= begin, now < chunks + lag))
            def stage():
                action(now - lag)

        for moment, action, *which in timed:

            @pl.when(now == moment)
            def once():
                action(*which)

    loop(chunks + lag_fourth, turn)
    go_head(3)
    arrive(layers - 1)
    forward(layers - 1)
    store(2, 0).start()

    def finish(chunk):
        second(chunk, False).wait_send()

        @pl.when(chunk < layers)
        def own_rows():
            third(chunk, 1 - side, False).wait_send()
            own_fourth(chunk, False).wait_send()

        @pl.when(chunk >= layers)
        def other_rows():
            third(chunk, 0, False).wait_send()
            third(chunk, 1, False).wait_send()
            fourth(chunk, False).wait_send()

    loop(chunks, finish)
    each(1, lambda hop: head_first(hop).wait_send())
    for which in range(3):
        head_next(which, False).wait_send()

    for layer in range(layers):

        each(1, lambda hop: first(layer, hop).wait_send())
        store(0, layer).wait()
        store(1, layer).wait()
    store(2, 0).wait()


def gather_weights(master, head_master, head_width, features, vectors, valid, space_count):
    layers, share, channels = master.shape
    rows, width, unused = features.shape
    deep_count = space_count // 2
    pixels = rows * width
    dims = (layers, rows, width, channels, NH, HD, space_count)
    low, wide_float = jnp.bfloat16, jnp.float32
    anywhere = pl.BlockSpec(memory_space=pl.ANY)
    vmem = pl.BlockSpec(memory_space=pltpu.VMEM)
    head_own = (head_master.shape[0] * LANES // head_width, head_width)
    head_shape = (2, 2, deep_count, 2) + head_own
    wide_shape = (layers, (rows + 2) * width, TAPS * channels)
    full, head_full, wide, hidden, last = pl.pallas_call(
        partial(gather_kernel, dims),
        out_shape=(
            jax.ShapeDtypeStruct((layers, deep_count, 2, share, channels), low),
            jax.ShapeDtypeStruct(head_shape, low),
            jax.ShapeDtypeStruct(wide_shape, low),
            jax.ShapeDtypeStruct((layers, pixels, channels), wide_float),
            jax.ShapeDtypeStruct((pixels, channels), low),
        ),
        in_specs=[vmem] * 4 + [pl.BlockSpec(memory_space=pltpu.SMEM)],
        out_specs=[anywhere] * 5,
        scratch_shapes=[
            pltpu.VMEM(master.shape, low),
            pltpu.VMEM(head_own, low),
            pltpu.VMEM((2, space_count * share, channels), low),
            pltpu.VMEM(wide_shape, low),
            pltpu.VMEM((layers, pixels, channels), wide_float),
            pltpu.VMEM((pixels, channels), low),
            pltpu.VMEM((layers, 2, width, channels), low),
            pltpu.SemaphoreType.DMA((layers + 1,)),
            pltpu.SemaphoreType.DMA((5, layers, deep_count)),
            pltpu.SemaphoreType.DMA((5, layers, deep_count)),
            pltpu.SemaphoreType.DMA((deep_count + 3,)),
            pltpu.SemaphoreType.DMA((deep_count + 3,)),
            pltpu.SemaphoreType.DMA((2, space_count)),
            pltpu.SemaphoreType.DMA((3, layers)),
            pltpu.SemaphoreType.DMA((layers, 2)),
            pltpu.SemaphoreType.DMA((layers, 2)),
        ],
        compiler_params=pltpu.CompilerParams(
            collective_id=0, has_side_effects=True, vmem_limit_bytes=VMEM_LIMIT
        ),
    )(master, head_master, features.reshape(pixels, channels), vectors, valid)
    return (
        full.reshape(layers, space_count * share, channels),
        head_full.reshape(-1, head_width),
        wide,
        hidden,
        last,
    )


def reduce_kernel(
    layers,
    deep_count,
    grads,
    vector,
    bases,
    first_in,
    second_moment_in,
    master_in,
    total,
    stats,
    vector_total,
    first_out,
    second_out,
    master_out,
    mine,
    core_in,
    second_in,
    kept,
    third_in,
    last,
    last_in,
    acc,
    stat_own,
    stat_in,
    stat_deep,
    vector_out,
    vector_in,
    vector_deep,
    moment_one,
    moment_two,
    master,
    local_sem,
    sends,
    receives,
    stat_sends,
    stat_receives,
    deep_sends,
    deep_receives,
    vector_sends,
    vector_receives,
    state_loads,
    state_stores,
):
    across, core, deep, side = place()
    block = 2 * core + across
    steps = layers * deep_count

    def split(step):
        layer, hop = step // deep_count, lax.rem(step + 1, deep_count)
        target = lax.rem(deep + hop, deep_count)
        return (layer, hop, target, lax.rem(target, 2))

    def first(step):
        layer, hop, target, odd = split(step)
        return remote(
            grads.at[layer, target, :, :, lanes(2 * (1 - core), 2)],
            core_in.at[step],
            sends.at[0, step],
            receives.at[0, step],
            at(across, 1 - core, deep, side),
        )

    def load(step):
        layer, hop, target, odd = split(step)
        return pltpu.make_async_copy(
            grads.at[layer, target, :, :, lanes(2 * core, 2)], mine.at[step], local_sem.at[step]
        )

    def second(step, half):
        layer, hop, target, odd = split(step)
        piece_side = (1 - odd) * half + odd * (1 - side)
        piece_lane = (1 - odd) * (1 - across) + odd * half
        to = at(lax.rem(across + 1 - odd, 2), core, deep, lax.rem(side + odd, 2))
        return remote(
            mine.at[step, piece_side, :, lanes(piece_lane)],
            second_in.at[step, half],
            sends.at[1 + half, step],
            receives.at[1 + half, step],
            to,
        )

    def third(step):
        layer, hop, target, odd = split(step)
        keep = (1 - odd) * side + odd * across
        to = at(lax.rem(across + odd, 2), core, deep, lax.rem(side + 1 - odd, 2))
        return remote(
            kept.at[step, 1 - keep],
            third_in.at[step],
            sends.at[3, step],
            receives.at[3, step],
            to,
        )

    def fourth(step):
        layer, hop, target, odd = split(step)
        return remote(
            last.at[step],
            last_in.at[step],
            sends.at[4, step],
            receives.at[4, step],
            at(across, core, target, side),
        )

    def fifth(layer, incoming):
        lane = 2 * core + (1 - across if incoming else across)
        piece = total.at[layer, :, lanes(lane)]
        to = at(1 - across, core, deep, side)
        return remote(piece, piece, sends.at[5, layer], receives.at[5, layer], to)

    def sixth(layer, incoming):
        column = 1 - core if incoming else core
        piece = total.at[layer, :, lanes(2 * column, 2)]
        to = at(across, 1 - core, deep, side)
        return remote(piece, piece, sends.at[6, layer], receives.at[6, layer], to)

    def run(low, high, action):
        def body(step, carry):
            action(step)
            return carry

        lax.fori_loop(low, high, body, 0)

    half_block = LANES // 2

    def stat_side(layer, incoming):
        rows = pl.ds(pl.multiple_of((1 - side) * half_block, half_block), half_block)
        return remote(
            stat_own.at[layer, rows],
            stat_in.at[layer],
            stat_sends.at[0, layer],
            stat_receives.at[0, layer],
            at(across, core, deep, 1 - side),
        )

    def stat_along(layer, hop):
        return remote(
            stat_deep.at[layer, deep],
            stat_deep.at[layer, deep],
            deep_sends.at[layer, hop],
            deep_receives.at[layer, hop],
            at(across, core, lax.rem(deep + hop, deep_count), side),
        )

    def stat_along_in(layer, hop):
        source = lax.rem(deep - hop + deep_count, deep_count)
        return remote(
            stat_deep.at[layer, source],
            stat_deep.at[layer, source],
            deep_sends.at[layer, hop],
            deep_receives.at[layer, hop],
            at(across, core, deep, side),
        )

    def half_rows(which):
        return pl.ds(pl.multiple_of(which * half_block, half_block), half_block)

    def stat_spread(which, layer, incoming):
        if which < 3:
            other_side = side if which == 1 else 1 - side
            other_across = across if which == 0 else 1 - across
            to = at(other_across, core, deep, other_side)
            if incoming:
                piece = stats.at[layer, 2 * core + other_across, half_rows(other_side)]
            else:
                piece = stats.at[layer, block, half_rows(side)]
        else:
            to = at(across, 1 - core, deep, side)
            piece = stats.at[layer, pl.ds(2 * (1 - core if incoming else core), 2)]
        slot = 1 + which
        return remote(piece, piece, stat_sends.at[slot, layer], stat_receives.at[slot, layer], to)

    def vector_step(which):
        to = (
            at(across, 1 - core, deep, side),
            at(1 - across, core, deep, side),
            at(across, core, deep, 1 - side),
        )[which]
        return remote(
            vector_out.at[which],
            vector_in.at[which],
            vector_sends.at[which],
            vector_receives.at[which],
            to,
        )

    def vector_along(hop):
        return remote(
            vector_deep.at[deep],
            vector_deep.at[deep],
            vector_sends.at[2 + hop],
            vector_receives.at[2 + hop],
            at(across, core, lax.rem(deep + hop, deep_count), side),
        )

    def vector_along_in(hop):
        source = lax.rem(deep - hop + deep_count, deep_count)
        return remote(
            vector_deep.at[source],
            vector_deep.at[source],
            vector_sends.at[2 + hop],
            vector_receives.at[2 + hop],
            at(across, core, deep, side),
        )

    def go_first(step):
        load(step).start()
        first(step).start()

    ahead = min(3, steps)
    piece_rows = 144 if total.shape[1] % 144 == 0 else total.shape[1]
    states = (
        (first_in, moment_one, first_out),
        (second_moment_in, moment_two, second_out),
        (master_in, master, master_out),
    )

    def load_state(which, layer):
        source, target, unused = states[which]
        return pltpu.make_async_copy(
            source.at[layer], target.at[layer], state_loads.at[which, layer]
        )

    def store_state(which, layer):
        unused, source, target = states[which]
        return pltpu.make_async_copy(
            source.at[layer], target.at[layer], state_stores.at[which, layer]
        )

    greet(partners(deep_count) + [at(1 - across, core, deep, 1 - side)])
    run(0, ahead, go_first)
    for layer in range(layers):
        for which in range(3):
            load_state(which, layer).start()

    def wide(left, right):
        return left.astype(jnp.float32) + right.astype(jnp.float32)

    def go_second(step):
        @pl.when(step + ahead < steps)
        def start_next():
            go_first(step + ahead)

        load(step).wait()
        first(step).wait_recv()
        mine[step] = wide(mine[step], core_in[step]).astype(jnp.bfloat16)
        second(step, 0).start()
        second(step, 1).start()

    def go_third(step):
        layer, hop, target, odd = split(step)
        for half in range(2):
            second(step, half).wait_recv()
            keep_side = (1 - odd) * half + odd * side
            keep_lane = (1 - odd) * across + odd * half
            kept[step, half] = wide(
                mine[step, keep_side, :, lanes(keep_lane)], second_in[step, half]
            ).astype(jnp.bfloat16)
        third(step).start()

    def go_fourth(step):
        layer, hop, target, odd = split(step)
        third(step).wait_recv()
        keep = (1 - odd) * side + odd * across
        last[step] = wide(kept[step, keep], third_in[step]).astype(jnp.bfloat16)

        @pl.when(hop > 0)
        def unused():
            fourth(step).start()

    def close(layer):
        acc[...] = last[layer * deep_count + deep_count - 1].astype(jnp.float32)

        def add(hop):
            step = layer * deep_count + hop - 1
            fourth(step).wait_recv()
            acc[...] += last_in[step].astype(jnp.float32)

        run(1, deep_count, add)
        total[layer, :, lanes(block)] = acc[...].astype(jnp.bfloat16)
        fifth(layer, False).start()

    def spread(layer):
        fifth(layer, True).wait_recv()
        sixth(layer, False).start()

    def measure(layer):
        sixth(layer, True).wait_recv()
        own_lanes = total[layer, :, lanes(block)]
        stat_own[layer] = lax.dot_general(
            own_lanes,
            total[layer],
            (((0,), (0,)), ((), ())),
            preferred_element_type=jnp.float32,
        ).astype(jnp.bfloat16)
        stat_side(layer, False).start()

    def pair(layer):
        stat_side(layer, True).wait_recv()
        stat_deep[layer, deep] = wide(
            stat_own[layer, half_rows(side)], stat_in[layer]
        ).astype(jnp.bfloat16)
        run(1, deep_count, lambda hop: stat_along(layer, hop).start())

    def settle(layer):
        run(1, deep_count, lambda hop: stat_along_in(layer, hop).wait_recv())
        whole = stat_deep[layer, 0].astype(jnp.float32)
        for source in range(1, deep_count):
            whole += stat_deep[layer, source].astype(jnp.float32)
        stats[layer, block, half_rows(side)] = whole.astype(jnp.bfloat16)
        for which in range(3):
            stat_spread(which, layer, False).start()

    def share_core(layer):
        for which in range(3):
            stat_spread(which, layer, True).wait_recv()
        stat_spread(3, layer, False).start()

    def refresh(layer):
        for which in range(3):
            load_state(which, layer).wait()
        high, rest = halves(bases[layer])

        def one_piece(index):
            here = pl.ds(pl.multiple_of(index * piece_rows, piece_rows), piece_rows)
            given = total[layer, here, :]
            rotated = mix(given, high, 1, 0) + mix(given, rest, 1, 0)
            first_new, second_new, direction = moments(
                rotated, moment_one[layer, here, :], moment_two[layer, here, :]
            )
            moment_one[layer, here, :] = first_new
            moment_two[layer, here, :] = second_new
            up, down = halves(direction)
            back = mix(up, high, 1, 1) + (mix(up, rest, 1, 1) + mix(down, high, 1, 1))
            old = master[layer, here, :]
            master[layer, here, :] = old - RATE_CONV * (back + DECAY * old)

        run(0, total.shape[1] // piece_rows, one_piece)
        for which in range(3):
            store_state(which, layer).start()

    def finish(layer):
        stat_spread(3, layer, True).wait_recv()
        fifth(layer, False).wait_send()
        sixth(layer, False).wait_send()
        stat_side(layer, False).wait_send()
        run(1, deep_count, lambda hop: stat_along(layer, hop).wait_send())
        for which in range(4):
            stat_spread(which, layer, False).wait_send()
        for which in range(3):
            store_state(which, layer).wait()

    def vector_next(which):
        vector_step(which).wait_recv()
        summed = vector_out[which] + vector_in[which]
        if which < 2:
            vector_out[which + 1] = summed
            vector_step(which + 1).start()
        else:
            vector_deep[deep] = summed
            run(1, deep_count, lambda hop: vector_along(hop).start())

    chunk_work = ((0, go_second), (2, go_third), (3, go_fourth))
    layer_work = (
        (4, close),
        (5, spread),
        (6, measure),
        (7, pair),
        (8, refresh),
        (9, settle),
        (10, share_core),
        (11, finish),
    )
    vector_out[0] = vector[...]
    vector_step(0).start()

    def turn(now):
        for lag, action in chunk_work:

            @pl.when(jnp.logical_and(now >= lag, now < steps + lag))
            def chunk():
                action(now - lag)

        for which in range(3):

            @pl.when(now == 2 * which + 1)
            def exchange():
                vector_next(which)

        for lag, action in layer_work:
            past = now - lag - (deep_count - 1)

            @pl.when(
                jnp.logical_and(
                    jnp.logical_and(past >= 0, past < steps), lax.rem(past, deep_count) == 0
                )
            )
            def whole_layer():
                action(past // deep_count)

    run(0, steps + layer_work[-1][0], turn)

    run(1, deep_count, lambda hop: vector_along_in(hop).wait_recv())
    summed = vector_deep[0]
    for source in range(1, deep_count):
        summed += vector_deep[source]
    vector_total[...] = summed
    for which in range(3):
        vector_step(which).wait_send()
    run(1, deep_count, lambda hop: vector_along(hop).wait_send())

    def drain(step):
        layer, hop, target, odd = split(step)
        first(step).wait_send()
        second(step, 0).wait_send()
        second(step, 1).wait_send()
        third(step).wait_send()

        @pl.when(hop > 0)
        def unused():
            fourth(step).wait_send()

    run(0, steps, drain)


def reduce_grads(grads, vector, bases, conv, space_count):
    layers, all_rows, columns = grads.shape
    deep_count, rows = space_count // 2, all_rows // space_count
    steps = layers * deep_count
    low = jnp.bfloat16
    blocks = columns // LANES
    vmem = pl.BlockSpec(memory_space=pltpu.VMEM)
    tall = jax.ShapeDtypeStruct((layers, rows, columns), jnp.float32)
    anywhere = pl.BlockSpec(memory_space=pl.ANY)
    total, stats, vector_total, *conv_new = pl.pallas_call(
        partial(reduce_kernel, layers, deep_count),
        out_shape=(
            jax.ShapeDtypeStruct((layers, rows, columns), low),
            jax.ShapeDtypeStruct((layers, blocks, LANES, columns), low),
            jax.ShapeDtypeStruct(vector.shape, jnp.float32),
            tall,
            tall,
            tall,
        ),
        in_specs=[anywhere, vmem, vmem] + [anywhere] * 3,
        out_specs=[vmem] * 3 + [anywhere] * 3,
        scratch_shapes=[
            pltpu.VMEM((steps, 2, rows, 2 * LANES), low),
            pltpu.VMEM((steps, 2, rows, 2 * LANES), low),
            pltpu.VMEM((steps, 2, rows, LANES), low),
            pltpu.VMEM((steps, 2, rows, LANES), low),
            pltpu.VMEM((steps, rows, LANES), low),
            pltpu.VMEM((steps, rows, LANES), low),
            pltpu.VMEM((steps, rows, LANES), low),
            pltpu.VMEM((rows, LANES), jnp.float32),
            pltpu.VMEM((layers, LANES, columns), low),
            pltpu.VMEM((layers, LANES // 2, columns), low),
            pltpu.VMEM((layers, deep_count, LANES // 2, columns), low),
            pltpu.VMEM((3,) + vector.shape, jnp.float32),
            pltpu.VMEM((3,) + vector.shape, jnp.float32),
            pltpu.VMEM((deep_count,) + vector.shape, jnp.float32),
            pltpu.VMEM(tall.shape, jnp.float32),
            pltpu.VMEM(tall.shape, jnp.float32),
            pltpu.VMEM(tall.shape, jnp.float32),
            pltpu.SemaphoreType.DMA((steps,)),
            pltpu.SemaphoreType.DMA((7, steps)),
            pltpu.SemaphoreType.DMA((7, steps)),
            pltpu.SemaphoreType.DMA((5, layers)),
            pltpu.SemaphoreType.DMA((5, layers)),
            pltpu.SemaphoreType.DMA((layers, deep_count)),
            pltpu.SemaphoreType.DMA((layers, deep_count)),
            pltpu.SemaphoreType.DMA((2 + deep_count,)),
            pltpu.SemaphoreType.DMA((2 + deep_count,)),
            pltpu.SemaphoreType.DMA((3, layers)),
            pltpu.SemaphoreType.DMA((3, layers)),
        ],
        compiler_params=pltpu.CompilerParams(
            collective_id=1, has_side_effects=True, vmem_limit_bytes=VMEM_LIMIT
        ),
    )(grads.reshape(layers, deep_count, 2, rows, columns), vector, bases, *conv)
    return (stats.reshape(layers, columns, columns), vector_total, conv_new)


def work_kernel(
    dims,
    weights_in,
    head_in,
    wide_in,
    hidden_in,
    last_in,
    vectors,
    cotangent_in,
    valid,
    merged,
    features_grad,
    grads_out,
    head_grad,
    vector,
    weights,
    head,
    cotangent,
    wide,
    hidden,
    last,
    last_turned,
    d_wide,
    d_active,
    grads,
    halo,
    term,
    term_in,
    load_sem,
    store_sem,
    send_sem,
    receive_sem,
    term_sends,
    term_receives,
    *head_refs,
):
    layers, rows, width, channels, heads, depth, space_count = dims
    deep_count = space_count // 2
    across, core, deep, side = place()
    spread_head = len(head_refs) > 0
    if spread_head:
        head_parts, core_in, across_in, side_in, deep_in, head_sends, head_receives = head_refs
        head_rows = head_parts.shape[4]
    tile = 2 * LANES
    tiles = channels // tile
    low = jnp.bfloat16

    loads = ((last_in, last), (head_in, head), (cotangent_in, cotangent))
    for layer in reversed(range(layers)):
        loads += (
            (hidden_in.at[layer], hidden.at[layer]),
            (wide_in.at[layer], wide.at[layer]),
            (weights_in.at[layer], weights.at[layer]),
        )

    def load(which):
        source, target = loads[which]
        return pltpu.make_async_copy(source, target, load_sem.at[which])

    for which in range(len(loads)):
        load(which).start()

    others = [
        at(across, 1 - core, deep, side),
        at(1 - across, core, deep, side),
        at(across, core, deep, 1 - side),
    ]
    if spread_head:
        others += [
            at(across, core, lax.rem(deep + hop, deep_count), side) for hop in range(1, deep_count)
        ]
    greet_edges(others, space_count)

    def term_lanes(index, which):
        return pl.ds(pl.multiple_of(index * depth + which * LANES, LANES), LANES)

    def term_step(which, index, incoming=False):
        if which == 0:
            source, target, to = term.at[:, term_lanes(index, 1 - core)], term_in.at[0, index], others[0]
        elif which == 1:
            source, target, to = term.at[:, term_lanes(index, core)], term_in.at[1, index], others[1]
        else:
            source = merged.at[:, term_lanes(index, 1 - core if incoming else core)]
            target, to = source, others[0]
        return remote(
            source, target, term_sends.at[which, index], term_receives.at[which, index], to
        )

    def term_pair(index):
        term_step(0, index).wait_recv()
        lane = term_lanes(index, core)
        both = term[:, lane].astype(jnp.float32) + term_in[0, index].astype(jnp.float32)
        term[:, lane] = both.astype(low)
        term_step(1, index).start()

    def term_total(index):
        term_step(1, index).wait_recv()
        lane = term_lanes(index, core)
        both = term[:, lane].astype(jnp.float32) + term_in[1, index].astype(jnp.float32)
        merged[:, lane] = both.astype(low)
        term_step(2, index).start()

    def term_end(index):
        term_step(2, index, True).wait_recv()
        for which in range(3):
            term_step(which, index).wait_send()

    def head_step(which):
        if which == 0:
            source, target, to = head_parts.at[:, 1 - core], core_in, others[0]
        elif which == 1:
            source = head_parts.at[pl.ds(0, 2), core, pl.ds(0, deep_count), 1 - side]
            target, to = side_in, others[2]
        else:
            source = head_parts.at[1 - across, core, pl.ds(0, deep_count), side]
            target, to = across_in, others[1]
        return remote(source, target, head_sends.at[which], head_receives.at[which], to)

    def head_along(hop):
        target = lax.rem(deep + hop, deep_count)
        return remote(
            head_parts.at[across, core, target, side],
            deep_in.at[hop],
            head_sends.at[2 + hop],
            head_receives.at[2 + hop],
            at(across, core, target, side),
        )

    def head_next(which):
        if not spread_head:
            return
        head_step(which).wait_recv()
        if which == 0:
            for part in range(2):
                both = head_parts[part, core].astype(jnp.float32) + core_in[part].astype(jnp.float32)
                head_parts[part, core] = both.astype(low)
            head_step(1).start()
        elif which == 1:
            for part in range(2):
                both = head_parts[part, core, pl.ds(0, deep_count), side].astype(jnp.float32)
                both += side_in[part].astype(jnp.float32)
                head_parts[part, core, pl.ds(0, deep_count), side] = both.astype(low)
            head_step(2).start()
        else:
            both = head_parts[across, core, pl.ds(0, deep_count), side].astype(jnp.float32)
            both += across_in[...].astype(jnp.float32)
            head_parts[across, core, pl.ds(0, deep_count), side] = both.astype(low)
            for hop in range(1, deep_count):
                head_along(hop).start()

    def head_end():
        if not spread_head:
            return
        whole = head_parts[across, core, deep, side].astype(jnp.float32)
        for hop in range(1, deep_count):
            head_along(hop).wait_recv()
            whole += deep_in[hop].astype(jnp.float32)
        blocks = heads * depth // LANES
        for lane in range(blocks):
            head_grad[pl.ds(lane, head_rows, stride=blocks), :] = whole[
                :, lane * LANES : (lane + 1) * LANES
            ]
        for which in range(3):
            head_step(which).wait_send()
        for hop in range(1, deep_count):
            head_along(hop).wait_send()

    send_edges, take_edges, put = edge_tools(dims, halo, send_sem, receive_sem)

    def loop(count, action):
        def body(index, carry):
            action(index)
            return carry

        lax.fori_loop(0, count, body, 0)

    def spot(index):
        return pl.multiple_of(index * tile, tile)

    masks, weights_row = row_weights(valid, rows)

    def put_vector(start, part, value):
        row = start // LANES + 2 * part
        vector[pl.ds(row, 1), :] = value[:, :LANES]
        vector[pl.ds(row + 1, 1), :] = value[:, LANES:]

    pixels = rows * width
    for which in range(3):
        load(which).wait()
    last_turned[...] = last[...].astype(jnp.float32).T.astype(low)
    d_active[...] = jnp.zeros_like(d_active)

    def one_head(index):
        lane = pl.ds(pl.multiple_of(index * depth, depth), depth)
        projected = mix(last[...], head[:, lane], 1, 0)
        projected += vector_lanes(vectors, layers * channels, index)
        gain = vector_lanes(vectors, layers * channels + heads * depth, index)
        gain_total = jnp.zeros((1, depth), jnp.float32)
        bias_total = jnp.zeros((1, depth), jnp.float32)
        rounded = []
        for row in range(rows):
            span = slice(row * width, (row + 1) * width)
            weight = weights_row[row]
            value = projected[span]
            inverse = lax.rsqrt(jnp.sum(value * value, -1, keepdims=True) + 1e-06)
            normed = value * inverse
            scaled = gain * weight
            term[span, lane] = (normed * scaled).astype(low)
            given = cotangent[span, lane].astype(jnp.float32)
            gain_total += jnp.sum(normed * given, 0, keepdims=True) * weight
            d_normed = given * scaled
            along = jnp.sum(normed * d_normed, -1, keepdims=True)
            d_low = (inverse * (d_normed - normed * along)).astype(low)
            bias_total += jnp.sum(d_low.astype(jnp.float32), 0, keepdims=True)
            rounded.append(d_low)
        term_step(0, index).start()
        put_vector(layers * channels + heads * depth, index, gain_total)
        put_vector(layers * channels, index, bias_total)
        d_low = jnp.concatenate(rounded, 0)
        grad = mix(last_turned[...], d_low, 1, 0)
        if spread_head:
            split = grad.reshape(2, 2, deep_count, 2, head_rows, depth)
            head_parts[:, :, :, :, :, lane] = split.astype(low)
        else:
            head_grad[:, lane] = grad.astype(low)
        d_active[...] += mix(d_low, head[:, lane], 1, 1)

        @pl.when(index > 0)
        def earlier():
            term_pair(index - 1)

    loop(heads, one_head)
    if spread_head:
        head_step(0).start()
    term_pair(heads - 1)

    def store(layer):
        slot = layer % 2
        return pltpu.make_async_copy(grads.at[slot], grads_out.at[layer], store_sem.at[slot])

    for layer in reversed(range(layers)):
        which = layers - 1 - layer
        for part in range(3):
            load(3 + 3 * which + part).wait()

        def enter(part):
            lane = pl.ds(spot(part), tile)
            total = jnp.zeros((1, tile), jnp.float32)
            for row in range(rows):
                span = slice(row * width, (row + 1) * width)
                slope = gelu_slope(hidden[layer, span, lane])
                value = slope * (masks[row] * d_active[span, lane])
                value = value.astype(low).astype(jnp.float32)
                total += jnp.sum(value, 0, keepdims=True)
                put(d_wide, row + 1, spot(part), tile, value)
            put_vector(layer * channels, part, total)

        loop(tiles, enter)
        send_edges(which, d_wide)
        if layer + 2 < layers:
            store(layer + 2).wait()

        def one_tap(tap):
            tap_row, tap_column = tap // TAPS, lax.rem(tap, TAPS)
            window = wide[
                layer,
                pl.ds(pl.multiple_of(tap_row * width, width), pixels),
                pl.ds(pl.multiple_of(tap_column * channels, channels), channels),
            ]
            d_hidden = d_wide[width : width + pixels, channels : 2 * channels]
            grads[layer % 2, pl.ds(pl.multiple_of(tap * channels, channels), channels), :] = mix(
                window, d_hidden, 0, 0
            ).astype(low)

        loop(TAPS * TAPS, one_tap)
        store(layer).start()
        head_next(layers - 1 - layer)
        take_edges(which, d_wide)

        def back(part):
            total = jnp.zeros((pixels, tile), jnp.float32)
            for tap_row in range(TAPS):
                for tap_column in range(TAPS):
                    window = d_wide[
                        (2 - tap_row) * width : (2 - tap_row) * width + pixels,
                        (2 - tap_column) * channels : (3 - tap_column) * channels,
                    ]
                    first = (TAPS * tap_row + tap_column) * channels
                    total += mix(
                        window, weights[layer, pl.ds(first + spot(part), tile), :], 1, 1
                    )
            d_active[:, pl.ds(spot(part), tile)] = total

        loop(tiles, back)

    loop(heads, term_total)
    features_grad[...] = d_active[...].astype(low)
    head_end()
    loop(heads, term_end)
    for layer in range(min(layers, 2)):
        store(layer).wait()


def run_block(
    weights, head, wide, hidden, last, vectors, cotangent, valid, space_count
):
    rows, width, unused = cotangent.shape
    layers, unused, channels = weights.shape
    head_width = head.shape[1]
    pixels = rows * width
    deep_count = space_count // 2
    head_rows = channels // (4 * space_count)
    spread_head = head_rows % 16 == 0
    low, full = jnp.bfloat16, jnp.float32
    dims = (layers, rows, width, channels, NH, HD, space_count)
    vmem = pl.BlockSpec(memory_space=pltpu.VMEM)
    anywhere = pl.BlockSpec(memory_space=pl.ANY)
    head_scratch = []
    head_out = jax.ShapeDtypeStruct((channels, head_width), low)
    if spread_head:
        head_out = jax.ShapeDtypeStruct((head_rows * head_width // LANES, LANES), full)
        head_scratch = [
            pltpu.VMEM((2, 2, deep_count, 2, head_rows, head_width), low),
            pltpu.VMEM((2, deep_count, 2, head_rows, head_width), low),
            pltpu.VMEM((deep_count, head_rows, head_width), low),
            pltpu.VMEM((2, deep_count, head_rows, head_width), low),
            pltpu.VMEM((deep_count, head_rows, head_width), low),
            pltpu.SemaphoreType.DMA((2 + deep_count,)),
            pltpu.SemaphoreType.DMA((2 + deep_count,)),
        ]
    outs = pl.pallas_call(
        partial(work_kernel, dims),
        out_shape=(
            jax.ShapeDtypeStruct((pixels, head_width), low),
            jax.ShapeDtypeStruct((pixels, channels), low),
            jax.ShapeDtypeStruct(weights.shape, low),
            head_out,
            jax.ShapeDtypeStruct(vectors.shape, full),
        ),
        in_specs=[
            anywhere,
            anywhere,
            anywhere,
            anywhere,
            anywhere,
            vmem,
            anywhere,
            pl.BlockSpec(memory_space=pltpu.SMEM),
        ],
        out_specs=[vmem, vmem, anywhere, vmem, vmem],
        scratch_shapes=[
            pltpu.VMEM(weights.shape, low),
            pltpu.VMEM(head.shape, low),
            pltpu.VMEM((pixels, head_width), low),
            pltpu.VMEM((layers, (rows + 2) * width, TAPS * channels), low),
            pltpu.VMEM((layers, pixels, channels), full),
            pltpu.VMEM((pixels, channels), low),
            pltpu.VMEM((channels, pixels), low),
            pltpu.VMEM(((rows + 2) * width, TAPS * channels), low),
            pltpu.VMEM((pixels, channels), full),
            pltpu.VMEM((2,) + weights.shape[1:], low),
            pltpu.VMEM((layers, 2, width, channels), low),
            pltpu.VMEM((pixels, head_width), low),
            pltpu.VMEM((2, NH, pixels, LANES), low),
            pltpu.SemaphoreType.DMA((3 * layers + 3,)),
            pltpu.SemaphoreType.DMA((2,)),
            pltpu.SemaphoreType.DMA((layers, 2)),
            pltpu.SemaphoreType.DMA((layers, 2)),
            pltpu.SemaphoreType.DMA((3, NH)),
            pltpu.SemaphoreType.DMA((3, NH)),
        ]
        + head_scratch,
        compiler_params=pltpu.CompilerParams(
            collective_id=2, has_side_effects=True, vmem_limit_bytes=VMEM_LIMIT
        ),
    )(
        weights,
        head,
        wide,
        hidden,
        last,
        vectors,
        cotangent.reshape(pixels, head_width),
        valid,
    )
    merged, features_grad, grads, head_grad, vector = outs
    if not spread_head:
        head_grad = lax.psum_scatter(
            head_grad.astype(full).reshape(-1), ("scale", "space"), scatter_dimension=0, tiled=True
        ).reshape(-1, LANES)
    return (merged, features_grad, grads, head_grad, vector)


def halves(value):
    high = value.astype(jnp.bfloat16)
    return (high, (value - high.astype(jnp.float32)).astype(jnp.bfloat16))


def dot(left, right, left_dim, right_dim):
    left_high, left_low = halves(left)
    right_high, right_low = halves(right)
    rest = mix(left_high, right_low, left_dim, right_dim) + mix(left_low, right_high, left_dim, right_dim)
    return mix(left_high, right_high, left_dim, right_dim) + rest


def quick(x):
    return pl.reciprocal(x,approx=True)
def eliminate(blocks, off, size, m=8):
    nl=len(blocks); nb=size//8; W=blocks[0][0].shape[1]
    sub=lax.broadcasted_iota(jnp.int32,(8,128),0)
    for k0 in range(0,size,m):
        b0=k0//8; s0=k0%8
        for l in range(nl):
            bl=blocks[l]
            top=bl[b0]
            def colb(b,j):
                return jnp.broadcast_to(bl[b][:,off+k0+j:off+k0+j+1],(8,128))
            c0=[colb(b0,j) for j in range(m)]
            a=[[None]*m for _ in range(m)]
            for j in range(m):
                for i in range(j,m):
                    a[i][j]=jnp.broadcast_to(c0[j][s0+i:s0+i+1,:],(8,128))
            inv=[]; low=[[None]*m for _ in range(m)]
            for k in range(m):
                r=quick(a[k][k]); inv.append(r)
                for i in range(k+1,m):
                    low[i][k]=a[i][k]*r
                for j in range(k+1,m):
                    for i in range(j,m):
                        a[i][j]=a[i][j]-low[i][k]*a[j][k]
            wid=lambda v: jnp.concatenate([v]*(W//128),1)
            rows=[jnp.broadcast_to(top[s0+i:s0+i+1,:],(8,W)) for i in range(m)]
            for i in range(m):
                for k in range(i):
                    rows[i]=rows[i]-wid(low[i][k])*rows[k]
            for b in range(b0,nb):
                if b==b0 and s0+m==8 and m==1: continue
                cs=list(c0) if b==b0 else [colb(b,j) for j in range(m)]
                for j in range(m):
                    for k in range(j):
                        cs[j]=cs[j]-low[j][k]*cs[k]
                acc=bl[b]
                for k in range(m):
                    w=cs[k]*inv[k]
                    if b==b0: w=jnp.where(sub>s0+k,w,0.0)
                    acc=acc-wid(w)*rows[k]
                bl[b]=acc
    out=[]
    lane=lax.broadcasted_iota(jnp.int32,(8,W),1)
    row8=lax.broadcasted_iota(jnp.int32,(8,W),0)
    for l in range(nl):
        res=[]
        for b in range(nb):
            v=blocks[l][b]
            d=jnp.sum(jnp.where(lane==row8+(off+8*b),v,0.0),1,keepdims=True)
            res.append(v*lax.rsqrt(d))
        out.append(jnp.concatenate(res,0))
    return out


def moments(grads, first, second):
    first_new = BETA_ONE * first + (1.0 - BETA_ONE) * grads
    second_new = BETA_TWO * second + (1.0 - BETA_TWO) * grads * grads
    direction = (
        first_new
        * (1.0 / (1.0 - BETA_ONE**STEP))
        / (jnp.sqrt(second_new * (1.0 / (1.0 - BETA_TWO**STEP))) + EPSILON)
    )
    return (first_new, second_new, direction)


def update_kernel(
    dims,
    *refs,
):
    moved = dims[4]
    inputs, outputs = refs[: moved + 11], refs[moved + 11 : -1 - moved]
    held = refs[-1 - moved : -1]
    update_body(
        dims, inputs[:moved], outputs[:moved], held, refs[-1], *inputs[moved:], *outputs[moved:]
    )


def update_body(
    dims,
    moved_in,
    moved_out,
    held,
    moved_sem,
    summed,
    statistics,
    bases,
    head_grad,
    head_first,
    head_second,
    head_master,
    vector_grad,
    vector_first,
    vector_second,
    vectors,
    stats_new,
    bases_new,
    head_first_new,
    head_second_new,
    head_new,
    vector_first_new,
    vector_second_new,
    vectors_new,
    system,
    pivot,
):
    layers, channels, bias_rows, panel, moved = dims
    block = LANES

    def take(which):
        return pltpu.make_async_copy(moved_in[which], held[which], moved_sem.at[0, which])

    def give(which):
        return pltpu.make_async_copy(held[which], moved_out[which], moved_sem.at[1, which])

    for which in range(moved):
        take(which).start()

    for layer in range(layers):
        fresh = BETA_TWO * statistics[layer] + (1.0 - BETA_TWO) * summed[layer].astype(jnp.float32)
        stats_new[layer] = fresh
        turned = dot(bases[layer], fresh, 0, 0)
        system[layer, :, channels : 2 * channels] = turned
        system[layer, :, 0:channels] = dot(turned, turned, 1, 1)

    head = moments(head_grad[...], head_first[...], head_second[...])
    head_first_new[...] = head[0]
    head_second_new[...] = head[1]
    head_new[...] = head_master[...] - RATE_HEAD * (head[2] + DECAY * head_master[...])
    vec = moments(vector_grad[...], vector_first[...], vector_second[...])
    vector_first_new[...] = vec[0]
    vector_second_new[...] = vec[1]
    row = lax.broadcasted_iota(jnp.int32, vectors.shape, 0)
    rates = jnp.where(row < bias_rows, RATE_BIAS, RATE_GAIN)
    vectors_new[...] = vectors[...] - rates * (vec[2] + DECAY * vectors[...])

    for which in range(moved):
        take(which).wait()
        give(which).start()
    eye = (
        lax.broadcasted_iota(jnp.int32, (block, block), 0)
        == lax.broadcasted_iota(jnp.int32, (block, block), 1)
    ).astype(jnp.float32)

    def outer(k, carry):
        here = pl.ds(pl.multiple_of(k * block, block), block)
        panels = [jnp.concatenate([system[layer, here, here], eye], 1) for layer in range(layers)]
        done = [[] for _ in range(layers)]
        for j in range(block // panel):
            blocks = [[p[8 * i : 8 * i + 8] for i in range(panel // 8)] for p in panels]
            tops = eliminate(blocks, panel * j, panel)
            for layer in range(layers):
                done[layer].append(tops[layer][:, block:])
                if j < block // panel - 1:
                    panels[layer] = panels[layer][panel:] - dot(
                        tops[layer][:, panel * (j + 1) : block], tops[layer], 0, 0
                    )
        for layer in range(layers):
            inverse = jnp.concatenate(done[layer], 0)
            pivot[layer] = dot(inverse, system[layer, here, :], 1, 0)
            system[layer, here, channels : 2 * channels] = pivot[layer, :, channels : 2 * channels]

        def inner(i, carry_in):
            below = pl.ds(pl.multiple_of(i * block, block), block)
            for layer in range(layers):
                system[layer, below, :] -= dot(pivot[layer, :, below], pivot[layer], 0, 0)
            return carry_in

        lax.fori_loop(k + 1, channels // block, inner, 0)
        return carry

    lax.fori_loop(0, channels // block, outer, 0)
    for layer in range(layers):
        bases_new[layer] = system[layer, :, channels : 2 * channels].T
    for which in range(moved):
        give(which).wait()


def update(arrays, summed, statistics, bases, head, vector, bias_rows):
    layers, channels, unused = statistics.shape
    dims = (layers, channels, bias_rows, 32, len(arrays))
    anywhere = pl.BlockSpec(memory_space=pl.ANY)
    vmem = pl.BlockSpec(memory_space=pltpu.VMEM)
    square = jax.ShapeDtypeStruct(statistics.shape, jnp.float32)
    head_shape = jax.ShapeDtypeStruct(head[0].shape, jnp.float32)
    vector_shape = jax.ShapeDtypeStruct(vector[0].shape, jnp.float32)
    return pl.pallas_call(
        partial(update_kernel, dims),
        out_shape=tuple(jax.ShapeDtypeStruct(array.shape, array.dtype) for array in arrays)
        + (square,) * 2 + (head_shape,) * 3 + (vector_shape,) * 3,
        in_specs=[anywhere] * len(arrays) + [vmem] * 11,
        out_specs=[anywhere] * len(arrays) + [vmem] * 8,
        scratch_shapes=[
            pltpu.VMEM((layers, channels, 2 * channels), jnp.float32),
            pltpu.VMEM((layers, LANES, 2 * channels), jnp.float32),
        ]
        + [pltpu.VMEM(array.shape, array.dtype) for array in arrays]
        + [pltpu.SemaphoreType.DMA((2, len(arrays)))],
        compiler_params=pltpu.CompilerParams(vmem_limit_bytes=VMEM_LIMIT),
        cost_estimate=pl.CostEstimate(
            flops=10**10, bytes_accessed=2 * 10**7, transcendentals=10**4
        ),
    )(*arrays, summed, statistics, bases, *head, *vector)


def local(
    features,
    valid_rows,
    conv_master,
    head_master,
    vectors,
    conv_first,
    conv_second,
    head_first,
    head_second,
    vec_first,
    vec_second,
    statistics,
    bases,
    cotangent,
):
    channels = features.shape[3]
    head_width = cotangent.shape[2]
    space_count = lax.axis_size("space")
    vectors, vec_first, vec_second, head_master, head_first, head_second = (
        array.reshape(-1, LANES)
        for array in (vectors, vec_first, vec_second, head_master, head_first, head_second)
    )
    conv_used, head_used, wide, hidden, last = gather_weights(
        conv_master, head_master, head_width, features[0], vectors, valid_rows, space_count
    )
    merged, features_grad, grads, owned_head, vector = run_block(
        conv_used,
        head_used,
        wide,
        hidden,
        last,
        vectors,
        cotangent,
        valid_rows,
        space_count,
    )
    summed_stats, grad_vec, conv_new = reduce_grads(
        grads, vector, bases, (conv_first, conv_second, conv_master), space_count
    )
    moved = (merged, features_grad, *conv_new)
    outs = update(
        moved,
        summed_stats,
        statistics,
        bases,
        (owned_head, head_first, head_second, head_master),
        (grad_vec, vec_first, vec_second, vectors),
        (3 * channels + head_width) // LANES,
    )
    merged, features_grad, *conv_new = outs[:5]
    stats_new, bases_new = outs[5:7]
    return (
        merged.reshape(cotangent.shape),
        features_grad.reshape(features.shape),
        *conv_new,
        *(out.reshape(-1) for out in outs[7:]),
        stats_new,
        bases_new,
    )


def solution(mesh):
    in_specs = (
        P("scale", "space", None, None),
        P(),
        P(None, "space", None),
        P(("scale", "space")),
        P(),
        P(None, "space", None),
        P(None, "space", None),
        P(("scale", "space")),
        P(("scale", "space")),
        P(),
        P(),
        P(),
        P(),
        P("space", None, None),
    )
    out_specs = (
        P("space", None, None),
        P("scale", "space", None, None),
        P(None, "space", None),
        P(None, "space", None),
        P(None, "space", None),
        P(("scale", "space")),
        P(("scale", "space")),
        P(("scale", "space")),
        P(),
        P(),
        P(),
        P(),
        P(),
    )
    return jax.shard_map(local, mesh=mesh, in_specs=in_specs, out_specs=out_specs, check_vma=False)
```

```python
from functools import partial

import jax
import jax.experimental.pallas as pl
import jax.experimental.pallas.tpu as pltpu
import jax.numpy as jnp
from jax import lax
from jax.sharding import PartitionSpec as P

NH = 7
HD = 256
STEP = 5


BETA_ONE = 0.9
BETA_TWO = 0.95
EPSILON = 1e-08
DECAY = 0.01
RATE_CONV = 0.04
RATE_HEAD = 0.08
RATE_BIAS = 0.5
RATE_GAIN = 20.0
VMEM_LIMIT = 60 * 2**20
GELU_SCALE = 0.7978845608028654
GELU_CUBE = 0.044715


MESH = pl.DeviceIdType.MESH
LANES = 128


def place():
    scale, space = lax.axis_index("scale"), lax.axis_index("space")
    across, core = scale // 2, lax.rem(scale, 2)
    deep, side = space // 2, lax.rem(space, 2)
    return (across, core, deep, side)


def at(across, core, deep, side):
    return (2 * across + core, 2 * deep + side)


def greet(peers):
    barrier = pltpu.get_barrier_semaphore()
    for peer in peers:
        pl.semaphore_signal(barrier, inc=1, device_id=peer, device_id_type=MESH)
    pl.semaphore_wait(barrier, len(peers))


def remote(source, target, send, receive, device):
    return pltpu.make_async_remote_copy(
        src_ref=source,
        dst_ref=target,
        send_sem=send,
        recv_sem=receive,
        device_id=device,
        device_id_type=MESH,
    )


def lanes(index, count=1):
    return pl.ds(pl.multiple_of(index * LANES, LANES), count * LANES)


def partners(deep_count):
    across, core, deep, side = place()
    peers = [
        at(across, 1 - core, deep, side),
        at(1 - across, core, deep, side),
        at(across, core, deep, 1 - side),
    ]
    peers += [
        at(across, core, lax.rem(deep + hop, deep_count), side) for hop in range(1, deep_count)
    ]
    return peers


TAPS = 3


def gelu_parts(value):
    inner = GELU_SCALE * (value + GELU_CUBE * value * value * value)
    return jnp.tanh(inner)


def gelu_value(value):
    return 0.5 * value * (1.0 + gelu_parts(value))


def gelu_slope(value):
    bend = gelu_parts(value)
    rise = GELU_SCALE * (1.0 + 3.0 * GELU_CUBE * value * value)
    return 0.5 * (1.0 + bend) + 0.5 * value * (1.0 - bend * bend) * rise


def mix(left, right, left_dim, right_dim):
    return lax.dot_general(
        left,
        right,
        (((left_dim,), (right_dim,)), ((), ())),
        preferred_element_type=jnp.float32,
    )


def row_weights(valid, rows):
    scale, space = lax.axis_index("scale"), lax.axis_index("space")
    scales = lax.axis_size("scale")
    masks, weights = [], []
    for row in range(rows):
        place_in = space * rows + row
        mask = jnp.where(place_in < valid[scale], 1.0, 0.0)
        count = jnp.float32(0.0)
        for other in range(scales):
            count += jnp.where(place_in < valid[other], 1.0, 0.0)
        masks.append(mask)
        weights.append(jnp.full((1, LANES), mask) / jnp.full((1, LANES), count))
    return (masks, [weight[:, :1] for weight in weights])


def vector_lanes(vectors, start, part):
    row = start // LANES + 2 * part
    return jnp.concatenate([vectors[pl.ds(row, 1), :], vectors[pl.ds(row + 1, 1), :]], 1)


def greet_edges(peers, space_count):
    barrier = pltpu.get_barrier_semaphore()
    scale, space = lax.axis_index("scale"), lax.axis_index("space")
    for peer in peers:
        pl.semaphore_signal(barrier, inc=1, device_id=peer, device_id_type=MESH)
    next_space = space - 1 + 2 * lax.rem(space, 2)
    has_next = jnp.logical_and(next_space >= 0, next_space < space_count)

    @pl.when(has_next)
    def greet_next():
        pl.semaphore_signal(barrier, inc=1, device_id=(scale, next_space), device_id_type=MESH)

    pl.semaphore_wait(barrier, len(peers) + has_next.astype(jnp.int32))


def edge_tools(dims, halo, send_sem, receive_sem):
    rows, width, channels, space_count = dims[1], dims[2], dims[3], dims[6]
    tile = 2 * LANES
    tiles = channels // tile
    scale, space = lax.axis_index("scale"), lax.axis_index("space")
    above, below = space > 0, space < space_count - 1
    low = jnp.bfloat16

    def up(which, source):
        return remote(
            source,
            halo.at[which, 1],
            send_sem.at[which, 0],
            receive_sem.at[which, 1],
            (scale, space - 1),
        )

    def down(which, source):
        return remote(
            source,
            halo.at[which, 0],
            send_sem.at[which, 1],
            receive_sem.at[which, 0],
            (scale, space + 1),
        )

    def edge(array, row):
        return array.at[pl.ds((row + 1) * width, width), pl.ds(channels, channels)]

    def send_edges(which, array):
        @pl.when(above)
        def go_up():
            up(which, edge(array, 0)).start()

        @pl.when(below)
        def go_down():
            down(which, edge(array, rows - 1)).start()

    column = lax.broadcasted_iota(jnp.int32, (width, 1), 0)

    def put(array, slot, lane, count, value):
        here = pl.ds(slot * width, width)
        left = jnp.where(column == 0, 0.0, pltpu.roll(value, 1, 0))
        right = jnp.where(column == width - 1, 0.0, pltpu.roll(value, width - 1, 0))
        for which, moved in enumerate((left, value, right)):
            start = pl.multiple_of(which * channels + lane, LANES)
            array[here, pl.ds(start, count)] = moved.astype(low)

    def take_edges(which, array):
        for side, present, slot in ((0, above, 0), (1, below, rows + 1)):

            @pl.when(present)
            def arrived():
                if side == 0:
                    up(which, edge(array, 0)).wait_send()
                    down(which, edge(array, 0)).wait_recv()
                else:
                    down(which, edge(array, 0)).wait_send()
                    up(which, edge(array, 0)).wait_recv()
                for part in range(tiles):
                    value = halo[which, side, :, part * tile : (part + 1) * tile]
                    put(array, slot, part * tile, tile, value.astype(jnp.float32))

            @pl.when(jnp.logical_not(present))
            def missing():
                array[pl.ds(slot * width, width), :] = jnp.zeros(
                    (width, TAPS * channels), low
                )

    return (send_edges, take_edges, put)


def gather_kernel(
    dims,
    master,
    head_master,
    features,
    vectors,
    valid,
    full,
    head_full,
    wide_out,
    hidden_out,
    last_out,
    own,
    head_own,
    weights,
    wide,
    hidden,
    last,
    halo,
    local_sem,
    sends,
    receives,
    head_sends,
    head_receives,
    load_sem,
    store_sem,
    edge_sends,
    edge_receives,
):
    layers, rows, width, channels, heads, depth, space_count = dims
    deep_count = space_count // 2
    across, core, deep, side = place()
    block = 2 * core + across
    low = jnp.bfloat16
    own[0] = master[0].astype(low)
    greet_edges(partners(deep_count), space_count)

    chunks = layers * deep_count

    def by_distance(index):
        left, right = deep, deep_count - 1 - deep
        short = jnp.minimum(left, right)
        both = (index + 1) // 2 * (2 * lax.rem(index, 2) - 1)
        one = (index - short) * jnp.where(left < right, 1, -1)
        return deep + jnp.where(index <= 2 * short, both, one)

    def split(chunk):
        rest = chunk - layers
        is_own = chunk < layers
        layer = jnp.where(is_own, chunk, rest // (deep_count - 1))
        hop = jnp.where(is_own, 0, 1 + lax.rem(rest + chunks, deep_count - 1))
        layer, hop = jnp.clip(layer, 0, layers - 1), jnp.clip(hop, 0, deep_count - 1)
        source = by_distance(hop)
        odd = jnp.where(is_own, 0, lax.rem(chunk, 2))
        return (layer, hop, source, odd)

    def first(layer, index):
        piece = own.at[layer, :, lanes(block)]
        target = full.at[layer, deep, side, :, lanes(block)]
        there = by_distance(index)
        to = at(across, core, there, side)
        return remote(piece, target, sends.at[0, layer, there], receives.at[0, layer, deep], to)

    def first_in(layer, index):
        source = by_distance(index)
        piece = full.at[layer, source, side, :, lanes(block)]
        return remote(
            piece,
            piece,
            sends.at[0, layer, source],
            receives.at[0, layer, source],
            at(across, core, source, side),
        )

    def second(chunk, incoming):
        layer, hop, source, odd = split(chunk)
        there_side = lax.rem(side + 1 - odd, 2)
        there_across = lax.rem(across + odd, 2)
        to = at(there_across, core, deep, there_side)
        if incoming:
            piece = full.at[layer, source, there_side, :, lanes(2 * core + there_across)]
        else:
            piece = full.at[layer, source, side, :, lanes(block)]
        return remote(piece, piece, sends.at[1, layer, hop], receives.at[1, layer, hop], to)

    def third(chunk, half, incoming):
        layer, hop, source, odd = split(chunk)
        there_side = lax.rem(side + odd, 2)
        there_across = lax.rem(across + 1 - odd, 2)
        to = at(there_across, core, deep, there_side)
        here = there_side if incoming else side
        lane = there_across if incoming else across
        piece_side = (1 - odd) * half + odd * here
        piece_lane = 2 * core + (1 - odd) * lane + odd * half
        piece = full.at[layer, source, piece_side, :, lanes(piece_lane)]
        return remote(
            piece, piece, sends.at[2 + half, layer, hop], receives.at[2 + half, layer, hop], to
        )

    def fourth(chunk, incoming):
        layer, hop, source, odd = split(chunk)
        column = 1 - core if incoming else core
        piece = full.at[layer, source, :, :, lanes(2 * column, 2)]
        to = at(across, 1 - core, deep, side)
        return remote(piece, piece, sends.at[4, layer, hop], receives.at[4, layer, hop], to)

    def own_fourth(layer, incoming):
        column = 1 - core if incoming else core
        piece = full.at[layer, deep, 1 - side, :, lanes(2 * column, 2)]
        to = at(across, 1 - core, deep, side)
        return remote(piece, piece, sends.at[4, layer, 0], receives.at[4, layer, 0], to)

    def local(layer):
        return pltpu.make_async_copy(
            own.at[layer], full.at[layer, deep, side], local_sem.at[layer]
        )

    def each(low, action):
        def step(hop, carry):
            action(hop)
            return carry

        lax.fori_loop(low, deep_count, step, 0)

    def head_local():
        return pltpu.make_async_copy(
            head_own, head_full.at[across, core, deep, side], local_sem.at[layers]
        )

    def head_first(hop):
        to = at(across, core, lax.rem(deep + hop, deep_count), side)
        target = head_full.at[across, core, deep, side]
        return remote(head_own, target, head_sends.at[hop], head_receives.at[hop], to)

    def head_first_in(hop):
        piece = head_full.at[across, core, lax.rem(deep - hop + deep_count, deep_count), side]
        to = at(across, core, deep, side)
        return remote(piece, piece, head_sends.at[hop], head_receives.at[hop], to)

    def head_next(which, incoming):
        if which == 0:
            to = at(across, core, deep, 1 - side)
            piece = head_full.at[across, core, :, 1 - side if incoming else side]
        elif which == 1:
            to = at(1 - across, core, deep, side)
            piece = head_full.at[1 - across if incoming else across, core]
        else:
            to = at(across, 1 - core, deep, side)
            piece = head_full.at[:, 1 - core if incoming else core]
        slot = deep_count + which
        return remote(piece, piece, head_sends.at[slot], head_receives.at[slot], to)

    def go_head(which):
        if which == 0:
            head_local().wait()
            each(1, lambda hop: head_first_in(hop).wait_recv())
        else:
            head_next(which - 1, True).wait_recv()
        if which < 3:
            head_next(which, False).start()

    send_edges, take_edges, put = edge_tools(dims, halo, edge_sends, edge_receives)
    tile = 2 * LANES
    tiles = channels // tile
    pixels = rows * width
    band = TAPS * channels
    masks, unused = row_weights(valid, rows)
    share = band * TAPS // space_count

    def loop(count, action):
        def body(index, carry):
            action(index)
            return carry

        lax.fori_loop(0, count, body, 0)

    def spot(index):
        return pl.multiple_of(index * tile, tile)

    def load(layer, owner):
        start = pl.multiple_of(owner * share, 8)
        return pltpu.make_async_copy(
            full.at[layer, owner // 2, lax.rem(owner, 2)],
            weights.at[layer % 2, pl.ds(start, share)],
            load_sem.at[layer % 2, owner],
        )

    def arrive(layer):
        own_fourth(layer, True).wait_recv()
        begin = layers + layer * (deep_count - 1)
        loop(deep_count - 1, lambda index: fourth(begin + index, True).wait_recv())
        loop(space_count, lambda owner: load(layer, owner).start())

    def store(which, layer):
        source, target = (
            (wide.at[layer], wide_out.at[layer]),
            (hidden.at[layer], hidden_out.at[layer]),
            (last, last_out),
        )[which]
        return pltpu.make_async_copy(source, target, store_sem.at[which, layer])

    def forward(layer):
        here = wide.at[layer]
        take_edges(layer, here)
        store(0, layer).start()
        loop(space_count, lambda owner: load(layer, owner).wait())

        def outer(part):
            lane = pl.ds(spot(part), tile)
            total = vector_lanes(vectors, layer * channels, part)
            for tap_row in range(TAPS):
                total += mix(
                    here[tap_row * width : tap_row * width + pixels, :],
                    weights[layer % 2, tap_row * band : (tap_row + 1) * band, lane],
                    1,
                    0,
                )
            hidden[layer, :, lane] = total
            for row in range(rows):
                span = slice(row * width, (row + 1) * width)
                value = gelu_value(hidden[layer, span, lane]) * masks[row]
                if layer < layers - 1:
                    put(wide.at[layer + 1], row + 1, spot(part), tile, value)
                else:
                    last[span, lane] = value.astype(low)

        loop(tiles, outer)
        store(1, layer).start()
        if layer < layers - 1:
            send_edges(layer + 1, wide.at[layer + 1])

    def go_second(chunk):
        layer, hop, source, odd = split(chunk)

        @pl.when(hop == 0)
        def own_rows():
            local(layer).wait()

        @pl.when(hop > 0)
        def other_rows():
            first_in(layer, hop).wait_recv()
            go_first(chunk - layers + z_ahead)

        second(chunk, False).start()

    def go_third(chunk):
        second(chunk, True).wait_recv()

        @pl.when(chunk < layers)
        def own_rows():
            third(chunk, 1 - side, False).start()

        @pl.when(chunk >= layers)
        def other_rows():
            third(chunk, 0, False).start()
            third(chunk, 1, False).start()

    def go_fourth(chunk):
        @pl.when(chunk < layers)
        def own_rows():
            third(chunk, 1 - side, True).wait_recv()
            own_fourth(chunk, False).start()

        @pl.when(chunk >= layers)
        def other_rows():
            third(chunk, 0, True).wait_recv()
            third(chunk, 1, True).wait_recv()
            fourth(chunk, False).start()

    def go_head_first():
        each(1, lambda hop: head_first(hop).start())

    def go_first(index):
        @pl.when(index < layers * (deep_count - 1))
        def more():
            first(index // (deep_count - 1), 1 + lax.rem(index, deep_count - 1)).start()

    z_ahead = 2
    for index in range(min(z_ahead, deep_count - 1)):
        go_first(index)
    local(0).start()
    go_second(0)
    for layer in range(1, layers):
        own[layer] = master[layer].astype(low)
        local(layer).start()
    head_rows, head_blocks = head_own.shape[0], heads * depth // LANES
    for lane in range(head_blocks):
        head_own[:, lane * LANES : (lane + 1) * LANES] = head_master[
            pl.ds(lane, head_rows, stride=head_blocks), :
        ].astype(low)
    head_local().start()
    for row in range(rows):
        for part in range(tiles):
            value = features[row * width : (row + 1) * width, part * tile : (part + 1) * tile]
            put(wide.at[0], row + 1, part * tile, tile, value.astype(jnp.float32))
    send_edges(0, wide.at[0])

    lag_third, lag_fourth = 2, 4
    others = deep_count - 1

    def last_of(layer):
        return layers + others * (layer + 1) - 1 + lag_fourth

    early = min(2, others)
    timed = [(layers + early, go_head_first)]
    timed += [(layers + others + 2 * which, go_head, which) for which in range(3)]
    for layer in range(layers - 1):
        timed += [(last_of(layer) + 1, arrive, layer), (last_of(layer) + 2, forward, layer)]

    def turn(now):
        for lag, action in ((0, go_second), (lag_third, go_third), (lag_fourth, go_fourth)):
            begin = max(lag, 1)

            @pl.when(jnp.logical_and(now >= begin, now < chunks + lag))
            def stage():
                action(now - lag)

        for moment, action, *which in timed:

            @pl.when(now == moment)
            def once():
                action(*which)

    loop(chunks + lag_fourth, turn)
    go_head(3)
    arrive(layers - 1)
    forward(layers - 1)
    store(2, 0).start()

    def finish(chunk):
        second(chunk, False).wait_send()

        @pl.when(chunk < layers)
        def own_rows():
            third(chunk, 1 - side, False).wait_send()
            own_fourth(chunk, False).wait_send()

        @pl.when(chunk >= layers)
        def other_rows():
            third(chunk, 0, False).wait_send()
            third(chunk, 1, False).wait_send()
            fourth(chunk, False).wait_send()

    loop(chunks, finish)
    each(1, lambda hop: head_first(hop).wait_send())
    for which in range(3):
        head_next(which, False).wait_send()

    for layer in range(layers):

        each(1, lambda hop: first(layer, hop).wait_send())
        store(0, layer).wait()
        store(1, layer).wait()
    store(2, 0).wait()


def gather_weights(master, head_master, head_width, features, vectors, valid, space_count):
    layers, share, channels = master.shape
    rows, width, unused = features.shape
    deep_count = space_count // 2
    pixels = rows * width
    dims = (layers, rows, width, channels, NH, HD, space_count)
    low, wide_float = jnp.bfloat16, jnp.float32
    anywhere = pl.BlockSpec(memory_space=pl.ANY)
    vmem = pl.BlockSpec(memory_space=pltpu.VMEM)
    head_own = (head_master.shape[0] * LANES // head_width, head_width)
    head_shape = (2, 2, deep_count, 2) + head_own
    wide_shape = (layers, (rows + 2) * width, TAPS * channels)
    full, head_full, wide, hidden, last = pl.pallas_call(
        partial(gather_kernel, dims),
        out_shape=(
            jax.ShapeDtypeStruct((layers, deep_count, 2, share, channels), low),
            jax.ShapeDtypeStruct(head_shape, low),
            jax.ShapeDtypeStruct(wide_shape, low),
            jax.ShapeDtypeStruct((layers, pixels, channels), wide_float),
            jax.ShapeDtypeStruct((pixels, channels), low),
        ),
        in_specs=[vmem] * 4 + [pl.BlockSpec(memory_space=pltpu.SMEM)],
        out_specs=[anywhere] * 5,
        scratch_shapes=[
            pltpu.VMEM(master.shape, low),
            pltpu.VMEM(head_own, low),
            pltpu.VMEM((2, space_count * share, channels), low),
            pltpu.VMEM(wide_shape, low),
            pltpu.VMEM((layers, pixels, channels), wide_float),
            pltpu.VMEM((pixels, channels), low),
            pltpu.VMEM((layers, 2, width, channels), low),
            pltpu.SemaphoreType.DMA((layers + 1,)),
            pltpu.SemaphoreType.DMA((5, layers, deep_count)),
            pltpu.SemaphoreType.DMA((5, layers, deep_count)),
            pltpu.SemaphoreType.DMA((deep_count + 3,)),
            pltpu.SemaphoreType.DMA((deep_count + 3,)),
            pltpu.SemaphoreType.DMA((2, space_count)),
            pltpu.SemaphoreType.DMA((3, layers)),
            pltpu.SemaphoreType.DMA((layers, 2)),
            pltpu.SemaphoreType.DMA((layers, 2)),
        ],
        compiler_params=pltpu.CompilerParams(
            collective_id=0, has_side_effects=True, vmem_limit_bytes=VMEM_LIMIT
        ),
    )(master, head_master, features.reshape(pixels, channels), vectors, valid)
    return (
        full.reshape(layers, space_count * share, channels),
        head_full.reshape(-1, head_width),
        wide,
        hidden,
        last,
    )


def reduce_kernel(
    layers,
    deep_count,
    grads,
    vector,
    bases,
    first_in,
    second_moment_in,
    master_in,
    total,
    stats,
    vector_total,
    first_out,
    second_out,
    master_out,
    mine,
    core_in,
    second_in,
    kept,
    third_in,
    last,
    last_in,
    acc,
    stat_own,
    stat_in,
    stat_deep,
    vector_out,
    vector_in,
    vector_deep,
    moment_one,
    moment_two,
    master,
    local_sem,
    sends,
    receives,
    stat_sends,
    stat_receives,
    deep_sends,
    deep_receives,
    vector_sends,
    vector_receives,
    state_loads,
    state_stores,
):
    across, core, deep, side = place()
    block = 2 * core + across
    steps = layers * deep_count

    def split(step):
        layer, hop = step // deep_count, lax.rem(step + 1, deep_count)
        target = lax.rem(deep + hop, deep_count)
        return (layer, hop, target, lax.rem(target, 2))

    def first(step):
        layer, hop, target, odd = split(step)
        return remote(
            grads.at[layer, target, :, :, lanes(2 * (1 - core), 2)],
            core_in.at[step],
            sends.at[0, step],
            receives.at[0, step],
            at(across, 1 - core, deep, side),
        )

    def load(step):
        layer, hop, target, odd = split(step)
        return pltpu.make_async_copy(
            grads.at[layer, target, :, :, lanes(2 * core, 2)], mine.at[step], local_sem.at[step]
        )

    def second(step, half):
        layer, hop, target, odd = split(step)
        piece_side = (1 - odd) * half + odd * (1 - side)
        piece_lane = (1 - odd) * (1 - across) + odd * half
        to = at(lax.rem(across + 1 - odd, 2), core, deep, lax.rem(side + odd, 2))
        return remote(
            mine.at[step, piece_side, :, lanes(piece_lane)],
            second_in.at[step, half],
            sends.at[1 + half, step],
            receives.at[1 + half, step],
            to,
        )

    def third(step):
        layer, hop, target, odd = split(step)
        keep = (1 - odd) * side + odd * across
        to = at(lax.rem(across + odd, 2), core, deep, lax.rem(side + 1 - odd, 2))
        return remote(
            kept.at[step, 1 - keep],
            third_in.at[step],
            sends.at[3, step],
            receives.at[3, step],
            to,
        )

    def fourth(step):
        layer, hop, target, odd = split(step)
        return remote(
            last.at[step],
            last_in.at[step],
            sends.at[4, step],
            receives.at[4, step],
            at(across, core, target, side),
        )

    def fifth(layer, incoming):
        lane = 2 * core + (1 - across if incoming else across)
        piece = total.at[layer, :, lanes(lane)]
        to = at(1 - across, core, deep, side)
        return remote(piece, piece, sends.at[5, layer], receives.at[5, layer], to)

    def sixth(layer, incoming):
        column = 1 - core if incoming else core
        piece = total.at[layer, :, lanes(2 * column, 2)]
        to = at(across, 1 - core, deep, side)
        return remote(piece, piece, sends.at[6, layer], receives.at[6, layer], to)

    def run(low, high, action):
        def body(step, carry):
            action(step)
            return carry

        lax.fori_loop(low, high, body, 0)

    half_block = LANES // 2

    def stat_side(layer, incoming):
        rows = pl.ds(pl.multiple_of((1 - side) * half_block, half_block), half_block)
        return remote(
            stat_own.at[layer, rows],
            stat_in.at[layer],
            stat_sends.at[0, layer],
            stat_receives.at[0, layer],
            at(across, core, deep, 1 - side),
        )

    def stat_along(layer, hop):
        return remote(
            stat_deep.at[layer, deep],
            stat_deep.at[layer, deep],
            deep_sends.at[layer, hop],
            deep_receives.at[layer, hop],
            at(across, core, lax.rem(deep + hop, deep_count), side),
        )

    def stat_along_in(layer, hop):
        source = lax.rem(deep - hop + deep_count, deep_count)
        return remote(
            stat_deep.at[layer, source],
            stat_deep.at[layer, source],
            deep_sends.at[layer, hop],
            deep_receives.at[layer, hop],
            at(across, core, deep, side),
        )

    def half_rows(which):
        return pl.ds(pl.multiple_of(which * half_block, half_block), half_block)

    def stat_spread(which, layer, incoming):
        if which < 3:
            other_side = side if which == 1 else 1 - side
            other_across = across if which == 0 else 1 - across
            to = at(other_across, core, deep, other_side)
            if incoming:
                piece = stats.at[layer, 2 * core + other_across, half_rows(other_side)]
            else:
                piece = stats.at[layer, block, half_rows(side)]
        else:
            to = at(across, 1 - core, deep, side)
            piece = stats.at[layer, pl.ds(2 * (1 - core if incoming else core), 2)]
        slot = 1 + which
        return remote(piece, piece, stat_sends.at[slot, layer], stat_receives.at[slot, layer], to)

    def vector_step(which):
        to = (
            at(across, 1 - core, deep, side),
            at(1 - across, core, deep, side),
            at(across, core, deep, 1 - side),
        )[which]
        return remote(
            vector_out.at[which],
            vector_in.at[which],
            vector_sends.at[which],
            vector_receives.at[which],
            to,
        )

    def vector_along(hop):
        return remote(
            vector_deep.at[deep],
            vector_deep.at[deep],
            vector_sends.at[2 + hop],
            vector_receives.at[2 + hop],
            at(across, core, lax.rem(deep + hop, deep_count), side),
        )

    def vector_along_in(hop):
        source = lax.rem(deep - hop + deep_count, deep_count)
        return remote(
            vector_deep.at[source],
            vector_deep.at[source],
            vector_sends.at[2 + hop],
            vector_receives.at[2 + hop],
            at(across, core, deep, side),
        )

    def go_first(step):
        load(step).start()
        first(step).start()

    ahead = min(3, steps)
    piece_rows = 144 if total.shape[1] % 144 == 0 else total.shape[1]
    states = (
        (first_in, moment_one, first_out),
        (second_moment_in, moment_two, second_out),
        (master_in, master, master_out),
    )

    def load_state(which, layer):
        source, target, unused = states[which]
        return pltpu.make_async_copy(
            source.at[layer], target.at[layer], state_loads.at[which, layer]
        )

    def store_state(which, layer):
        unused, source, target = states[which]
        return pltpu.make_async_copy(
            source.at[layer], target.at[layer], state_stores.at[which, layer]
        )

    greet(partners(deep_count) + [at(1 - across, core, deep, 1 - side)])
    run(0, ahead, go_first)
    for layer in range(layers):
        for which in range(3):
            load_state(which, layer).start()

    def wide(left, right):
        return left.astype(jnp.float32) + right.astype(jnp.float32)

    def go_second(step):
        @pl.when(step + ahead < steps)
        def start_next():
            go_first(step + ahead)

        load(step).wait()
        first(step).wait_recv()
        mine[step] = wide(mine[step], core_in[step]).astype(jnp.bfloat16)
        second(step, 0).start()
        second(step, 1).start()

    def go_third(step):
        layer, hop, target, odd = split(step)
        for half in range(2):
            second(step, half).wait_recv()
            keep_side = (1 - odd) * half + odd * side
            keep_lane = (1 - odd) * across + odd * half
            kept[step, half] = wide(
                mine[step, keep_side, :, lanes(keep_lane)], second_in[step, half]
            ).astype(jnp.bfloat16)
        third(step).start()

    def go_fourth(step):
        layer, hop, target, odd = split(step)
        third(step).wait_recv()
        keep = (1 - odd) * side + odd * across
        last[step] = wide(kept[step, keep], third_in[step]).astype(jnp.bfloat16)

        @pl.when(hop > 0)
        def unused():
            fourth(step).start()

    def close(layer):
        acc[...] = last[layer * deep_count + deep_count - 1].astype(jnp.float32)

        def add(hop):
            step = layer * deep_count + hop - 1
            fourth(step).wait_recv()
            acc[...] += last_in[step].astype(jnp.float32)

        run(1, deep_count, add)
        total[layer, :, lanes(block)] = acc[...].astype(jnp.bfloat16)
        fifth(layer, False).start()

    def spread(layer):
        fifth(layer, True).wait_recv()
        sixth(layer, False).start()

    def measure(layer):
        sixth(layer, True).wait_recv()
        own_lanes = total[layer, :, lanes(block)]
        stat_own[layer] = lax.dot_general(
            own_lanes,
            total[layer],
            (((0,), (0,)), ((), ())),
            preferred_element_type=jnp.float32,
        ).astype(jnp.bfloat16)
        stat_side(layer, False).start()

    def pair(layer):
        stat_side(layer, True).wait_recv()
        stat_deep[layer, deep] = wide(
            stat_own[layer, half_rows(side)], stat_in[layer]
        ).astype(jnp.bfloat16)
        run(1, deep_count, lambda hop: stat_along(layer, hop).start())

    def settle(layer):
        run(1, deep_count, lambda hop: stat_along_in(layer, hop).wait_recv())
        whole = stat_deep[layer, 0].astype(jnp.float32)
        for source in range(1, deep_count):
            whole += stat_deep[layer, source].astype(jnp.float32)
        stats[layer, block, half_rows(side)] = whole.astype(jnp.bfloat16)
        for which in range(3):
            stat_spread(which, layer, False).start()

    def share_core(layer):
        for which in range(3):
            stat_spread(which, layer, True).wait_recv()
        stat_spread(3, layer, False).start()

    def refresh(layer):
        for which in range(3):
            load_state(which, layer).wait()
        high, rest = halves(bases[layer])

        def one_piece(index):
            here = pl.ds(pl.multiple_of(index * piece_rows, piece_rows), piece_rows)
            given = total[layer, here, :]
            rotated = mix(given, high, 1, 0) + mix(given, rest, 1, 0)
            first_new, second_new, direction = moments(
                rotated, moment_one[layer, here, :], moment_two[layer, here, :]
            )
            moment_one[layer, here, :] = first_new
            moment_two[layer, here, :] = second_new
            up, down = halves(direction)
            back = mix(up, high, 1, 1) + (mix(up, rest, 1, 1) + mix(down, high, 1, 1))
            old = master[layer, here, :]
            master[layer, here, :] = old - RATE_CONV * (back + DECAY * old)

        run(0, total.shape[1] // piece_rows, one_piece)
        for which in range(3):
            store_state(which, layer).start()

    def finish(layer):
        stat_spread(3, layer, True).wait_recv()
        fifth(layer, False).wait_send()
        sixth(layer, False).wait_send()
        stat_side(layer, False).wait_send()
        run(1, deep_count, lambda hop: stat_along(layer, hop).wait_send())
        for which in range(4):
            stat_spread(which, layer, False).wait_send()
        for which in range(3):
            store_state(which, layer).wait()

    def vector_next(which):
        vector_step(which).wait_recv()
        summed = vector_out[which] + vector_in[which]
        if which < 2:
            vector_out[which + 1] = summed
            vector_step(which + 1).start()
        else:
            vector_deep[deep] = summed
            run(1, deep_count, lambda hop: vector_along(hop).start())

    chunk_work = ((0, go_second), (2, go_third), (3, go_fourth))
    layer_work = (
        (4, close),
        (5, spread),
        (6, measure),
        (7, pair),
        (8, refresh),
        (9, settle),
        (10, share_core),
        (11, finish),
    )
    vector_out[0] = vector[...]
    vector_step(0).start()

    def turn(now):
        for lag, action in chunk_work:

            @pl.when(jnp.logical_and(now >= lag, now < steps + lag))
            def chunk():
                action(now - lag)

        for which in range(3):

            @pl.when(now == 2 * which + 1)
            def exchange():
                vector_next(which)

        for lag, action in layer_work:
            past = now - lag - (deep_count - 1)

            @pl.when(
                jnp.logical_and(
                    jnp.logical_and(past >= 0, past < steps), lax.rem(past, deep_count) == 0
                )
            )
            def whole_layer():
                action(past // deep_count)

    run(0, steps + layer_work[-1][0], turn)

    run(1, deep_count, lambda hop: vector_along_in(hop).wait_recv())
    summed = vector_deep[0]
    for source in range(1, deep_count):
        summed += vector_deep[source]
    vector_total[...] = summed
    for which in range(3):
        vector_step(which).wait_send()
    run(1, deep_count, lambda hop: vector_along(hop).wait_send())

    def drain(step):
        layer, hop, target, odd = split(step)
        first(step).wait_send()
        second(step, 0).wait_send()
        second(step, 1).wait_send()
        third(step).wait_send()

        @pl.when(hop > 0)
        def unused():
            fourth(step).wait_send()

    run(0, steps, drain)


def reduce_grads(grads, vector, bases, conv, space_count):
    layers, all_rows, columns = grads.shape
    deep_count, rows = space_count // 2, all_rows // space_count
    steps = layers * deep_count
    low = jnp.bfloat16
    blocks = columns // LANES
    vmem = pl.BlockSpec(memory_space=pltpu.VMEM)
    tall = jax.ShapeDtypeStruct((layers, rows, columns), jnp.float32)
    anywhere = pl.BlockSpec(memory_space=pl.ANY)
    total, stats, vector_total, *conv_new = pl.pallas_call(
        partial(reduce_kernel, layers, deep_count),
        out_shape=(
            jax.ShapeDtypeStruct((layers, rows, columns), low),
            jax.ShapeDtypeStruct((layers, blocks, LANES, columns), low),
            jax.ShapeDtypeStruct(vector.shape, jnp.float32),
            tall,
            tall,
            tall,
        ),
        in_specs=[anywhere, vmem, vmem] + [anywhere] * 3,
        out_specs=[vmem] * 3 + [anywhere] * 3,
        scratch_shapes=[
            pltpu.VMEM((steps, 2, rows, 2 * LANES), low),
            pltpu.VMEM((steps, 2, rows, 2 * LANES), low),
            pltpu.VMEM((steps, 2, rows, LANES), low),
            pltpu.VMEM((steps, 2, rows, LANES), low),
            pltpu.VMEM((steps, rows, LANES), low),
            pltpu.VMEM((steps, rows, LANES), low),
            pltpu.VMEM((steps, rows, LANES), low),
            pltpu.VMEM((rows, LANES), jnp.float32),
            pltpu.VMEM((layers, LANES, columns), low),
            pltpu.VMEM((layers, LANES // 2, columns), low),
            pltpu.VMEM((layers, deep_count, LANES // 2, columns), low),
            pltpu.VMEM((3,) + vector.shape, jnp.float32),
            pltpu.VMEM((3,) + vector.shape, jnp.float32),
            pltpu.VMEM((deep_count,) + vector.shape, jnp.float32),
            pltpu.VMEM(tall.shape, jnp.float32),
            pltpu.VMEM(tall.shape, jnp.float32),
            pltpu.VMEM(tall.shape, jnp.float32),
            pltpu.SemaphoreType.DMA((steps,)),
            pltpu.SemaphoreType.DMA((7, steps)),
            pltpu.SemaphoreType.DMA((7, steps)),
            pltpu.SemaphoreType.DMA((5, layers)),
            pltpu.SemaphoreType.DMA((5, layers)),
            pltpu.SemaphoreType.DMA((layers, deep_count)),
            pltpu.SemaphoreType.DMA((layers, deep_count)),
            pltpu.SemaphoreType.DMA((2 + deep_count,)),
            pltpu.SemaphoreType.DMA((2 + deep_count,)),
            pltpu.SemaphoreType.DMA((3, layers)),
            pltpu.SemaphoreType.DMA((3, layers)),
        ],
        compiler_params=pltpu.CompilerParams(
            collective_id=1, has_side_effects=True, vmem_limit_bytes=VMEM_LIMIT
        ),
    )(grads.reshape(layers, deep_count, 2, rows, columns), vector, bases, *conv)
    return (stats.reshape(layers, columns, columns), vector_total, conv_new)


def work_kernel(
    dims,
    weights_in,
    head_in,
    wide_in,
    hidden_in,
    last_in,
    vectors,
    cotangent_in,
    valid,
    merged,
    features_grad,
    grads_out,
    head_grad,
    vector,
    weights,
    head,
    cotangent,
    wide,
    hidden,
    last,
    last_turned,
    d_wide,
    d_active,
    grads,
    halo,
    term,
    term_in,
    load_sem,
    store_sem,
    send_sem,
    receive_sem,
    term_sends,
    term_receives,
    *head_refs,
):
    layers, rows, width, channels, heads, depth, space_count = dims
    deep_count = space_count // 2
    across, core, deep, side = place()
    spread_head = len(head_refs) > 0
    if spread_head:
        head_parts, core_in, across_in, side_in, deep_in, head_sends, head_receives = head_refs
        head_rows = head_parts.shape[4]
    tile = 2 * LANES
    tiles = channels // tile
    low = jnp.bfloat16

    loads = ((last_in, last), (head_in, head), (cotangent_in, cotangent))
    for layer in reversed(range(layers)):
        loads += (
            (hidden_in.at[layer], hidden.at[layer]),
            (wide_in.at[layer], wide.at[layer]),
            (weights_in.at[layer], weights.at[layer]),
        )

    def load(which):
        source, target = loads[which]
        return pltpu.make_async_copy(source, target, load_sem.at[which])

    for which in range(len(loads)):
        load(which).start()

    others = [
        at(across, 1 - core, deep, side),
        at(1 - across, core, deep, side),
        at(across, core, deep, 1 - side),
    ]
    if spread_head:
        others += [
            at(across, core, lax.rem(deep + hop, deep_count), side) for hop in range(1, deep_count)
        ]
    greet_edges(others, space_count)

    def term_lanes(index, which):
        return pl.ds(pl.multiple_of(index * depth + which * LANES, LANES), LANES)

    def term_step(which, index, incoming=False):
        if which == 0:
            source, target, to = term.at[:, term_lanes(index, 1 - core)], term_in.at[0, index], others[0]
        elif which == 1:
            source, target, to = term.at[:, term_lanes(index, core)], term_in.at[1, index], others[1]
        else:
            source = merged.at[:, term_lanes(index, 1 - core if incoming else core)]
            target, to = source, others[0]
        return remote(
            source, target, term_sends.at[which, index], term_receives.at[which, index], to
        )

    def term_pair(index):
        term_step(0, index).wait_recv()
        lane = term_lanes(index, core)
        both = term[:, lane].astype(jnp.float32) + term_in[0, index].astype(jnp.float32)
        term[:, lane] = both.astype(low)
        term_step(1, index).start()

    def term_total(index):
        term_step(1, index).wait_recv()
        lane = term_lanes(index, core)
        both = term[:, lane].astype(jnp.float32) + term_in[1, index].astype(jnp.float32)
        merged[:, lane] = both.astype(low)
        term_step(2, index).start()

    def term_end(index):
        term_step(2, index, True).wait_recv()
        for which in range(3):
            term_step(which, index).wait_send()

    def head_step(which):
        if which == 0:
            source, target, to = head_parts.at[:, 1 - core], core_in, others[0]
        elif which == 1:
            source = head_parts.at[pl.ds(0, 2), core, pl.ds(0, deep_count), 1 - side]
            target, to = side_in, others[2]
        else:
            source = head_parts.at[1 - across, core, pl.ds(0, deep_count), side]
            target, to = across_in, others[1]
        return remote(source, target, head_sends.at[which], head_receives.at[which], to)

    def head_along(hop):
        target = lax.rem(deep + hop, deep_count)
        return remote(
            head_parts.at[across, core, target, side],
            deep_in.at[hop],
            head_sends.at[2 + hop],
            head_receives.at[2 + hop],
            at(across, core, target, side),
        )

    def head_next(which):
        if not spread_head:
            return
        head_step(which).wait_recv()
        if which == 0:
            for part in range(2):
                both = head_parts[part, core].astype(jnp.float32) + core_in[part].astype(jnp.float32)
                head_parts[part, core] = both.astype(low)
            head_step(1).start()
        elif which == 1:
            for part in range(2):
                both = head_parts[part, core, pl.ds(0, deep_count), side].astype(jnp.float32)
                both += side_in[part].astype(jnp.float32)
                head_parts[part, core, pl.ds(0, deep_count), side] = both.astype(low)
            head_step(2).start()
        else:
            both = head_parts[across, core, pl.ds(0, deep_count), side].astype(jnp.float32)
            both += across_in[...].astype(jnp.float32)
            head_parts[across, core, pl.ds(0, deep_count), side] = both.astype(low)
            for hop in range(1, deep_count):
                head_along(hop).start()

    def head_end():
        if not spread_head:
            return
        whole = head_parts[across, core, deep, side].astype(jnp.float32)
        for hop in range(1, deep_count):
            head_along(hop).wait_recv()
            whole += deep_in[hop].astype(jnp.float32)
        blocks = heads * depth // LANES
        for lane in range(blocks):
            head_grad[pl.ds(lane, head_rows, stride=blocks), :] = whole[
                :, lane * LANES : (lane + 1) * LANES
            ]
        for which in range(3):
            head_step(which).wait_send()
        for hop in range(1, deep_count):
            head_along(hop).wait_send()

    send_edges, take_edges, put = edge_tools(dims, halo, send_sem, receive_sem)

    def loop(count, action):
        def body(index, carry):
            action(index)
            return carry

        lax.fori_loop(0, count, body, 0)

    def spot(index):
        return pl.multiple_of(index * tile, tile)

    masks, weights_row = row_weights(valid, rows)

    def put_vector(start, part, value):
        row = start // LANES + 2 * part
        vector[pl.ds(row, 1), :] = value[:, :LANES]
        vector[pl.ds(row + 1, 1), :] = value[:, LANES:]

    pixels = rows * width
    for which in range(3):
        load(which).wait()
    last_turned[...] = last[...].astype(jnp.float32).T.astype(low)
    d_active[...] = jnp.zeros_like(d_active)

    def one_head(index):
        lane = pl.ds(pl.multiple_of(index * depth, depth), depth)
        projected = mix(last[...], head[:, lane], 1, 0)
        projected += vector_lanes(vectors, layers * channels, index)
        gain = vector_lanes(vectors, layers * channels + heads * depth, index)
        gain_total = jnp.zeros((1, depth), jnp.float32)
        bias_total = jnp.zeros((1, depth), jnp.float32)
        rounded = []
        for row in range(rows):
            span = slice(row * width, (row + 1) * width)
            weight = weights_row[row]
            value = projected[span]
            inverse = lax.rsqrt(jnp.sum(value * value, -1, keepdims=True) + 1e-06)
            normed = value * inverse
            scaled = gain * weight
            term[span, lane] = (normed * scaled).astype(low)
            given = cotangent[span, lane].astype(jnp.float32)
            gain_total += jnp.sum(normed * given, 0, keepdims=True) * weight
            d_normed = given * scaled
            along = jnp.sum(normed * d_normed, -1, keepdims=True)
            d_low = (inverse * (d_normed - normed * along)).astype(low)
            bias_total += jnp.sum(d_low.astype(jnp.float32), 0, keepdims=True)
            rounded.append(d_low)
        term_step(0, index).start()
        put_vector(layers * channels + heads * depth, index, gain_total)
        put_vector(layers * channels, index, bias_total)
        d_low = jnp.concatenate(rounded, 0)
        grad = mix(last_turned[...], d_low, 1, 0)
        if spread_head:
            split = grad.reshape(2, 2, deep_count, 2, head_rows, depth)
            head_parts[:, :, :, :, :, lane] = split.astype(low)
        else:
            head_grad[:, lane] = grad.astype(low)
        d_active[...] += mix(d_low, head[:, lane], 1, 1)

        @pl.when(index > 0)
        def earlier():
            term_pair(index - 1)

    loop(heads, one_head)
    if spread_head:
        head_step(0).start()
    term_pair(heads - 1)

    def store(layer):
        slot = layer % 2
        return pltpu.make_async_copy(grads.at[slot], grads_out.at[layer], store_sem.at[slot])

    for layer in reversed(range(layers)):
        which = layers - 1 - layer
        for part in range(3):
            load(3 + 3 * which + part).wait()

        def enter(part):
            lane = pl.ds(spot(part), tile)
            total = jnp.zeros((1, tile), jnp.float32)
            for row in range(rows):
                span = slice(row * width, (row + 1) * width)
                slope = gelu_slope(hidden[layer, span, lane])
                value = slope * (masks[row] * d_active[span, lane])
                value = value.astype(low).astype(jnp.float32)
                total += jnp.sum(value, 0, keepdims=True)
                put(d_wide, row + 1, spot(part), tile, value)
            put_vector(layer * channels, part, total)

        loop(tiles, enter)
        send_edges(which, d_wide)
        if layer + 2 < layers:
            store(layer + 2).wait()

        def one_tap(tap):
            tap_row, tap_column = tap // TAPS, lax.rem(tap, TAPS)
            window = wide[
                layer,
                pl.ds(pl.multiple_of(tap_row * width, width), pixels),
                pl.ds(pl.multiple_of(tap_column * channels, channels), channels),
            ]
            d_hidden = d_wide[width : width + pixels, channels : 2 * channels]
            grads[layer % 2, pl.ds(pl.multiple_of(tap * channels, channels), channels), :] = mix(
                window, d_hidden, 0, 0
            ).astype(low)

        loop(TAPS * TAPS, one_tap)
        store(layer).start()
        head_next(layers - 1 - layer)
        if layer == 0:
            loop(heads, term_total)
        take_edges(which, d_wide)

        def back(part):
            total = jnp.zeros((pixels, tile), jnp.float32)
            for tap_row in range(TAPS):
                for tap_column in range(TAPS):
                    window = d_wide[
                        (2 - tap_row) * width : (2 - tap_row) * width + pixels,
                        (2 - tap_column) * channels : (3 - tap_column) * channels,
                    ]
                    first = (TAPS * tap_row + tap_column) * channels
                    total += mix(
                        window, weights[layer, pl.ds(first + spot(part), tile), :], 1, 1
                    )
            d_active[:, pl.ds(spot(part), tile)] = total

        loop(tiles, back)

    features_grad[...] = d_active[...].astype(low)
    head_end()
    loop(heads, term_end)
    for layer in range(min(layers, 2)):
        store(layer).wait()


def run_block(
    weights, head, wide, hidden, last, vectors, cotangent, valid, space_count
):
    rows, width, unused = cotangent.shape
    layers, unused, channels = weights.shape
    head_width = head.shape[1]
    pixels = rows * width
    deep_count = space_count // 2
    head_rows = channels // (4 * space_count)
    spread_head = head_rows % 16 == 0
    low, full = jnp.bfloat16, jnp.float32
    dims = (layers, rows, width, channels, NH, HD, space_count)
    vmem = pl.BlockSpec(memory_space=pltpu.VMEM)
    anywhere = pl.BlockSpec(memory_space=pl.ANY)
    head_scratch = []
    head_out = jax.ShapeDtypeStruct((channels, head_width), low)
    if spread_head:
        head_out = jax.ShapeDtypeStruct((head_rows * head_width // LANES, LANES), full)
        head_scratch = [
            pltpu.VMEM((2, 2, deep_count, 2, head_rows, head_width), low),
            pltpu.VMEM((2, deep_count, 2, head_rows, head_width), low),
            pltpu.VMEM((deep_count, head_rows, head_width), low),
            pltpu.VMEM((2, deep_count, head_rows, head_width), low),
            pltpu.VMEM((deep_count, head_rows, head_width), low),
            pltpu.SemaphoreType.DMA((2 + deep_count,)),
            pltpu.SemaphoreType.DMA((2 + deep_count,)),
        ]
    outs = pl.pallas_call(
        partial(work_kernel, dims),
        out_shape=(
            jax.ShapeDtypeStruct((pixels, head_width), low),
            jax.ShapeDtypeStruct((pixels, channels), low),
            jax.ShapeDtypeStruct(weights.shape, low),
            head_out,
            jax.ShapeDtypeStruct(vectors.shape, full),
        ),
        in_specs=[
            anywhere,
            anywhere,
            anywhere,
            anywhere,
            anywhere,
            vmem,
            anywhere,
            pl.BlockSpec(memory_space=pltpu.SMEM),
        ],
        out_specs=[vmem, vmem, anywhere, vmem, vmem],
        scratch_shapes=[
            pltpu.VMEM(weights.shape, low),
            pltpu.VMEM(head.shape, low),
            pltpu.VMEM((pixels, head_width), low),
            pltpu.VMEM((layers, (rows + 2) * width, TAPS * channels), low),
            pltpu.VMEM((layers, pixels, channels), full),
            pltpu.VMEM((pixels, channels), low),
            pltpu.VMEM((channels, pixels), low),
            pltpu.VMEM(((rows + 2) * width, TAPS * channels), low),
            pltpu.VMEM((pixels, channels), full),
            pltpu.VMEM((2,) + weights.shape[1:], low),
            pltpu.VMEM((layers, 2, width, channels), low),
            pltpu.VMEM((pixels, head_width), low),
            pltpu.VMEM((2, NH, pixels, LANES), low),
            pltpu.SemaphoreType.DMA((3 * layers + 3,)),
            pltpu.SemaphoreType.DMA((2,)),
            pltpu.SemaphoreType.DMA((layers, 2)),
            pltpu.SemaphoreType.DMA((layers, 2)),
            pltpu.SemaphoreType.DMA((3, NH)),
            pltpu.SemaphoreType.DMA((3, NH)),
        ]
        + head_scratch,
        compiler_params=pltpu.CompilerParams(
            collective_id=2, has_side_effects=True, vmem_limit_bytes=VMEM_LIMIT
        ),
    )(
        weights,
        head,
        wide,
        hidden,
        last,
        vectors,
        cotangent.reshape(pixels, head_width),
        valid,
    )
    merged, features_grad, grads, head_grad, vector = outs
    if not spread_head:
        head_grad = lax.psum_scatter(
            head_grad.astype(full).reshape(-1), ("scale", "space"), scatter_dimension=0, tiled=True
        ).reshape(-1, LANES)
    return (merged, features_grad, grads, head_grad, vector)


def halves(value):
    high = value.astype(jnp.bfloat16)
    return (high, (value - high.astype(jnp.float32)).astype(jnp.bfloat16))


def dot(left, right, left_dim, right_dim):
    left_high, left_low = halves(left)
    right_high, right_low = halves(right)
    rest = mix(left_high, right_low, left_dim, right_dim) + mix(left_low, right_high, left_dim, right_dim)
    return mix(left_high, right_high, left_dim, right_dim) + rest


def quick(x):
    return pl.reciprocal(x,approx=True)
def eliminate(blocks, off, size, m=8):
    nl=len(blocks); nb=size//8; W=blocks[0][0].shape[1]
    sub=lax.broadcasted_iota(jnp.int32,(8,128),0)
    for k0 in range(0,size,m):
        b0=k0//8; s0=k0%8
        for l in range(nl):
            bl=blocks[l]
            top=bl[b0]
            def colb(b,j):
                return jnp.broadcast_to(bl[b][:,off+k0+j:off+k0+j+1],(8,128))
            c0=[colb(b0,j) for j in range(m)]
            a=[[None]*m for _ in range(m)]
            for j in range(m):
                for i in range(j,m):
                    a[i][j]=jnp.broadcast_to(c0[j][s0+i:s0+i+1,:],(8,128))
            inv=[]; low=[[None]*m for _ in range(m)]
            for k in range(m):
                r=quick(a[k][k]); inv.append(r)
                for i in range(k+1,m):
                    low[i][k]=a[i][k]*r
                for j in range(k+1,m):
                    for i in range(j,m):
                        a[i][j]=a[i][j]-low[i][k]*a[j][k]
            wid=lambda v: jnp.concatenate([v]*(W//128),1)
            rows=[jnp.broadcast_to(top[s0+i:s0+i+1,:],(8,W)) for i in range(m)]
            for i in range(m):
                for k in range(i):
                    rows[i]=rows[i]-wid(low[i][k])*rows[k]
            for b in range(b0,nb):
                if b==b0 and s0+m==8 and m==1: continue
                cs=list(c0) if b==b0 else [colb(b,j) for j in range(m)]
                for j in range(m):
                    for k in range(j):
                        cs[j]=cs[j]-low[j][k]*cs[k]
                acc=bl[b]
                for k in range(m):
                    w=cs[k]*inv[k]
                    if b==b0: w=jnp.where(sub>s0+k,w,0.0)
                    acc=acc-wid(w)*rows[k]
                bl[b]=acc
    out=[]
    lane=lax.broadcasted_iota(jnp.int32,(8,W),1)
    row8=lax.broadcasted_iota(jnp.int32,(8,W),0)
    for l in range(nl):
        res=[]
        for b in range(nb):
            v=blocks[l][b]
            d=jnp.sum(jnp.where(lane==row8+(off+8*b),v,0.0),1,keepdims=True)
            res.append(v*lax.rsqrt(d))
        out.append(jnp.concatenate(res,0))
    return out


def moments(grads, first, second):
    first_new = BETA_ONE * first + (1.0 - BETA_ONE) * grads
    second_new = BETA_TWO * second + (1.0 - BETA_TWO) * grads * grads
    direction = (
        first_new
        * (1.0 / (1.0 - BETA_ONE**STEP))
        / (jnp.sqrt(second_new * (1.0 / (1.0 - BETA_TWO**STEP))) + EPSILON)
    )
    return (first_new, second_new, direction)


def update_kernel(
    dims,
    *refs,
):
    moved = dims[4]
    inputs, outputs = refs[: moved + 11], refs[moved + 11 : -1 - moved]
    held = refs[-1 - moved : -1]
    update_body(
        dims, inputs[:moved], outputs[:moved], held, refs[-1], *inputs[moved:], *outputs[moved:]
    )


def update_body(
    dims,
    moved_in,
    moved_out,
    held,
    moved_sem,
    summed,
    statistics,
    bases,
    head_grad,
    head_first,
    head_second,
    head_master,
    vector_grad,
    vector_first,
    vector_second,
    vectors,
    stats_new,
    bases_new,
    head_first_new,
    head_second_new,
    head_new,
    vector_first_new,
    vector_second_new,
    vectors_new,
    system,
    pivot_high,
    pivot_rest,
):
    layers, channels, bias_rows, panel, moved = dims
    block = LANES

    def take(which):
        return pltpu.make_async_copy(moved_in[which], held[which], moved_sem.at[0, which])

    def give(which):
        return pltpu.make_async_copy(held[which], moved_out[which], moved_sem.at[1, which])

    for which in range(moved):
        take(which).start()

    for layer in range(layers):
        fresh = BETA_TWO * statistics[layer] + (1.0 - BETA_TWO) * summed[layer].astype(jnp.float32)
        stats_new[layer] = fresh
        turned = dot(bases[layer], fresh, 0, 0)
        system[layer, :, channels : 2 * channels] = turned
        system[layer, :, 0:channels] = dot(turned, turned, 1, 1)

    head = moments(head_grad[...], head_first[...], head_second[...])
    head_first_new[...] = head[0]
    head_second_new[...] = head[1]
    head_new[...] = head_master[...] - RATE_HEAD * (head[2] + DECAY * head_master[...])
    vec = moments(vector_grad[...], vector_first[...], vector_second[...])
    vector_first_new[...] = vec[0]
    vector_second_new[...] = vec[1]
    row = lax.broadcasted_iota(jnp.int32, vectors.shape, 0)
    rates = jnp.where(row < bias_rows, RATE_BIAS, RATE_GAIN)
    vectors_new[...] = vectors[...] - rates * (vec[2] + DECAY * vectors[...])

    for which in range(moved):
        take(which).wait()
        give(which).start()
    eye = (
        lax.broadcasted_iota(jnp.int32, (block, block), 0)
        == lax.broadcasted_iota(jnp.int32, (block, block), 1)
    ).astype(jnp.float32)

    def outer(k, carry):
        here = pl.ds(pl.multiple_of(k * block, block), block)
        panels = [jnp.concatenate([system[layer, here, here], eye], 1) for layer in range(layers)]
        done = [[] for _ in range(layers)]
        for j in range(block // panel):
            blocks = [[p[8 * i : 8 * i + 8] for i in range(panel // 8)] for p in panels]
            tops = eliminate(blocks, panel * j, panel)
            for layer in range(layers):
                done[layer].append(tops[layer][:, block:])
                if j < block // panel - 1:
                    panels[layer] = panels[layer][panel:] - dot(
                        tops[layer][:, panel * (j + 1) : block], tops[layer], 0, 0
                    )
        half = channels // 2
        spans = (slice(0, half), slice(half, channels), slice(channels, 2 * channels))
        after = (k + 1) * block
        split_inverse = [halves(jnp.concatenate(parts, 0)) for parts in done]

        def eliminated(span):
            for layer in range(layers):
                high, rest = split_inverse[layer]
                right_high, right_rest = halves(system[layer, here, span])
                value = mix(high, right_high, 1, 0) + (
                    mix(high, right_rest, 1, 0) + mix(rest, right_high, 1, 0)
                )
                pivot_high[layer, :, span], pivot_rest[layer, :, span] = halves(value)
                if span is spans[2]:
                    system[layer, here, span] = value

        eliminated(spans[2])

        @pl.when(after < channels)
        def right_half():
            eliminated(spans[1])

        @pl.when(after < half)
        def left_half():
            eliminated(spans[0])

        def inner(i, carry_in):
            below = pl.ds(pl.multiple_of(i * block, block), block)

            def subtract(span):
                for layer in range(layers):
                    left_high, left_rest = pivot_high[layer, :, below], pivot_rest[layer, :, below]
                    right_high, right_rest = pivot_high[layer, :, span], pivot_rest[layer, :, span]
                    system[layer, below, span] -= mix(left_high, right_high, 0, 0) + (
                        mix(left_high, right_rest, 0, 0) + mix(left_rest, right_high, 0, 0)
                    )

            subtract(slice(half, 2 * channels))

            @pl.when(i * block < half)
            def left_half():
                subtract(spans[0])

            return carry_in

        lax.fori_loop(k + 1, channels // block, inner, 0)
        return carry

    lax.fori_loop(0, channels // block, outer, 0)
    for layer in range(layers):
        bases_new[layer] = system[layer, :, channels : 2 * channels].T
    for which in range(moved):
        give(which).wait()


def update(arrays, summed, statistics, bases, head, vector, bias_rows):
    layers, channels, unused = statistics.shape
    dims = (layers, channels, bias_rows, 32, len(arrays))
    anywhere = pl.BlockSpec(memory_space=pl.ANY)
    vmem = pl.BlockSpec(memory_space=pltpu.VMEM)
    square = jax.ShapeDtypeStruct(statistics.shape, jnp.float32)
    head_shape = jax.ShapeDtypeStruct(head[0].shape, jnp.float32)
    vector_shape = jax.ShapeDtypeStruct(vector[0].shape, jnp.float32)
    return pl.pallas_call(
        partial(update_kernel, dims),
        out_shape=tuple(jax.ShapeDtypeStruct(array.shape, array.dtype) for array in arrays)
        + (square,) * 2 + (head_shape,) * 3 + (vector_shape,) * 3,
        in_specs=[anywhere] * len(arrays) + [vmem] * 11,
        out_specs=[anywhere] * len(arrays) + [vmem] * 8,
        scratch_shapes=[
            pltpu.VMEM((layers, channels, 2 * channels), jnp.float32),
            pltpu.VMEM((layers, LANES, 2 * channels), jnp.bfloat16),
            pltpu.VMEM((layers, LANES, 2 * channels), jnp.bfloat16),
        ]
        + [pltpu.VMEM(array.shape, array.dtype) for array in arrays]
        + [pltpu.SemaphoreType.DMA((2, len(arrays)))],
        compiler_params=pltpu.CompilerParams(vmem_limit_bytes=VMEM_LIMIT),
        cost_estimate=pl.CostEstimate(
            flops=10**10, bytes_accessed=2 * 10**7, transcendentals=10**4
        ),
    )(*arrays, summed, statistics, bases, *head, *vector)


def local(
    features,
    valid_rows,
    conv_master,
    head_master,
    vectors,
    conv_first,
    conv_second,
    head_first,
    head_second,
    vec_first,
    vec_second,
    statistics,
    bases,
    cotangent,
):
    channels = features.shape[3]
    head_width = cotangent.shape[2]
    space_count = lax.axis_size("space")
    vectors, vec_first, vec_second, head_master, head_first, head_second = (
        array.reshape(-1, LANES)
        for array in (vectors, vec_first, vec_second, head_master, head_first, head_second)
    )
    conv_used, head_used, wide, hidden, last = gather_weights(
        conv_master, head_master, head_width, features[0], vectors, valid_rows, space_count
    )
    merged, features_grad, grads, owned_head, vector = run_block(
        conv_used,
        head_used,
        wide,
        hidden,
        last,
        vectors,
        cotangent,
        valid_rows,
        space_count,
    )
    summed_stats, grad_vec, conv_new = reduce_grads(
        grads, vector, bases, (conv_first, conv_second, conv_master), space_count
    )
    moved = (merged, features_grad, *conv_new)
    outs = update(
        moved,
        summed_stats,
        statistics,
        bases,
        (owned_head, head_first, head_second, head_master),
        (grad_vec, vec_first, vec_second, vectors),
        (3 * channels + head_width) // LANES,
    )
    merged, features_grad, *conv_new = outs[:5]
    stats_new, bases_new = outs[5:7]
    return (
        merged.reshape(cotangent.shape),
        features_grad.reshape(features.shape),
        *conv_new,
        *(out.reshape(-1) for out in outs[7:]),
        stats_new,
        bases_new,
    )


def solution(mesh):
    in_specs = (
        P("scale", "space", None, None),
        P(),
        P(None, "space", None),
        P(("scale", "space")),
        P(),
        P(None, "space", None),
        P(None, "space", None),
        P(("scale", "space")),
        P(("scale", "space")),
        P(),
        P(),
        P(),
        P(),
        P("space", None, None),
    )
    out_specs = (
        P("space", None, None),
        P("scale", "space", None, None),
        P(None, "space", None),
        P(None, "space", None),
        P(None, "space", None),
        P(("scale", "space")),
        P(("scale", "space")),
        P(("scale", "space")),
        P(),
        P(),
        P(),
        P(),
        P(),
    )
    return jax.shard_map(local, mesh=mesh, in_specs=in_specs, out_specs=out_specs, check_vma=False)
```

```python
from functools import partial

import jax
import jax.experimental.pallas as pl
import jax.experimental.pallas.tpu as pltpu
import jax.numpy as jnp
from jax import lax
from jax.sharding import PartitionSpec as P

NH = 7
HD = 256
STEP = 5


BETA_ONE = 0.9
BETA_TWO = 0.95
EPSILON = 1e-08
DECAY = 0.01
RATE_CONV = 0.04
RATE_HEAD = 0.08
RATE_BIAS = 0.5
RATE_GAIN = 20.0
VMEM_LIMIT = 60 * 2**20
GELU_SCALE = 0.7978845608028654
GELU_CUBE = 0.044715


MESH = pl.DeviceIdType.MESH
LANES = 128


def place():
    scale, space = lax.axis_index("scale"), lax.axis_index("space")
    across, core = scale // 2, lax.rem(scale, 2)
    deep, side = space // 2, lax.rem(space, 2)
    return (across, core, deep, side)


def at(across, core, deep, side):
    return (2 * across + core, 2 * deep + side)


def greet(peers):
    barrier = pltpu.get_barrier_semaphore()
    for peer in peers:
        pl.semaphore_signal(barrier, inc=1, device_id=peer, device_id_type=MESH)
    pl.semaphore_wait(barrier, len(peers))


def remote(source, target, send, receive, device):
    return pltpu.make_async_remote_copy(
        src_ref=source,
        dst_ref=target,
        send_sem=send,
        recv_sem=receive,
        device_id=device,
        device_id_type=MESH,
    )


def lanes(index, count=1):
    return pl.ds(pl.multiple_of(index * LANES, LANES), count * LANES)


def nearest(deep, deep_count, index):
    left, right = deep, deep_count - 1 - deep
    short = jnp.minimum(left, right)
    both = (index + 1) // 2 * (2 * lax.rem(index, 2) - 1)
    one = (index - short) * jnp.where(left < right, 1, -1)
    return deep + jnp.where(index <= 2 * short, both, one)


def partners(deep_count):
    across, core, deep, side = place()
    peers = [
        at(across, 1 - core, deep, side),
        at(1 - across, core, deep, side),
        at(across, core, deep, 1 - side),
    ]
    peers += [
        at(across, core, lax.rem(deep + hop, deep_count), side) for hop in range(1, deep_count)
    ]
    return peers


TAPS = 3


def gelu_parts(value):
    inner = GELU_SCALE * (value + GELU_CUBE * value * value * value)
    return jnp.tanh(inner)


def gelu_value(value):
    return 0.5 * value * (1.0 + gelu_parts(value))


def gelu_slope(value):
    bend = gelu_parts(value)
    rise = GELU_SCALE * (1.0 + 3.0 * GELU_CUBE * value * value)
    return 0.5 * (1.0 + bend) + 0.5 * value * (1.0 - bend * bend) * rise


def mix(left, right, left_dim, right_dim):
    return lax.dot_general(
        left,
        right,
        (((left_dim,), (right_dim,)), ((), ())),
        preferred_element_type=jnp.float32,
    )


def row_weights(valid, rows):
    scale, space = lax.axis_index("scale"), lax.axis_index("space")
    scales = lax.axis_size("scale")
    masks, weights = [], []
    for row in range(rows):
        place_in = space * rows + row
        mask = jnp.where(place_in < valid[scale], 1.0, 0.0)
        count = jnp.float32(0.0)
        for other in range(scales):
            count += jnp.where(place_in < valid[other], 1.0, 0.0)
        masks.append(mask)
        weights.append(jnp.full((1, LANES), mask) / jnp.full((1, LANES), count))
    return (masks, [weight[:, :1] for weight in weights])


def vector_lanes(vectors, start, part):
    row = start // LANES + 2 * part
    return jnp.concatenate([vectors[pl.ds(row, 1), :], vectors[pl.ds(row + 1, 1), :]], 1)


def greet_edges(peers, space_count):
    barrier = pltpu.get_barrier_semaphore()
    scale, space = lax.axis_index("scale"), lax.axis_index("space")
    for peer in peers:
        pl.semaphore_signal(barrier, inc=1, device_id=peer, device_id_type=MESH)
    next_space = space - 1 + 2 * lax.rem(space, 2)
    has_next = jnp.logical_and(next_space >= 0, next_space < space_count)

    @pl.when(has_next)
    def greet_next():
        pl.semaphore_signal(barrier, inc=1, device_id=(scale, next_space), device_id_type=MESH)

    pl.semaphore_wait(barrier, len(peers) + has_next.astype(jnp.int32))


def edge_tools(dims, halo, send_sem, receive_sem):
    rows, width, channels, space_count = dims[1], dims[2], dims[3], dims[6]
    tile = 2 * LANES
    tiles = channels // tile
    scale, space = lax.axis_index("scale"), lax.axis_index("space")
    above, below = space > 0, space < space_count - 1
    low = jnp.bfloat16

    def up(which, source):
        return remote(
            source,
            halo.at[which, 1],
            send_sem.at[which, 0],
            receive_sem.at[which, 1],
            (scale, space - 1),
        )

    def down(which, source):
        return remote(
            source,
            halo.at[which, 0],
            send_sem.at[which, 1],
            receive_sem.at[which, 0],
            (scale, space + 1),
        )

    def edge(array, row):
        return array.at[pl.ds((row + 1) * width, width), pl.ds(channels, channels)]

    def send_edges(which, array):
        @pl.when(above)
        def go_up():
            up(which, edge(array, 0)).start()

        @pl.when(below)
        def go_down():
            down(which, edge(array, rows - 1)).start()

    column = lax.broadcasted_iota(jnp.int32, (width, 1), 0)

    def put(array, slot, lane, count, value):
        here = pl.ds(slot * width, width)
        left = jnp.where(column == 0, 0.0, pltpu.roll(value, 1, 0))
        right = jnp.where(column == width - 1, 0.0, pltpu.roll(value, width - 1, 0))
        for which, moved in enumerate((left, value, right)):
            start = pl.multiple_of(which * channels + lane, LANES)
            array[here, pl.ds(start, count)] = moved.astype(low)

    def take_edges(which, array):
        for side, present, slot in ((0, above, 0), (1, below, rows + 1)):

            @pl.when(present)
            def arrived():
                if side == 0:
                    up(which, edge(array, 0)).wait_send()
                    down(which, edge(array, 0)).wait_recv()
                else:
                    down(which, edge(array, 0)).wait_send()
                    up(which, edge(array, 0)).wait_recv()
                for part in range(tiles):
                    value = halo[which, side, :, part * tile : (part + 1) * tile]
                    put(array, slot, part * tile, tile, value.astype(jnp.float32))

            @pl.when(jnp.logical_not(present))
            def missing():
                array[pl.ds(slot * width, width), :] = jnp.zeros(
                    (width, TAPS * channels), low
                )

    return (send_edges, take_edges, put)


def gather_kernel(
    dims,
    master,
    head_master,
    features,
    vectors,
    valid,
    full,
    head_full,
    wide_out,
    hidden_out,
    last_out,
    own,
    head_own,
    weights,
    wide,
    hidden,
    last,
    halo,
    local_sem,
    sends,
    receives,
    head_sends,
    head_receives,
    load_sem,
    store_sem,
    edge_sends,
    edge_receives,
):
    layers, rows, width, channels, heads, depth, space_count = dims
    deep_count = space_count // 2
    across, core, deep, side = place()
    block = 2 * core + across
    low = jnp.bfloat16
    own[0] = master[0].astype(low)
    greet_edges(partners(deep_count), space_count)

    chunks = layers * deep_count

    def by_distance(index):
        return nearest(deep, deep_count, index)

    def split(chunk):
        rest = chunk - layers
        is_own = chunk < layers
        layer = jnp.where(is_own, chunk, rest // (deep_count - 1))
        hop = jnp.where(is_own, 0, 1 + lax.rem(rest + chunks, deep_count - 1))
        layer, hop = jnp.clip(layer, 0, layers - 1), jnp.clip(hop, 0, deep_count - 1)
        source = by_distance(hop)
        odd = jnp.where(is_own, 0, lax.rem(chunk, 2))
        return (layer, hop, source, odd)

    def first(layer, index):
        piece = own.at[layer, :, lanes(block)]
        target = full.at[layer, deep, side, :, lanes(block)]
        there = by_distance(index)
        to = at(across, core, there, side)
        return remote(piece, target, sends.at[0, layer, there], receives.at[0, layer, deep], to)

    def first_in(layer, index):
        source = by_distance(index)
        piece = full.at[layer, source, side, :, lanes(block)]
        return remote(
            piece,
            piece,
            sends.at[0, layer, source],
            receives.at[0, layer, source],
            at(across, core, source, side),
        )

    def second(chunk, incoming):
        layer, hop, source, odd = split(chunk)
        there_side = lax.rem(side + 1 - odd, 2)
        there_across = lax.rem(across + odd, 2)
        to = at(there_across, core, deep, there_side)
        if incoming:
            piece = full.at[layer, source, there_side, :, lanes(2 * core + there_across)]
        else:
            piece = full.at[layer, source, side, :, lanes(block)]
        return remote(piece, piece, sends.at[1, layer, hop], receives.at[1, layer, hop], to)

    def third(chunk, half, incoming):
        layer, hop, source, odd = split(chunk)
        there_side = lax.rem(side + odd, 2)
        there_across = lax.rem(across + 1 - odd, 2)
        to = at(there_across, core, deep, there_side)
        here = there_side if incoming else side
        lane = there_across if incoming else across
        piece_side = (1 - odd) * half + odd * here
        piece_lane = 2 * core + (1 - odd) * lane + odd * half
        piece = full.at[layer, source, piece_side, :, lanes(piece_lane)]
        return remote(
            piece, piece, sends.at[2 + half, layer, hop], receives.at[2 + half, layer, hop], to
        )

    def fourth(chunk, incoming):
        layer, hop, source, odd = split(chunk)
        column = 1 - core if incoming else core
        piece = full.at[layer, source, :, :, lanes(2 * column, 2)]
        to = at(across, 1 - core, deep, side)
        return remote(piece, piece, sends.at[4, layer, hop], receives.at[4, layer, hop], to)

    def own_fourth(layer, incoming):
        column = 1 - core if incoming else core
        piece = full.at[layer, deep, 1 - side, :, lanes(2 * column, 2)]
        to = at(across, 1 - core, deep, side)
        return remote(piece, piece, sends.at[4, layer, 0], receives.at[4, layer, 0], to)

    def local(layer):
        return pltpu.make_async_copy(
            own.at[layer], full.at[layer, deep, side], local_sem.at[layer]
        )

    def each(low, action):
        def step(hop, carry):
            action(hop)
            return carry

        lax.fori_loop(low, deep_count, step, 0)

    def head_local():
        return pltpu.make_async_copy(
            head_own, head_full.at[across, core, deep, side], local_sem.at[layers]
        )

    def head_first(hop):
        to = at(across, core, lax.rem(deep + hop, deep_count), side)
        target = head_full.at[across, core, deep, side]
        return remote(head_own, target, head_sends.at[hop], head_receives.at[hop], to)

    def head_first_in(hop):
        piece = head_full.at[across, core, lax.rem(deep - hop + deep_count, deep_count), side]
        to = at(across, core, deep, side)
        return remote(piece, piece, head_sends.at[hop], head_receives.at[hop], to)

    def head_next(which, incoming):
        if which == 0:
            to = at(across, core, deep, 1 - side)
            piece = head_full.at[across, core, :, 1 - side if incoming else side]
        elif which == 1:
            to = at(1 - across, core, deep, side)
            piece = head_full.at[1 - across if incoming else across, core]
        else:
            to = at(across, 1 - core, deep, side)
            piece = head_full.at[:, 1 - core if incoming else core]
        slot = deep_count + which
        return remote(piece, piece, head_sends.at[slot], head_receives.at[slot], to)

    def go_head(which):
        if which == 0:
            head_local().wait()
            each(1, lambda hop: head_first_in(hop).wait_recv())
        else:
            head_next(which - 1, True).wait_recv()
        if which < 3:
            head_next(which, False).start()

    send_edges, take_edges, put = edge_tools(dims, halo, edge_sends, edge_receives)
    tile = 2 * LANES
    tiles = channels // tile
    pixels = rows * width
    band = TAPS * channels
    masks, unused = row_weights(valid, rows)
    share = band * TAPS // space_count

    def loop(count, action):
        def body(index, carry):
            action(index)
            return carry

        lax.fori_loop(0, count, body, 0)

    def spot(index):
        return pl.multiple_of(index * tile, tile)

    def load(layer, owner):
        start = pl.multiple_of(owner * share, 8)
        return pltpu.make_async_copy(
            full.at[layer, owner // 2, lax.rem(owner, 2)],
            weights.at[layer % 2, pl.ds(start, share)],
            load_sem.at[layer % 2, owner],
        )

    def arrive(layer):
        own_fourth(layer, True).wait_recv()
        begin = layers + layer * (deep_count - 1)
        loop(deep_count - 1, lambda index: fourth(begin + index, True).wait_recv())
        loop(space_count, lambda owner: load(layer, owner).start())

    def store(which, layer):
        source, target = (
            (wide.at[layer], wide_out.at[layer]),
            (hidden.at[layer], hidden_out.at[layer]),
            (last, last_out),
        )[which]
        return pltpu.make_async_copy(source, target, store_sem.at[which, layer])

    def forward(layer):
        here = wide.at[layer]
        take_edges(layer, here)
        store(0, layer).start()
        loop(space_count, lambda owner: load(layer, owner).wait())

        def outer(part):
            lane = pl.ds(spot(part), tile)
            total = vector_lanes(vectors, layer * channels, part)
            for tap_row in range(TAPS):
                total += mix(
                    here[tap_row * width : tap_row * width + pixels, :],
                    weights[layer % 2, tap_row * band : (tap_row + 1) * band, lane],
                    1,
                    0,
                )
            hidden[layer, :, lane] = total
            for row in range(rows):
                span = slice(row * width, (row + 1) * width)
                value = gelu_value(hidden[layer, span, lane]) * masks[row]
                if layer < layers - 1:
                    put(wide.at[layer + 1], row + 1, spot(part), tile, value)
                else:
                    last[span, lane] = value.astype(low)

        loop(tiles, outer)
        store(1, layer).start()
        if layer < layers - 1:
            send_edges(layer + 1, wide.at[layer + 1])

    def go_second(chunk):
        layer, hop, source, odd = split(chunk)

        @pl.when(hop == 0)
        def own_rows():
            local(layer).wait()

        @pl.when(hop > 0)
        def other_rows():
            first_in(layer, hop).wait_recv()
            go_first(chunk - layers + z_ahead)

        second(chunk, False).start()

    def go_third(chunk):
        second(chunk, True).wait_recv()

        @pl.when(chunk < layers)
        def own_rows():
            third(chunk, 1 - side, False).start()

        @pl.when(chunk >= layers)
        def other_rows():
            third(chunk, 0, False).start()
            third(chunk, 1, False).start()

    def go_fourth(chunk):
        @pl.when(chunk < layers)
        def own_rows():
            third(chunk, 1 - side, True).wait_recv()
            own_fourth(chunk, False).start()

        @pl.when(chunk >= layers)
        def other_rows():
            third(chunk, 0, True).wait_recv()
            third(chunk, 1, True).wait_recv()
            fourth(chunk, False).start()

    def go_head_first():
        each(1, lambda hop: head_first(hop).start())

    def go_first(index):
        @pl.when(index < layers * (deep_count - 1))
        def more():
            first(index // (deep_count - 1), 1 + lax.rem(index, deep_count - 1)).start()

    z_ahead = 2
    for index in range(min(z_ahead, deep_count - 1)):
        go_first(index)
    local(0).start()
    go_second(0)
    for layer in range(1, layers):
        own[layer] = master[layer].astype(low)
        local(layer).start()
    head_rows, head_blocks = head_own.shape[0], heads * depth // LANES
    for lane in range(head_blocks):
        head_own[:, lane * LANES : (lane + 1) * LANES] = head_master[
            pl.ds(lane, head_rows, stride=head_blocks), :
        ].astype(low)
    head_local().start()
    for row in range(rows):
        for part in range(tiles):
            value = features[row * width : (row + 1) * width, part * tile : (part + 1) * tile]
            put(wide.at[0], row + 1, part * tile, tile, value.astype(jnp.float32))
    send_edges(0, wide.at[0])

    lag_third, lag_fourth = 2, 4
    others = deep_count - 1

    def last_of(layer):
        return layers + others * (layer + 1) - 1 + lag_fourth

    early = min(2, others)
    timed = [(layers + early, go_head_first)]
    timed += [(layers + others + 2 * which, go_head, which) for which in range(3)]
    for layer in range(layers - 1):
        timed += [(last_of(layer) + 1, arrive, layer), (last_of(layer) + 2, forward, layer)]

    def turn(now):
        for lag, action in ((0, go_second), (lag_third, go_third), (lag_fourth, go_fourth)):
            begin = max(lag, 1)

            @pl.when(jnp.logical_and(now >= begin, now < chunks + lag))
            def stage():
                action(now - lag)

        for moment, action, *which in timed:

            @pl.when(now == moment)
            def once():
                action(*which)

    loop(chunks + lag_fourth, turn)
    go_head(3)
    arrive(layers - 1)
    forward(layers - 1)
    store(2, 0).start()

    def finish(chunk):
        second(chunk, False).wait_send()

        @pl.when(chunk < layers)
        def own_rows():
            third(chunk, 1 - side, False).wait_send()
            own_fourth(chunk, False).wait_send()

        @pl.when(chunk >= layers)
        def other_rows():
            third(chunk, 0, False).wait_send()
            third(chunk, 1, False).wait_send()
            fourth(chunk, False).wait_send()

    loop(chunks, finish)
    each(1, lambda hop: head_first(hop).wait_send())
    for which in range(3):
        head_next(which, False).wait_send()

    for layer in range(layers):

        each(1, lambda hop: first(layer, hop).wait_send())
        store(0, layer).wait()
        store(1, layer).wait()
    store(2, 0).wait()


def gather_weights(master, head_master, head_width, features, vectors, valid, space_count):
    layers, share, channels = master.shape
    rows, width, unused = features.shape
    deep_count = space_count // 2
    pixels = rows * width
    dims = (layers, rows, width, channels, NH, HD, space_count)
    low, wide_float = jnp.bfloat16, jnp.float32
    anywhere = pl.BlockSpec(memory_space=pl.ANY)
    vmem = pl.BlockSpec(memory_space=pltpu.VMEM)
    head_own = (head_master.shape[0] * LANES // head_width, head_width)
    head_shape = (2, 2, deep_count, 2) + head_own
    wide_shape = (layers, (rows + 2) * width, TAPS * channels)
    full, head_full, wide, hidden, last = pl.pallas_call(
        partial(gather_kernel, dims),
        out_shape=(
            jax.ShapeDtypeStruct((layers, deep_count, 2, share, channels), low),
            jax.ShapeDtypeStruct(head_shape, low),
            jax.ShapeDtypeStruct(wide_shape, low),
            jax.ShapeDtypeStruct((layers, pixels, channels), wide_float),
            jax.ShapeDtypeStruct((pixels, channels), low),
        ),
        in_specs=[vmem] * 4 + [pl.BlockSpec(memory_space=pltpu.SMEM)],
        out_specs=[anywhere] * 5,
        scratch_shapes=[
            pltpu.VMEM(master.shape, low),
            pltpu.VMEM(head_own, low),
            pltpu.VMEM((2, space_count * share, channels), low),
            pltpu.VMEM(wide_shape, low),
            pltpu.VMEM((layers, pixels, channels), wide_float),
            pltpu.VMEM((pixels, channels), low),
            pltpu.VMEM((layers, 2, width, channels), low),
            pltpu.SemaphoreType.DMA((layers + 1,)),
            pltpu.SemaphoreType.DMA((5, layers, deep_count)),
            pltpu.SemaphoreType.DMA((5, layers, deep_count)),
            pltpu.SemaphoreType.DMA((deep_count + 3,)),
            pltpu.SemaphoreType.DMA((deep_count + 3,)),
            pltpu.SemaphoreType.DMA((2, space_count)),
            pltpu.SemaphoreType.DMA((3, layers)),
            pltpu.SemaphoreType.DMA((layers, 2)),
            pltpu.SemaphoreType.DMA((layers, 2)),
        ],
        compiler_params=pltpu.CompilerParams(
            collective_id=0, has_side_effects=True, vmem_limit_bytes=VMEM_LIMIT
        ),
    )(master, head_master, features.reshape(pixels, channels), vectors, valid)
    return (
        full.reshape(layers, space_count * share, channels),
        head_full.reshape(-1, head_width),
        wide,
        hidden,
        last,
    )


def reduce_kernel(
    layers,
    deep_count,
    grads,
    vector,
    bases,
    first_in,
    second_moment_in,
    master_in,
    total,
    stats,
    vector_total,
    first_out,
    second_out,
    master_out,
    mine,
    core_in,
    second_in,
    kept,
    third_in,
    last,
    last_in,
    acc,
    stat_own,
    stat_in,
    stat_deep,
    vector_out,
    vector_in,
    vector_deep,
    moment_one,
    moment_two,
    master,
    local_sem,
    sends,
    receives,
    stat_sends,
    stat_receives,
    deep_sends,
    deep_receives,
    vector_sends,
    vector_receives,
    state_loads,
    state_stores,
):
    across, core, deep, side = place()
    block = 2 * core + across
    steps = layers * deep_count

    def split(step):
        layer, hop = step // deep_count, deep_count - 1 - lax.rem(step, deep_count)
        return (layer, hop, nearest(deep, deep_count, hop), lax.rem(step, 2))

    def first(step):
        layer, hop, target, odd = split(step)
        return remote(
            grads.at[layer, target, :, :, lanes(2 * (1 - core), 2)],
            core_in.at[step],
            sends.at[0, step],
            receives.at[0, step],
            at(across, 1 - core, deep, side),
        )

    def load(step):
        layer, hop, target, odd = split(step)
        return pltpu.make_async_copy(
            grads.at[layer, target, :, :, lanes(2 * core, 2)], mine.at[step], local_sem.at[step]
        )

    def second(step, half):
        layer, hop, target, odd = split(step)
        piece_side = (1 - odd) * half + odd * (1 - side)
        piece_lane = (1 - odd) * (1 - across) + odd * half
        to = at(lax.rem(across + 1 - odd, 2), core, deep, lax.rem(side + odd, 2))
        return remote(
            mine.at[step, piece_side, :, lanes(piece_lane)],
            second_in.at[step, half],
            sends.at[1 + half, step],
            receives.at[1 + half, step],
            to,
        )

    def third(step):
        layer, hop, target, odd = split(step)
        keep = (1 - odd) * side + odd * across
        to = at(lax.rem(across + odd, 2), core, deep, lax.rem(side + 1 - odd, 2))
        return remote(
            kept.at[step, 1 - keep],
            third_in.at[step],
            sends.at[3, step],
            receives.at[3, step],
            to,
        )

    def fourth(step):
        layer, hop, target, odd = split(step)
        slot = layer * deep_count + deep
        return remote(
            last.at[step],
            last_in.at[slot],
            sends.at[4, step],
            receives.at[4, slot],
            at(across, core, target, side),
        )

    def fourth_in(layer, hop):
        source = nearest(deep, deep_count, hop)
        slot = layer * deep_count + source
        return (
            slot,
            remote(
                last_in.at[slot],
                last_in.at[slot],
                sends.at[4, slot],
                receives.at[4, slot],
                at(across, core, source, side),
            ),
        )

    def fifth(layer, incoming):
        lane = 2 * core + (1 - across if incoming else across)
        piece = total.at[layer, :, lanes(lane)]
        to = at(1 - across, core, deep, side)
        return remote(piece, piece, sends.at[5, layer], receives.at[5, layer], to)

    def sixth(layer, incoming):
        column = 1 - core if incoming else core
        piece = total.at[layer, :, lanes(2 * column, 2)]
        to = at(across, 1 - core, deep, side)
        return remote(piece, piece, sends.at[6, layer], receives.at[6, layer], to)

    def run(low, high, action):
        def body(step, carry):
            action(step)
            return carry

        lax.fori_loop(low, high, body, 0)

    half_block = LANES // 2

    def stat_side(layer, incoming):
        rows = pl.ds(pl.multiple_of((1 - side) * half_block, half_block), half_block)
        return remote(
            stat_own.at[layer, rows],
            stat_in.at[layer],
            stat_sends.at[0, layer],
            stat_receives.at[0, layer],
            at(across, core, deep, 1 - side),
        )

    def stat_along(layer, hop):
        return remote(
            stat_deep.at[layer, deep],
            stat_deep.at[layer, deep],
            deep_sends.at[layer, hop],
            deep_receives.at[layer, hop],
            at(across, core, lax.rem(deep + hop, deep_count), side),
        )

    def stat_along_in(layer, hop):
        source = lax.rem(deep - hop + deep_count, deep_count)
        return remote(
            stat_deep.at[layer, source],
            stat_deep.at[layer, source],
            deep_sends.at[layer, hop],
            deep_receives.at[layer, hop],
            at(across, core, deep, side),
        )

    def half_rows(which):
        return pl.ds(pl.multiple_of(which * half_block, half_block), half_block)

    def stat_spread(which, layer, incoming):
        if which < 3:
            other_side = side if which == 1 else 1 - side
            other_across = across if which == 0 else 1 - across
            to = at(other_across, core, deep, other_side)
            if incoming:
                piece = stats.at[layer, 2 * core + other_across, half_rows(other_side)]
            else:
                piece = stats.at[layer, block, half_rows(side)]
        else:
            to = at(across, 1 - core, deep, side)
            piece = stats.at[layer, pl.ds(2 * (1 - core if incoming else core), 2)]
        slot = 1 + which
        return remote(piece, piece, stat_sends.at[slot, layer], stat_receives.at[slot, layer], to)

    def vector_step(which):
        to = (
            at(across, 1 - core, deep, side),
            at(1 - across, core, deep, side),
            at(across, core, deep, 1 - side),
        )[which]
        return remote(
            vector_out.at[which],
            vector_in.at[which],
            vector_sends.at[which],
            vector_receives.at[which],
            to,
        )

    def vector_along(hop):
        return remote(
            vector_deep.at[deep],
            vector_deep.at[deep],
            vector_sends.at[2 + hop],
            vector_receives.at[2 + hop],
            at(across, core, lax.rem(deep + hop, deep_count), side),
        )

    def vector_along_in(hop):
        source = lax.rem(deep - hop + deep_count, deep_count)
        return remote(
            vector_deep.at[source],
            vector_deep.at[source],
            vector_sends.at[2 + hop],
            vector_receives.at[2 + hop],
            at(across, core, deep, side),
        )

    def go_first(step):
        load(step).start()
        first(step).start()

    ahead = min(3, steps)
    piece_rows = 144 if total.shape[1] % 144 == 0 else total.shape[1]
    states = (
        (first_in, moment_one, first_out),
        (second_moment_in, moment_two, second_out),
        (master_in, master, master_out),
    )

    def load_state(which, layer):
        source, target, unused = states[which]
        return pltpu.make_async_copy(
            source.at[layer], target.at[layer], state_loads.at[which, layer]
        )

    def store_state(which, layer):
        unused, source, target = states[which]
        return pltpu.make_async_copy(
            source.at[layer], target.at[layer], state_stores.at[which, layer]
        )

    greet(partners(deep_count) + [at(1 - across, core, deep, 1 - side)])
    run(0, ahead, go_first)
    for layer in range(layers):
        for which in range(3):
            load_state(which, layer).start()

    def wide(left, right):
        return left.astype(jnp.float32) + right.astype(jnp.float32)

    def go_second(step):
        @pl.when(step + ahead < steps)
        def start_next():
            go_first(step + ahead)

        load(step).wait()
        first(step).wait_recv()
        mine[step] = wide(mine[step], core_in[step]).astype(jnp.bfloat16)
        second(step, 0).start()
        second(step, 1).start()

    def go_third(step):
        layer, hop, target, odd = split(step)
        for half in range(2):
            second(step, half).wait_recv()
            keep_side = (1 - odd) * half + odd * side
            keep_lane = (1 - odd) * across + odd * half
            kept[step, half] = wide(
                mine[step, keep_side, :, lanes(keep_lane)], second_in[step, half]
            ).astype(jnp.bfloat16)
        third(step).start()

    def go_fourth(step):
        layer, hop, target, odd = split(step)
        third(step).wait_recv()
        keep = (1 - odd) * side + odd * across
        last[step] = wide(kept[step, keep], third_in[step]).astype(jnp.bfloat16)

        @pl.when(hop > 0)
        def unused():
            fourth(step).start()

    def close(layer):
        acc[...] = last[layer * deep_count + deep_count - 1].astype(jnp.float32)

        def add(hop):
            slot, copy = fourth_in(layer, hop)
            copy.wait_recv()
            acc[...] += last_in[slot].astype(jnp.float32)

        run(1, deep_count, add)
        total[layer, :, lanes(block)] = acc[...].astype(jnp.bfloat16)
        fifth(layer, False).start()

    def spread(layer):
        fifth(layer, True).wait_recv()
        sixth(layer, False).start()

    def measure(layer):
        sixth(layer, True).wait_recv()
        own_lanes = total[layer, :, lanes(block)]
        stat_own[layer] = lax.dot_general(
            own_lanes,
            total[layer],
            (((0,), (0,)), ((), ())),
            preferred_element_type=jnp.float32,
        ).astype(jnp.bfloat16)
        stat_side(layer, False).start()

    def pair(layer):
        stat_side(layer, True).wait_recv()
        stat_deep[layer, deep] = wide(
            stat_own[layer, half_rows(side)], stat_in[layer]
        ).astype(jnp.bfloat16)
        run(1, deep_count, lambda hop: stat_along(layer, hop).start())

    def settle(layer):
        run(1, deep_count, lambda hop: stat_along_in(layer, hop).wait_recv())
        whole = stat_deep[layer, 0].astype(jnp.float32)
        for source in range(1, deep_count):
            whole += stat_deep[layer, source].astype(jnp.float32)
        stats[layer, block, half_rows(side)] = whole.astype(jnp.bfloat16)
        for which in range(3):
            stat_spread(which, layer, False).start()

    def share_core(layer):
        for which in range(3):
            stat_spread(which, layer, True).wait_recv()
        stat_spread(3, layer, False).start()

    def refresh(layer):
        for which in range(3):
            load_state(which, layer).wait()
        high, rest = halves(bases[layer])

        def one_piece(index):
            here = pl.ds(pl.multiple_of(index * piece_rows, piece_rows), piece_rows)
            given = total[layer, here, :]
            rotated = mix(given, high, 1, 0) + mix(given, rest, 1, 0)
            first_new, second_new, direction = moments(
                rotated, moment_one[layer, here, :], moment_two[layer, here, :]
            )
            moment_one[layer, here, :] = first_new
            moment_two[layer, here, :] = second_new
            up, down = halves(direction)
            back = mix(up, high, 1, 1) + (mix(up, rest, 1, 1) + mix(down, high, 1, 1))
            old = master[layer, here, :]
            master[layer, here, :] = old - RATE_CONV * (back + DECAY * old)

        run(0, total.shape[1] // piece_rows, one_piece)
        for which in range(3):
            store_state(which, layer).start()

    def finish(layer):
        stat_spread(3, layer, True).wait_recv()
        fifth(layer, False).wait_send()
        sixth(layer, False).wait_send()
        stat_side(layer, False).wait_send()
        run(1, deep_count, lambda hop: stat_along(layer, hop).wait_send())
        for which in range(4):
            stat_spread(which, layer, False).wait_send()
        for which in range(3):
            store_state(which, layer).wait()

    def vector_next(which):
        vector_step(which).wait_recv()
        summed = vector_out[which] + vector_in[which]
        if which < 2:
            vector_out[which + 1] = summed
            vector_step(which + 1).start()
        else:
            vector_deep[deep] = summed
            run(1, deep_count, lambda hop: vector_along(hop).start())

    chunk_work = ((0, go_second), (2, go_third), (3, go_fourth))
    layer_work = (
        (4, close),
        (5, spread),
        (6, measure),
        (7, pair),
        (8, refresh),
        (9, settle),
        (10, share_core),
        (11, finish),
    )
    vector_out[0] = vector[...]
    vector_step(0).start()

    def turn(now):
        for lag, action in chunk_work:

            @pl.when(jnp.logical_and(now >= lag, now < steps + lag))
            def chunk():
                action(now - lag)

        for which in range(3):

            @pl.when(now == 2 * which + 1)
            def exchange():
                vector_next(which)

        for lag, action in layer_work:
            past = now - lag - (deep_count - 1)

            @pl.when(
                jnp.logical_and(
                    jnp.logical_and(past >= 0, past < steps), lax.rem(past, deep_count) == 0
                )
            )
            def whole_layer():
                action(past // deep_count)

    run(0, steps + layer_work[-1][0], turn)

    run(1, deep_count, lambda hop: vector_along_in(hop).wait_recv())
    summed = vector_deep[0]
    for source in range(1, deep_count):
        summed += vector_deep[source]
    vector_total[...] = summed
    for which in range(3):
        vector_step(which).wait_send()
    run(1, deep_count, lambda hop: vector_along(hop).wait_send())

    def drain(step):
        layer, hop, target, odd = split(step)
        first(step).wait_send()
        second(step, 0).wait_send()
        second(step, 1).wait_send()
        third(step).wait_send()

        @pl.when(hop > 0)
        def unused():
            fourth(step).wait_send()

    run(0, steps, drain)


def reduce_grads(grads, vector, bases, conv, space_count):
    layers, all_rows, columns = grads.shape
    deep_count, rows = space_count // 2, all_rows // space_count
    steps = layers * deep_count
    low = jnp.bfloat16
    blocks = columns // LANES
    vmem = pl.BlockSpec(memory_space=pltpu.VMEM)
    tall = jax.ShapeDtypeStruct((layers, rows, columns), jnp.float32)
    anywhere = pl.BlockSpec(memory_space=pl.ANY)
    total, stats, vector_total, *conv_new = pl.pallas_call(
        partial(reduce_kernel, layers, deep_count),
        out_shape=(
            jax.ShapeDtypeStruct((layers, rows, columns), low),
            jax.ShapeDtypeStruct((layers, blocks, LANES, columns), low),
            jax.ShapeDtypeStruct(vector.shape, jnp.float32),
            tall,
            tall,
            tall,
        ),
        in_specs=[anywhere, vmem, vmem] + [anywhere] * 3,
        out_specs=[vmem] * 3 + [anywhere] * 3,
        scratch_shapes=[
            pltpu.VMEM((steps, 2, rows, 2 * LANES), low),
            pltpu.VMEM((steps, 2, rows, 2 * LANES), low),
            pltpu.VMEM((steps, 2, rows, LANES), low),
            pltpu.VMEM((steps, 2, rows, LANES), low),
            pltpu.VMEM((steps, rows, LANES), low),
            pltpu.VMEM((steps, rows, LANES), low),
            pltpu.VMEM((steps, rows, LANES), low),
            pltpu.VMEM((rows, LANES), jnp.float32),
            pltpu.VMEM((layers, LANES, columns), low),
            pltpu.VMEM((layers, LANES // 2, columns), low),
            pltpu.VMEM((layers, deep_count, LANES // 2, columns), low),
            pltpu.VMEM((3,) + vector.shape, jnp.float32),
            pltpu.VMEM((3,) + vector.shape, jnp.float32),
            pltpu.VMEM((deep_count,) + vector.shape, jnp.float32),
            pltpu.VMEM(tall.shape, jnp.float32),
            pltpu.VMEM(tall.shape, jnp.float32),
            pltpu.VMEM(tall.shape, jnp.float32),
            pltpu.SemaphoreType.DMA((steps,)),
            pltpu.SemaphoreType.DMA((7, steps)),
            pltpu.SemaphoreType.DMA((7, steps)),
            pltpu.SemaphoreType.DMA((5, layers)),
            pltpu.SemaphoreType.DMA((5, layers)),
            pltpu.SemaphoreType.DMA((layers, deep_count)),
            pltpu.SemaphoreType.DMA((layers, deep_count)),
            pltpu.SemaphoreType.DMA((2 + deep_count,)),
            pltpu.SemaphoreType.DMA((2 + deep_count,)),
            pltpu.SemaphoreType.DMA((3, layers)),
            pltpu.SemaphoreType.DMA((3, layers)),
        ],
        compiler_params=pltpu.CompilerParams(
            collective_id=1, has_side_effects=True, vmem_limit_bytes=VMEM_LIMIT
        ),
    )(grads.reshape(layers, deep_count, 2, rows, columns), vector, bases, *conv)
    return (stats.reshape(layers, columns, columns), vector_total, conv_new)


def work_kernel(
    dims,
    weights_in,
    head_in,
    wide_in,
    hidden_in,
    last_in,
    vectors,
    cotangent_in,
    valid,
    merged,
    features_grad,
    grads_out,
    head_grad,
    vector,
    weights,
    head,
    cotangent,
    wide,
    hidden,
    last,
    last_turned,
    d_wide,
    d_active,
    grads,
    halo,
    term,
    term_in,
    load_sem,
    store_sem,
    send_sem,
    receive_sem,
    term_sends,
    term_receives,
    *head_refs,
):
    layers, rows, width, channels, heads, depth, space_count = dims
    deep_count = space_count // 2
    across, core, deep, side = place()
    spread_head = len(head_refs) > 0
    if spread_head:
        head_parts, core_in, across_in, side_in, deep_in, head_sends, head_receives = head_refs
        head_rows = head_parts.shape[4]
    tile = 2 * LANES
    tiles = channels // tile
    low = jnp.bfloat16

    loads = ((last_in, last), (head_in, head), (cotangent_in, cotangent))
    for layer in reversed(range(layers)):
        loads += (
            (hidden_in.at[layer], hidden.at[layer]),
            (wide_in.at[layer], wide.at[layer]),
            (weights_in.at[layer], weights.at[layer]),
        )

    def load(which):
        source, target = loads[which]
        return pltpu.make_async_copy(source, target, load_sem.at[which])

    for which in range(len(loads)):
        load(which).start()

    others = [
        at(across, 1 - core, deep, side),
        at(1 - across, core, deep, side),
        at(across, core, deep, 1 - side),
    ]
    if spread_head:
        others += [
            at(across, core, lax.rem(deep + hop, deep_count), side) for hop in range(1, deep_count)
        ]
    greet_edges(others, space_count)

    def term_lanes(index, which):
        return pl.ds(pl.multiple_of(index * depth + which * LANES, LANES), LANES)

    def term_step(which, index, incoming=False):
        if which == 0:
            source, target, to = term.at[:, term_lanes(index, 1 - core)], term_in.at[0, index], others[0]
        elif which == 1:
            source, target, to = term.at[:, term_lanes(index, core)], term_in.at[1, index], others[1]
        else:
            source = merged.at[:, term_lanes(index, 1 - core if incoming else core)]
            target, to = source, others[0]
        return remote(
            source, target, term_sends.at[which, index], term_receives.at[which, index], to
        )

    def term_pair(index):
        term_step(0, index).wait_recv()
        lane = term_lanes(index, core)
        both = term[:, lane].astype(jnp.float32) + term_in[0, index].astype(jnp.float32)
        term[:, lane] = both.astype(low)
        term_step(1, index).start()

    def term_total(index):
        term_step(1, index).wait_recv()
        lane = term_lanes(index, core)
        both = term[:, lane].astype(jnp.float32) + term_in[1, index].astype(jnp.float32)
        merged[:, lane] = both.astype(low)
        term_step(2, index).start()

    def term_end(index):
        term_step(2, index, True).wait_recv()
        for which in range(3):
            term_step(which, index).wait_send()

    def head_step(which):
        if which == 0:
            source, target, to = head_parts.at[:, 1 - core], core_in, others[0]
        elif which == 1:
            source = head_parts.at[pl.ds(0, 2), core, pl.ds(0, deep_count), 1 - side]
            target, to = side_in, others[2]
        else:
            source = head_parts.at[1 - across, core, pl.ds(0, deep_count), side]
            target, to = across_in, others[1]
        return remote(source, target, head_sends.at[which], head_receives.at[which], to)

    def head_along(hop):
        target = lax.rem(deep + hop, deep_count)
        return remote(
            head_parts.at[across, core, target, side],
            deep_in.at[hop],
            head_sends.at[2 + hop],
            head_receives.at[2 + hop],
            at(across, core, target, side),
        )

    def head_next(which):
        if not spread_head:
            return
        head_step(which).wait_recv()
        if which == 0:
            for part in range(2):
                both = head_parts[part, core].astype(jnp.float32) + core_in[part].astype(jnp.float32)
                head_parts[part, core] = both.astype(low)
            head_step(1).start()
        elif which == 1:
            for part in range(2):
                both = head_parts[part, core, pl.ds(0, deep_count), side].astype(jnp.float32)
                both += side_in[part].astype(jnp.float32)
                head_parts[part, core, pl.ds(0, deep_count), side] = both.astype(low)
            head_step(2).start()
        else:
            both = head_parts[across, core, pl.ds(0, deep_count), side].astype(jnp.float32)
            both += across_in[...].astype(jnp.float32)
            head_parts[across, core, pl.ds(0, deep_count), side] = both.astype(low)
            for hop in range(1, deep_count):
                head_along(hop).start()

    def head_end():
        if not spread_head:
            return
        whole = head_parts[across, core, deep, side].astype(jnp.float32)
        for hop in range(1, deep_count):
            head_along(hop).wait_recv()
            whole += deep_in[hop].astype(jnp.float32)
        blocks = heads * depth // LANES
        for lane in range(blocks):
            head_grad[pl.ds(lane, head_rows, stride=blocks), :] = whole[
                :, lane * LANES : (lane + 1) * LANES
            ]
        for which in range(3):
            head_step(which).wait_send()
        for hop in range(1, deep_count):
            head_along(hop).wait_send()

    send_edges, take_edges, put = edge_tools(dims, halo, send_sem, receive_sem)

    def loop(count, action):
        def body(index, carry):
            action(index)
            return carry

        lax.fori_loop(0, count, body, 0)

    def spot(index):
        return pl.multiple_of(index * tile, tile)

    masks, weights_row = row_weights(valid, rows)

    def put_vector(start, part, value):
        row = start // LANES + 2 * part
        vector[pl.ds(row, 1), :] = value[:, :LANES]
        vector[pl.ds(row + 1, 1), :] = value[:, LANES:]

    pixels = rows * width
    for which in range(3):
        load(which).wait()
    last_turned[...] = last[...].astype(jnp.float32).T.astype(low)
    d_active[...] = jnp.zeros_like(d_active)

    def one_head(index):
        lane = pl.ds(pl.multiple_of(index * depth, depth), depth)
        projected = mix(last[...], head[:, lane], 1, 0)
        projected += vector_lanes(vectors, layers * channels, index)
        gain = vector_lanes(vectors, layers * channels + heads * depth, index)
        gain_total = jnp.zeros((1, depth), jnp.float32)
        bias_total = jnp.zeros((1, depth), jnp.float32)
        rounded = []
        for row in range(rows):
            span = slice(row * width, (row + 1) * width)
            weight = weights_row[row]
            value = projected[span]
            inverse = lax.rsqrt(jnp.sum(value * value, -1, keepdims=True) + 1e-06)
            normed = value * inverse
            scaled = gain * weight
            term[span, lane] = (normed * scaled).astype(low)
            given = cotangent[span, lane].astype(jnp.float32)
            gain_total += jnp.sum(normed * given, 0, keepdims=True) * weight
            d_normed = given * scaled
            along = jnp.sum(normed * d_normed, -1, keepdims=True)
            d_low = (inverse * (d_normed - normed * along)).astype(low)
            bias_total += jnp.sum(d_low.astype(jnp.float32), 0, keepdims=True)
            rounded.append(d_low)
        term_step(0, index).start()
        put_vector(layers * channels + heads * depth, index, gain_total)
        put_vector(layers * channels, index, bias_total)
        d_low = jnp.concatenate(rounded, 0)
        grad = mix(last_turned[...], d_low, 1, 0)
        if spread_head:
            split = grad.reshape(2, 2, deep_count, 2, head_rows, depth)
            head_parts[:, :, :, :, :, lane] = split.astype(low)
        else:
            head_grad[:, lane] = grad.astype(low)
        d_active[...] += mix(d_low, head[:, lane], 1, 1)

        @pl.when(index > 0)
        def earlier():
            term_pair(index - 1)

    loop(heads, one_head)
    if spread_head:
        head_step(0).start()
    term_pair(heads - 1)

    def store(layer):
        slot = layer % 2
        return pltpu.make_async_copy(grads.at[slot], grads_out.at[layer], store_sem.at[slot])

    for layer in reversed(range(layers)):
        which = layers - 1 - layer
        for part in range(3):
            load(3 + 3 * which + part).wait()

        def enter(part):
            lane = pl.ds(spot(part), tile)
            total = jnp.zeros((1, tile), jnp.float32)
            for row in range(rows):
                span = slice(row * width, (row + 1) * width)
                slope = gelu_slope(hidden[layer, span, lane])
                value = slope * (masks[row] * d_active[span, lane])
                value = value.astype(low).astype(jnp.float32)
                total += jnp.sum(value, 0, keepdims=True)
                put(d_wide, row + 1, spot(part), tile, value)
            put_vector(layer * channels, part, total)

        loop(tiles, enter)
        send_edges(which, d_wide)
        if layer + 2 < layers:
            store(layer + 2).wait()

        def one_tap(tap):
            tap_row, tap_column = tap // TAPS, lax.rem(tap, TAPS)
            window = wide[
                layer,
                pl.ds(pl.multiple_of(tap_row * width, width), pixels),
                pl.ds(pl.multiple_of(tap_column * channels, channels), channels),
            ]
            d_hidden = d_wide[width : width + pixels, channels : 2 * channels]
            grads[layer % 2, pl.ds(pl.multiple_of(tap * channels, channels), channels), :] = mix(
                window, d_hidden, 0, 0
            ).astype(low)

        loop(TAPS * TAPS, one_tap)
        store(layer).start()
        head_next(layers - 1 - layer)
        if layer == 0:
            loop(heads, term_total)
        take_edges(which, d_wide)

        def back(part):
            total = jnp.zeros((pixels, tile), jnp.float32)
            for tap_row in range(TAPS):
                for tap_column in range(TAPS):
                    window = d_wide[
                        (2 - tap_row) * width : (2 - tap_row) * width + pixels,
                        (2 - tap_column) * channels : (3 - tap_column) * channels,
                    ]
                    first = (TAPS * tap_row + tap_column) * channels
                    total += mix(
                        window, weights[layer, pl.ds(first + spot(part), tile), :], 1, 1
                    )
            d_active[:, pl.ds(spot(part), tile)] = total

        loop(tiles, back)

    features_grad[...] = d_active[...].astype(low)
    head_end()
    loop(heads, term_end)
    for layer in range(min(layers, 2)):
        store(layer).wait()


def run_block(
    weights, head, wide, hidden, last, vectors, cotangent, valid, space_count
):
    rows, width, unused = cotangent.shape
    layers, unused, channels = weights.shape
    head_width = head.shape[1]
    pixels = rows * width
    deep_count = space_count // 2
    head_rows = channels // (4 * space_count)
    spread_head = head_rows % 16 == 0
    low, full = jnp.bfloat16, jnp.float32
    dims = (layers, rows, width, channels, NH, HD, space_count)
    vmem = pl.BlockSpec(memory_space=pltpu.VMEM)
    anywhere = pl.BlockSpec(memory_space=pl.ANY)
    head_scratch = []
    head_out = jax.ShapeDtypeStruct((channels, head_width), low)
    if spread_head:
        head_out = jax.ShapeDtypeStruct((head_rows * head_width // LANES, LANES), full)
        head_scratch = [
            pltpu.VMEM((2, 2, deep_count, 2, head_rows, head_width), low),
            pltpu.VMEM((2, deep_count, 2, head_rows, head_width), low),
            pltpu.VMEM((deep_count, head_rows, head_width), low),
            pltpu.VMEM((2, deep_count, head_rows, head_width), low),
            pltpu.VMEM((deep_count, head_rows, head_width), low),
            pltpu.SemaphoreType.DMA((2 + deep_count,)),
            pltpu.SemaphoreType.DMA((2 + deep_count,)),
        ]
    outs = pl.pallas_call(
        partial(work_kernel, dims),
        out_shape=(
            jax.ShapeDtypeStruct((pixels, head_width), low),
            jax.ShapeDtypeStruct((pixels, channels), low),
            jax.ShapeDtypeStruct(weights.shape, low),
            head_out,
            jax.ShapeDtypeStruct(vectors.shape, full),
        ),
        in_specs=[
            anywhere,
            anywhere,
            anywhere,
            anywhere,
            anywhere,
            vmem,
            anywhere,
            pl.BlockSpec(memory_space=pltpu.SMEM),
        ],
        out_specs=[vmem, vmem, anywhere, vmem, vmem],
        scratch_shapes=[
            pltpu.VMEM(weights.shape, low),
            pltpu.VMEM(head.shape, low),
            pltpu.VMEM((pixels, head_width), low),
            pltpu.VMEM((layers, (rows + 2) * width, TAPS * channels), low),
            pltpu.VMEM((layers, pixels, channels), full),
            pltpu.VMEM((pixels, channels), low),
            pltpu.VMEM((channels, pixels), low),
            pltpu.VMEM(((rows + 2) * width, TAPS * channels), low),
            pltpu.VMEM((pixels, channels), full),
            pltpu.VMEM((2,) + weights.shape[1:], low),
            pltpu.VMEM((layers, 2, width, channels), low),
            pltpu.VMEM((pixels, head_width), low),
            pltpu.VMEM((2, NH, pixels, LANES), low),
            pltpu.SemaphoreType.DMA((3 * layers + 3,)),
            pltpu.SemaphoreType.DMA((2,)),
            pltpu.SemaphoreType.DMA((layers, 2)),
            pltpu.SemaphoreType.DMA((layers, 2)),
            pltpu.SemaphoreType.DMA((3, NH)),
            pltpu.SemaphoreType.DMA((3, NH)),
        ]
        + head_scratch,
        compiler_params=pltpu.CompilerParams(
            collective_id=2, has_side_effects=True, vmem_limit_bytes=VMEM_LIMIT
        ),
    )(
        weights,
        head,
        wide,
        hidden,
        last,
        vectors,
        cotangent.reshape(pixels, head_width),
        valid,
    )
    merged, features_grad, grads, head_grad, vector = outs
    if not spread_head:
        head_grad = lax.psum_scatter(
            head_grad.astype(full).reshape(-1), ("scale", "space"), scatter_dimension=0, tiled=True
        ).reshape(-1, LANES)
    return (merged, features_grad, grads, head_grad, vector)


def halves(value):
    high = value.astype(jnp.bfloat16)
    return (high, (value - high.astype(jnp.float32)).astype(jnp.bfloat16))


def dot(left, right, left_dim, right_dim):
    left_high, left_low = halves(left)
    right_high, right_low = halves(right)
    rest = mix(left_high, right_low, left_dim, right_dim) + mix(left_low, right_high, left_dim, right_dim)
    return mix(left_high, right_high, left_dim, right_dim) + rest


def quick(x):
    return pl.reciprocal(x,approx=True)
def eliminate(blocks, off, size, m=8):
    nl=len(blocks); nb=size//8; W=blocks[0][0].shape[1]
    sub=lax.broadcasted_iota(jnp.int32,(8,128),0)
    for k0 in range(0,size,m):
        b0=k0//8; s0=k0%8
        for l in range(nl):
            bl=blocks[l]
            top=bl[b0]
            def colb(b,j):
                return jnp.broadcast_to(bl[b][:,off+k0+j:off+k0+j+1],(8,128))
            c0=[colb(b0,j) for j in range(m)]
            a=[[None]*m for _ in range(m)]
            for j in range(m):
                for i in range(j,m):
                    a[i][j]=jnp.broadcast_to(c0[j][s0+i:s0+i+1,:],(8,128))
            inv=[]; low=[[None]*m for _ in range(m)]
            for k in range(m):
                r=quick(a[k][k]); inv.append(r)
                for i in range(k+1,m):
                    low[i][k]=a[i][k]*r
                for j in range(k+1,m):
                    for i in range(j,m):
                        a[i][j]=a[i][j]-low[i][k]*a[j][k]
            wid=lambda v: jnp.concatenate([v]*(W//128),1)
            rows=[jnp.broadcast_to(top[s0+i:s0+i+1,:],(8,W)) for i in range(m)]
            for i in range(m):
                for k in range(i):
                    rows[i]=rows[i]-wid(low[i][k])*rows[k]
            for b in range(b0,nb):
                if b==b0 and s0+m==8 and m==1: continue
                cs=list(c0) if b==b0 else [colb(b,j) for j in range(m)]
                for j in range(m):
                    for k in range(j):
                        cs[j]=cs[j]-low[j][k]*cs[k]
                acc=bl[b]
                for k in range(m):
                    w=cs[k]*inv[k]
                    if b==b0: w=jnp.where(sub>s0+k,w,0.0)
                    acc=acc-wid(w)*rows[k]
                bl[b]=acc
    out=[]
    lane=lax.broadcasted_iota(jnp.int32,(8,W),1)
    row8=lax.broadcasted_iota(jnp.int32,(8,W),0)
    for l in range(nl):
        res=[]
        for b in range(nb):
            v=blocks[l][b]
            d=jnp.sum(jnp.where(lane==row8+(off+8*b),v,0.0),1,keepdims=True)
            res.append(v*lax.rsqrt(d))
        out.append(jnp.concatenate(res,0))
    return out


def moments(grads, first, second):
    first_new = BETA_ONE * first + (1.0 - BETA_ONE) * grads
    second_new = BETA_TWO * second + (1.0 - BETA_TWO) * grads * grads
    direction = (
        first_new
        * (1.0 / (1.0 - BETA_ONE**STEP))
        / (jnp.sqrt(second_new * (1.0 / (1.0 - BETA_TWO**STEP))) + EPSILON)
    )
    return (first_new, second_new, direction)


def update_kernel(
    dims,
    *refs,
):
    moved = dims[4]
    inputs, outputs = refs[: moved + 11], refs[moved + 11 : -1 - moved]
    held = refs[-1 - moved : -1]
    update_body(
        dims, inputs[:moved], outputs[:moved], held, refs[-1], *inputs[moved:], *outputs[moved:]
    )


def update_body(
    dims,
    moved_in,
    moved_out,
    held,
    moved_sem,
    summed,
    statistics,
    bases,
    head_grad,
    head_first,
    head_second,
    head_master,
    vector_grad,
    vector_first,
    vector_second,
    vectors,
    stats_new,
    bases_new,
    head_first_new,
    head_second_new,
    head_new,
    vector_first_new,
    vector_second_new,
    vectors_new,
    system,
    pivot_high,
    pivot_rest,
):
    layers, channels, bias_rows, panel, moved = dims
    block = LANES

    def take(which):
        return pltpu.make_async_copy(moved_in[which], held[which], moved_sem.at[0, which])

    def give(which):
        return pltpu.make_async_copy(held[which], moved_out[which], moved_sem.at[1, which])

    for which in range(moved):
        take(which).start()

    for layer in range(layers):
        fresh = BETA_TWO * statistics[layer] + (1.0 - BETA_TWO) * summed[layer].astype(jnp.float32)
        stats_new[layer] = fresh
        turned = dot(bases[layer], fresh, 0, 0)
        system[layer, :, channels : 2 * channels] = turned
        system[layer, :, 0:channels] = dot(turned, turned, 1, 1)

    head = moments(head_grad[...], head_first[...], head_second[...])
    head_first_new[...] = head[0]
    head_second_new[...] = head[1]
    head_new[...] = head_master[...] - RATE_HEAD * (head[2] + DECAY * head_master[...])
    vec = moments(vector_grad[...], vector_first[...], vector_second[...])
    vector_first_new[...] = vec[0]
    vector_second_new[...] = vec[1]
    row = lax.broadcasted_iota(jnp.int32, vectors.shape, 0)
    rates = jnp.where(row < bias_rows, RATE_BIAS, RATE_GAIN)
    vectors_new[...] = vectors[...] - rates * (vec[2] + DECAY * vectors[...])

    for which in range(moved):
        take(which).wait()
        give(which).start()
    eye = (
        lax.broadcasted_iota(jnp.int32, (block, block), 0)
        == lax.broadcasted_iota(jnp.int32, (block, block), 1)
    ).astype(jnp.float32)

    def outer(k, carry):
        here = pl.ds(pl.multiple_of(k * block, block), block)
        panels = [jnp.concatenate([system[layer, here, here], eye], 1) for layer in range(layers)]
        done = [[] for _ in range(layers)]
        for j in range(block // panel):
            blocks = [[p[8 * i : 8 * i + 8] for i in range(panel // 8)] for p in panels]
            tops = eliminate(blocks, panel * j, panel)
            for layer in range(layers):
                done[layer].append(tops[layer][:, block:])
                if j < block // panel - 1:
                    panels[layer] = panels[layer][panel:] - dot(
                        tops[layer][:, panel * (j + 1) : block], tops[layer], 0, 0
                    )
        half = channels // 2
        spans = (slice(0, half), slice(half, channels), slice(channels, 2 * channels))
        after = (k + 1) * block
        split_inverse = [halves(jnp.concatenate(parts, 0)) for parts in done]

        def eliminated(span):
            for layer in range(layers):
                high, rest = split_inverse[layer]
                right_high, right_rest = halves(system[layer, here, span])
                value = mix(high, right_high, 1, 0) + (
                    mix(high, right_rest, 1, 0) + mix(rest, right_high, 1, 0)
                )
                pivot_high[layer, :, span], pivot_rest[layer, :, span] = halves(value)
                if span is spans[2]:
                    system[layer, here, span] = value

        eliminated(spans[2])

        @pl.when(after < channels)
        def right_half():
            eliminated(spans[1])

        @pl.when(after < half)
        def left_half():
            eliminated(spans[0])

        def inner(i, carry_in):
            below = pl.ds(pl.multiple_of(i * block, block), block)

            def subtract(span):
                for layer in range(layers):
                    left_high, left_rest = pivot_high[layer, :, below], pivot_rest[layer, :, below]
                    right_high, right_rest = pivot_high[layer, :, span], pivot_rest[layer, :, span]
                    system[layer, below, span] -= mix(left_high, right_high, 0, 0) + (
                        mix(left_high, right_rest, 0, 0) + mix(left_rest, right_high, 0, 0)
                    )

            subtract(slice(half, 2 * channels))

            @pl.when(i * block < half)
            def left_half():
                subtract(spans[0])

            return carry_in

        lax.fori_loop(k + 1, channels // block, inner, 0)
        return carry

    lax.fori_loop(0, channels // block, outer, 0)
    for layer in range(layers):
        bases_new[layer] = system[layer, :, channels : 2 * channels].T
    for which in range(moved):
        give(which).wait()


def update(arrays, summed, statistics, bases, head, vector, bias_rows):
    layers, channels, unused = statistics.shape
    dims = (layers, channels, bias_rows, 32, len(arrays))
    anywhere = pl.BlockSpec(memory_space=pl.ANY)
    vmem = pl.BlockSpec(memory_space=pltpu.VMEM)
    square = jax.ShapeDtypeStruct(statistics.shape, jnp.float32)
    head_shape = jax.ShapeDtypeStruct(head[0].shape, jnp.float32)
    vector_shape = jax.ShapeDtypeStruct(vector[0].shape, jnp.float32)
    return pl.pallas_call(
        partial(update_kernel, dims),
        out_shape=tuple(jax.ShapeDtypeStruct(array.shape, array.dtype) for array in arrays)
        + (square,) * 2 + (head_shape,) * 3 + (vector_shape,) * 3,
        in_specs=[anywhere] * len(arrays) + [vmem] * 11,
        out_specs=[anywhere] * len(arrays) + [vmem] * 8,
        scratch_shapes=[
            pltpu.VMEM((layers, channels, 2 * channels), jnp.float32),
            pltpu.VMEM((layers, LANES, 2 * channels), jnp.bfloat16),
            pltpu.VMEM((layers, LANES, 2 * channels), jnp.bfloat16),
        ]
        + [pltpu.VMEM(array.shape, array.dtype) for array in arrays]
        + [pltpu.SemaphoreType.DMA((2, len(arrays)))],
        compiler_params=pltpu.CompilerParams(vmem_limit_bytes=VMEM_LIMIT),
        cost_estimate=pl.CostEstimate(
            flops=10**10, bytes_accessed=2 * 10**7, transcendentals=10**4
        ),
    )(*arrays, summed, statistics, bases, *head, *vector)


def local(
    features,
    valid_rows,
    conv_master,
    head_master,
    vectors,
    conv_first,
    conv_second,
    head_first,
    head_second,
    vec_first,
    vec_second,
    statistics,
    bases,
    cotangent,
):
    channels = features.shape[3]
    head_width = cotangent.shape[2]
    space_count = lax.axis_size("space")
    vectors, vec_first, vec_second, head_master, head_first, head_second = (
        array.reshape(-1, LANES)
        for array in (vectors, vec_first, vec_second, head_master, head_first, head_second)
    )
    conv_used, head_used, wide, hidden, last = gather_weights(
        conv_master, head_master, head_width, features[0], vectors, valid_rows, space_count
    )
    merged, features_grad, grads, owned_head, vector = run_block(
        conv_used,
        head_used,
        wide,
        hidden,
        last,
        vectors,
        cotangent,
        valid_rows,
        space_count,
    )
    summed_stats, grad_vec, conv_new = reduce_grads(
        grads, vector, bases, (conv_first, conv_second, conv_master), space_count
    )
    moved = (merged, features_grad, *conv_new)
    outs = update(
        moved,
        summed_stats,
        statistics,
        bases,
        (owned_head, head_first, head_second, head_master),
        (grad_vec, vec_first, vec_second, vectors),
        (3 * channels + head_width) // LANES,
    )
    merged, features_grad, *conv_new = outs[:5]
    stats_new, bases_new = outs[5:7]
    return (
        merged.reshape(cotangent.shape),
        features_grad.reshape(features.shape),
        *conv_new,
        *(out.reshape(-1) for out in outs[7:]),
        stats_new,
        bases_new,
    )


def solution(mesh):
    in_specs = (
        P("scale", "space", None, None),
        P(),
        P(None, "space", None),
        P(("scale", "space")),
        P(),
        P(None, "space", None),
        P(None, "space", None),
        P(("scale", "space")),
        P(("scale", "space")),
        P(),
        P(),
        P(),
        P(),
        P("space", None, None),
    )
    out_specs = (
        P("space", None, None),
        P("scale", "space", None, None),
        P(None, "space", None),
        P(None, "space", None),
        P(None, "space", None),
        P(("scale", "space")),
        P(("scale", "space")),
        P(("scale", "space")),
        P(),
        P(),
        P(),
        P(),
        P(),
    )
    return jax.shard_map(local, mesh=mesh, in_specs=in_specs, out_specs=out_specs, check_vma=False)
```

```python
from functools import partial

import jax
import jax.experimental.pallas as pl
import jax.experimental.pallas.tpu as pltpu
import jax.numpy as jnp
from jax import lax
from jax.sharding import PartitionSpec as P

NH = 7
HD = 256
STEP = 5


BETA_ONE = 0.9
BETA_TWO = 0.95
EPSILON = 1e-08
DECAY = 0.01
RATE_CONV = 0.04
RATE_HEAD = 0.08
RATE_BIAS = 0.5
RATE_GAIN = 20.0
VMEM_LIMIT = 60 * 2**20
GELU_SCALE = 0.7978845608028654
GELU_CUBE = 0.044715


MESH = pl.DeviceIdType.MESH
LANES = 128


def place():
    scale, space = lax.axis_index("scale"), lax.axis_index("space")
    across, core = scale // 2, lax.rem(scale, 2)
    deep, side = space // 2, lax.rem(space, 2)
    return (across, core, deep, side)


def at(across, core, deep, side):
    return (2 * across + core, 2 * deep + side)


def greet(peers):
    barrier = pltpu.get_barrier_semaphore()
    for peer in peers:
        pl.semaphore_signal(barrier, inc=1, device_id=peer, device_id_type=MESH)
    pl.semaphore_wait(barrier, len(peers))


def remote(source, target, send, receive, device):
    return pltpu.make_async_remote_copy(
        src_ref=source,
        dst_ref=target,
        send_sem=send,
        recv_sem=receive,
        device_id=device,
        device_id_type=MESH,
    )


def lanes(index, count=1):
    return pl.ds(pl.multiple_of(index * LANES, LANES), count * LANES)


def nearest(deep, deep_count, index):
    left, right = deep, deep_count - 1 - deep
    short = jnp.minimum(left, right)
    both = (index + 1) // 2 * (2 * lax.rem(index, 2) - 1)
    one = (index - short) * jnp.where(left < right, 1, -1)
    return deep + jnp.where(index <= 2 * short, both, one)


def partners(deep_count):
    across, core, deep, side = place()
    peers = [
        at(across, 1 - core, deep, side),
        at(1 - across, core, deep, side),
        at(across, core, deep, 1 - side),
    ]
    peers += [
        at(across, core, lax.rem(deep + hop, deep_count), side) for hop in range(1, deep_count)
    ]
    return peers


TAPS = 3


def gelu_parts(value):
    inner = GELU_SCALE * (value + GELU_CUBE * value * value * value)
    return jnp.tanh(inner)


def gelu_value(value):
    return 0.5 * value * (1.0 + gelu_parts(value))


def gelu_slope(value):
    bend = gelu_parts(value)
    rise = GELU_SCALE * (1.0 + 3.0 * GELU_CUBE * value * value)
    return 0.5 * (1.0 + bend) + 0.5 * value * (1.0 - bend * bend) * rise


def mix(left, right, left_dim, right_dim):
    return lax.dot_general(
        left,
        right,
        (((left_dim,), (right_dim,)), ((), ())),
        preferred_element_type=jnp.float32,
    )


def row_weights(valid, rows):
    scale, space = lax.axis_index("scale"), lax.axis_index("space")
    scales = lax.axis_size("scale")
    masks, weights = [], []
    for row in range(rows):
        place_in = space * rows + row
        mask = jnp.where(place_in < valid[scale], 1.0, 0.0)
        count = jnp.float32(0.0)
        for other in range(scales):
            count += jnp.where(place_in < valid[other], 1.0, 0.0)
        masks.append(mask)
        weights.append(jnp.full((1, LANES), mask) / jnp.full((1, LANES), count))
    return (masks, [weight[:, :1] for weight in weights])


def vector_lanes(vectors, start, part):
    row = start // LANES + 2 * part
    return jnp.concatenate([vectors[pl.ds(row, 1), :], vectors[pl.ds(row + 1, 1), :]], 1)


def greet_edges(peers, space_count):
    barrier = pltpu.get_barrier_semaphore()
    scale, space = lax.axis_index("scale"), lax.axis_index("space")
    for peer in peers:
        pl.semaphore_signal(barrier, inc=1, device_id=peer, device_id_type=MESH)
    next_space = space - 1 + 2 * lax.rem(space, 2)
    has_next = jnp.logical_and(next_space >= 0, next_space < space_count)

    @pl.when(has_next)
    def greet_next():
        pl.semaphore_signal(barrier, inc=1, device_id=(scale, next_space), device_id_type=MESH)

    pl.semaphore_wait(barrier, len(peers) + has_next.astype(jnp.int32))


def edge_tools(dims, halo, send_sem, receive_sem):
    rows, width, channels, space_count = dims[1], dims[2], dims[3], dims[6]
    tile = 2 * LANES
    tiles = channels // tile
    scale, space = lax.axis_index("scale"), lax.axis_index("space")
    above, below = space > 0, space < space_count - 1
    low = jnp.bfloat16

    def up(which, source):
        return remote(
            source,
            halo.at[which, 1],
            send_sem.at[which, 0],
            receive_sem.at[which, 1],
            (scale, space - 1),
        )

    def down(which, source):
        return remote(
            source,
            halo.at[which, 0],
            send_sem.at[which, 1],
            receive_sem.at[which, 0],
            (scale, space + 1),
        )

    def edge(array, row):
        return array.at[pl.ds((row + 1) * width, width), pl.ds(channels, channels)]

    def send_edges(which, array):
        @pl.when(above)
        def go_up():
            up(which, edge(array, 0)).start()

        @pl.when(below)
        def go_down():
            down(which, edge(array, rows - 1)).start()

    column = lax.broadcasted_iota(jnp.int32, (width, 1), 0)

    def put(array, slot, lane, count, value):
        here = pl.ds(slot * width, width)
        left = jnp.where(column == 0, 0.0, pltpu.roll(value, 1, 0))
        right = jnp.where(column == width - 1, 0.0, pltpu.roll(value, width - 1, 0))
        for which, moved in enumerate((left, value, right)):
            start = pl.multiple_of(which * channels + lane, LANES)
            array[here, pl.ds(start, count)] = moved.astype(low)

    def take_edges(which, array):
        for side, present, slot in ((0, above, 0), (1, below, rows + 1)):

            @pl.when(present)
            def arrived():
                if side == 0:
                    up(which, edge(array, 0)).wait_send()
                    down(which, edge(array, 0)).wait_recv()
                else:
                    down(which, edge(array, 0)).wait_send()
                    up(which, edge(array, 0)).wait_recv()
                for part in range(tiles):
                    value = halo[which, side, :, part * tile : (part + 1) * tile]
                    put(array, slot, part * tile, tile, value.astype(jnp.float32))

            @pl.when(jnp.logical_not(present))
            def missing():
                array[pl.ds(slot * width, width), :] = jnp.zeros(
                    (width, TAPS * channels), low
                )

    return (send_edges, take_edges, put)


def gather_kernel(
    dims,
    master_in,
    head_master,
    features,
    vectors,
    valid,
    full,
    head_full,
    wide_out,
    hidden_out,
    last_out,
    own,
    head_own,
    weights,
    wide,
    hidden,
    last,
    halo,
    local_sem,
    sends,
    receives,
    head_sends,
    head_receives,
    load_sem,
    store_sem,
    edge_sends,
    edge_receives,
    master,
    master_sem,
):
    layers, rows, width, channels, heads, depth, space_count = dims
    deep_count = space_count // 2
    across, core, deep, side = place()
    block = 2 * core + across
    low = jnp.bfloat16

    def fetch(layer):
        return pltpu.make_async_copy(
            master_in.at[layer], master.at[layer], master_sem.at[layer]
        )

    for layer in range(layers):
        fetch(layer).start()
    fetch(0).wait()
    own[0] = master[0].astype(low)
    greet_edges(partners(deep_count), space_count)

    chunks = layers * deep_count

    def by_distance(index):
        return nearest(deep, deep_count, index)

    def split(chunk):
        rest = chunk - layers
        is_own = chunk < layers
        layer = jnp.where(is_own, chunk, rest // (deep_count - 1))
        hop = jnp.where(is_own, 0, 1 + lax.rem(rest + chunks, deep_count - 1))
        layer, hop = jnp.clip(layer, 0, layers - 1), jnp.clip(hop, 0, deep_count - 1)
        source = by_distance(hop)
        odd = jnp.where(is_own, 0, lax.rem(chunk, 2))
        return (layer, hop, source, odd)

    def first(layer, index):
        piece = own.at[layer, :, lanes(block)]
        target = full.at[layer, deep, side, :, lanes(block)]
        there = by_distance(index)
        to = at(across, core, there, side)
        return remote(piece, target, sends.at[0, layer, there], receives.at[0, layer, deep], to)

    def first_in(layer, index):
        source = by_distance(index)
        piece = full.at[layer, source, side, :, lanes(block)]
        return remote(
            piece,
            piece,
            sends.at[0, layer, source],
            receives.at[0, layer, source],
            at(across, core, source, side),
        )

    def second(chunk, incoming):
        layer, hop, source, odd = split(chunk)
        there_side = lax.rem(side + 1 - odd, 2)
        there_across = lax.rem(across + odd, 2)
        to = at(there_across, core, deep, there_side)
        if incoming:
            piece = full.at[layer, source, there_side, :, lanes(2 * core + there_across)]
        else:
            piece = full.at[layer, source, side, :, lanes(block)]
        return remote(piece, piece, sends.at[1, layer, hop], receives.at[1, layer, hop], to)

    def third(chunk, half, incoming):
        layer, hop, source, odd = split(chunk)
        there_side = lax.rem(side + odd, 2)
        there_across = lax.rem(across + 1 - odd, 2)
        to = at(there_across, core, deep, there_side)
        here = there_side if incoming else side
        lane = there_across if incoming else across
        piece_side = (1 - odd) * half + odd * here
        piece_lane = 2 * core + (1 - odd) * lane + odd * half
        piece = full.at[layer, source, piece_side, :, lanes(piece_lane)]
        return remote(
            piece, piece, sends.at[2 + half, layer, hop], receives.at[2 + half, layer, hop], to
        )

    def fourth(chunk, incoming):
        layer, hop, source, odd = split(chunk)
        column = 1 - core if incoming else core
        piece = full.at[layer, source, :, :, lanes(2 * column, 2)]
        to = at(across, 1 - core, deep, side)
        return remote(piece, piece, sends.at[4, layer, hop], receives.at[4, layer, hop], to)

    def own_fourth(layer, incoming):
        column = 1 - core if incoming else core
        piece = full.at[layer, deep, 1 - side, :, lanes(2 * column, 2)]
        to = at(across, 1 - core, deep, side)
        return remote(piece, piece, sends.at[4, layer, 0], receives.at[4, layer, 0], to)

    def local(layer):
        return pltpu.make_async_copy(
            own.at[layer], full.at[layer, deep, side], local_sem.at[layer]
        )

    def each(low, action):
        def step(hop, carry):
            action(hop)
            return carry

        lax.fori_loop(low, deep_count, step, 0)

    def head_local():
        return pltpu.make_async_copy(
            head_own, head_full.at[across, core, deep, side], local_sem.at[layers]
        )

    def head_first(hop):
        to = at(across, core, lax.rem(deep + hop, deep_count), side)
        target = head_full.at[across, core, deep, side]
        return remote(head_own, target, head_sends.at[hop], head_receives.at[hop], to)

    def head_first_in(hop):
        piece = head_full.at[across, core, lax.rem(deep - hop + deep_count, deep_count), side]
        to = at(across, core, deep, side)
        return remote(piece, piece, head_sends.at[hop], head_receives.at[hop], to)

    def head_next(which, incoming):
        if which == 0:
            to = at(across, core, deep, 1 - side)
            piece = head_full.at[across, core, :, 1 - side if incoming else side]
        elif which == 1:
            to = at(1 - across, core, deep, side)
            piece = head_full.at[1 - across if incoming else across, core]
        else:
            to = at(across, 1 - core, deep, side)
            piece = head_full.at[:, 1 - core if incoming else core]
        slot = deep_count + which
        return remote(piece, piece, head_sends.at[slot], head_receives.at[slot], to)

    def go_head(which):
        if which == 0:
            head_local().wait()
            each(1, lambda hop: head_first_in(hop).wait_recv())
        else:
            head_next(which - 1, True).wait_recv()
        if which < 3:
            head_next(which, False).start()

    send_edges, take_edges, put = edge_tools(dims, halo, edge_sends, edge_receives)
    tile = 2 * LANES
    tiles = channels // tile
    pixels = rows * width
    band = TAPS * channels
    masks, unused = row_weights(valid, rows)
    share = band * TAPS // space_count

    def loop(count, action):
        def body(index, carry):
            action(index)
            return carry

        lax.fori_loop(0, count, body, 0)

    def spot(index):
        return pl.multiple_of(index * tile, tile)

    def load(layer, owner):
        start = pl.multiple_of(owner * share, 8)
        return pltpu.make_async_copy(
            full.at[layer, owner // 2, lax.rem(owner, 2)],
            weights.at[layer % 2, pl.ds(start, share)],
            load_sem.at[layer % 2, owner],
        )

    def arrive(layer):
        own_fourth(layer, True).wait_recv()
        begin = layers + layer * (deep_count - 1)
        loop(deep_count - 1, lambda index: fourth(begin + index, True).wait_recv())
        loop(space_count, lambda owner: load(layer, owner).start())

    def store(which, layer):
        source, target = (
            (wide.at[layer], wide_out.at[layer]),
            (hidden.at[layer], hidden_out.at[layer]),
            (last, last_out),
        )[which]
        return pltpu.make_async_copy(source, target, store_sem.at[which, layer])

    def forward(layer):
        here = wide.at[layer]
        take_edges(layer, here)
        store(0, layer).start()
        loop(space_count, lambda owner: load(layer, owner).wait())

        def outer(part):
            lane = pl.ds(spot(part), tile)
            total = vector_lanes(vectors, layer * channels, part)
            for tap_row in range(TAPS):
                total += mix(
                    here[tap_row * width : tap_row * width + pixels, :],
                    weights[layer % 2, tap_row * band : (tap_row + 1) * band, lane],
                    1,
                    0,
                )
            hidden[layer, :, lane] = total
            for row in range(rows):
                span = slice(row * width, (row + 1) * width)
                value = gelu_value(hidden[layer, span, lane]) * masks[row]
                if layer < layers - 1:
                    put(wide.at[layer + 1], row + 1, spot(part), tile, value)
                else:
                    last[span, lane] = value.astype(low)

        loop(tiles, outer)
        store(1, layer).start()
        if layer < layers - 1:
            send_edges(layer + 1, wide.at[layer + 1])

    def go_second(chunk):
        layer, hop, source, odd = split(chunk)

        @pl.when(hop == 0)
        def own_rows():
            local(layer).wait()

        @pl.when(hop > 0)
        def other_rows():
            first_in(layer, hop).wait_recv()
            go_first(chunk - layers + z_ahead)

        second(chunk, False).start()

    def go_third(chunk):
        second(chunk, True).wait_recv()

        @pl.when(chunk < layers)
        def own_rows():
            third(chunk, 1 - side, False).start()

        @pl.when(chunk >= layers)
        def other_rows():
            third(chunk, 0, False).start()
            third(chunk, 1, False).start()

    def go_fourth(chunk):
        @pl.when(chunk < layers)
        def own_rows():
            third(chunk, 1 - side, True).wait_recv()
            own_fourth(chunk, False).start()

        @pl.when(chunk >= layers)
        def other_rows():
            third(chunk, 0, True).wait_recv()
            third(chunk, 1, True).wait_recv()
            fourth(chunk, False).start()

    def go_head_first():
        each(1, lambda hop: head_first(hop).start())

    def go_first(index):
        @pl.when(index < layers * (deep_count - 1))
        def more():
            first(index // (deep_count - 1), 1 + lax.rem(index, deep_count - 1)).start()

    z_ahead = 2
    for index in range(min(z_ahead, deep_count - 1)):
        go_first(index)
    local(0).start()
    go_second(0)
    for layer in range(1, layers):
        fetch(layer).wait()
        own[layer] = master[layer].astype(low)
        local(layer).start()
    head_rows, head_blocks = head_own.shape[0], heads * depth // LANES
    for lane in range(head_blocks):
        head_own[:, lane * LANES : (lane + 1) * LANES] = head_master[
            pl.ds(lane, head_rows, stride=head_blocks), :
        ].astype(low)
    head_local().start()
    for row in range(rows):
        for part in range(tiles):
            value = features[row * width : (row + 1) * width, part * tile : (part + 1) * tile]
            put(wide.at[0], row + 1, part * tile, tile, value.astype(jnp.float32))
    send_edges(0, wide.at[0])

    lag_third, lag_fourth = 2, 4
    others = deep_count - 1

    def last_of(layer):
        return layers + others * (layer + 1) - 1 + lag_fourth

    early = min(2, others)
    timed = [(layers + early, go_head_first)]
    timed += [(layers + others + 2 * which, go_head, which) for which in range(3)]
    for layer in range(layers - 1):
        timed += [(last_of(layer) + 1, arrive, layer), (last_of(layer) + 2, forward, layer)]

    def turn(now):
        for lag, action in ((0, go_second), (lag_third, go_third), (lag_fourth, go_fourth)):
            begin = max(lag, 1)

            @pl.when(jnp.logical_and(now >= begin, now < chunks + lag))
            def stage():
                action(now - lag)

        for moment, action, *which in timed:

            @pl.when(now == moment)
            def once():
                action(*which)

    loop(chunks + lag_fourth, turn)
    go_head(3)
    arrive(layers - 1)
    forward(layers - 1)
    store(2, 0).start()

    def finish(chunk):
        second(chunk, False).wait_send()

        @pl.when(chunk < layers)
        def own_rows():
            third(chunk, 1 - side, False).wait_send()
            own_fourth(chunk, False).wait_send()

        @pl.when(chunk >= layers)
        def other_rows():
            third(chunk, 0, False).wait_send()
            third(chunk, 1, False).wait_send()
            fourth(chunk, False).wait_send()

    loop(chunks, finish)
    each(1, lambda hop: head_first(hop).wait_send())
    for which in range(3):
        head_next(which, False).wait_send()

    for layer in range(layers):

        each(1, lambda hop: first(layer, hop).wait_send())
        store(0, layer).wait()
        store(1, layer).wait()
    store(2, 0).wait()


def gather_weights(master, head_master, head_width, features, vectors, valid, space_count):
    layers, share, channels = master.shape
    rows, width, unused = features.shape
    deep_count = space_count // 2
    pixels = rows * width
    dims = (layers, rows, width, channels, NH, HD, space_count)
    low, wide_float = jnp.bfloat16, jnp.float32
    anywhere = pl.BlockSpec(memory_space=pl.ANY)
    vmem = pl.BlockSpec(memory_space=pltpu.VMEM)
    head_own = (head_master.shape[0] * LANES // head_width, head_width)
    head_shape = (2, 2, deep_count, 2) + head_own
    wide_shape = (layers, (rows + 2) * width, TAPS * channels)
    full, head_full, wide, hidden, last = pl.pallas_call(
        partial(gather_kernel, dims),
        out_shape=(
            jax.ShapeDtypeStruct((layers, deep_count, 2, share, channels), low),
            jax.ShapeDtypeStruct(head_shape, low),
            jax.ShapeDtypeStruct(wide_shape, low),
            jax.ShapeDtypeStruct((layers, pixels, channels), wide_float),
            jax.ShapeDtypeStruct((pixels, channels), low),
        ),
        in_specs=[anywhere] + [vmem] * 3 + [pl.BlockSpec(memory_space=pltpu.SMEM)],
        out_specs=[anywhere] * 5,
        scratch_shapes=[
            pltpu.VMEM(master.shape, low),
            pltpu.VMEM(head_own, low),
            pltpu.VMEM((2, space_count * share, channels), low),
            pltpu.VMEM(wide_shape, low),
            pltpu.VMEM((layers, pixels, channels), wide_float),
            pltpu.VMEM((pixels, channels), low),
            pltpu.VMEM((layers, 2, width, channels), low),
            pltpu.SemaphoreType.DMA((layers + 1,)),
            pltpu.SemaphoreType.DMA((5, layers, deep_count)),
            pltpu.SemaphoreType.DMA((5, layers, deep_count)),
            pltpu.SemaphoreType.DMA((deep_count + 3,)),
            pltpu.SemaphoreType.DMA((deep_count + 3,)),
            pltpu.SemaphoreType.DMA((2, space_count)),
            pltpu.SemaphoreType.DMA((3, layers)),
            pltpu.SemaphoreType.DMA((layers, 2)),
            pltpu.SemaphoreType.DMA((layers, 2)),
            pltpu.VMEM(master.shape, wide_float),
            pltpu.SemaphoreType.DMA((layers,)),
        ],
        compiler_params=pltpu.CompilerParams(
            collective_id=0, has_side_effects=True, vmem_limit_bytes=VMEM_LIMIT
        ),
    )(master, head_master, features.reshape(pixels, channels), vectors, valid)
    return (
        full.reshape(layers, space_count * share, channels),
        head_full.reshape(-1, head_width),
        wide,
        hidden,
        last,
    )


def reduce_kernel(
    layers,
    deep_count,
    grads,
    vector,
    bases,
    first_in,
    second_moment_in,
    master_in,
    total,
    stats,
    vector_total,
    first_out,
    second_out,
    master_out,
    mine,
    core_in,
    second_in,
    kept,
    third_in,
    last,
    last_in,
    acc,
    stat_own,
    stat_in,
    stat_deep,
    vector_out,
    vector_in,
    vector_deep,
    moment_one,
    moment_two,
    master,
    local_sem,
    sends,
    receives,
    stat_sends,
    stat_receives,
    deep_sends,
    deep_receives,
    vector_sends,
    vector_receives,
    state_loads,
    state_stores,
):
    across, core, deep, side = place()
    block = 2 * core + across
    steps = layers * deep_count

    def split(step):
        layer, hop = step // deep_count, deep_count - 1 - lax.rem(step, deep_count)
        return (layer, hop, nearest(deep, deep_count, hop), lax.rem(step, 2))

    def first(step):
        layer, hop, target, odd = split(step)
        return remote(
            grads.at[layer, target, :, :, lanes(2 * (1 - core), 2)],
            core_in.at[step],
            sends.at[0, step],
            receives.at[0, step],
            at(across, 1 - core, deep, side),
        )

    def load(step):
        layer, hop, target, odd = split(step)
        return pltpu.make_async_copy(
            grads.at[layer, target, :, :, lanes(2 * core, 2)], mine.at[step], local_sem.at[step]
        )

    def second(step, half):
        layer, hop, target, odd = split(step)
        piece_side = (1 - odd) * half + odd * (1 - side)
        piece_lane = (1 - odd) * (1 - across) + odd * half
        to = at(lax.rem(across + 1 - odd, 2), core, deep, lax.rem(side + odd, 2))
        return remote(
            mine.at[step, piece_side, :, lanes(piece_lane)],
            second_in.at[step, half],
            sends.at[1 + half, step],
            receives.at[1 + half, step],
            to,
        )

    def third(step):
        layer, hop, target, odd = split(step)
        keep = (1 - odd) * side + odd * across
        to = at(lax.rem(across + odd, 2), core, deep, lax.rem(side + 1 - odd, 2))
        return remote(
            kept.at[step, 1 - keep],
            third_in.at[step],
            sends.at[3, step],
            receives.at[3, step],
            to,
        )

    def fourth(step):
        layer, hop, target, odd = split(step)
        slot = layer * deep_count + deep
        return remote(
            last.at[step],
            last_in.at[slot],
            sends.at[4, step],
            receives.at[4, slot],
            at(across, core, target, side),
        )

    def fourth_in(layer, hop):
        source = nearest(deep, deep_count, hop)
        slot = layer * deep_count + source
        return (
            slot,
            remote(
                last_in.at[slot],
                last_in.at[slot],
                sends.at[4, slot],
                receives.at[4, slot],
                at(across, core, source, side),
            ),
        )

    def fifth(layer, incoming):
        lane = 2 * core + (1 - across if incoming else across)
        piece = total.at[layer, :, lanes(lane)]
        to = at(1 - across, core, deep, side)
        return remote(piece, piece, sends.at[5, layer], receives.at[5, layer], to)

    def sixth(layer, incoming):
        column = 1 - core if incoming else core
        piece = total.at[layer, :, lanes(2 * column, 2)]
        to = at(across, 1 - core, deep, side)
        return remote(piece, piece, sends.at[6, layer], receives.at[6, layer], to)

    def run(low, high, action):
        def body(step, carry):
            action(step)
            return carry

        lax.fori_loop(low, high, body, 0)

    half_block = LANES // 2

    def stat_side(layer, incoming):
        rows = pl.ds(pl.multiple_of((1 - side) * half_block, half_block), half_block)
        return remote(
            stat_own.at[layer, rows],
            stat_in.at[layer],
            stat_sends.at[0, layer],
            stat_receives.at[0, layer],
            at(across, core, deep, 1 - side),
        )

    def stat_along(layer, hop):
        return remote(
            stat_deep.at[layer, deep],
            stat_deep.at[layer, deep],
            deep_sends.at[layer, hop],
            deep_receives.at[layer, hop],
            at(across, core, lax.rem(deep + hop, deep_count), side),
        )

    def stat_along_in(layer, hop):
        source = lax.rem(deep - hop + deep_count, deep_count)
        return remote(
            stat_deep.at[layer, source],
            stat_deep.at[layer, source],
            deep_sends.at[layer, hop],
            deep_receives.at[layer, hop],
            at(across, core, deep, side),
        )

    def half_rows(which):
        return pl.ds(pl.multiple_of(which * half_block, half_block), half_block)

    def stat_spread(which, layer, incoming):
        if which < 3:
            other_side = side if which == 1 else 1 - side
            other_across = across if which == 0 else 1 - across
            to = at(other_across, core, deep, other_side)
            if incoming:
                piece = stats.at[layer, 2 * core + other_across, half_rows(other_side)]
            else:
                piece = stats.at[layer, block, half_rows(side)]
        else:
            to = at(across, 1 - core, deep, side)
            piece = stats.at[layer, pl.ds(2 * (1 - core if incoming else core), 2)]
        slot = 1 + which
        return remote(piece, piece, stat_sends.at[slot, layer], stat_receives.at[slot, layer], to)

    def vector_step(which):
        to = (
            at(across, 1 - core, deep, side),
            at(1 - across, core, deep, side),
            at(across, core, deep, 1 - side),
        )[which]
        return remote(
            vector_out.at[which],
            vector_in.at[which],
            vector_sends.at[which],
            vector_receives.at[which],
            to,
        )

    def vector_along(hop):
        return remote(
            vector_deep.at[deep],
            vector_deep.at[deep],
            vector_sends.at[2 + hop],
            vector_receives.at[2 + hop],
            at(across, core, lax.rem(deep + hop, deep_count), side),
        )

    def vector_along_in(hop):
        source = lax.rem(deep - hop + deep_count, deep_count)
        return remote(
            vector_deep.at[source],
            vector_deep.at[source],
            vector_sends.at[2 + hop],
            vector_receives.at[2 + hop],
            at(across, core, deep, side),
        )

    def go_first(step):
        load(step).start()
        first(step).start()

    ahead = min(3, steps)
    piece_rows = 144 if total.shape[1] % 144 == 0 else total.shape[1]
    states = (
        (first_in, moment_one, first_out),
        (second_moment_in, moment_two, second_out),
        (master_in, master, master_out),
    )

    def load_state(which, layer):
        source, target, unused = states[which]
        return pltpu.make_async_copy(
            source.at[layer], target.at[layer], state_loads.at[which, layer]
        )

    def store_state(which, layer):
        unused, source, target = states[which]
        return pltpu.make_async_copy(
            source.at[layer], target.at[layer], state_stores.at[which, layer]
        )

    greet(partners(deep_count) + [at(1 - across, core, deep, 1 - side)])
    run(0, ahead, go_first)
    for layer in range(layers):
        for which in range(3):
            load_state(which, layer).start()

    def wide(left, right):
        return left.astype(jnp.float32) + right.astype(jnp.float32)

    def go_second(step):
        @pl.when(step + ahead < steps)
        def start_next():
            go_first(step + ahead)

        load(step).wait()
        first(step).wait_recv()
        mine[step] = wide(mine[step], core_in[step]).astype(jnp.bfloat16)
        second(step, 0).start()
        second(step, 1).start()

    def go_third(step):
        layer, hop, target, odd = split(step)
        for half in range(2):
            second(step, half).wait_recv()
            keep_side = (1 - odd) * half + odd * side
            keep_lane = (1 - odd) * across + odd * half
            kept[step, half] = wide(
                mine[step, keep_side, :, lanes(keep_lane)], second_in[step, half]
            ).astype(jnp.bfloat16)
        third(step).start()

    def go_fourth(step):
        layer, hop, target, odd = split(step)
        third(step).wait_recv()
        keep = (1 - odd) * side + odd * across
        last[step] = wide(kept[step, keep], third_in[step]).astype(jnp.bfloat16)

        @pl.when(hop > 0)
        def unused():
            fourth(step).start()

    def close(layer):
        acc[...] = last[layer * deep_count + deep_count - 1].astype(jnp.float32)

        def add(hop):
            slot, copy = fourth_in(layer, hop)
            copy.wait_recv()
            acc[...] += last_in[slot].astype(jnp.float32)

        run(1, deep_count, add)
        total[layer, :, lanes(block)] = acc[...].astype(jnp.bfloat16)
        fifth(layer, False).start()

    def spread(layer):
        fifth(layer, True).wait_recv()
        sixth(layer, False).start()

    def measure(layer):
        sixth(layer, True).wait_recv()
        own_lanes = total[layer, :, lanes(block)]
        stat_own[layer] = lax.dot_general(
            own_lanes,
            total[layer],
            (((0,), (0,)), ((), ())),
            preferred_element_type=jnp.float32,
        ).astype(jnp.bfloat16)
        stat_side(layer, False).start()

    def pair(layer):
        stat_side(layer, True).wait_recv()
        stat_deep[layer, deep] = wide(
            stat_own[layer, half_rows(side)], stat_in[layer]
        ).astype(jnp.bfloat16)
        run(1, deep_count, lambda hop: stat_along(layer, hop).start())

    def settle(layer):
        run(1, deep_count, lambda hop: stat_along_in(layer, hop).wait_recv())
        whole = stat_deep[layer, 0].astype(jnp.float32)
        for source in range(1, deep_count):
            whole += stat_deep[layer, source].astype(jnp.float32)
        stats[layer, block, half_rows(side)] = whole.astype(jnp.bfloat16)
        for which in range(3):
            stat_spread(which, layer, False).start()

    def share_core(layer):
        for which in range(3):
            stat_spread(which, layer, True).wait_recv()
        stat_spread(3, layer, False).start()

    def refresh(layer):
        for which in range(3):
            load_state(which, layer).wait()
        high, rest = halves(bases[layer])

        def one_piece(index):
            here = pl.ds(pl.multiple_of(index * piece_rows, piece_rows), piece_rows)
            given = total[layer, here, :]
            rotated = mix(given, high, 1, 0) + mix(given, rest, 1, 0)
            first_new, second_new, direction = moments(
                rotated, moment_one[layer, here, :], moment_two[layer, here, :]
            )
            moment_one[layer, here, :] = first_new
            moment_two[layer, here, :] = second_new
            up, down = halves(direction)
            back = mix(up, high, 1, 1) + (mix(up, rest, 1, 1) + mix(down, high, 1, 1))
            old = master[layer, here, :]
            master[layer, here, :] = old - RATE_CONV * (back + DECAY * old)

        run(0, total.shape[1] // piece_rows, one_piece)
        for which in range(3):
            store_state(which, layer).start()

    def finish(layer):
        stat_spread(3, layer, True).wait_recv()
        fifth(layer, False).wait_send()
        sixth(layer, False).wait_send()
        stat_side(layer, False).wait_send()
        run(1, deep_count, lambda hop: stat_along(layer, hop).wait_send())
        for which in range(4):
            stat_spread(which, layer, False).wait_send()
        for which in range(3):
            store_state(which, layer).wait()

    def vector_next(which):
        vector_step(which).wait_recv()
        summed = vector_out[which] + vector_in[which]
        if which < 2:
            vector_out[which + 1] = summed
            vector_step(which + 1).start()
        else:
            vector_deep[deep] = summed
            run(1, deep_count, lambda hop: vector_along(hop).start())

    chunk_work = ((0, go_second), (2, go_third), (3, go_fourth))
    layer_work = (
        (4, close),
        (5, spread),
        (6, measure),
        (7, pair),
        (8, refresh),
        (9, settle),
        (10, share_core),
        (11, finish),
    )
    vector_out[0] = vector[...]
    vector_step(0).start()

    def turn(now):
        for lag, action in chunk_work:

            @pl.when(jnp.logical_and(now >= lag, now < steps + lag))
            def chunk():
                action(now - lag)

        for which in range(3):

            @pl.when(now == 2 * which + 1)
            def exchange():
                vector_next(which)

        for lag, action in layer_work:
            past = now - lag - (deep_count - 1)

            @pl.when(
                jnp.logical_and(
                    jnp.logical_and(past >= 0, past < steps), lax.rem(past, deep_count) == 0
                )
            )
            def whole_layer():
                action(past // deep_count)

    run(0, steps + layer_work[-1][0], turn)

    run(1, deep_count, lambda hop: vector_along_in(hop).wait_recv())
    summed = vector_deep[0]
    for source in range(1, deep_count):
        summed += vector_deep[source]
    vector_total[...] = summed
    for which in range(3):
        vector_step(which).wait_send()
    run(1, deep_count, lambda hop: vector_along(hop).wait_send())

    def drain(step):
        layer, hop, target, odd = split(step)
        first(step).wait_send()
        second(step, 0).wait_send()
        second(step, 1).wait_send()
        third(step).wait_send()

        @pl.when(hop > 0)
        def unused():
            fourth(step).wait_send()

    run(0, steps, drain)


def reduce_grads(grads, vector, bases, conv, space_count):
    layers, all_rows, columns = grads.shape
    deep_count, rows = space_count // 2, all_rows // space_count
    steps = layers * deep_count
    low = jnp.bfloat16
    blocks = columns // LANES
    vmem = pl.BlockSpec(memory_space=pltpu.VMEM)
    tall = jax.ShapeDtypeStruct((layers, rows, columns), jnp.float32)
    anywhere = pl.BlockSpec(memory_space=pl.ANY)
    total, stats, vector_total, *conv_new = pl.pallas_call(
        partial(reduce_kernel, layers, deep_count),
        out_shape=(
            jax.ShapeDtypeStruct((layers, rows, columns), low),
            jax.ShapeDtypeStruct((layers, blocks, LANES, columns), low),
            jax.ShapeDtypeStruct(vector.shape, jnp.float32),
            tall,
            tall,
            tall,
        ),
        in_specs=[anywhere, vmem, vmem] + [anywhere] * 3,
        out_specs=[vmem] * 3 + [anywhere] * 3,
        scratch_shapes=[
            pltpu.VMEM((steps, 2, rows, 2 * LANES), low),
            pltpu.VMEM((steps, 2, rows, 2 * LANES), low),
            pltpu.VMEM((steps, 2, rows, LANES), low),
            pltpu.VMEM((steps, 2, rows, LANES), low),
            pltpu.VMEM((steps, rows, LANES), low),
            pltpu.VMEM((steps, rows, LANES), low),
            pltpu.VMEM((steps, rows, LANES), low),
            pltpu.VMEM((rows, LANES), jnp.float32),
            pltpu.VMEM((layers, LANES, columns), low),
            pltpu.VMEM((layers, LANES // 2, columns), low),
            pltpu.VMEM((layers, deep_count, LANES // 2, columns), low),
            pltpu.VMEM((3,) + vector.shape, jnp.float32),
            pltpu.VMEM((3,) + vector.shape, jnp.float32),
            pltpu.VMEM((deep_count,) + vector.shape, jnp.float32),
            pltpu.VMEM(tall.shape, jnp.float32),
            pltpu.VMEM(tall.shape, jnp.float32),
            pltpu.VMEM(tall.shape, jnp.float32),
            pltpu.SemaphoreType.DMA((steps,)),
            pltpu.SemaphoreType.DMA((7, steps)),
            pltpu.SemaphoreType.DMA((7, steps)),
            pltpu.SemaphoreType.DMA((5, layers)),
            pltpu.SemaphoreType.DMA((5, layers)),
            pltpu.SemaphoreType.DMA((layers, deep_count)),
            pltpu.SemaphoreType.DMA((layers, deep_count)),
            pltpu.SemaphoreType.DMA((2 + deep_count,)),
            pltpu.SemaphoreType.DMA((2 + deep_count,)),
            pltpu.SemaphoreType.DMA((3, layers)),
            pltpu.SemaphoreType.DMA((3, layers)),
        ],
        compiler_params=pltpu.CompilerParams(
            collective_id=1, has_side_effects=True, vmem_limit_bytes=VMEM_LIMIT
        ),
    )(grads.reshape(layers, deep_count, 2, rows, columns), vector, bases, *conv)
    return (stats.reshape(layers, columns, columns), vector_total, conv_new)


def work_kernel(
    dims,
    weights_in,
    head_in,
    wide_in,
    hidden_in,
    last_in,
    vectors,
    cotangent_in,
    valid,
    merged,
    features_grad,
    grads_out,
    head_grad,
    vector,
    weights,
    head,
    cotangent,
    wide,
    hidden,
    last,
    last_turned,
    d_wide,
    d_active,
    grads,
    halo,
    term,
    term_in,
    load_sem,
    store_sem,
    send_sem,
    receive_sem,
    term_sends,
    term_receives,
    *head_refs,
):
    layers, rows, width, channels, heads, depth, space_count = dims
    deep_count = space_count // 2
    across, core, deep, side = place()
    spread_head = len(head_refs) > 0
    if spread_head:
        head_parts, core_in, across_in, side_in, deep_in, head_sends, head_receives = head_refs
        head_rows = head_parts.shape[4]
    tile = 2 * LANES
    tiles = channels // tile
    low = jnp.bfloat16

    loads = ((last_in, last), (head_in, head), (cotangent_in, cotangent))
    for layer in reversed(range(layers)):
        loads += (
            (hidden_in.at[layer], hidden.at[layer]),
            (wide_in.at[layer], wide.at[layer]),
            (weights_in.at[layer], weights.at[layer]),
        )

    def load(which):
        source, target = loads[which]
        return pltpu.make_async_copy(source, target, load_sem.at[which])

    for which in range(len(loads)):
        load(which).start()

    others = [
        at(across, 1 - core, deep, side),
        at(1 - across, core, deep, side),
        at(across, core, deep, 1 - side),
    ]
    if spread_head:
        others += [
            at(across, core, lax.rem(deep + hop, deep_count), side) for hop in range(1, deep_count)
        ]
    greet_edges(others, space_count)

    def term_lanes(index, which):
        return pl.ds(pl.multiple_of(index * depth + which * LANES, LANES), LANES)

    def term_step(which, index, incoming=False):
        if which == 0:
            source, target, to = term.at[:, term_lanes(index, 1 - core)], term_in.at[0, index], others[0]
        elif which == 1:
            source, target, to = term.at[:, term_lanes(index, core)], term_in.at[1, index], others[1]
        else:
            source = merged.at[:, term_lanes(index, 1 - core if incoming else core)]
            target, to = source, others[0]
        return remote(
            source, target, term_sends.at[which, index], term_receives.at[which, index], to
        )

    def term_pair(index):
        term_step(0, index).wait_recv()
        lane = term_lanes(index, core)
        both = term[:, lane].astype(jnp.float32) + term_in[0, index].astype(jnp.float32)
        term[:, lane] = both.astype(low)
        term_step(1, index).start()

    def term_total(index):
        term_step(1, index).wait_recv()
        lane = term_lanes(index, core)
        both = term[:, lane].astype(jnp.float32) + term_in[1, index].astype(jnp.float32)
        merged[:, lane] = both.astype(low)
        term_step(2, index).start()

    def term_end(index):
        term_step(2, index, True).wait_recv()
        for which in range(3):
            term_step(which, index).wait_send()

    def head_step(which):
        if which == 0:
            source, target, to = head_parts.at[:, 1 - core], core_in, others[0]
        elif which == 1:
            source = head_parts.at[pl.ds(0, 2), core, pl.ds(0, deep_count), 1 - side]
            target, to = side_in, others[2]
        else:
            source = head_parts.at[1 - across, core, pl.ds(0, deep_count), side]
            target, to = across_in, others[1]
        return remote(source, target, head_sends.at[which], head_receives.at[which], to)

    def head_along(hop):
        target = lax.rem(deep + hop, deep_count)
        return remote(
            head_parts.at[across, core, target, side],
            deep_in.at[hop],
            head_sends.at[2 + hop],
            head_receives.at[2 + hop],
            at(across, core, target, side),
        )

    def head_next(which):
        if not spread_head:
            return
        head_step(which).wait_recv()
        if which == 0:
            for part in range(2):
                both = head_parts[part, core].astype(jnp.float32) + core_in[part].astype(jnp.float32)
                head_parts[part, core] = both.astype(low)
            head_step(1).start()
        elif which == 1:
            for part in range(2):
                both = head_parts[part, core, pl.ds(0, deep_count), side].astype(jnp.float32)
                both += side_in[part].astype(jnp.float32)
                head_parts[part, core, pl.ds(0, deep_count), side] = both.astype(low)
            head_step(2).start()
        else:
            both = head_parts[across, core, pl.ds(0, deep_count), side].astype(jnp.float32)
            both += across_in[...].astype(jnp.float32)
            head_parts[across, core, pl.ds(0, deep_count), side] = both.astype(low)
            for hop in range(1, deep_count):
                head_along(hop).start()

    def head_end():
        if not spread_head:
            return
        whole = head_parts[across, core, deep, side].astype(jnp.float32)
        for hop in range(1, deep_count):
            head_along(hop).wait_recv()
            whole += deep_in[hop].astype(jnp.float32)
        blocks = heads * depth // LANES
        for lane in range(blocks):
            head_grad[pl.ds(lane, head_rows, stride=blocks), :] = whole[
                :, lane * LANES : (lane + 1) * LANES
            ]
        for which in range(3):
            head_step(which).wait_send()
        for hop in range(1, deep_count):
            head_along(hop).wait_send()

    send_edges, take_edges, put = edge_tools(dims, halo, send_sem, receive_sem)

    def loop(count, action):
        def body(index, carry):
            action(index)
            return carry

        lax.fori_loop(0, count, body, 0)

    def spot(index):
        return pl.multiple_of(index * tile, tile)

    masks, weights_row = row_weights(valid, rows)

    def put_vector(start, part, value):
        row = start // LANES + 2 * part
        vector[pl.ds(row, 1), :] = value[:, :LANES]
        vector[pl.ds(row + 1, 1), :] = value[:, LANES:]

    pixels = rows * width
    for which in range(3):
        load(which).wait()
    last_turned[...] = last[...].astype(jnp.float32).T.astype(low)
    d_active[...] = jnp.zeros_like(d_active)

    def one_head(index):
        lane = pl.ds(pl.multiple_of(index * depth, depth), depth)
        projected = mix(last[...], head[:, lane], 1, 0)
        projected += vector_lanes(vectors, layers * channels, index)
        gain = vector_lanes(vectors, layers * channels + heads * depth, index)
        gain_total = jnp.zeros((1, depth), jnp.float32)
        bias_total = jnp.zeros((1, depth), jnp.float32)
        rounded = []
        for row in range(rows):
            span = slice(row * width, (row + 1) * width)
            weight = weights_row[row]
            value = projected[span]
            inverse = lax.rsqrt(jnp.sum(value * value, -1, keepdims=True) + 1e-06)
            normed = value * inverse
            scaled = gain * weight
            term[span, lane] = (normed * scaled).astype(low)
            given = cotangent[span, lane].astype(jnp.float32)
            gain_total += jnp.sum(normed * given, 0, keepdims=True) * weight
            d_normed = given * scaled
            along = jnp.sum(normed * d_normed, -1, keepdims=True)
            d_low = (inverse * (d_normed - normed * along)).astype(low)
            bias_total += jnp.sum(d_low.astype(jnp.float32), 0, keepdims=True)
            rounded.append(d_low)
        term_step(0, index).start()
        put_vector(layers * channels + heads * depth, index, gain_total)
        put_vector(layers * channels, index, bias_total)
        d_low = jnp.concatenate(rounded, 0)
        grad = mix(last_turned[...], d_low, 1, 0)
        if spread_head:
            split = grad.reshape(2, 2, deep_count, 2, head_rows, depth)
            head_parts[:, :, :, :, :, lane] = split.astype(low)
        else:
            head_grad[:, lane] = grad.astype(low)
        d_active[...] += mix(d_low, head[:, lane], 1, 1)

        @pl.when(index > 0)
        def earlier():
            term_pair(index - 1)

    loop(heads, one_head)
    if spread_head:
        head_step(0).start()
    term_pair(heads - 1)

    def store(layer):
        slot = layer % 2
        return pltpu.make_async_copy(grads.at[slot], grads_out.at[layer], store_sem.at[slot])

    for layer in reversed(range(layers)):
        which = layers - 1 - layer
        for part in range(3):
            load(3 + 3 * which + part).wait()

        def enter(part):
            lane = pl.ds(spot(part), tile)
            total = jnp.zeros((1, tile), jnp.float32)
            for row in range(rows):
                span = slice(row * width, (row + 1) * width)
                slope = gelu_slope(hidden[layer, span, lane])
                value = slope * (masks[row] * d_active[span, lane])
                value = value.astype(low).astype(jnp.float32)
                total += jnp.sum(value, 0, keepdims=True)
                put(d_wide, row + 1, spot(part), tile, value)
            put_vector(layer * channels, part, total)

        loop(tiles, enter)
        send_edges(which, d_wide)
        if layer + 2 < layers:
            store(layer + 2).wait()

        def one_tap(tap):
            tap_row, tap_column = tap // TAPS, lax.rem(tap, TAPS)
            window = wide[
                layer,
                pl.ds(pl.multiple_of(tap_row * width, width), pixels),
                pl.ds(pl.multiple_of(tap_column * channels, channels), channels),
            ]
            d_hidden = d_wide[width : width + pixels, channels : 2 * channels]
            grads[layer % 2, pl.ds(pl.multiple_of(tap * channels, channels), channels), :] = mix(
                window, d_hidden, 0, 0
            ).astype(low)

        loop(TAPS * TAPS, one_tap)
        store(layer).start()
        head_next(layers - 1 - layer)
        if layer == 0:
            loop(heads, term_total)
        take_edges(which, d_wide)

        def back(part):
            total = jnp.zeros((pixels, tile), jnp.float32)
            for tap_row in range(TAPS):
                for tap_column in range(TAPS):
                    window = d_wide[
                        (2 - tap_row) * width : (2 - tap_row) * width + pixels,
                        (2 - tap_column) * channels : (3 - tap_column) * channels,
                    ]
                    first = (TAPS * tap_row + tap_column) * channels
                    total += mix(
                        window, weights[layer, pl.ds(first + spot(part), tile), :], 1, 1
                    )
            d_active[:, pl.ds(spot(part), tile)] = total

        loop(tiles, back)

    features_grad[...] = d_active[...].astype(low)
    head_end()
    loop(heads, term_end)
    for layer in range(min(layers, 2)):
        store(layer).wait()


def run_block(
    weights, head, wide, hidden, last, vectors, cotangent, valid, space_count
):
    rows, width, unused = cotangent.shape
    layers, unused, channels = weights.shape
    head_width = head.shape[1]
    pixels = rows * width
    deep_count = space_count // 2
    head_rows = channels // (4 * space_count)
    spread_head = head_rows % 16 == 0
    low, full = jnp.bfloat16, jnp.float32
    dims = (layers, rows, width, channels, NH, HD, space_count)
    vmem = pl.BlockSpec(memory_space=pltpu.VMEM)
    anywhere = pl.BlockSpec(memory_space=pl.ANY)
    head_scratch = []
    head_out = jax.ShapeDtypeStruct((channels, head_width), low)
    if spread_head:
        head_out = jax.ShapeDtypeStruct((head_rows * head_width // LANES, LANES), full)
        head_scratch = [
            pltpu.VMEM((2, 2, deep_count, 2, head_rows, head_width), low),
            pltpu.VMEM((2, deep_count, 2, head_rows, head_width), low),
            pltpu.VMEM((deep_count, head_rows, head_width), low),
            pltpu.VMEM((2, deep_count, head_rows, head_width), low),
            pltpu.VMEM((deep_count, head_rows, head_width), low),
            pltpu.SemaphoreType.DMA((2 + deep_count,)),
            pltpu.SemaphoreType.DMA((2 + deep_count,)),
        ]
    outs = pl.pallas_call(
        partial(work_kernel, dims),
        out_shape=(
            jax.ShapeDtypeStruct((pixels, head_width), low),
            jax.ShapeDtypeStruct((pixels, channels), low),
            jax.ShapeDtypeStruct(weights.shape, low),
            head_out,
            jax.ShapeDtypeStruct(vectors.shape, full),
        ),
        in_specs=[
            anywhere,
            anywhere,
            anywhere,
            anywhere,
            anywhere,
            vmem,
            anywhere,
            pl.BlockSpec(memory_space=pltpu.SMEM),
        ],
        out_specs=[vmem, vmem, anywhere, vmem, vmem],
        scratch_shapes=[
            pltpu.VMEM(weights.shape, low),
            pltpu.VMEM(head.shape, low),
            pltpu.VMEM((pixels, head_width), low),
            pltpu.VMEM((layers, (rows + 2) * width, TAPS * channels), low),
            pltpu.VMEM((layers, pixels, channels), full),
            pltpu.VMEM((pixels, channels), low),
            pltpu.VMEM((channels, pixels), low),
            pltpu.VMEM(((rows + 2) * width, TAPS * channels), low),
            pltpu.VMEM((pixels, channels), full),
            pltpu.VMEM((2,) + weights.shape[1:], low),
            pltpu.VMEM((layers, 2, width, channels), low),
            pltpu.VMEM((pixels, head_width), low),
            pltpu.VMEM((2, NH, pixels, LANES), low),
            pltpu.SemaphoreType.DMA((3 * layers + 3,)),
            pltpu.SemaphoreType.DMA((2,)),
            pltpu.SemaphoreType.DMA((layers, 2)),
            pltpu.SemaphoreType.DMA((layers, 2)),
            pltpu.SemaphoreType.DMA((3, NH)),
            pltpu.SemaphoreType.DMA((3, NH)),
        ]
        + head_scratch,
        compiler_params=pltpu.CompilerParams(
            collective_id=2, has_side_effects=True, vmem_limit_bytes=VMEM_LIMIT
        ),
    )(
        weights,
        head,
        wide,
        hidden,
        last,
        vectors,
        cotangent.reshape(pixels, head_width),
        valid,
    )
    merged, features_grad, grads, head_grad, vector = outs
    if not spread_head:
        head_grad = lax.psum_scatter(
            head_grad.astype(full).reshape(-1), ("scale", "space"), scatter_dimension=0, tiled=True
        ).reshape(-1, LANES)
    return (merged, features_grad, grads, head_grad, vector)


def halves(value):
    high = value.astype(jnp.bfloat16)
    return (high, (value - high.astype(jnp.float32)).astype(jnp.bfloat16))


def dot(left, right, left_dim, right_dim):
    left_high, left_low = halves(left)
    right_high, right_low = halves(right)
    rest = mix(left_high, right_low, left_dim, right_dim) + mix(left_low, right_high, left_dim, right_dim)
    return mix(left_high, right_high, left_dim, right_dim) + rest


def quick(x):
    return pl.reciprocal(x,approx=True)
def eliminate(blocks, off, size, m=8):
    nl=len(blocks); nb=size//8; W=blocks[0][0].shape[1]
    sub=lax.broadcasted_iota(jnp.int32,(8,128),0)
    for k0 in range(0,size,m):
        b0=k0//8; s0=k0%8
        for l in range(nl):
            bl=blocks[l]
            top=bl[b0]
            def colb(b,j):
                return jnp.broadcast_to(bl[b][:,off+k0+j:off+k0+j+1],(8,128))
            c0=[colb(b0,j) for j in range(m)]
            a=[[None]*m for _ in range(m)]
            for j in range(m):
                for i in range(j,m):
                    a[i][j]=jnp.broadcast_to(c0[j][s0+i:s0+i+1,:],(8,128))
            inv=[]; low=[[None]*m for _ in range(m)]
            for k in range(m):
                r=quick(a[k][k]); inv.append(r)
                for i in range(k+1,m):
                    low[i][k]=a[i][k]*r
                for j in range(k+1,m):
                    for i in range(j,m):
                        a[i][j]=a[i][j]-low[i][k]*a[j][k]
            wid=lambda v: jnp.concatenate([v]*(W//128),1)
            rows=[jnp.broadcast_to(top[s0+i:s0+i+1,:],(8,W)) for i in range(m)]
            for i in range(m):
                for k in range(i):
                    rows[i]=rows[i]-wid(low[i][k])*rows[k]
            for b in range(b0,nb):
                if b==b0 and s0+m==8 and m==1: continue
                cs=list(c0) if b==b0 else [colb(b,j) for j in range(m)]
                for j in range(m):
                    for k in range(j):
                        cs[j]=cs[j]-low[j][k]*cs[k]
                acc=bl[b]
                for k in range(m):
                    w=cs[k]*inv[k]
                    if b==b0: w=jnp.where(sub>s0+k,w,0.0)
                    acc=acc-wid(w)*rows[k]
                bl[b]=acc
    out=[]
    lane=lax.broadcasted_iota(jnp.int32,(8,W),1)
    row8=lax.broadcasted_iota(jnp.int32,(8,W),0)
    for l in range(nl):
        res=[]
        for b in range(nb):
            v=blocks[l][b]
            d=jnp.sum(jnp.where(lane==row8+(off+8*b),v,0.0),1,keepdims=True)
            res.append(v*lax.rsqrt(d))
        out.append(jnp.concatenate(res,0))
    return out


def moments(grads, first, second):
    first_new = BETA_ONE * first + (1.0 - BETA_ONE) * grads
    second_new = BETA_TWO * second + (1.0 - BETA_TWO) * grads * grads
    direction = (
        first_new
        * (1.0 / (1.0 - BETA_ONE**STEP))
        / (jnp.sqrt(second_new * (1.0 / (1.0 - BETA_TWO**STEP))) + EPSILON)
    )
    return (first_new, second_new, direction)


def update_kernel(
    dims,
    *refs,
):
    moved = dims[4]
    inputs, outputs = refs[: moved + 11], refs[moved + 11 : -1 - moved]
    held = refs[-1 - moved : -1]
    update_body(
        dims, inputs[:moved], outputs[:moved], held, refs[-1], *inputs[moved:], *outputs[moved:]
    )


def update_body(
    dims,
    moved_in,
    moved_out,
    held,
    moved_sem,
    summed,
    statistics,
    bases,
    head_grad,
    head_first,
    head_second,
    head_master,
    vector_grad,
    vector_first,
    vector_second,
    vectors,
    stats_new,
    bases_new,
    head_first_new,
    head_second_new,
    head_new,
    vector_first_new,
    vector_second_new,
    vectors_new,
    system,
    pivot_high,
    pivot_rest,
):
    layers, channels, bias_rows, panel, moved = dims
    block = LANES

    def take(which):
        return pltpu.make_async_copy(moved_in[which], held[which], moved_sem.at[0, which])

    def give(which):
        return pltpu.make_async_copy(held[which], moved_out[which], moved_sem.at[1, which])

    for which in range(moved):
        take(which).start()

    for layer in range(layers):
        fresh = BETA_TWO * statistics[layer] + (1.0 - BETA_TWO) * summed[layer].astype(jnp.float32)
        stats_new[layer] = fresh
        turned = dot(bases[layer], fresh, 0, 0)
        system[layer, :, channels : 2 * channels] = turned
        system[layer, :, 0:channels] = dot(turned, turned, 1, 1)

    head = moments(head_grad[...], head_first[...], head_second[...])
    head_first_new[...] = head[0]
    head_second_new[...] = head[1]
    head_new[...] = head_master[...] - RATE_HEAD * (head[2] + DECAY * head_master[...])
    vec = moments(vector_grad[...], vector_first[...], vector_second[...])
    vector_first_new[...] = vec[0]
    vector_second_new[...] = vec[1]
    row = lax.broadcasted_iota(jnp.int32, vectors.shape, 0)
    rates = jnp.where(row < bias_rows, RATE_BIAS, RATE_GAIN)
    vectors_new[...] = vectors[...] - rates * (vec[2] + DECAY * vectors[...])

    for which in range(moved):
        take(which).wait()
        give(which).start()
    eye = (
        lax.broadcasted_iota(jnp.int32, (block, block), 0)
        == lax.broadcasted_iota(jnp.int32, (block, block), 1)
    ).astype(jnp.float32)

    def outer(k, carry):
        here = pl.ds(pl.multiple_of(k * block, block), block)
        panels = [jnp.concatenate([system[layer, here, here], eye], 1) for layer in range(layers)]
        done = [[] for _ in range(layers)]
        for j in range(block // panel):
            blocks = [[p[8 * i : 8 * i + 8] for i in range(panel // 8)] for p in panels]
            tops = eliminate(blocks, panel * j, panel)
            for layer in range(layers):
                done[layer].append(tops[layer][:, block:])
                if j < block // panel - 1:
                    panels[layer] = panels[layer][panel:] - dot(
                        tops[layer][:, panel * (j + 1) : block], tops[layer], 0, 0
                    )
        half = channels // 2
        spans = (slice(0, half), slice(half, channels), slice(channels, 2 * channels))
        after = (k + 1) * block
        split_inverse = [halves(jnp.concatenate(parts, 0)) for parts in done]

        def eliminated(span):
            for layer in range(layers):
                high, rest = split_inverse[layer]
                right_high, right_rest = halves(system[layer, here, span])
                value = mix(high, right_high, 1, 0) + (
                    mix(high, right_rest, 1, 0) + mix(rest, right_high, 1, 0)
                )
                pivot_high[layer, :, span], pivot_rest[layer, :, span] = halves(value)
                if span is spans[2]:
                    system[layer, here, span] = value

        eliminated(spans[2])

        @pl.when(after < channels)
        def right_half():
            eliminated(spans[1])

        @pl.when(after < half)
        def left_half():
            eliminated(spans[0])

        def inner(i, carry_in):
            below = pl.ds(pl.multiple_of(i * block, block), block)

            def subtract(span):
                for layer in range(layers):
                    left_high, left_rest = pivot_high[layer, :, below], pivot_rest[layer, :, below]
                    right_high, right_rest = pivot_high[layer, :, span], pivot_rest[layer, :, span]
                    system[layer, below, span] -= mix(left_high, right_high, 0, 0) + (
                        mix(left_high, right_rest, 0, 0) + mix(left_rest, right_high, 0, 0)
                    )

            subtract(slice(half, 2 * channels))

            @pl.when(i * block < half)
            def left_half():
                subtract(spans[0])

            return carry_in

        lax.fori_loop(k + 1, channels // block, inner, 0)
        return carry

    lax.fori_loop(0, channels // block, outer, 0)
    for layer in range(layers):
        bases_new[layer] = system[layer, :, channels : 2 * channels].T
    for which in range(moved):
        give(which).wait()


def update(arrays, summed, statistics, bases, head, vector, bias_rows):
    layers, channels, unused = statistics.shape
    dims = (layers, channels, bias_rows, 32, len(arrays))
    anywhere = pl.BlockSpec(memory_space=pl.ANY)
    vmem = pl.BlockSpec(memory_space=pltpu.VMEM)
    square = jax.ShapeDtypeStruct(statistics.shape, jnp.float32)
    head_shape = jax.ShapeDtypeStruct(head[0].shape, jnp.float32)
    vector_shape = jax.ShapeDtypeStruct(vector[0].shape, jnp.float32)
    return pl.pallas_call(
        partial(update_kernel, dims),
        out_shape=tuple(jax.ShapeDtypeStruct(array.shape, array.dtype) for array in arrays)
        + (square,) * 2 + (head_shape,) * 3 + (vector_shape,) * 3,
        in_specs=[anywhere] * len(arrays) + [vmem] * 11,
        out_specs=[anywhere] * len(arrays) + [vmem] * 8,
        scratch_shapes=[
            pltpu.VMEM((layers, channels, 2 * channels), jnp.float32),
            pltpu.VMEM((layers, LANES, 2 * channels), jnp.bfloat16),
            pltpu.VMEM((layers, LANES, 2 * channels), jnp.bfloat16),
        ]
        + [pltpu.VMEM(array.shape, array.dtype) for array in arrays]
        + [pltpu.SemaphoreType.DMA((2, len(arrays)))],
        compiler_params=pltpu.CompilerParams(vmem_limit_bytes=VMEM_LIMIT),
        cost_estimate=pl.CostEstimate(
            flops=10**10, bytes_accessed=2 * 10**7, transcendentals=10**4
        ),
    )(*arrays, summed, statistics, bases, *head, *vector)


def local(
    features,
    valid_rows,
    conv_master,
    head_master,
    vectors,
    conv_first,
    conv_second,
    head_first,
    head_second,
    vec_first,
    vec_second,
    statistics,
    bases,
    cotangent,
):
    channels = features.shape[3]
    head_width = cotangent.shape[2]
    space_count = lax.axis_size("space")
    vectors, vec_first, vec_second, head_master, head_first, head_second = (
        array.reshape(-1, LANES)
        for array in (vectors, vec_first, vec_second, head_master, head_first, head_second)
    )
    conv_used, head_used, wide, hidden, last = gather_weights(
        conv_master, head_master, head_width, features[0], vectors, valid_rows, space_count
    )
    merged, features_grad, grads, owned_head, vector = run_block(
        conv_used,
        head_used,
        wide,
        hidden,
        last,
        vectors,
        cotangent,
        valid_rows,
        space_count,
    )
    summed_stats, grad_vec, conv_new = reduce_grads(
        grads, vector, bases, (conv_first, conv_second, conv_master), space_count
    )
    moved = (merged, features_grad, *conv_new)
    outs = update(
        moved,
        summed_stats,
        statistics,
        bases,
        (owned_head, head_first, head_second, head_master),
        (grad_vec, vec_first, vec_second, vectors),
        (3 * channels + head_width) // LANES,
    )
    merged, features_grad, *conv_new = outs[:5]
    stats_new, bases_new = outs[5:7]
    return (
        merged.reshape(cotangent.shape),
        features_grad.reshape(features.shape),
        *conv_new,
        *(out.reshape(-1) for out in outs[7:]),
        stats_new,
        bases_new,
    )


def solution(mesh):
    in_specs = (
        P("scale", "space", None, None),
        P(),
        P(None, "space", None),
        P(("scale", "space")),
        P(),
        P(None, "space", None),
        P(None, "space", None),
        P(("scale", "space")),
        P(("scale", "space")),
        P(),
        P(),
        P(),
        P(),
        P("space", None, None),
    )
    out_specs = (
        P("space", None, None),
        P("scale", "space", None, None),
        P(None, "space", None),
        P(None, "space", None),
        P(None, "space", None),
        P(("scale", "space")),
        P(("scale", "space")),
        P(("scale", "space")),
        P(),
        P(),
        P(),
        P(),
        P(),
    )
    return jax.shard_map(local, mesh=mesh, in_specs=in_specs, out_specs=out_specs, check_vma=False)
```
